32 devices in a mesh: wide: 8 (over y, x, core), narrow: 4 (over z).
Axes of the slice: x: 2, y: 2, z: 4, core: 2. Of those that a mesh axis runs over, the one named last changes fastest.
Arguments:
- inputs: bfloat16 [8, 1088, 1024], P('wide', 'narrow'), may hold values from -6 to 6
- w_qkv: bfloat16 [1024, 3072], P('narrow'), may hold values from -0.1875 to 0.1875
- w_out: bfloat16 [1024, 1024], P('narrow'), may hold values from -0.1875 to 0.1875
- w_fc1: bfloat16 [1024, 4096], P('narrow'), may hold values from -0.1875 to 0.1875
- w_fc2: bfloat16 [4096, 1024], P('narrow'), may hold values from -0.09375 to 0.09375
- norm_gain: bfloat16 [4, 1024], P(None, 'narrow'), may hold values from 0.5 to 1.5
- shifts: bfloat16 [12, 1024], P(None, 'narrow'), may hold values from -3 to 3
- text_len: int32 [8], P('wide'), may hold values from 1 to 64, as said below
- cotangent: bfloat16 [8, 1088, 1024], P('wide', 'narrow'), may hold values from -6 to 6
Outputs:
- activations: bfloat16 [8, 1088, 1024], P('wide', 'narrow')
- input_grad: bfloat16 [8, 1088, 1024], P('wide', 'narrow')
- grad_qkv: float32 [1024, 3072], P('narrow')
- grad_out: float32 [1024, 1024], P('narrow')
- grad_fc1: float32 [1024, 4096], P('narrow')
- grad_fc2: float32 [4096, 1024], P('narrow')
- grad_gain: float32 [4, 1024], P(None, 'narrow')
- grad_shift: float32 [12, 1024], P(None, 'narrow')
The draws below stay inside these ranges and needn't reach their ends.
Inputs may be any that keep to these rules, and one draw needn't show every extreme that they name: Text positions from text_len to 63 are padding that no query reads; the first item has 64 and the last has 1.
All inputs are finite; a program needn't handle non-finite values.
Results may differ from the reference program's by a relative error of at most 0.014.
Values may be sent and summed in bfloat16 or wider, within the bound.
A program may use at most 192 MiB of HBM per device.

```python
import math
import jax
import jax.numpy as jnp
from jax import lax

D = 1024
FF = 4096
HEADS = 16
SEQ = 1088
TEXT = 64
ALL_ITEMS = 8


def draw_text_len(key, part):
    key = jax.random.fold_in(key, 7)
    drawn = jax.random.randint(key, (ALL_ITEMS,), 1, TEXT + 1)
    return drawn.at[0].set(TEXT).at[ALL_ITEMS - 1].set(1).astype(jnp.int32)


def level_of(stream_key, shape, pieces, smallest, high):
    def one(dim, parts):
        steps = jax.random.uniform(jax.random.fold_in(jax.random.fold_in(stream_key, 6), dim), (parts,), jnp.float32, smallest / len(pieces), high / len(pieces))
        return jnp.repeat(jnp.exp(steps), shape[dim] // parts).reshape((-1,) + (1,) * (len(shape) - dim - 1))

    factor_of = one(*pieces[0])
    for cut in pieces[1:]:
        factor_of = factor_of * one(*cut)
    return factor_of


def gaussian(stream_key, extent, scale, bound, pieces=(), held_as=jnp.bfloat16):
    level = level_of(stream_key, extent, pieces, -0.22, 0.18) if pieces else 1.0
    values = jax.random.normal(stream_key, extent, jnp.float32) * scale * level
    return jnp.minimum(jnp.maximum(values, -bound), bound).astype(held_as)


def setup_inputs(seed: int = 0) -> dict:
    keys = jax.random.split(jax.random.key(seed), 10)
    return {
        "inputs": gaussian(keys[0], (ALL_ITEMS, SEQ, D), 1.0, 6.0, ((0, 8), (1, 4))),
        "w_qkv": gaussian(keys[1], (D, 3 * D), D ** -0.5, 0.1875, ((0, 4),)),
        "w_out": gaussian(keys[2], (D, D), D ** -0.5, 0.1875, ((0, 4),)),
        "w_fc1": gaussian(keys[3], (D, FF), D ** -0.5, 0.1875, ((0, 4),)),
        "w_fc2": gaussian(keys[4], (FF, D), FF ** -0.5, 0.09375, ((0, 4),)),
        "norm_gain": jnp.clip(1.0 + 0.1 * jax.random.normal(keys[5], (4, D), jnp.float32), 0.5, 1.5).astype(jnp.bfloat16),
        "shifts": gaussian(keys[6], (12, D), 0.5, 3.0, ((1, 4),)),
        "text_len": draw_text_len(jax.random.fold_in(keys[9], 71), 0),
        "cotangent": gaussian(keys[8], (ALL_ITEMS, SEQ, D), 1.0, 6.0, ((0, 8), (1, 4))),
    }


norm_eps = 1e-05
relax_alpha = 32.0
masked_fill = -1e+30
highest = lax.Precision.HIGHEST

@jax.custom_vjp
def low(v):
    return lax.optimization_barrier(v.astype(jnp.bfloat16)).astype(jnp.float32)

@jax.custom_vjp
def low_back(v):
    return v

def low_keep(v):
    return (low(v), None)

def low_pass(kept, grad):
    return (grad,)

def back_keep(v):
    return (v, None)

def back_low(kept, grad):
    return (low(grad),)
low.defvjp(low_keep, low_pass)
low_back.defvjp(back_keep, back_low)

def layer_norm(values, gain, shift):
    average = lax.optimization_barrier(jnp.mean(values, -1, keepdims=True))
    centred = values - average
    spread = lax.optimization_barrier(jnp.mean(centred * centred, -1, keepdims=True))
    return centred * lax.rsqrt(spread + norm_eps) * gain + shift

def matmul(left, right):
    return jnp.dot(left, right, precision=highest, preferred_element_type=jnp.float32)

def forward(inputs, w_qkv, w_out, w_fc1, w_fc2, norm_gain, shifts, text_len):
    length, model_width = inputs.shape
    head_size = model_width // HEADS
    normed = low(layer_norm(inputs, norm_gain[0], shifts[0]))
    joined = matmul(normed, w_qkv)
    queries = low(low_back(joined[:, :model_width] + shifts[4]))
    key_rows = low(low_back(joined[:, model_width:2 * model_width]))
    value_rows = low(low_back(joined[:, 2 * model_width:] + shifts[5]))
    raw = low_back(jnp.einsum('qhe,khe->hqk', queries.reshape(length, HEADS, head_size), key_rows.reshape(length, HEADS, head_size), precision=highest))
    position = jnp.arange(length, dtype=jnp.int32)
    allowed = (position[None, :] <= position[:, None]) & ((position[None, :] >= TEXT) | (position[None, :] < text_len))
    scaled = jnp.where(allowed[None], raw * (1.0 / (relax_alpha * math.sqrt(head_size))), masked_fill)
    row_top = lax.optimization_barrier(jnp.max(scaled, -1, keepdims=True))
    weights_exp = jnp.exp((scaled - row_top) * relax_alpha)
    probs = low(weights_exp / lax.optimization_barrier(jnp.sum(weights_exp, -1, keepdims=True)))
    attended = jnp.einsum('hqk,khe->qhe', probs, value_rows.reshape(length, HEADS, head_size), precision=highest).reshape(length, model_width)
    attended = low(low_back(attended))
    branch = low_back(matmul(attended, w_out) + shifts[6])
    middle = inputs + layer_norm(branch, norm_gain[1], shifts[1])
    normed_mid = low(layer_norm(middle, norm_gain[2], shifts[2]))
    hidden = low_back(matmul(normed_mid, w_fc1) + shifts[8:12].reshape(-1))
    active = low(jax.nn.gelu(hidden))
    mlp_out = low_back(matmul(active, w_fc2) + shifts[7])
    return middle + layer_norm(mlp_out, norm_gain[3], shifts[3])

def reference(inputs, w_qkv, w_out, w_fc1, w_fc2, norm_gain, shifts, text_len, cotangent):
    params = tuple((weight.astype(jnp.float32) for weight in (w_qkv, w_out, w_fc1, w_fc2, norm_gain, shifts)))

    def item_step(sums, item):
        item_in, item_cot, item_len = item
        result, pull = jax.vjp(lambda values, *weights: forward(values, *weights, item_len), item_in.astype(jnp.float32), *params)
        pulled = pull(item_cot.astype(jnp.float32))
        sums = tuple((first + second for first, second in zip(sums, pulled[1:])))
        return (sums, (result.astype(jnp.bfloat16), pulled[0].astype(jnp.bfloat16)))
    start = tuple((jnp.zeros(weight.shape, jnp.float32) for weight in params))
    sums, (result, input_grad) = lax.scan(item_step, start, (inputs, cotangent, text_len))
    return (result, input_grad, sums[0], sums[1], sums[2], sums[3], sums[4], sums[5])
```

```python
import functools
import math

import jax
import jax.numpy as jnp
from jax import lax
from jax.experimental import pallas as pl
from jax.experimental.pallas import tpu as pltpu
from jax.sharding import PartitionSpec as P

HEADS = 16
TEXT = 64
EPS = 1e-5
GROUP = 8
MESH = pl.DeviceIdType.MESH
F32 = jnp.float32
BF16 = jnp.bfloat16
ANY = pl.BlockSpec(memory_space=pl.ANY)
VMEM = pl.BlockSpec(memory_space=pltpu.VMEM)
SMEM = pl.BlockSpec(memory_space=pltpu.SMEM)
DMA = pltpu.SemaphoreType.DMA


def at(start, size, step=16):
    return pl.ds(pl.multiple_of(start, step), size)


def place():
    w = lax.axis_index("wide")
    z = lax.axis_index("narrow")
    return w, z, lax.rem(w, 2), lax.rem(lax.div(w, 2), 2), lax.rem(lax.div(w, 4), 2)


def flips(w, core, x, y, j):
    return (
        w
        + (j & 1) * (1 - 2 * core)
        + ((j >> 1) & 1) * (2 - 4 * x)
        + ((j >> 2) & 1) * (4 - 8 * y)
    )


def remote(src, dst, send_sem, recv_sem, device):
    return pltpu.make_async_remote_copy(
        src_ref=src,
        dst_ref=dst,
        send_sem=send_sem,
        recv_sem=recv_sem,
        device_id=device,
        device_id_type=MESH,
    )


def meet(devices):
    barrier = pltpu.get_barrier_semaphore()
    for device in devices:
        pl.semaphore_signal(barrier, inc=1, device_id=device, device_id_type=MESH)
    pl.semaphore_wait(barrier, len(devices))


def dot(left, right):
    return lax.dot_general(left, right, (((1,), (0,)), ((), ())), preferred_element_type=F32)


def dot_nt(left, right):
    return lax.dot_general(left, right, (((1,), (1,)), ((), ())), preferred_element_type=F32)


def dot_tn(left, right):
    return lax.dot_general(left, right, (((0,), (0,)), ((), ())), preferred_element_type=F32)


def norm(values):
    centred = values - jnp.mean(values, -1, keepdims=True)
    inverse = lax.rsqrt(jnp.mean(centred * centred, -1, keepdims=True) + EPS)
    return centred * inverse, inverse


def norm_back(incoming, normed, inverse, gain):
    scaled = incoming * gain
    return inverse * (
        scaled
        - jnp.mean(scaled, -1, keepdims=True)
        - normed * jnp.mean(scaled * normed, -1, keepdims=True)
    )


def rowsum(values):
    return jnp.sum(values, 0, keepdims=True)


def lanes(rows, width, head):
    lane = lax.broadcasted_iota(jnp.int32, (rows, width), 1)
    size = width // 4
    return ((lane >= head * size) & (lane < head * size + size)).astype(F32)


def widths(rows, blocks):
    return [-(-rows * (b + 1) // 128) * 128 for b in range(blocks)]


def attend_kernel(
    NZ,
    x_ref,
    par_ref,
    len_ref,
    wqkv_ref,
    wout_ref,
    wfc1_ref,
    wfc2_ref,
    o4_out,
    h1_out,
    q_out,
    k_out,
    v_out,
    wq_out,
    a_out,
    b_out,
    wo_out,
    par_out,
    p_out,
    par_all,
    par_f,
    stage,
    wq,
    a_ref,
    b_ref,
    wo_ref,
    h1,
    q_s,
    k_s,
    v_s,
    mask_s,
    p_s,
    o_acc,
    o_send,
    o4,
    loc_sem,
    par_s,
    par_r,
    wz_s,
    wz_r,
    wp_s,
    wp_r,
    up_s,
    up_r,
    dn_s,
    dn_r,
    fz_s,
    fz_r,
    fp_s,
    fp_r,
    sib_s,
    sib_r,
    o_s,
    o_r,
    out_sem,
):
    R, D = x_ref.shape
    C = D // NZ
    FH = wfc1_ref.shape[1] // (2 * NZ)
    w, z, core, x, y = place()
    chip = x + 2 * y
    w8 = core + 2 * chip
    near = {j: flips(w, core, x, y, j) for j in range(1, GROUP)}
    zto = [lax.rem(z + j, NZ) for j in range(NZ)]
    zfrom = [lax.rem(z + NZ - j, NZ) for j in range(NZ)]
    hops = range(1, NZ)
    pending = []

    meet([(w, zto[j]) for j in hops] + [(near[j], z) for j in range(1, GROUP)])

    def go(copy):
        copy.start()
        pending.append(copy)

    for j in hops:
        go(remote(par_ref, par_all.at[z], par_s.at[j], par_r.at[j], (w, zto[j])))
    own_par = pltpu.make_async_copy(par_ref, par_all.at[z], loc_sem.at[0])
    own_par.start()

    staged = []
    for d in range(NZ):
        for t in range(3):
            copy = pltpu.make_async_copy(
                wqkv_ref.at[:, pl.ds(t * D + d * C, C)],
                stage.at[d, :, pl.ds(t * C, C)],
                loc_sem.at[1 + 3 * d + t],
            )
            copy.start()
            staged.append(copy)
    local = 1 + 3 * NZ
    owned = []
    for j in range(NZ):
        owned.append(
            pltpu.make_async_copy(
                wfc1_ref.at[:, at((2 * j) * FH + core * FH, FH, 128)],
                a_ref.at[at(z * C, C), pl.ds(j * FH, FH)],
                loc_sem.at[local + j],
            )
        )
    owned.append(
        pltpu.make_async_copy(
            wfc2_ref.at[at(core * FH, FH)], b_ref.at[z], loc_sem.at[local + NZ]
        )
    )
    owned.append(
        pltpu.make_async_copy(wout_ref, wo_ref.at[at(z * C, C)], loc_sem.at[local + NZ + 1])
    )
    for copy in owned:
        copy.start()

    normed, _ = norm(x_ref[...].astype(F32))
    for copy in staged:
        copy.wait()
    RW = C // GROUP
    for j in hops:
        go(
            remote(
                stage.at[zto[j], at(w8 * RW, RW)],
                wq.at[at(z * C + w8 * RW, RW)],
                wz_s.at[j],
                wz_r.at[j],
                (w, zto[j]),
            )
        )
    own_wq = pltpu.make_async_copy(stage.at[z], wq.at[at(z * C, C)], loc_sem.at[local + NZ + 2])
    own_wq.start()
    own_par.wait()
    for j in hops:
        remote(
            par_ref, par_all.at[zfrom[j]], par_s.at[j], par_r.at[j], (w, zto[j])
        ).wait_recv()
    for d in range(NZ):
        par_f[:, d * C : (d + 1) * C] = par_all[d].astype(F32)
    h1[at(z * R, R), :] = (normed * par_f[0:1, :] + par_f[4:5, :]).astype(BF16)

    def upward(k):
        block = h1.at[at(jnp.maximum(z - k, 0) * R, R)]
        return remote(block, block, up_s.at[k], up_r.at[k], (w, jnp.minimum(z + 1, NZ - 1)))

    def downward(k):
        block = h1.at[at(jnp.minimum(z + k, NZ - 1) * R, R)]
        return remote(block, block, dn_s.at[k], dn_r.at[k], (w, jnp.maximum(z - 1, 0)))

    def from_below(k):
        block = h1.at[at(jnp.maximum(z - 1 - k, 0) * R, R)]
        return remote(block, block, up_s.at[k], up_r.at[k], (w, jnp.minimum(z + 1, NZ - 1)))

    def from_above(k):
        block = h1.at[at(jnp.minimum(z + 1 + k, NZ - 1) * R, R)]
        return remote(block, block, dn_s.at[k], dn_r.at[k], (w, jnp.maximum(z - 1, 0)))

    def relay(k):
        up, down = upward(k), downward(k)

        @pl.when((z - k >= 0) & (z < NZ - 1))
        def _():
            up.start()

        @pl.when((z + k <= NZ - 1) & (z > 0))
        def _():
            down.start()

    relay(0)

    def piece(kind, source, quarter):
        if kind == 0:
            n = C // 4
            return a_ref.at[at(source * C + quarter * n, n)]
        if kind == 1:
            n = FH // 4
            return b_ref.at[source, at(quarter * n, n)]
        n = C // 8
        return wo_ref.at[at(source * C + core * (C // 2) + quarter * n, n)]

    def fetch(kind):
        for j in hops:
            part = piece(kind, z, chip)
            go(remote(part, part, fz_s.at[kind, j], fz_r.at[kind, j], (w, zto[j])))

    def spread(kind):
        for j in hops:
            part = piece(kind, zfrom[j], chip)
            remote(part, part, fz_s.at[kind, j], fz_r.at[kind, j], (w, zto[j])).wait_recv()
            for t in range(1, 4):
                go(
                    remote(
                        part,
                        part,
                        fp_s.at[kind, j, t],
                        fp_r.at[kind, j, t],
                        (near[2 * t], z),
                    )
                )

    def gathered(kind):
        for j in hops:
            for t in range(1, 4):
                other = (x + (t & 1) * (1 - 2 * x)) + 2 * (y + (t >> 1) * (1 - 2 * y))
                part = piece(kind, zfrom[j], other)
                remote(
                    part, part, fp_s.at[kind, j, t], fp_r.at[kind, j, t], (near[2 * t], z)
                ).wait_recv()

    for copy in owned:
        copy.wait()
    fetch(0)

    for j in hops:
        part = wq.at[at(zfrom[j] * C + w8 * RW, RW)]
        remote(part, part, wz_s.at[j], wz_r.at[j], (w, zto[j])).wait_recv()
        for t in range(1, GROUP):
            go(remote(part, part, wp_s.at[j, t], wp_r.at[j, t], (near[t], z)))
    own_wq.wait()
    for j in hops:
        for t in range(1, GROUP):
            other = near[t] - w + w8
            part = wq.at[at(zfrom[j] * C + other * RW, RW)]
            remote(part, part, wp_s.at[j, t], wp_r.at[j, t], (near[t], z)).wait_recv()

    rows_k = k_s.shape[0]
    total = NZ * R
    if rows_k > total:
        k_s[total:rows_k, :] = jnp.zeros((rows_k - total, C), BF16)
        v_s[total:rows_k, :] = jnp.zeros((rows_k - total, C), BF16)
    bias_q = par_ref[...].astype(F32)[8:9, :]
    bias_v = par_ref[...].astype(F32)[9:10, :]

    def project(block):
        rows = at(block * R, R)
        q_s[rows, :] = (dot(h1[rows, :], wq[:, 0:C]) + bias_q).astype(BF16)
        k_s[rows, :] = dot(h1[rows, :], wq[:, C : 2 * C]).astype(BF16)
        v_s[rows, :] = (dot(h1[rows, :], wq[:, 2 * C : 3 * C]) + bias_v).astype(BF16)

    project(z)
    for k in range(NZ - 1):
        below, above = from_below(k), from_above(k)

        @pl.when(z - 1 - k >= 0)
        def _():
            below.wait_recv()

        @pl.when(z + 1 + k <= NZ - 1)
        def _():
            above.wait_recv()

        if k + 1 < NZ - 1:
            relay(k + 1)
        if k == 0:
            fetch(1)
            fetch(2)
        if k == 1:
            spread(0)

        @pl.when(z - 1 - k >= 0)
        def _():
            project(z - 1 - k)

        @pl.when(z + 1 + k <= NZ - 1)
        def _():
            project(z + 1 + k)

    outs = []

    def emit(src, dst, sem):
        copy = pltpu.make_async_copy(src, dst, out_sem.at[sem])
        copy.start()
        outs.append(copy)

    emit(h1, h1_out, 0)
    emit(q_s, q_out, 1)
    emit(k_s, k_out, 2)
    emit(v_s, v_out, 3)
    emit(wq, wq_out, 4)
    emit(par_f, par_out, 5)
    spread(1)
    spread(2)

    scale = math.log2(math.e) / math.sqrt(C // 4)
    text_len = len_ref[0]
    for b, width in enumerate(widths(R, NZ)):
        row = lax.broadcasted_iota(jnp.int32, (R, width), 0) + b * R
        col = lax.broadcasted_iota(jnp.int32, (R, width), 1)
        allowed = (col <= row) & ((col >= TEXT) | (col < text_len))
        mask_s[:, :width] = jnp.where(allowed, 0.0, -1e30)
        o_acc[...] = jnp.zeros_like(o_acc)

        @pl.loop(0, 4)
        def _(h):
            pick = lanes(R, C, h)
            q_h = q_s[b * R : (b + 1) * R, :] * pick.astype(BF16)
            s = dot_nt(q_h, k_s[:width, :]) + mask_s[:, :width]
            e = jnp.exp2((s - jnp.max(s, -1, keepdims=True)) * scale)
            p = (e * (1.0 / jnp.sum(e, -1, keepdims=True))).astype(BF16)
            p_s[b, at(h * R, R), :width] = p
            o_acc[...] += dot(p, v_s[:width, :]) * pick

        emit(p_s.at[b, :, pl.ds(0, width)], p_out.at[b, :, pl.ds(0, width)], 6 + b)
        o_send[b * R : (b + 1) * R, :] = o_acc[...].astype(BF16)
        send = remote(
            o_send.at[pl.ds(b * R, R)], o4.at[z], o_s.at[b], o_r.at[z], (w, jnp.int32(b))
        )

        @pl.when(z != b)
        def _():
            send.start()

        @pl.when(z == b)
        def _():
            o4[z] = o_send[b * R : (b + 1) * R, :]

    for kind in range(3):
        gathered(kind)
    for j in hops:
        part = wo_ref.at[at(zfrom[j] * C + core * (C // 2), C // 2)]
        go(remote(part, part, sib_s.at[j], sib_r.at[j], (near[1], z)))
    for d in range(NZ):
        send = remote(
            o_send.at[pl.ds(d * R, R)], o4.at[d], o_s.at[d], o_r.at[d], (w, jnp.int32(d))
        )

        @pl.when(z != d)
        def _():
            send.wait_send()
            send.wait_recv()

    emit(o4, o4_out, 6 + NZ)
    emit(a_ref, a_out, 7 + NZ)
    emit(b_ref, b_out, 8 + NZ)
    for j in hops:
        part = wo_ref.at[at(zfrom[j] * C + (1 - core) * (C // 2), C // 2)]
        remote(part, part, sib_s.at[j], sib_r.at[j], (near[1], z)).wait_recv()
    emit(wo_ref, wo_out, 9 + NZ)
    for k in range(NZ - 1):
        up, down = upward(k), downward(k)

        @pl.when((z - k >= 0) & (z < NZ - 1))
        def _():
            up.wait_send()

        @pl.when((z + k <= NZ - 1) & (z > 0))
        def _():
            down.wait_send()

    for copy in pending:
        copy.wait_send()
    for copy in outs:
        copy.wait()


def attend(NZ, inputs, par, text_len, w_qkv, w_out, w_fc1, w_fc2):
    R, D = inputs.shape
    C = D // NZ
    FH = w_fc1.shape[1] // (2 * NZ)
    T = NZ * R
    wide = widths(R, NZ)[-1]
    shape = jax.ShapeDtypeStruct
    return pl.pallas_call(
        functools.partial(attend_kernel, NZ),
        out_shape=[
            shape((NZ, R, C), BF16),
            shape((T, D), BF16),
            shape((T, C), BF16),
            shape((wide, C), BF16),
            shape((wide, C), BF16),
            shape((D, 3 * C), BF16),
            shape((D, NZ * FH), BF16),
            shape((NZ, FH, D), BF16),
            shape((D, D), BF16),
            shape((16, D), F32),
            shape((NZ, 4 * R, wide), BF16),
        ],
        in_specs=[VMEM, VMEM, SMEM, ANY, ANY, ANY, ANY],
        out_specs=[ANY] * 11,
        scratch_shapes=[
            pltpu.VMEM((NZ, 16, C), BF16),
            pltpu.VMEM((16, D), F32),
            pltpu.VMEM((NZ, C, 3 * C), BF16),
            pltpu.VMEM((D, 3 * C), BF16),
            pltpu.VMEM((D, NZ * FH), BF16),
            pltpu.VMEM((NZ, FH, D), BF16),
            pltpu.VMEM((D, D), BF16),
            pltpu.VMEM((T, D), BF16),
            pltpu.VMEM((T, C), BF16),
            pltpu.VMEM((wide, C), BF16),
            pltpu.VMEM((wide, C), BF16),
            pltpu.VMEM((R, wide), F32),
            pltpu.VMEM((NZ, 4 * R, wide), BF16),
            pltpu.VMEM((R, C), F32),
            pltpu.VMEM((T, C), BF16),
            pltpu.VMEM((NZ, R, C), BF16),
            DMA((4 * NZ + 4,)),
            DMA((NZ,)),
            DMA((NZ,)),
            DMA((NZ,)),
            DMA((NZ,)),
            DMA((NZ, GROUP)),
            DMA((NZ, GROUP)),
            DMA((NZ,)),
            DMA((NZ,)),
            DMA((NZ,)),
            DMA((NZ,)),
            DMA((3, NZ)),
            DMA((3, NZ)),
            DMA((3, NZ, 4)),
            DMA((3, NZ, 4)),
            DMA((NZ,)),
            DMA((NZ,)),
            DMA((NZ,)),
            DMA((NZ,)),
            DMA((10 + NZ,)),
        ],
        compiler_params=pltpu.CompilerParams(
            collective_id=0, has_side_effects=True, vmem_limit_bytes=56 * 2**20
        ),
    )(inputs, par, text_len, w_qkv, w_out, w_fc1, w_fc2)


def feed_kernel(
    NZ,
    x_ref,
    cot_ref,
    o4_ref,
    par_ref,
    a_hbm,
    b_hbm,
    wo_hbm,
    act_ref,
    dmid_ref,
    do_ref,
    ga_out,
    gb_out,
    go_out,
    small_ref,
    wa,
    wb,
    wo,
    h3,
    gate,
    slope,
    dm,
    du,
    part,
    far_m,
    far_h,
    mid_s,
    n2_s,
    n3_s,
    ga,
    gb,
    go_s,
    load_sem,
    send_sem,
    recv_sem,
    out_sem,
):
    R, D = x_ref.shape
    C = D // NZ
    FH = b_hbm.shape[1]
    w, z, core, x, y = place()
    other = (flips(w, core, x, y, 1), z)
    loads = [
        pltpu.make_async_copy(src, dst, load_sem.at[i])
        for i, (src, dst) in enumerate(((wo_hbm, wo), (a_hbm, wa), (b_hbm, wb)))
    ]
    for copy in loads:
        copy.start()
    meet([other])
    swaps = []

    def swap(src, dst, i):
        copy = remote(src, dst, send_sem.at[i], recv_sem.at[i], other)
        copy.start()
        swaps.append(copy)
        return copy

    def param(row):
        return par_ref[row : row + 1, :]

    shift = 4
    mine, theirs = slice(0, R), slice(R, 2 * R)

    loads[0].wait()
    branch = dot(o4_ref[0], wo[0:C, :])
    for s in range(1, NZ):
        branch += dot(o4_ref[s], wo[s * C : (s + 1) * C, :])
    n2, r2 = norm(branch + param(shift + 6))
    mid = x_ref[...].astype(F32) + n2 * param(1) + param(shift + 1)
    n2_s[...] = n2
    mid_s[...] = mid
    n3, r3 = norm(mid)
    n3_s[...] = n3
    h3[mine, :] = (n3 * param(2) + param(shift + 2)).astype(BF16)
    swap_h = swap(h3.at[pl.ds(0, R)], h3.at[pl.ds(R, R)], 0)
    loads[1].wait()

    def hidden(rows):
        for s in range(NZ):
            cols = slice(s * FH, (s + 1) * FH)
            line = par_ref[shift + 8 + s : shift + 9 + s, :]
            bias = jnp.where(core == 0, line[:, :FH], line[:, FH:])
            u = dot(h3[rows, :], wa[:, cols]) + bias
            k = math.sqrt(2.0 / math.pi)
            sq = u * u
            t = jnp.tanh(u * (k + k * 0.044715 * sq))
            half = 0.5 + 0.5 * t
            gate[rows, cols] = (u * half).astype(BF16)
            slope[rows, cols] = (
                half + (0.5 * u) * (1.0 - t * t) * (k + 3.0 * k * 0.044715 * sq)
            ).astype(BF16)

    def contract(rows):
        total = dot(gate[rows, 0:FH], wb[0])
        for s in range(1, NZ):
            total += dot(gate[rows, s * FH : (s + 1) * FH], wb[s])
        return total

    hidden(mine)
    loads[2].wait()
    swap_h.wait_recv()
    hidden(theirs)
    part[0] = contract(theirs).astype(BF16)
    swap_m = swap(part.at[0], far_m, 1)
    m_near = contract(mine)
    swap_m.wait_recv()
    n4, r4 = norm(m_near + far_m[...].astype(F32) + param(shift + 7))
    act_ref[...] = (mid_s[...] + n4 * param(3) + param(shift + 3)).astype(BF16)

    e = cot_ref[...].astype(F32)
    small_ref[...] = jnp.zeros_like(small_ref)
    small_ref[3:4, :] = rowsum(e * n4)
    small_ref[shift + 3 : shift + 4, :] = rowsum(e)
    dm_low = norm_back(e, n4, r4, param(3)).astype(BF16)
    dm[mine, :] = dm_low
    small_ref[shift + 7 : shift + 8, :] = rowsum(dm_low.astype(F32))
    swap_d = swap(dm.at[pl.ds(0, R)], dm.at[pl.ds(R, R)], 2)

    def unhidden(rows):
        for s in range(NZ):
            cols = slice(s * FH, (s + 1) * FH)
            du[rows, cols] = (
                dot_nt(dm[rows, :], wb[s]) * slope[rows, cols].astype(F32)
            ).astype(BF16)

    unhidden(mine)
    swap_d.wait_recv()
    unhidden(theirs)
    part[1] = dot_nt(du[theirs, :], wa[...]).astype(BF16)
    swap_u = swap(part.at[1], far_h, 3)
    outs = []

    def emit(src, dst, i):
        copy = pltpu.make_async_copy(src, dst, out_sem.at[i])
        copy.start()
        outs.append(copy)

    for s in range(NZ):
        cols = slice(s * FH, (s + 1) * FH)
        gb[s] = dot_tn(gate[:, cols], dm[...]).astype(BF16)
    emit(gb, gb_out, 0)
    for s in range(NZ):
        cols = slice(s * FH, (s + 1) * FH)
        ga[:, cols] = dot_tn(h3[...], du[:, cols]).astype(BF16)
        total = rowsum(du[:, cols].astype(F32))
        row = shift + 8 + s
        small_ref[row : row + 1, 0:FH] = jnp.where(core == 0, total, 0.0)
        small_ref[row : row + 1, FH:] = jnp.where(core == 0, 0.0, total)
    emit(ga, ga_out, 1)
    dh3 = dot_nt(du[mine, :], wa[...])
    swap_u.wait_recv()
    dh3 += far_h[...].astype(F32)
    n3 = n3_s[...]
    small_ref[2:3, :] = rowsum(dh3 * n3)
    small_ref[shift + 2 : shift + 3, :] = rowsum(dh3)
    dmid = e + norm_back(dh3, n3, r3, param(2))
    dmid_ref[...] = dmid
    n2 = n2_s[...]
    small_ref[1:2, :] = rowsum(dmid * n2)
    small_ref[shift + 1 : shift + 2, :] = rowsum(dmid)
    da = norm_back(dmid, n2, r2, param(1)).astype(BF16)
    small_ref[shift + 6 : shift + 7, :] = rowsum(da.astype(F32))
    for s in range(NZ):
        do_ref[s] = dot_nt(da, wo[s * C : (s + 1) * C, :]).astype(BF16)
        go_s[s] = dot_tn(o4_ref[s], da).astype(BF16)
    emit(go_s, go_out, 2)
    for copy in swaps:
        copy.wait_send()
    for copy in outs:
        copy.wait()


def feed(NZ, inputs, cotangent, o4, par, wa, wb, wo):
    R, D = inputs.shape
    C = D // NZ
    FH = wb.shape[1]
    shape = jax.ShapeDtypeStruct
    return pl.pallas_call(
        functools.partial(feed_kernel, NZ),
        out_shape=[
            shape((R, D), BF16),
            shape((R, D), F32),
            shape((NZ, R, C), BF16),
            shape((D, NZ * FH), BF16),
            shape((NZ, FH, D), BF16),
            shape((NZ, C, D), BF16),
            shape((16, D), F32),
        ],
        in_specs=[VMEM, VMEM, VMEM, VMEM, ANY, ANY, ANY],
        out_specs=[VMEM, VMEM, VMEM, ANY, ANY, ANY, VMEM],
        scratch_shapes=[
            pltpu.VMEM((D, NZ * FH), BF16),
            pltpu.VMEM((NZ, FH, D), BF16),
            pltpu.VMEM((D, D), BF16),
            pltpu.VMEM((2 * R, D), BF16),
            pltpu.VMEM((2 * R, NZ * FH), BF16),
            pltpu.VMEM((2 * R, NZ * FH), BF16),
            pltpu.VMEM((2 * R, D), BF16),
            pltpu.VMEM((2 * R, NZ * FH), BF16),
            pltpu.VMEM((2, R, D), BF16),
            pltpu.VMEM((R, D), BF16),
            pltpu.VMEM((R, D), BF16),
            pltpu.VMEM((R, D), F32),
            pltpu.VMEM((R, D), F32),
            pltpu.VMEM((R, D), F32),
            pltpu.VMEM((D, NZ * FH), BF16),
            pltpu.VMEM((NZ, FH, D), BF16),
            pltpu.VMEM((NZ, C, D), BF16),
            DMA((3,)),
            DMA((4,)),
            DMA((4,)),
            DMA((3,)),
        ],
        compiler_params=pltpu.CompilerParams(
            collective_id=1, has_side_effects=True, vmem_limit_bytes=58 * 2**20
        ),
    )(inputs, cotangent, o4, par, wa, wb, wo)


def reduce_kernel(
    NZ,
    x_ref,
    dmid_ref,
    par_ref,
    small_in,
    do4_ref,
    wq_ref,
    q_ref,
    k_ref,
    v_ref,
    h1_hbm,
    p_hbm,
    ga_hbm,
    gb_hbm,
    go_hbm,
    dx_ref,
    gb_out,
    ga_out,
    go_out,
    gq_out,
    small_out,
    h1,
    p_s,
    ga,
    gb,
    go_s,
    go_far,
    go_w,
    gq_s,
    gq_far,
    gq_w,
    r1_b,
    r1_a,
    r1_o,
    r1_q,
    r2_b,
    r2_a,
    r2_o,
    r2_q,
    rz_b,
    rz_a,
    rz_o,
    f_b,
    f_a,
    f_o,
    f_q,
    do_all,
    do_st,
    q_st,
    ds_s,
    dq_f,
    dk_f,
    dv_f,
    dqkv,
    dh,
    rel,
    acc,
    s_f,
    s_b,
    s_z,
    s_p,
    s_g,
    load_sem,
    p_sem,
    do_s,
    do_r,
    pair_s,
    pair_r,
    s1_s,
    s1_r,
    s2_s,
    s2_r,
    z_s,
    z_r,
    g_s,
    g_r,
    sib_s,
    sib_r,
    ru_s,
    ru_r,
    rd_s,
    rd_r,
    sz_s,
    sz_r,
    sp_s,
    sp_r,
    out_sem,
):
    R, D = x_ref.shape
    C = D // NZ
    T = NZ * R
    FH = gb.shape[1]
    w, z, core, x, y = place()
    near = {j: flips(w, core, x, y, j) for j in range(1, GROUP)}
    zto = [lax.rem(z + j, NZ) for j in range(NZ)]
    zfrom = [lax.rem(z + NZ - j, NZ) for j in range(NZ)]
    hops = range(1, NZ)
    pending = []

    def go(copy):
        copy.start()
        pending.append(copy)

    loads = [
        pltpu.make_async_copy(src, dst, load_sem.at[i])
        for i, (src, dst) in enumerate(((gb_hbm, gb), (ga_hbm, ga), (go_hbm, go_s), (h1_hbm, h1)))
    ]
    for copy in loads:
        copy.start()
    spans = widths(R, NZ)

    def load_p(b):
        span = pl.ds(0, spans[b])
        return pltpu.make_async_copy(
            p_hbm.at[b, :, span], p_s.at[b % 2, :, span], p_sem.at[b % 2]
        )

    load_p(0).start()
    load_p(1).start()

    meet([(w, zto[j]) for j in hops] + [(near[j], z) for j in range(1, GROUP)])

    first = (x, y)
    second = (y, x)
    flip_first = (2, 4)
    flip_second = (4, 2)
    half = (FH // 4, C // 2, C // 4, C // 4)
    r1 = (r1_b, r1_a, r1_o, r1_q)
    r2 = (r2_b, r2_a, r2_o, r2_q)
    rz = (rz_b, rz_a, rz_o)
    final = (f_b, f_a, f_o, f_q)
    out = (gb_out, ga_out, go_out, gq_out)
    work = (gb, ga, go_w, gq_w)

    def index(kind, part, start, n):
        if kind == 0:
            return at(part * (FH // 2) + start, n), slice(None)
        width = work[kind].shape[2] // 2
        return at(start, n), pl.ds(part * width, width)

    def sub(kind, part, start, n):
        return work[kind].at[(slice(None),) + index(kind, part, start, n)]

    def kept(kind, part):
        return half[kind] * first[part] + (half[kind] // 2) * second[part]

    def step_one(kind, part):
        n = half[kind]
        return remote(
            sub(kind, part, n * (1 - first[part]), n),
            r1[kind].at[part],
            s1_s.at[kind, part],
            s1_r.at[kind, part],
            (near[flip_first[part]], z),
        )

    def step_two(kind, part):
        n = half[kind] // 2
        return remote(
            sub(kind, part, 2 * n * first[part] + n * (1 - second[part]), n),
            r2[kind].at[part],
            s2_s.at[kind, part],
            s2_r.at[kind, part],
            (near[flip_second[part]], z),
        )

    def add_one(kind):
        n = half[kind]
        for part in range(2):
            step_one(kind, part).wait_recv()
            idx = index(kind, part, n * first[part], n)

            @pl.loop(0, NZ)
            def _(d):
                work[kind][(d,) + idx] += r1[kind][part, d]

            go(step_two(kind, part))

    def add_two(kind):
        n = half[kind] // 2
        for part in range(2):
            step_two(kind, part).wait_recv()
            idx = index(kind, part, kept(kind, part), n)

            @pl.loop(0, NZ)
            def _(d):
                work[kind][(d,) + idx] += r2[kind][part, d]

            for j in hops:
                go(along(kind, part, j))

    def along(kind, part, j):
        n = half[kind] // 2
        idx = index(kind, part, kept(kind, part), n)
        target = rz[kind].at[part, j - 1] if kind < 3 else f_q.at[(z,) + idx]
        return remote(
            work[kind].at[(zto[j],) + idx],
            target,
            z_s.at[kind, part, j],
            z_r.at[kind, part, j],
            (w, zto[j]),
        )

    def add_line(kind):
        n = half[kind] // 2
        for part in range(2):
            idx = index(kind, part, kept(kind, part), n)
            for j in hops:
                along(kind, part, j).wait_recv()
            if kind < 3:
                total = work[kind][(z,) + idx].astype(F32)
                for j in hops:
                    total += rz[kind][part, j - 1].astype(F32)
                final[kind][idx] = total.astype(BF16)
            else:
                f_q[(z,) + idx] = work[kind][(z,) + idx]
            for t in range(1, 4):
                go(share(kind, part, t))

    def share(kind, part, t):
        n = half[kind] // 2
        idx = index(kind, part, kept(kind, part), n)
        if kind == 3:
            idx = (slice(None),) + idx
        ref = final[kind].at[idx]
        return remote(
            ref, ref, g_s.at[kind, part, t], g_r.at[kind, part, t], (near[2 * t], z)
        )

    outs = []

    def shared(kind):
        n = half[kind] // 2
        for part in range(2):
            for t in range(1, 4):
                ox = x + (t & 1) * (1 - 2 * x)
                oy = y + (t >> 1) * (1 - 2 * y)
                a, b = (ox, oy) if part == 0 else (oy, ox)
                idx = index(kind, part, half[kind] * a + n * b, n)
                if kind == 3:
                    idx = (slice(None),) + idx
                ref = final[kind].at[idx]
                remote(
                    ref, ref, g_s.at[kind, part, t], g_r.at[kind, part, t], (near[2 * t], z)
                ).wait_recv()
        go(
            remote(
                final[kind], out[kind].at[core], sib_s.at[kind], sib_r.at[kind], (near[1], z)
            )
        )
        copy = pltpu.make_async_copy(final[kind], out[kind].at[core], out_sem.at[kind])
        copy.start()
        outs.append(copy)

    loads[0].wait()
    for part in range(2):
        go(step_one(0, part))
    for j in hops:
        go(
            remote(
                do4_ref.at[zto[j]],
                do_all.at[at(z * R, R)],
                do_s.at[j],
                do_r.at[j],
                (w, zto[j]),
            )
        )
    loads[1].wait()
    for part in range(2):
        go(step_one(1, part))
    loads[2].wait()
    CH = C // 2
    pair_o = remote(
        go_s.at[:, at((1 - core) * CH, CH)], go_far, pair_s.at[0], pair_r.at[0], (near[1], z)
    )
    go(pair_o)
    do_all[at(z * R, R), :] = do4_ref[z]
    dk_f[...] = jnp.zeros_like(dk_f)
    dv_f[...] = jnp.zeros_like(dv_f)
    pair_o.wait_recv()

    @pl.loop(0, NZ)
    def _(d):
        go_w[d] = go_s[d, at(core * CH, CH), :] + go_far[d]

    for part in range(2):
        go(step_one(2, part))
    for j in hops:
        remote(
            do4_ref.at[zto[j]],
            do_all.at[at(zfrom[j] * R, R)],
            do_s.at[j],
            do_r.at[j],
            (w, zto[j]),
        ).wait_recv()

    for b, width in enumerate(spans):
        load_p(b).wait()
        block = slice(b * R, (b + 1) * R)
        slot = b % 2
        dq_f[...] = jnp.zeros_like(dq_f)

        @pl.loop(0, 4)
        def _(h):
            pick = lanes(R, C, h)
            rows = at(h * R, R)
            do_h = do_all[block, :] * pick.astype(BF16)
            do_st[rows, :] = do_h
            q_st[rows, :] = q_ref[block, :] * pick.astype(BF16)
            p = p_s[slot, rows, :width].astype(F32)
            t = p * dot_nt(do_h, v_ref[:width, :])
            ds = (t - p * jnp.sum(t, -1, keepdims=True)).astype(BF16)
            ds_s[rows, :width] = ds
            dq_f[...] += dot(ds, k_ref[:width, :]) * pick

        @pl.loop(0, width // 128)
        def _(n):
            keys = at(n * 128, 128, 128)
            dv_f[keys, :] += dot_tn(p_s[slot, :, keys], do_st[...])
            dk_f[keys, :] += dot_tn(ds_s[:, keys], q_st[...])

        if b + 2 < NZ:
            load_p(b + 2).start()
        dqkv[block, 0:C] = (dq_f[...] * 0.125).astype(BF16)
        if b == NZ - 2:
            add_one(0)
    dqkv[:, C : 2 * C] = (dk_f[:T, :] * 0.125).astype(BF16)
    dqkv[:, 2 * C :] = dv_f[:T, :].astype(BF16)

    for d in range(NZ):
        dh[d] = dot_nt(dqkv[d * R : (d + 1) * R, :], wq_ref[...]).astype(BF16)

    def rise(d):
        return remote(
            dh.at[d], rel.at[d], ru_s.at[d], ru_r.at[d], (w, jnp.minimum(z + 1, NZ - 1))
        )

    def fall(d, last):
        return remote(
            dh.at[d], rel.at[NZ if last else d], rd_s.at[d], rd_r.at[d], (w, jnp.maximum(z - 1, 0))
        )

    def up_step(here, d):
        if here > 0:
            rise(d).wait_recv()
            dh[d] += rel[d]
        rise(d).start()

    def down_step(here, d):
        if here < NZ - 1:
            fall(d, False).wait_recv()
            dh[d] += rel[d]
        fall(d, here - 1 == d).start()

    def actions(here):
        ups = [(up_step, d) for d in range(NZ - 1, here, -1)]
        downs = [(down_step, d) for d in range(here)]
        return ups + downs if here < NZ // 2 else downs + ups

    def line_step(k):
        for here in range(NZ):
            act, d = actions(here)[k]

            @pl.when(z == here)
            def _():
                act(here, d)

    line_step(0)

    loads[3].wait()
    for d in range(NZ):
        gq_s[d] = dot_tn(h1[:, d * C : (d + 1) * C], dqkv[...]).astype(BF16)
    pair_q = remote(
        gq_s.at[:, at((1 - core) * CH, CH)], gq_far, pair_s.at[1], pair_r.at[1], (near[1], z)
    )
    go(pair_q)
    for d in range(NZ):
        s_f[d] = small_in[:, d * C : (d + 1) * C]
    s_f[z, 8:9, :] = rowsum(dqkv[:, 0:C].astype(F32))
    s_f[z, 9:10, :] = rowsum(dqkv[:, 2 * C :].astype(F32))
    add_one(1)
    pair_q.wait_recv()

    @pl.loop(0, NZ)
    def _(d):
        gq_w[d] = gq_s[d, at(core * CH, CH), :] + gq_far[d]

    for part in range(2):
        go(step_one(3, part))
    line_step(1)
    add_one(2)
    add_two(0)
    line_step(2)
    add_one(3)
    add_two(1)
    add_two(2)
    add_two(3)

    acc[...] = dh[z].astype(F32)

    @pl.when(z > 0)
    def _():
        remote(
            dh.at[z], rel.at[z], ru_s.at[z], ru_r.at[z], (w, jnp.minimum(z + 1, NZ - 1))
        ).wait_recv()
        acc[...] += rel[z].astype(F32)

    @pl.when(z < NZ - 1)
    def _():
        remote(
            dh.at[z], rel.at[NZ], rd_s.at[z], rd_r.at[z], (w, jnp.maximum(z - 1, 0))
        ).wait_recv()
        acc[...] += rel[NZ].astype(F32)

    dh1 = acc[...]
    n1, inverse = norm(x_ref[...].astype(F32))
    dx_ref[...] = (dmid_ref[...] + norm_back(dh1, n1, inverse, par_ref[0:1, :])).astype(BF16)
    gain = rowsum(dh1 * n1)
    shift = rowsum(dh1)
    for d in range(NZ):
        s_f[d, 0:1, :] = gain[:, d * C : (d + 1) * C]
        s_f[d, 4:5, :] = shift[:, d * C : (d + 1) * C]
    s_b[...] = s_f[...].astype(BF16)
    for j in hops:
        go(remote(s_b.at[zto[j]], s_z.at[j], sz_s.at[j], sz_r.at[j], (w, zto[j])))
    for j in hops:
        remote(s_b.at[zto[j]], s_z.at[j], sz_s.at[j], sz_r.at[j], (w, zto[j])).wait_recv()
    total = s_f[z]
    for j in hops:
        total += s_z[j].astype(F32)
    s_p[...] = total.astype(BF16)
    for j in range(1, GROUP):
        go(remote(s_p, s_g.at[j], sp_s.at[j], sp_r.at[j], (near[j], z)))

    for kind in range(4):
        add_line(kind)
    for j in range(1, GROUP):
        remote(s_p, s_g.at[j], sp_s.at[j], sp_r.at[j], (near[j], z)).wait_recv()
        total += s_g[j].astype(F32)
    small_out[...] = total
    for kind in range(4):
        shared(kind)
    for kind in range(4):
        remote(
            final[kind], out[kind].at[1 - core], sib_s.at[kind], sib_r.at[kind], (near[1], z)
        ).wait_recv()
    for here in range(NZ):

        @pl.when(z == here)
        def _():
            for act, d in actions(here):
                if act is up_step:
                    rise(d).wait_send()
                else:
                    fall(d, here - 1 == d).wait_send()

    for copy in pending:
        copy.wait_send()
    for copy in outs:
        copy.wait()


def reduce(NZ, inputs, dmid, par, small, do4, wq, q, k, v, h1, p, ga, gb, go):
    R, D = inputs.shape
    C = D // NZ
    T = NZ * R
    FH = gb.shape[1]
    wide = p.shape[2]
    F = NZ * FH
    shape = jax.ShapeDtypeStruct
    buf = pltpu.VMEM
    return pl.pallas_call(
        functools.partial(reduce_kernel, NZ),
        out_shape=[
            shape((R, D), BF16),
            shape((2, FH, D), BF16),
            shape((2, C, F), BF16),
            shape((2, C // 2, D), BF16),
            shape((2, NZ, C // 2, 3 * C), BF16),
            shape((16, C), F32),
        ],
        in_specs=[VMEM] * 9 + [ANY] * 5,
        out_specs=[VMEM, ANY, ANY, ANY, ANY, VMEM],
        scratch_shapes=[
            buf((T, D), BF16),
            buf((2, 4 * R, wide), BF16),
            buf((NZ, C, F), BF16),
            buf((NZ, FH, D), BF16),
            buf((NZ, C, D), BF16),
            buf((NZ, C // 2, D), BF16),
            buf((NZ, C // 2, D), BF16),
            buf((NZ, C, 3 * C), BF16),
            buf((NZ, C // 2, 3 * C), BF16),
            buf((NZ, C // 2, 3 * C), BF16),
            buf((2, NZ, FH // 4, D), BF16),
            buf((2, NZ, C // 2, F // 2), BF16),
            buf((2, NZ, C // 4, D // 2), BF16),
            buf((2, NZ, C // 4, 3 * C // 2), BF16),
            buf((2, NZ, FH // 8, D), BF16),
            buf((2, NZ, C // 4, F // 2), BF16),
            buf((2, NZ, C // 8, D // 2), BF16),
            buf((2, NZ, C // 8, 3 * C // 2), BF16),
            buf((2, NZ - 1, FH // 8, D), BF16),
            buf((2, NZ - 1, C // 4, F // 2), BF16),
            buf((2, NZ - 1, C // 8, D // 2), BF16),
            buf((FH, D), BF16),
            buf((C, F), BF16),
            buf((C // 2, D), BF16),
            buf((NZ, C // 2, 3 * C), BF16),
            buf((T, C), BF16),
            buf((4 * R, C), BF16),
            buf((4 * R, C), BF16),
            buf((4 * R, wide), BF16),
            buf((R, C), F32),
            buf((wide, C), F32),
            buf((wide, C), F32),
            buf((T, 3 * C), BF16),
            buf((NZ, R, D), BF16),
            buf((NZ + 1, R, D), BF16),
            buf((R, D), F32),
            buf((NZ, 16, C), F32),
            buf((NZ, 16, C), BF16),
            buf((NZ, 16, C), BF16),
            buf((16, C), BF16),
            buf((GROUP, 16, C), BF16),
            DMA((4,)),
            DMA((2,)),
            DMA((NZ,)),
            DMA((NZ,)),
            DMA((2,)),
            DMA((2,)),
            DMA((4, 2)),
            DMA((4, 2)),
            DMA((4, 2)),
            DMA((4, 2)),
            DMA((4, 2, NZ)),
            DMA((4, 2, NZ)),
            DMA((4, 2, 4)),
            DMA((4, 2, 4)),
            DMA((4,)),
            DMA((4,)),
            DMA((NZ,)),
            DMA((NZ,)),
            DMA((NZ,)),
            DMA((NZ,)),
            DMA((NZ,)),
            DMA((NZ,)),
            DMA((GROUP,)),
            DMA((GROUP,)),
            DMA((4,)),
        ],
        compiler_params=pltpu.CompilerParams(
            collective_id=2, has_side_effects=True, vmem_limit_bytes=60 * 2**20
        ),
    )(inputs, dmid, par, small, do4, wq, q, k, v, h1, p, ga, gb, go)


def shards(NZ, W, inputs, w_qkv, w_out, w_fc1, w_fc2, norm_gain, shifts, text_len, cotangent):
    R, D = inputs.shape[1:]
    C = D // NZ
    FF = w_fc1.shape[1]
    FH = FF // (2 * NZ)
    par = jnp.concatenate([norm_gain, shifts], 0)
    o4, h1, q, k, v, wq, wa, wb, wo, par_f, p = attend(
        NZ, inputs[0], par, text_len, w_qkv, w_out, w_fc1, w_fc2
    )
    act, dmid, do4, ga, gb, go, small = feed(NZ, inputs[0], cotangent[0], o4, par_f, wa, wb, wo)
    ga = ga.reshape(NZ, C, NZ * FH)
    dx, gb, ga, go, gq, small = reduce(
        NZ, inputs[0], dmid, par_f, small, do4, wq, q, k, v, h1, p, ga, gb, go
    )
    grads = (
        gq.reshape(2, NZ, C // 2, 3, C).transpose(0, 2, 3, 1, 4).reshape(C, 3 * D).astype(F32),
        go.reshape(C, D).astype(F32),
        ga.reshape(2, C, NZ, FH).transpose(1, 2, 0, 3).reshape(C, FF).astype(F32),
        gb.reshape(2 * FH, D).astype(F32),
        small,
    )
    if W > GROUP:
        groups = [list(range(i, W, GROUP)) for i in range(GROUP)]
        grads = lax.psum(grads, "wide", axis_index_groups=groups)
    return (act[None], dx[None]) + tuple(grads[:4]) + (grads[4][:4], grads[4][4:])


def solution(mesh):
    return jax.shard_map(
        functools.partial(shards, mesh.shape["narrow"], mesh.shape["wide"]),
        mesh=mesh,
        in_specs=(
            P("wide", "narrow", None),
            P("narrow", None),
            P("narrow", None),
            P("narrow", None),
            P("narrow", None),
            P(None, "narrow"),
            P(None, "narrow"),
            P("wide"),
            P("wide", "narrow", None),
        ),
        out_specs=(
            P("wide", "narrow", None),
            P("wide", "narrow", None),
            P("narrow", None),
            P("narrow", None),
            P("narrow", None),
            P("narrow", None),
            P(None, "narrow"),
            P(None, "narrow"),
        ),
        check_vma=False,
    )
```

```python
import functools
import math

import jax
import jax.numpy as jnp
from jax import lax
from jax.experimental import pallas as pl
from jax.experimental.pallas import tpu as pltpu
from jax.sharding import PartitionSpec as P

HEADS = 16
TEXT = 64
EPS = 1e-5
GROUP = 8
WINDOW = 3
MESH = pl.DeviceIdType.MESH
F32 = jnp.float32
BF16 = jnp.bfloat16
ANY = pl.BlockSpec(memory_space=pl.ANY)
VMEM = pl.BlockSpec(memory_space=pltpu.VMEM)
SMEM = pl.BlockSpec(memory_space=pltpu.SMEM)
DMA = pltpu.SemaphoreType.DMA


def at(start, size, step=16):
    return pl.ds(pl.multiple_of(start, step), size)


def place():
    w = lax.axis_index("wide")
    z = lax.axis_index("narrow")
    return w, z, lax.rem(w, 2), lax.rem(lax.div(w, 2), 2), lax.rem(lax.div(w, 4), 2)


def flips(w, core, x, y, j):
    return (
        w
        + (j & 1) * (1 - 2 * core)
        + ((j >> 1) & 1) * (2 - 4 * x)
        + ((j >> 2) & 1) * (4 - 8 * y)
    )


def remote(src, dst, send_sem, recv_sem, device):
    return pltpu.make_async_remote_copy(
        src_ref=src,
        dst_ref=dst,
        send_sem=send_sem,
        recv_sem=recv_sem,
        device_id=device,
        device_id_type=MESH,
    )


def meet(devices):
    barrier = pltpu.get_barrier_semaphore()
    for device in devices:
        pl.semaphore_signal(barrier, inc=1, device_id=device, device_id_type=MESH)
    pl.semaphore_wait(barrier, len(devices))


def dot(left, right):
    return lax.dot_general(left, right, (((1,), (0,)), ((), ())), preferred_element_type=F32)


def dot_nt(left, right):
    return lax.dot_general(left, right, (((1,), (1,)), ((), ())), preferred_element_type=F32)


def dot_tn(left, right):
    return lax.dot_general(left, right, (((0,), (0,)), ((), ())), preferred_element_type=F32)


def norm(values):
    centred = values - jnp.mean(values, -1, keepdims=True)
    inverse = lax.rsqrt(jnp.mean(centred * centred, -1, keepdims=True) + EPS)
    return centred * inverse, inverse


def norm_back(incoming, normed, inverse, gain):
    scaled = incoming * gain
    return inverse * (
        scaled
        - jnp.mean(scaled, -1, keepdims=True)
        - normed * jnp.mean(scaled * normed, -1, keepdims=True)
    )


def rowsum(values):
    return jnp.sum(values, 0, keepdims=True)


def lanes(rows, width, head):
    lane = lax.broadcasted_iota(jnp.int32, (rows, width), 1)
    size = width // 4
    return ((lane >= head * size) & (lane < head * size + size)).astype(F32)


def widths(rows, blocks):
    return [-(-rows * (b + 1) // 128) * 128 for b in range(blocks)]


def attend_kernel(
    NZ,
    x_ref,
    par_ref,
    len_ref,
    wqkv_ref,
    wout_ref,
    wfc1_ref,
    wfc2_ref,
    o4_out,
    h1_out,
    q_out,
    k_out,
    v_out,
    wq_out,
    a_out,
    b_out,
    wo_out,
    par_out,
    p_out,
    par_all,
    par_f,
    stage,
    wq,
    a_ref,
    b_ref,
    wo_ref,
    h1,
    q_s,
    k_s,
    v_s,
    mask_s,
    p_s,
    o_acc,
    o_send,
    o4,
    loc_sem,
    par_s,
    par_r,
    wz_s,
    wz_r,
    wp_s,
    wp_r,
    h_s,
    h_r,
    fz_s,
    fz_r,
    fp_s,
    fp_r,
    fq_s,
    fq_r,
    sib_s,
    sib_r,
    o_s,
    o_r,
    out_sem,
):
    R, D = x_ref.shape
    C = D // NZ
    FH = wfc1_ref.shape[1] // (2 * NZ)
    w, z, core, x, y = place()
    chip = x + 2 * y
    w8 = core + 2 * chip
    near = {j: flips(w, core, x, y, j) for j in range(1, GROUP)}
    zto = [lax.rem(z + j, NZ) for j in range(NZ)]
    zfrom = [lax.rem(z + NZ - j, NZ) for j in range(NZ)]
    hops = range(1, NZ)
    pending = []

    def go(copy):
        copy.start()
        pending.append(copy)

    first = (x, y)
    second = (y, x)
    flip_first = (2, 4)
    flip_second = (4, 2)
    local = 1 + 3 * NZ
    RW = C // GROUP
    staged = [
        pltpu.make_async_copy(
            wqkv_ref.at[:, pl.ds(t * D + d * C, C)],
            stage.at[d, :, pl.ds(t * C, C)],
            loc_sem.at[1 + 3 * d + t],
        )
        for d in range(NZ)
        for t in range(3)
    ]
    owned = [
        pltpu.make_async_copy(
            wfc1_ref.at[:, at((2 * j) * FH + core * FH, FH, 128)],
            a_ref.at[at(z * C, C), pl.ds(j * FH, FH)],
            loc_sem.at[local + j],
        )
        for j in range(NZ)
    ]
    owned.append(
        pltpu.make_async_copy(
            wfc2_ref.at[at(core * FH, FH)], b_ref.at[z], loc_sem.at[local + NZ]
        )
    )
    owned.append(
        pltpu.make_async_copy(wout_ref, wo_ref.at[at(z * C, C)], loc_sem.at[local + NZ + 1])
    )
    own_par = pltpu.make_async_copy(par_ref, par_all.at[z], loc_sem.at[0])
    own_wq = pltpu.make_async_copy(stage.at[z], wq.at[at(z * C, C)], loc_sem.at[local + NZ + 2])

    def par_copy(j, source):
        return remote(par_ref, par_all.at[source], par_s.at[j], par_r.at[j], (w, zto[j]))

    def start():
        for copy in (own_par, *staged, *owned):
            copy.start()
        meet([(w, zto[j]) for j in hops] + [(near[j], z) for j in range(1, GROUP)])
        for j in hops:
            go(par_copy(j, z))

    def wq_line(j, source):
        return remote(
            stage.at[zto[j], at(w8 * RW, RW)],
            wq.at[at(source * C + w8 * RW, RW)],
            wz_s.at[j],
            wz_r.at[j],
            (w, zto[j]),
        )

    def wq_plane(j, t, owner):
        part = wq.at[at(zfrom[j] * C + owner * RW, RW)]
        return remote(part, part, wp_s.at[j, t], wp_r.at[j, t], (near[t], z))

    def wq_send():
        for copy in staged:
            copy.wait()
        for j in hops:
            go(wq_line(j, z))
        own_wq.start()

    def wq_pass():
        for j in hops:
            wq_line(j, zfrom[j]).wait_recv()
            for t in range(1, GROUP):
                go(wq_plane(j, t, w8))

    def wq_wait():
        own_wq.wait()
        for j in hops:
            for t in range(1, GROUP):
                wq_plane(j, t, near[t] - w + w8).wait_recv()

    def first_norm():
        normed, _ = norm(x_ref[...].astype(F32))
        own_par.wait()
        for j in hops:
            par_copy(j, zfrom[j]).wait_recv()
        for d in range(NZ):
            par_f[:, d * C : (d + 1) * C] = par_all[d].astype(F32)
        h1[at(z * R, R), :] = (normed * par_f[0:1, :] + par_f[4:5, :]).astype(BF16)

    def sends(way, k):
        if way == 0:
            return (z - k >= 0) & (z < NZ - 1)
        return (z + k <= NZ - 1) & (z > 0)

    def comes(way, k):
        return z - 1 - k >= 0 if way == 0 else z + 1 + k <= NZ - 1

    def sent(way, k):
        return jnp.maximum(z - k, 0) if way == 0 else jnp.minimum(z + k, NZ - 1)

    def got(way, k):
        return jnp.maximum(z - 1 - k, 0) if way == 0 else jnp.minimum(z + 1 + k, NZ - 1)

    ahead = ((w, jnp.minimum(z + 1, NZ - 1)), (w, jnp.maximum(z - 1, 0)))
    relays = []

    def h1_copy(way, k, block):
        ref = h1.at[at(block * R, R)]
        return remote(ref, ref, h_s.at[way, k], h_r.at[way, k], ahead[way])

    def h1_send(k):
        for way in range(2):
            copy = h1_copy(way, k, sent(way, k))
            relays.append((sends(way, k), copy))

            @pl.when(sends(way, k))
            def _():
                copy.start()

    def h1_come(k):
        for way in range(2):
            copy = h1_copy(way, k, got(way, k))

            @pl.when(comes(way, k))
            def _():
                copy.wait_recv()

        if k + 1 < NZ - 1:
            h1_send(k + 1)

    def rows_of(kind):
        return (C // 4, FH // 4, C // 8)[kind]

    def piece(kind, part, source, start, n):
        if kind == 0:
            half = a_ref.shape[1] // 2
            return a_ref.at[at(source * C + start, n), pl.ds(part * half, half)]
        if kind == 1:
            half = D // 2
            return b_ref.at[source, at(start, n), pl.ds(part * half, half)]
        half = D // 2
        return wo_ref.at[
            at(source * C + core * (C // 2) + start, n), pl.ds(part * half, half)
        ]

    def quarter(kind, part, source):
        n = rows_of(kind)
        return piece(kind, part, source, n * (2 * first[part] + second[part]), n)

    def w_copy(kind, part, way, k, source):
        ref = quarter(kind, part, source)
        return remote(
            ref, ref, fz_s.at[kind, part, way, k], fz_r.at[kind, part, way, k], ahead[way]
        )

    def w_send(kind, k):
        if k == 0:
            for copy in {0: owned[:NZ], 1: owned[NZ : NZ + 1], 2: owned[NZ + 1 :]}[kind]:
                copy.wait()
        for part in range(2):
            for way in range(2):
                copy = w_copy(kind, part, way, k, sent(way, k))
                relays.append((sends(way, k), copy))

                @pl.when(sends(way, k))
                def _():
                    copy.start()

    def share_one(kind, part, way, k):
        ref = quarter(kind, part, got(way, k))
        return remote(
            ref,
            ref,
            fp_s.at[kind, part, way, k],
            fp_r.at[kind, part, way, k],
            (near[flip_second[part]], z),
        )

    def share_two(kind, part, way, k):
        n = 2 * rows_of(kind)
        ref = piece(kind, part, got(way, k), n * first[part], n)
        return remote(
            ref,
            ref,
            fq_s.at[kind, part, way, k],
            fq_r.at[kind, part, way, k],
            (near[flip_first[part]], z),
        )

    def w_come(kind, k):
        for part in range(2):
            for way in range(2):
                copy = w_copy(kind, part, way, k, got(way, k))
                share = share_one(kind, part, way, k)
                relays.append((comes(way, k), share))

                @pl.when(comes(way, k))
                def _():
                    copy.wait_recv()
                    share.start()

        if k + 1 < NZ - 1:
            w_send(kind, k + 1)

    def w_double(kind, k):
        for part in range(2):
            for way in range(2):
                source = got(way, k)
                n = rows_of(kind)
                start = n * (2 * first[part] + (1 - second[part]))
                ref = piece(kind, part, source, start, n)
                copy = remote(
                    ref,
                    ref,
                    fp_s.at[kind, part, way, k],
                    fp_r.at[kind, part, way, k],
                    (near[flip_second[part]], z),
                )
                share = share_two(kind, part, way, k)
                relays.append((comes(way, k), share))

                @pl.when(comes(way, k))
                def _():
                    copy.wait_recv()
                    share.start()

    def w_done(kind, k):
        for part in range(2):
            for way in range(2):
                n = 2 * rows_of(kind)
                ref = piece(kind, part, got(way, k), n * (1 - first[part]), n)
                copy = remote(
                    ref,
                    ref,
                    fq_s.at[kind, part, way, k],
                    fq_r.at[kind, part, way, k],
                    (near[flip_first[part]], z),
                )

                @pl.when(comes(way, k))
                def _():
                    copy.wait_recv()

    rows_k = k_s.shape[0]
    total = NZ * R

    def project(block):
        rows = at(block * R, R)
        bias = par_ref[...].astype(F32)
        q_s[rows, :] = (dot(h1[rows, :], wq[:, 0:C]) + bias[8:9, :]).astype(BF16)
        k_s[rows, :] = dot(h1[rows, :], wq[:, C : 2 * C]).astype(BF16)
        v_s[rows, :] = (dot(h1[rows, :], wq[:, 2 * C : 3 * C]) + bias[9:10, :]).astype(BF16)

    def project_own():
        if rows_k > total:
            k_s[total:rows_k, :] = jnp.zeros((rows_k - total, C), BF16)
            v_s[total:rows_k, :] = jnp.zeros((rows_k - total, C), BF16)
        project(z)

    def project_come(k):
        for way in range(2):

            @pl.when(comes(way, k))
            def _():
                project(got(way, k))

    outs = []

    def emit(src, dst, sem):
        copy = pltpu.make_async_copy(src, dst, out_sem.at[sem])
        copy.start()
        outs.append(copy)

    def emit_qkv():
        emit(h1, h1_out, 0)
        emit(q_s, q_out, 1)
        emit(k_s, k_out, 2)
        emit(v_s, v_out, 3)
        emit(wq, wq_out, 4)
        emit(par_f, par_out, 5)

    scale = math.log2(math.e) / math.sqrt(C // 4)
    text_len = len_ref[0]
    spans = widths(R, NZ)

    def o_copy(b):
        return remote(
            o_send.at[pl.ds(b * R, R)], o4.at[z], o_s.at[b], o_r.at[z], (w, jnp.int32(b))
        )

    def attention(b):
        width = spans[b]
        row = lax.broadcasted_iota(jnp.int32, (R, width), 0) + b * R
        col = lax.broadcasted_iota(jnp.int32, (R, width), 1)
        allowed = (col <= row) & ((col >= TEXT) | (col < text_len))
        mask_s[:, :width] = jnp.where(allowed, 0.0, -1e30)
        o_acc[...] = jnp.zeros_like(o_acc)

        @pl.loop(0, 4)
        def _(h):
            pick = lanes(R, C, h)
            q_h = q_s[b * R : (b + 1) * R, :] * pick.astype(BF16)
            s = dot_nt(q_h, k_s[:width, :]) + mask_s[:, :width]
            e = jnp.exp2((s - jnp.max(s, -1, keepdims=True)) * scale)
            p = (e * (1.0 / jnp.sum(e, -1, keepdims=True))).astype(BF16)
            p_s[b, at(h * R, R), :width] = p
            o_acc[...] += dot(p, v_s[:width, :]) * pick

        emit(p_s.at[b, :, pl.ds(0, width)], p_out.at[b, :, pl.ds(0, width)], 6 + b)
        o_send[b * R : (b + 1) * R, :] = o_acc[...].astype(BF16)
        send = o_copy(b)

        @pl.when(z != b)
        def _():
            send.start()

        @pl.when(z == b)
        def _():
            o4[z] = o_send[b * R : (b + 1) * R, :]

    def o_come():
        for d in range(NZ):
            copy = remote(
                o_send.at[pl.ds(d * R, R)], o4.at[d], o_s.at[d], o_r.at[d], (w, jnp.int32(d))
            )

            @pl.when(z != d)
            def _():
                copy.wait_send()
                copy.wait_recv()

        emit(o4, o4_out, 6 + NZ)

    def emit_a():
        emit(a_ref, a_out, 7 + NZ)

    def emit_b():
        emit(b_ref, b_out, 8 + NZ)

    def sibling(j, half):
        part = wo_ref.at[at(zfrom[j] * C + half * (C // 2), C // 2)]
        return remote(part, part, sib_s.at[j], sib_r.at[j], (near[1], z))

    def wo_swap():
        for j in hops:
            go(sibling(j, core))

    def wo_done():
        for j in hops:
            sibling(j, 1 - core).wait_recv()
        emit(wo_ref, wo_out, 9 + NZ)

    for act, *where in (
        (start,),
        (w_send, 1, 0),
        (w_send, 2, 0),
        (w_come, 1, 0),
        (w_send, 0, 0),
        (w_come, 1, 1),
        (wq_send,),
        (w_double, 1, 1),
        (w_come, 0, 0),
        (w_double, 1, 0),
        (first_norm,),
        (h1_send, 0),
        (w_come, 2, 0),
        (wq_pass,),
        (w_come, 2, 1),
        (w_come, 2, 2),
        (w_come, 1, 2),
        (h1_come, 0),
        (w_double, 2, 0),
        (w_done, 1, 1),
        (w_double, 0, 0),
        (w_double, 1, 2),
        (w_double, 2, 2),
        (w_double, 2, 1),
        (h1_come, 1),
        (wq_wait,),
        (project_own,),
        (w_come, 0, 1),
        (project_come, 1),
        (w_done, 1, 2),
        (project_come, 0),
        (w_done, 1, 0),
        (w_done, 0, 0),
        (w_double, 0, 1),
        (w_done, 2, 0),
        (h1_come, 2),
        (project_come, 2),
        (attention, 3),
        (w_come, 0, 2),
        (attention, 0),
        (w_done, 2, 1),
        (w_done, 0, 1),
        (attention, 1),
        (w_done, 2, 2),
        (w_double, 0, 2),
        (attention, 2),
        (w_done, 0, 2),
        (wo_swap,),
        (emit_qkv,),
        (wo_done,),
        (emit_a,),
        (emit_b,),
        (o_come,),
    ):
        act(*where)
    for ok, copy in relays:

        @pl.when(ok)
        def _():
            copy.wait_send()

    for copy in pending:
        copy.wait_send()
    for copy in outs:
        copy.wait()


def attend(NZ, inputs, par, text_len, w_qkv, w_out, w_fc1, w_fc2):
    R, D = inputs.shape
    C = D // NZ
    FH = w_fc1.shape[1] // (2 * NZ)
    T = NZ * R
    wide = widths(R, NZ)[-1]
    shape = jax.ShapeDtypeStruct
    return pl.pallas_call(
        functools.partial(attend_kernel, NZ),
        out_shape=[
            shape((NZ, R, C), BF16),
            shape((T, D), BF16),
            shape((T, C), BF16),
            shape((wide, C), BF16),
            shape((wide, C), BF16),
            shape((D, 3 * C), BF16),
            shape((D, NZ * FH), BF16),
            shape((NZ, FH, D), BF16),
            shape((D, D), BF16),
            shape((16, D), F32),
            shape((NZ, 4 * R, wide), BF16),
        ],
        in_specs=[VMEM, VMEM, SMEM, ANY, ANY, ANY, ANY],
        out_specs=[ANY] * 11,
        scratch_shapes=[
            pltpu.VMEM((NZ, 16, C), BF16),
            pltpu.VMEM((16, D), F32),
            pltpu.VMEM((NZ, C, 3 * C), BF16),
            pltpu.VMEM((D, 3 * C), BF16),
            pltpu.VMEM((D, NZ * FH), BF16),
            pltpu.VMEM((NZ, FH, D), BF16),
            pltpu.VMEM((D, D), BF16),
            pltpu.VMEM((T, D), BF16),
            pltpu.VMEM((T, C), BF16),
            pltpu.VMEM((wide, C), BF16),
            pltpu.VMEM((wide, C), BF16),
            pltpu.VMEM((R, wide), F32),
            pltpu.VMEM((NZ, 4 * R, wide), BF16),
            pltpu.VMEM((R, C), F32),
            pltpu.VMEM((T, C), BF16),
            pltpu.VMEM((NZ, R, C), BF16),
            DMA((4 * NZ + 4,)),
            DMA((NZ,)),
            DMA((NZ,)),
            DMA((NZ,)),
            DMA((NZ,)),
            DMA((NZ, GROUP)),
            DMA((NZ, GROUP)),
            DMA((2, NZ)),
            DMA((2, NZ)),
            DMA((3, 2, 2, NZ)),
            DMA((3, 2, 2, NZ)),
            DMA((3, 2, 2, NZ)),
            DMA((3, 2, 2, NZ)),
            DMA((3, 2, 2, NZ)),
            DMA((3, 2, 2, NZ)),
            DMA((NZ,)),
            DMA((NZ,)),
            DMA((NZ,)),
            DMA((NZ,)),
            DMA((10 + NZ,)),
        ],
        compiler_params=pltpu.CompilerParams(
            collective_id=0, has_side_effects=True, vmem_limit_bytes=56 * 2**20
        ),
    )(inputs, par, text_len, w_qkv, w_out, w_fc1, w_fc2)


def feed_kernel(
    NZ,
    x_ref,
    cot_ref,
    o4_ref,
    par_ref,
    a_hbm,
    b_hbm,
    wo_hbm,
    act_ref,
    dmid_ref,
    do_ref,
    g_out,
    go_out,
    small_ref,
    wa,
    wb,
    wo,
    h3,
    gate,
    slope,
    dm,
    du,
    part,
    far_m,
    far_h,
    mid_s,
    n2_s,
    n3_s,
    g_s,
    go_s,
    load_sem,
    send_sem,
    recv_sem,
    out_sem,
):
    R, D = x_ref.shape
    C = D // NZ
    FH = b_hbm.shape[1]
    w, z, core, x, y = place()
    other = (flips(w, core, x, y, 1), z)
    loads = [
        pltpu.make_async_copy(src, dst, load_sem.at[i])
        for i, (src, dst) in enumerate(((wo_hbm, wo), (a_hbm, wa), (b_hbm, wb)))
    ]
    for copy in loads:
        copy.start()
    meet([other])
    swaps = []

    def swap(src, dst, i):
        copy = remote(src, dst, send_sem.at[i], recv_sem.at[i], other)
        copy.start()
        swaps.append(copy)
        return copy

    def param(row):
        return par_ref[row : row + 1, :]

    shift = 4
    mine, theirs = slice(0, R), slice(R, 2 * R)

    loads[0].wait()
    branch = dot(o4_ref[0], wo[0:C, :])
    for s in range(1, NZ):
        branch += dot(o4_ref[s], wo[s * C : (s + 1) * C, :])
    n2, r2 = norm(branch + param(shift + 6))
    mid = x_ref[...].astype(F32) + n2 * param(1) + param(shift + 1)
    n2_s[...] = n2
    mid_s[...] = mid
    n3, r3 = norm(mid)
    n3_s[...] = n3
    h3[mine, :] = (n3 * param(2) + param(shift + 2)).astype(BF16)
    swap_h = swap(h3.at[pl.ds(0, R)], h3.at[pl.ds(R, R)], 0)
    loads[1].wait()

    def hidden(rows):
        for s in range(NZ):
            cols = slice(s * FH, (s + 1) * FH)
            line = par_ref[shift + 8 + s : shift + 9 + s, :]
            bias = jnp.where(core == 0, line[:, :FH], line[:, FH:])
            u = dot(h3[rows, :], wa[:, cols]) + bias
            k = math.sqrt(2.0 / math.pi)
            sq = u * u
            t = jnp.tanh(u * (k + k * 0.044715 * sq))
            half = 0.5 + 0.5 * t
            gate[rows, cols] = (u * half).astype(BF16)
            slope[rows, cols] = (
                half + (0.5 * u) * (1.0 - t * t) * (k + 3.0 * k * 0.044715 * sq)
            ).astype(BF16)

    def contract(rows):
        total = dot(gate[rows, 0:FH], wb[0])
        for s in range(1, NZ):
            total += dot(gate[rows, s * FH : (s + 1) * FH], wb[s])
        return total

    hidden(mine)
    loads[2].wait()
    swap_h.wait_recv()
    hidden(theirs)
    part[0] = contract(theirs).astype(BF16)
    swap_m = swap(part.at[0], far_m, 1)
    m_near = contract(mine)
    swap_m.wait_recv()
    n4, r4 = norm(m_near + far_m[...].astype(F32) + param(shift + 7))
    act_ref[...] = (mid_s[...] + n4 * param(3) + param(shift + 3)).astype(BF16)

    e = cot_ref[...].astype(F32)
    small_ref[...] = jnp.zeros_like(small_ref)
    small_ref[3:4, :] = rowsum(e * n4)
    small_ref[shift + 3 : shift + 4, :] = rowsum(e)
    dm_low = norm_back(e, n4, r4, param(3)).astype(BF16)
    dm[mine, :] = dm_low
    small_ref[shift + 7 : shift + 8, :] = rowsum(dm_low.astype(F32))
    swap_d = swap(dm.at[pl.ds(0, R)], dm.at[pl.ds(R, R)], 2)

    def unhidden(rows):
        for s in range(NZ):
            cols = slice(s * FH, (s + 1) * FH)
            du[rows, cols] = (
                dot_nt(dm[rows, :], wb[s]) * slope[rows, cols].astype(F32)
            ).astype(BF16)

    unhidden(mine)
    swap_d.wait_recv()
    unhidden(theirs)
    part[1] = dot_nt(du[theirs, :], wa[...]).astype(BF16)
    swap_u = swap(part.at[1], far_h, 3)
    outs = []

    def emit(src, dst, i):
        copy = pltpu.make_async_copy(src, dst, out_sem.at[i])
        copy.start()
        outs.append(copy)

    for s in range(NZ):
        cols = slice(s * FH, (s + 1) * FH)
        g_s[0, s] = dot_tn(gate[:, cols], dm[...]).astype(BF16)
    emit(g_s.at[0], g_out.at[0], 0)
    for s in range(NZ):
        cols = slice(s * FH, (s + 1) * FH)
        tile = dot_tn(h3[...], du[:, cols]).astype(BF16)
        low, left = (s // 2) * C, (s % 2) * FH
        for d in range(NZ):
            g_s[1, d, low : low + C, left : left + FH] = tile[d * C : (d + 1) * C, :]
        total = rowsum(du[:, cols].astype(F32))
        row = shift + 8 + s
        small_ref[row : row + 1, 0:FH] = jnp.where(core == 0, total, 0.0)
        small_ref[row : row + 1, FH:] = jnp.where(core == 0, 0.0, total)
    emit(g_s.at[1], g_out.at[1], 1)
    dh3 = dot_nt(du[mine, :], wa[...])
    swap_u.wait_recv()
    dh3 += far_h[...].astype(F32)
    n3 = n3_s[...]
    small_ref[2:3, :] = rowsum(dh3 * n3)
    small_ref[shift + 2 : shift + 3, :] = rowsum(dh3)
    dmid = e + norm_back(dh3, n3, r3, param(2))
    dmid_ref[...] = dmid
    n2 = n2_s[...]
    small_ref[1:2, :] = rowsum(dmid * n2)
    small_ref[shift + 1 : shift + 2, :] = rowsum(dmid)
    da = norm_back(dmid, n2, r2, param(1)).astype(BF16)
    small_ref[shift + 6 : shift + 7, :] = rowsum(da.astype(F32))
    for s in range(NZ):
        do_ref[s] = dot_nt(da, wo[s * C : (s + 1) * C, :]).astype(BF16)
        go_s[s] = dot_tn(o4_ref[s], da).astype(BF16)
    emit(go_s, go_out, 2)
    for copy in swaps:
        copy.wait_send()
    for copy in outs:
        copy.wait()


def feed(NZ, inputs, cotangent, o4, par, wa, wb, wo):
    R, D = inputs.shape
    C = D // NZ
    FH = wb.shape[1]
    shape = jax.ShapeDtypeStruct
    return pl.pallas_call(
        functools.partial(feed_kernel, NZ),
        out_shape=[
            shape((R, D), BF16),
            shape((R, D), F32),
            shape((NZ, R, C), BF16),
            shape((2, NZ, FH, D), BF16),
            shape((NZ, C, D), BF16),
            shape((16, D), F32),
        ],
        in_specs=[VMEM, VMEM, VMEM, VMEM, ANY, ANY, ANY],
        out_specs=[VMEM, VMEM, VMEM, ANY, ANY, VMEM],
        scratch_shapes=[
            pltpu.VMEM((D, NZ * FH), BF16),
            pltpu.VMEM((NZ, FH, D), BF16),
            pltpu.VMEM((D, D), BF16),
            pltpu.VMEM((2 * R, D), BF16),
            pltpu.VMEM((2 * R, NZ * FH), BF16),
            pltpu.VMEM((2 * R, NZ * FH), BF16),
            pltpu.VMEM((2 * R, D), BF16),
            pltpu.VMEM((2 * R, NZ * FH), BF16),
            pltpu.VMEM((2, R, D), BF16),
            pltpu.VMEM((R, D), BF16),
            pltpu.VMEM((R, D), BF16),
            pltpu.VMEM((R, D), F32),
            pltpu.VMEM((R, D), F32),
            pltpu.VMEM((R, D), F32),
            pltpu.VMEM((2, NZ, FH, D), BF16),
            pltpu.VMEM((NZ, C, D), BF16),
            DMA((3,)),
            DMA((4,)),
            DMA((4,)),
            DMA((3,)),
        ],
        compiler_params=pltpu.CompilerParams(
            collective_id=1, has_side_effects=True, vmem_limit_bytes=58 * 2**20
        ),
    )(inputs, cotangent, o4, par, wa, wb, wo)


def reduce_kernel(
    NZ,
    x_ref,
    dmid_ref,
    par_ref,
    small_in,
    do4_ref,
    wq_ref,
    q_ref,
    k_ref,
    v_ref,
    h1_hbm,
    p_hbm,
    g_hbm,
    go_hbm,
    dx_ref,
    g_out,
    go_out,
    gq_out,
    small_out,
    h1,
    p_s,
    g,
    go_s,
    go_far,
    go_w,
    gq_s,
    gq_far,
    gq_w,
    r1,
    r1_o,
    r1_q,
    r2,
    r2_o,
    r2_q,
    rz,
    rz_o,
    f_g,
    f_o,
    f_q,
    do_all,
    do_st,
    q_st,
    ds_s,
    dq_f,
    dk_f,
    dv_f,
    dqkv,
    dh,
    rel,
    s_f,
    s_b,
    s_z,
    s_p,
    s_g,
    load_sem,
    p_sem,
    do_s,
    do_r,
    pair_s,
    pair_r,
    s1_s,
    s1_r,
    s2_s,
    s2_r,
    c1_s,
    c1_r,
    c2_s,
    c2_r,
    z_s,
    z_r,
    g_s,
    g_r,
    sib_s,
    sib_r,
    ru_s,
    ru_r,
    sz_s,
    sz_r,
    sp_s,
    sp_r,
    out_sem,
):
    R, D = x_ref.shape
    C = D // NZ
    T = NZ * R
    FH = g.shape[2]
    w, z, core, x, y = place()
    near = {j: flips(w, core, x, y, j) for j in range(1, GROUP)}
    zto = [lax.rem(z + j, NZ) for j in range(NZ)]
    zfrom = [lax.rem(z + NZ - j, NZ) for j in range(NZ)]
    hops = range(1, NZ)
    pending = []

    def go(copy):
        copy.start()
        pending.append(copy)

    pair = z + 1 - 2 * lax.rem(z, 2)
    across = lax.rem(z + 2, NZ)
    goals = (pair, lax.rem(pair + 2, NZ), across, z)
    chunks = [(kind, j) for j in range(NZ) for kind in range(2)]
    loads = [
        pltpu.make_async_copy(
            g_hbm.at[kind, goals[j]], g.at[kind, goals[j]], load_sem.at[i]
        )
        for i, (kind, j) in enumerate(chunks)
    ]
    loads.append(pltpu.make_async_copy(go_hbm, go_s, load_sem.at[len(chunks)]))
    loads.append(pltpu.make_async_copy(h1_hbm, h1, load_sem.at[len(chunks) + 1]))
    for copy in loads:
        copy.start()
    spans = widths(R, NZ)

    def load_p(b):
        span = pl.ds(0, spans[b])
        return pltpu.make_async_copy(
            p_hbm.at[b, :, span], p_s.at[b % 2, :, span], p_sem.at[b % 2]
        )

    load_p(NZ - 1).start()
    load_p(NZ - 2).start()

    meet([(w, zto[j]) for j in hops] + [(near[j], z) for j in range(1, GROUP)])

    first = (x, y)
    second = (y, x)
    flip_first = (2, 4)
    flip_second = (4, 2)
    half = (FH // 4, FH // 4, C // 4, C // 4)
    side_one = {2: r1_o, 3: r1_q}
    side_two = {2: r2_o, 3: r2_q}
    side_work = {2: go_w, 3: gq_w}
    final = {0: f_g.at[0], 1: f_g.at[1], 2: f_o, 3: f_q}
    out = {0: g_out.at[0], 1: g_out.at[1], 2: go_out, 3: gq_out}
    outs = []

    def index(kind, part, start, n):
        if kind < 2:
            return at(part * (FH // 2) + start, n), slice(None)
        width = side_work[kind].shape[2] // 2
        return at(start, n), pl.ds(part * width, width)

    def kept(kind, part):
        return half[kind] * first[part] + (half[kind] // 2) * second[part]

    def chunk_one(c, part):
        kind, j = chunks[c]
        n = half[kind]
        return remote(
            g.at[(kind, goals[j]) + index(kind, part, n * (1 - first[part]), n)],
            r1.at[c, part],
            c1_s.at[c, part],
            c1_r.at[c, part],
            (near[flip_first[part]], z),
        )

    def chunk_two(c, part):
        kind, j = chunks[c]
        n = half[kind] // 2
        start = 2 * n * first[part] + n * (1 - second[part])
        return remote(
            g.at[(kind, goals[j]) + index(kind, part, start, n)],
            r2.at[c, part],
            c2_s.at[c, part],
            c2_r.at[c, part],
            (near[flip_second[part]], z),
        )

    def launch(c):
        loads[c].wait()
        for part in range(2):
            go(chunk_one(c, part))

    def reduce_one(c):
        kind, j = chunks[c]
        n = half[kind]
        for part in range(2):
            chunk_one(c, part).wait_recv()
            idx = (kind, goals[j]) + index(kind, part, n * first[part], n)
            g[idx] += r1[c, part]
            go(chunk_two(c, part))

    def reduce_two(c):
        kind, j = chunks[c]
        n = half[kind] // 2
        for part in range(2):
            chunk_two(c, part).wait_recv()
            idx = (kind, goals[j]) + index(kind, part, kept(kind, part), n)
            g[idx] += r2[c, part]
            if j < 2:
                go(pairwise(kind, part, j))
            elif j == 2:
                cross(kind, part)

    def step_one(kind, part):
        n = half[kind]
        return remote(
            side_work[kind].at[(slice(None),) + index(kind, part, n * (1 - first[part]), n)],
            side_one[kind].at[part],
            s1_s.at[kind - 2, part],
            s1_r.at[kind - 2, part],
            (near[flip_first[part]], z),
        )

    def step_two(kind, part):
        n = half[kind] // 2
        start = 2 * n * first[part] + n * (1 - second[part])
        return remote(
            side_work[kind].at[(slice(None),) + index(kind, part, start, n)],
            side_two[kind].at[part],
            s2_s.at[kind - 2, part],
            s2_r.at[kind - 2, part],
            (near[flip_second[part]], z),
        )

    def add_one(kind):
        n = half[kind]
        for part in range(2):
            step_one(kind, part).wait_recv()
            idx = (slice(None),) + index(kind, part, n * first[part], n)
            side_work[kind][idx] += side_one[kind][part]
            go(step_two(kind, part))

    def add_two(kind):
        n = half[kind] // 2
        for part in range(2):
            step_two(kind, part).wait_recv()
            idx = (slice(None),) + index(kind, part, kept(kind, part), n)
            side_work[kind][idx] += side_two[kind][part]
            if kind == 2:
                for j in range(2):
                    go(pairwise(kind, part, j))
            else:
                for j in hops:
                    go(along(part, j))

    def held(kind, part, j):
        idx = (goals[j],) + index(kind, part, kept(kind, part), half[kind] // 2)
        return (g, (kind,) + idx) if kind < 2 else (go_w, idx)

    def pairwise(kind, part, j):
        ref, idx = held(kind, part, j)
        dst = rz.at[kind, part, j] if kind < 2 else rz_o.at[part, j]
        return remote(
            ref.at[idx], dst, z_s.at[kind, part, j], z_r.at[kind, part, j], (w, pair)
        )

    def crosswise(kind, part):
        ref, idx = held(kind, part, 2)
        dst = rz.at[kind, part, 2] if kind < 2 else rz_o.at[part, 2]
        return remote(
            ref.at[idx], dst, z_s.at[kind, part, 2], z_r.at[kind, part, 2], (w, across)
        )

    def cross(kind, part):
        pairwise(kind, part, 1).wait_recv()
        ref, idx = held(kind, part, 2)
        ref[idx] += rz[kind, part, 1] if kind < 2 else rz_o[part, 1]
        go(crosswise(kind, part))

    def cross_out():
        for part in range(2):
            cross(2, part)

    def along(part, j):
        idx = index(3, part, kept(3, part), half[3] // 2)
        return remote(
            gq_w.at[(zto[j],) + idx],
            f_q.at[(z,) + idx],
            z_s.at[3, part, j],
            z_r.at[3, part, j],
            (w, zto[j]),
        )

    def add_line(kind):
        for part in range(2):
            idx = index(kind, part, kept(kind, part), half[kind] // 2)
            if kind < 3:
                pairwise(kind, part, 0).wait_recv()
                crosswise(kind, part).wait_recv()
                ref, own = held(kind, part, 3)
                far = rz.at[kind] if kind < 2 else rz_o
                total = (
                    ref[own].astype(F32)
                    + far[part, 0].astype(F32)
                    + far[part, 2].astype(F32)
                ).astype(BF16)
                if kind < 2:
                    f_g[(kind,) + idx] = total
                else:
                    f_o[idx] = total
            else:
                for j in hops:
                    along(part, j).wait_recv()
                f_q[(z,) + idx] = gq_w[(z,) + idx]
            go(share_one(kind, part))

    def region(kind, part, start, n):
        idx = index(kind, part, start, n)
        if kind == 3:
            idx = (slice(None),) + idx
        return final[kind].at[idx]

    def share_one(kind, part):
        ref = region(kind, part, kept(kind, part), half[kind] // 2)
        return remote(
            ref,
            ref,
            g_s.at[kind, part, 0],
            g_r.at[kind, part, 0],
            (near[flip_second[part]], z),
        )

    def share_two(kind, part):
        ref = region(kind, part, half[kind] * first[part], half[kind])
        return remote(
            ref,
            ref,
            g_s.at[kind, part, 1],
            g_r.at[kind, part, 1],
            (near[flip_first[part]], z),
        )

    def relayed(kind):
        for part in range(2):
            n = half[kind] // 2
            start = half[kind] * first[part] + n * (1 - second[part])
            ref = region(kind, part, start, n)
            remote(
                ref,
                ref,
                g_s.at[kind, part, 0],
                g_r.at[kind, part, 0],
                (near[flip_second[part]], z),
            ).wait_recv()
            go(share_two(kind, part))

    def shared(kind):
        for part in range(2):
            ref = region(kind, part, half[kind] * (1 - first[part]), half[kind])
            remote(
                ref,
                ref,
                g_s.at[kind, part, 1],
                g_r.at[kind, part, 1],
                (near[flip_first[part]], z),
            ).wait_recv()
        go(
            remote(
                final[kind], out[kind].at[core], sib_s.at[kind], sib_r.at[kind], (near[1], z)
            )
        )
        copy = pltpu.make_async_copy(final[kind], out[kind].at[core], out_sem.at[kind])
        copy.start()
        outs.append(copy)

    CH = C // 2
    pair_o = remote(
        go_s.at[:, at((1 - core) * CH, CH)], go_far, pair_s.at[0], pair_r.at[0], (near[1], z)
    )
    pair_q = remote(
        gq_s.at[:, at((1 - core) * CH, CH)], gq_far, pair_s.at[1], pair_r.at[1], (near[1], z)
    )

    def do_block(j, rows):
        return remote(
            do4_ref.at[zto[j]], do_all.at[rows], do_s.at[j], do_r.at[j], (w, zto[j])
        )

    def do_send():
        for j in hops:
            go(do_block(j, at(z * R, R)))
        do_all[at(z * R, R), :] = do4_ref[z]

    def do_wait(b):
        j = lax.rem(z + NZ - b, NZ)
        block = remote(
            do4_ref.at[b], do_all.at[pl.ds(b * R, R)], do_s.at[j], do_r.at[j], (w, zto[0])
        )

        @pl.when(z != b)
        def _():
            block.wait_recv()

    def pair_out():
        loads[len(chunks)].wait()
        go(pair_o)

    def pair_out_done():
        pair_o.wait_recv()
        go_w[...] = go_s[:, at(core * CH, CH), :] + go_far[...]
        for part in range(2):
            go(step_one(2, part))

    def heads(b):
        width, slot = spans[b], b % 2
        block = slice(b * R, (b + 1) * R)
        load_p(b).wait()
        dq_f[...] = jnp.zeros_like(dq_f)

        @pl.loop(0, 4)
        def _(h):
            pick = lanes(R, C, h)
            rows = at(h * R, R)
            do_h = do_all[block, :] * pick.astype(BF16)
            do_st[rows, :] = do_h
            q_st[rows, :] = q_ref[block, :] * pick.astype(BF16)
            p = p_s[slot, rows, :width].astype(F32)
            t = p * dot_nt(do_h, v_ref[:width, :])
            ds = (t - p * jnp.sum(t, -1, keepdims=True)).astype(BF16)
            ds_s[rows, :width] = ds
            dq_f[...] += dot(ds, k_ref[:width, :]) * pick

        dqkv[block, 0:C] = (dq_f[...] * 0.125).astype(BF16)

    def keys(b):
        width, slot = spans[b], b % 2

        @pl.loop(0, width // 128)
        def _(n):
            cols = at(n * 128, 128, 128)
            dv = dot_tn(p_s[slot, :, cols], do_st[...])
            dk = dot_tn(ds_s[:, cols], q_st[...])
            if b == NZ - 1:
                dv_f[cols, :] = dv
                dk_f[cols, :] = dk
            else:
                dv_f[cols, :] += dv
                dk_f[cols, :] += dk

        if b >= 2:
            load_p(b - 2).start()
        block = slice(b * R, (b + 1) * R)
        dqkv[block, C : 2 * C] = (dk_f[block, :] * 0.125).astype(BF16)
        dqkv[block, 2 * C :] = dv_f[block, :].astype(BF16)

    def partial(d):
        dh[d] = dot_nt(dqkv[d * R : (d + 1) * R, :], wq_ref[...]).astype(BF16)

    def hand(j):
        dst = rel.at[j]
        return remote(dh.at[goals[j]], dst, ru_s.at[j], ru_r.at[j], (w, across if j == 2 else pair))

    def hand_over(d):
        for j in range(2):

            @pl.when(goals[j] == d)
            def _():
                hand(j).start()

    def hand_across(lower):
        @pl.when((z < NZ // 2) if lower else (z >= NZ // 2))
        def _():
            hand(1).wait_recv()
            dh[across] += rel[1]
            hand(2).start()

    def grad_qkv():
        loads[len(chunks) + 1].wait()
        for d in range(NZ):
            gq_s[d] = dot_tn(h1[:, d * C : (d + 1) * C], dqkv[...]).astype(BF16)
        go(pair_q)
        for d in range(NZ):
            s_f[d] = small_in[:, d * C : (d + 1) * C]
        s_f[z, 8:9, :] = rowsum(dqkv[:, 0:C].astype(F32))
        s_f[z, 9:10, :] = rowsum(dqkv[:, 2 * C :].astype(F32))

    def pair_qkv_done():
        pair_q.wait_recv()
        gq_w[...] = gq_s[:, at(core * CH, CH), :] + gq_far[...]
        for part in range(2):
            go(step_one(3, part))

    def line_copy(j):
        return remote(s_b.at[zto[j]], s_z.at[j], sz_s.at[j], sz_r.at[j], (w, zto[j]))

    def plane_copy(j):
        return remote(s_p, s_g.at[j], sp_s.at[j], sp_r.at[j], (near[j], z))

    def input_grad():
        hand(0).wait_recv()
        hand(2).wait_recv()
        dh1 = dh[z].astype(F32) + rel[0].astype(F32) + rel[2].astype(F32)
        n1, inverse = norm(x_ref[...].astype(F32))
        dx_ref[...] = (dmid_ref[...] + norm_back(dh1, n1, inverse, par_ref[0:1, :])).astype(BF16)
        gain = rowsum(dh1 * n1)
        shift = rowsum(dh1)
        for d in range(NZ):
            s_f[d, 0:1, :] = gain[:, d * C : (d + 1) * C]
            s_f[d, 4:5, :] = shift[:, d * C : (d + 1) * C]
        s_b[...] = s_f[...].astype(BF16)
        for j in hops:
            go(line_copy(j))

    def small_line():
        total = s_f[z]
        for j in hops:
            line_copy(j).wait_recv()
            total += s_z[j].astype(F32)
        small_out[...] = total
        s_p[...] = total.astype(BF16)
        for j in range(1, GROUP):
            go(plane_copy(j))

    def small_plane():
        total = small_out[...]
        for j in range(1, GROUP):
            plane_copy(j).wait_recv()
            total += s_g[j].astype(F32)
        small_out[...] = total

    for act, *where in (
        (launch, 0),
        (do_send,),
        (launch, 1),
        (reduce_one, 0),
        (launch, 2),
        (launch, 3),
        (do_wait, 3),
        (heads, 3),
        (launch, 4),
        (do_wait, 1),
        (pair_out,),
        (reduce_two, 0),
        (do_wait, 2),
        (keys, 3),
        (partial, 3),
        (heads, 2),
        (hand_over, 3),
        (reduce_one, 2),
        (keys, 2),
        (do_wait, 0),
        (partial, 2),
        (hand_over, 2),
        (reduce_one, 3),
        (reduce_one, 4),
        (heads, 1),
        (pair_out_done,),
        (reduce_two, 2),
        (keys, 1),
        (launch, 5),
        (partial, 1),
        (heads, 0),
        (keys, 0),
        (reduce_two, 3),
        (grad_qkv,),
        (reduce_two, 4),
        (partial, 0),
        (pair_qkv_done,),
        (add_one, 2),
        (hand_over, 0),
        (hand_over, 1),
        (add_one, 3),
        (reduce_one, 5),
        (launch, 6),
        (add_two, 3),
        (reduce_one, 1),
        (reduce_two, 5),
        (launch, 7),
        (reduce_one, 6),
        (reduce_two, 1),
        (hand_across, True),
        (hand_across, False),
        (reduce_one, 7),
        (add_line, 3),
        (reduce_two, 6),
        (reduce_two, 7),
        (add_line, 0),
        (add_two, 2),
        (relayed, 3),
        (add_line, 1),
        (relayed, 0),
        (relayed, 1),
        (shared, 0),
        (cross_out,),
        (input_grad,),
        (add_line, 2),
        (shared, 1),
        (shared, 3),
        (relayed, 2),
        (small_line,),
        (shared, 2),
        (small_plane,),
    ):
        act(*where)
    for kind in range(4):
        remote(
            final[kind], out[kind].at[1 - core], sib_s.at[kind], sib_r.at[kind], (near[1], z)
        ).wait_recv()
    for j in range(3):
        hand(j).wait_send()
    for copy in pending:
        copy.wait_send()
    for copy in outs:
        copy.wait()


def reduce(NZ, inputs, dmid, par, small, do4, wq, q, k, v, h1, p, g, go):
    R, D = inputs.shape
    C = D // NZ
    T = NZ * R
    FH = g.shape[2]
    wide = p.shape[2]
    shape = jax.ShapeDtypeStruct
    buf = pltpu.VMEM
    return pl.pallas_call(
        functools.partial(reduce_kernel, NZ),
        out_shape=[
            shape((R, D), BF16),
            shape((2, 2, FH, D), BF16),
            shape((2, C // 2, D), BF16),
            shape((2, NZ, C // 2, 3 * C), BF16),
            shape((16, C), F32),
        ],
        in_specs=[VMEM] * 9 + [ANY] * 4,
        out_specs=[VMEM, ANY, ANY, ANY, VMEM],
        scratch_shapes=[
            buf((T, D), BF16),
            buf((2, 4 * R, wide), BF16),
            buf((2, NZ, FH, D), BF16),
            buf((NZ, C, D), BF16),
            buf((NZ, C // 2, D), BF16),
            buf((NZ, C // 2, D), BF16),
            buf((NZ, C, 3 * C), BF16),
            buf((NZ, C // 2, 3 * C), BF16),
            buf((NZ, C // 2, 3 * C), BF16),
            buf((2 * NZ, 2, FH // 4, D), BF16),
            buf((2, NZ, C // 4, D // 2), BF16),
            buf((2, NZ, C // 4, 3 * C // 2), BF16),
            buf((2 * NZ, 2, FH // 8, D), BF16),
            buf((2, NZ, C // 8, D // 2), BF16),
            buf((2, NZ, C // 8, 3 * C // 2), BF16),
            buf((2, 2, NZ - 1, FH // 8, D), BF16),
            buf((2, NZ - 1, C // 8, D // 2), BF16),
            buf((2, FH, D), BF16),
            buf((C // 2, D), BF16),
            buf((NZ, C // 2, 3 * C), BF16),
            buf((T, C), BF16),
            buf((4 * R, C), BF16),
            buf((4 * R, C), BF16),
            buf((4 * R, wide), BF16),
            buf((R, C), F32),
            buf((wide, C), F32),
            buf((wide, C), F32),
            buf((T, 3 * C), BF16),
            buf((NZ, R, D), BF16),
            buf((3, R, D), BF16),
            buf((NZ, 16, C), F32),
            buf((NZ, 16, C), BF16),
            buf((NZ, 16, C), BF16),
            buf((16, C), BF16),
            buf((GROUP, 16, C), BF16),
            DMA((2 * NZ + 2,)),
            DMA((2,)),
            DMA((NZ,)),
            DMA((NZ,)),
            DMA((2,)),
            DMA((2,)),
            DMA((2, 2)),
            DMA((2, 2)),
            DMA((2, 2)),
            DMA((2, 2)),
            DMA((2 * NZ, 2)),
            DMA((2 * NZ, 2)),
            DMA((2 * NZ, 2)),
            DMA((2 * NZ, 2)),
            DMA((4, 2, NZ)),
            DMA((4, 2, NZ)),
            DMA((4, 2, 2)),
            DMA((4, 2, 2)),
            DMA((4,)),
            DMA((4,)),
            DMA((3,)),
            DMA((3,)),
            DMA((NZ,)),
            DMA((NZ,)),
            DMA((GROUP,)),
            DMA((GROUP,)),
            DMA((4,)),
        ],
        compiler_params=pltpu.CompilerParams(
            collective_id=2, has_side_effects=True, vmem_limit_bytes=60 * 2**20
        ),
    )(inputs, dmid, par, small, do4, wq, q, k, v, h1, p, g, go)


def widen_kernel(fc2, fc1, out, qkv, d_fc2, d_fc1, d_out, d_qkv):
    step = pl.program_id(0)
    C = d_qkv.shape[0]
    d_fc2[...] = fc2[0, 0].astype(F32)
    d_fc1[...] = fc1[0, 0].astype(F32)
    d_out[...] = out[0].astype(F32)
    NZ = pl.num_programs(0) // 2
    for t in range(3):
        cols = at(t * (d_qkv.shape[1] // 3) + lax.rem(step, NZ) * (C), C, 128)
        d_qkv[at(lax.div(step, NZ) * (C // 2), C // 2), cols] = qkv[
            0, 0, :, t * C : (t + 1) * C
        ].astype(F32)


def widen(g, go, gq):
    FH, D = g.shape[2:]
    NZ, CH = gq.shape[1:3]
    C = 2 * CH
    steps = 2 * NZ
    shape = jax.ShapeDtypeStruct
    return pl.pallas_call(
        widen_kernel,
        grid=(steps,),
        out_shape=[
            shape((2 * FH, D), F32),
            shape((C, 2 * NZ * FH), F32),
            shape((C, D), F32),
            shape((C, 3 * D), F32),
        ],
        in_specs=[
            pl.BlockSpec((1, 1, 2 * FH // steps, D), lambda i: (0, i // NZ, i % NZ, 0)),
            pl.BlockSpec(
                (1, 1, C, FH), lambda i: (1, i % 2, i // 2 // 2, i // 2 % 2)
            ),
            pl.BlockSpec((1, C // steps, D), lambda i: (i // NZ, i % NZ, 0)),
            pl.BlockSpec((1, 1, CH, 3 * C), lambda i: (i // NZ, i % NZ, 0, 0)),
        ],
        out_specs=[
            pl.BlockSpec((2 * FH // steps, D), lambda i: (i, 0)),
            pl.BlockSpec((C, FH), lambda i: (0, i)),
            pl.BlockSpec((C // steps, D), lambda i: (i, 0)),
            pl.BlockSpec((C, 3 * D), lambda i: (0, 0)),
        ],
        compiler_params=pltpu.CompilerParams(vmem_limit_bytes=48 * 2**20),
    )(g, g, go, gq)


def shards(NZ, W, inputs, w_qkv, w_out, w_fc1, w_fc2, norm_gain, shifts, text_len, cotangent):
    R, D = inputs.shape[1:]
    C = D // NZ
    FF = w_fc1.shape[1]
    FH = FF // (2 * NZ)
    par = jnp.concatenate([norm_gain, shifts], 0)
    o4, h1, q, k, v, wq, wa, wb, wo, par_f, p = attend(
        NZ, inputs[0], par, text_len, w_qkv, w_out, w_fc1, w_fc2
    )
    act, dmid, do4, g, go, small = feed(NZ, inputs[0], cotangent[0], o4, par_f, wa, wb, wo)
    dx, g, go, gq, small = reduce(
        NZ, inputs[0], dmid, par_f, small, do4, wq, q, k, v, h1, p, g, go
    )
    fc2, fc1, out, qkv = widen(g, go, gq)
    grads = (qkv, out, fc1, fc2, small)
    if W > GROUP:
        groups = [list(range(i, W, GROUP)) for i in range(GROUP)]
        grads = lax.psum(grads, "wide", axis_index_groups=groups)
    return (act[None], dx[None]) + tuple(grads[:4]) + (grads[4][:4], grads[4][4:])


def solution(mesh):
    return jax.shard_map(
        functools.partial(shards, mesh.shape["narrow"], mesh.shape["wide"]),
        mesh=mesh,
        in_specs=(
            P("wide", "narrow", None),
            P("narrow", None),
            P("narrow", None),
            P("narrow", None),
            P("narrow", None),
            P(None, "narrow"),
            P(None, "narrow"),
            P("wide"),
            P("wide", "narrow", None),
        ),
        out_specs=(
            P("wide", "narrow", None),
            P("wide", "narrow", None),
            P("narrow", None),
            P("narrow", None),
            P("narrow", None),
            P("narrow", None),
            P(None, "narrow"),
            P(None, "narrow"),
        ),
        check_vma=False,
    )
```

```python
import functools
import math

import jax
import jax.numpy as jnp
from jax import lax
from jax.experimental import pallas as pl
from jax.experimental.pallas import tpu as pltpu
from jax.sharding import PartitionSpec as P

HEADS = 16
TEXT = 64
EPS = 1e-5
GROUP = 8
WINDOW = 3
MESH = pl.DeviceIdType.MESH
F32 = jnp.float32
BF16 = jnp.bfloat16
ANY = pl.BlockSpec(memory_space=pl.ANY)
VMEM = pl.BlockSpec(memory_space=pltpu.VMEM)
SMEM = pl.BlockSpec(memory_space=pltpu.SMEM)
DMA = pltpu.SemaphoreType.DMA


def at(start, size, step=16):
    return pl.ds(pl.multiple_of(start, step), size)


def place():
    w = lax.axis_index("wide")
    z = lax.axis_index("narrow")
    return w, z, lax.rem(w, 2), lax.rem(lax.div(w, 2), 2), lax.rem(lax.div(w, 4), 2)


def flips(w, core, x, y, j):
    return (
        w
        + (j & 1) * (1 - 2 * core)
        + ((j >> 1) & 1) * (2 - 4 * x)
        + ((j >> 2) & 1) * (4 - 8 * y)
    )


def remote(src, dst, send_sem, recv_sem, device):
    return pltpu.make_async_remote_copy(
        src_ref=src,
        dst_ref=dst,
        send_sem=send_sem,
        recv_sem=recv_sem,
        device_id=device,
        device_id_type=MESH,
    )


def meet(devices):
    barrier = pltpu.get_barrier_semaphore()
    for device in devices:
        pl.semaphore_signal(barrier, inc=1, device_id=device, device_id_type=MESH)
    pl.semaphore_wait(barrier, len(devices))


def dot(left, right):
    return lax.dot_general(left, right, (((1,), (0,)), ((), ())), preferred_element_type=F32)


def dot_nt(left, right):
    return lax.dot_general(left, right, (((1,), (1,)), ((), ())), preferred_element_type=F32)


def dot_tn(left, right):
    return lax.dot_general(left, right, (((0,), (0,)), ((), ())), preferred_element_type=F32)


def norm(values):
    centred = values - jnp.mean(values, -1, keepdims=True)
    inverse = lax.rsqrt(jnp.mean(centred * centred, -1, keepdims=True) + EPS)
    return centred * inverse, inverse


def norm_back(incoming, normed, inverse, gain):
    scaled = incoming * gain
    return inverse * (
        scaled
        - jnp.mean(scaled, -1, keepdims=True)
        - normed * jnp.mean(scaled * normed, -1, keepdims=True)
    )


def rowsum(values):
    return jnp.sum(values, 0, keepdims=True)


def lanes(rows, width, head):
    lane = lax.broadcasted_iota(jnp.int32, (rows, width), 1)
    size = width // 4
    return ((lane >= head * size) & (lane < head * size + size)).astype(F32)


def widths(rows, blocks):
    return [-(-rows * (b + 1) // 128) * 128 for b in range(blocks)]


def forward_kernel(
    NZ,
    x_ref,
    par_ref,
    len_ref,
    cot_ref,
    wqkv_ref,
    wout_ref,
    wfc1_ref,
    wfc2_ref,
    h1_out,
    q_out,
    k_out,
    v_out,
    wq_out,
    par_out,
    p_out,
    act_ref,
    dmid_ref,
    do_ref,
    g_out,
    go_out,
    small_ref,
    par_all,
    par_f,
    stage,
    wq,
    a_ref,
    b_ref,
    wo_ref,
    h1,
    q_s,
    k_s,
    v_s,
    mid_s,
    big_one,
    big_two,
    o_acc,
    o_send,
    o4,
    h3,
    dm,
    part,
    far_m,
    far_h,
    n2_s,
    n3_s,
    g_s,
    go_s,
    loc_sem,
    par_s,
    par_r,
    wz_s,
    wz_r,
    wp_s,
    wp_r,
    h_s,
    h_r,
    fz_s,
    fz_r,
    fp_s,
    fp_r,
    fq_s,
    fq_r,
    sib_s,
    sib_r,
    o_s,
    o_r,
    out_sem,
    swap_s,
    swap_r,
):
    R, D = x_ref.shape
    C = D // NZ
    FH = wfc1_ref.shape[1] // (2 * NZ)
    w, z, core, x, y = place()
    chip = x + 2 * y
    w8 = core + 2 * chip
    near = {j: flips(w, core, x, y, j) for j in range(1, GROUP)}
    zto = [lax.rem(z + j, NZ) for j in range(NZ)]
    zfrom = [lax.rem(z + NZ - j, NZ) for j in range(NZ)]
    hops = range(1, NZ)
    pending = []

    def go(copy):
        copy.start()
        pending.append(copy)

    first = (x, y)
    second = (y, x)
    flip_first = (2, 4)
    flip_second = (4, 2)
    local = 1 + 3 * NZ
    RW = C // GROUP
    staged = [
        pltpu.make_async_copy(
            wqkv_ref.at[:, pl.ds(t * D + d * C, C)],
            stage.at[d, :, pl.ds(t * C, C)],
            loc_sem.at[1 + 3 * d + t],
        )
        for d in range(NZ)
        for t in range(3)
    ]
    owned = [
        pltpu.make_async_copy(
            wfc1_ref.at[:, at((2 * j) * FH + core * FH, FH, 128)],
            a_ref.at[at(z * C, C), pl.ds(j * FH, FH)],
            loc_sem.at[local + j],
        )
        for j in range(NZ)
    ]
    owned.append(
        pltpu.make_async_copy(
            wfc2_ref.at[at(core * FH, FH)], b_ref.at[z], loc_sem.at[local + NZ]
        )
    )
    owned.append(
        pltpu.make_async_copy(wout_ref, wo_ref.at[at(z * C, C)], loc_sem.at[local + NZ + 1])
    )
    own_par = pltpu.make_async_copy(par_ref, par_all.at[z], loc_sem.at[0])
    own_wq = pltpu.make_async_copy(stage.at[z], wq.at[at(z * C, C)], loc_sem.at[local + NZ + 2])

    def par_copy(j, source):
        return remote(par_ref, par_all.at[source], par_s.at[j], par_r.at[j], (w, zto[j]))

    def start():
        for copy in (own_par, *staged, *owned):
            copy.start()
        meet([(w, zto[j]) for j in hops] + [(near[j], z) for j in range(1, GROUP)])
        for j in hops:
            go(par_copy(j, z))

    def wq_line(j, source):
        return remote(
            stage.at[zto[j], at(w8 * RW, RW)],
            wq.at[at(source * C + w8 * RW, RW)],
            wz_s.at[j],
            wz_r.at[j],
            (w, zto[j]),
        )

    def wq_plane(j, t, owner):
        part = wq.at[at(zfrom[j] * C + owner * RW, RW)]
        return remote(part, part, wp_s.at[j, t], wp_r.at[j, t], (near[t], z))

    def wq_send():
        for copy in staged:
            copy.wait()
        for j in hops:
            go(wq_line(j, z))
        own_wq.start()

    def wq_pass():
        for j in hops:
            wq_line(j, zfrom[j]).wait_recv()
            for t in range(1, GROUP):
                go(wq_plane(j, t, w8))

    def wq_wait():
        own_wq.wait()
        for j in hops:
            for t in range(1, GROUP):
                wq_plane(j, t, near[t] - w + w8).wait_recv()

    def first_norm():
        normed, _ = norm(x_ref[...].astype(F32))
        own_par.wait()
        for j in hops:
            par_copy(j, zfrom[j]).wait_recv()
        for d in range(NZ):
            par_f[:, d * C : (d + 1) * C] = par_all[d].astype(F32)
        h1[at(z * R, R), :] = (normed * par_f[0:1, :] + par_f[4:5, :]).astype(BF16)

    def sends(way, k):
        if way == 0:
            return (z - k >= 0) & (z < NZ - 1)
        return (z + k <= NZ - 1) & (z > 0)

    def comes(way, k):
        return z - 1 - k >= 0 if way == 0 else z + 1 + k <= NZ - 1

    def sent(way, k):
        return jnp.maximum(z - k, 0) if way == 0 else jnp.minimum(z + k, NZ - 1)

    def got(way, k):
        return jnp.maximum(z - 1 - k, 0) if way == 0 else jnp.minimum(z + 1 + k, NZ - 1)

    ahead = ((w, jnp.minimum(z + 1, NZ - 1)), (w, jnp.maximum(z - 1, 0)))
    relays = []

    def h1_copy(way, k, block):
        ref = h1.at[at(block * R, R)]
        return remote(ref, ref, h_s.at[way, k], h_r.at[way, k], ahead[way])

    def h1_send(k):
        for way in range(2):
            copy = h1_copy(way, k, sent(way, k))
            relays.append((sends(way, k), copy))

            @pl.when(sends(way, k))
            def _():
                copy.start()

    def h1_come(k):
        for way in range(2):
            copy = h1_copy(way, k, got(way, k))

            @pl.when(comes(way, k))
            def _():
                copy.wait_recv()

        if k + 1 < NZ - 1:
            h1_send(k + 1)

    def rows_of(kind):
        return (C // 4, FH // 4, C // 8)[kind]

    def piece(kind, part, source, start, n):
        if kind == 0:
            half = a_ref.shape[1] // 2
            return a_ref.at[at(source * C + start, n), pl.ds(part * half, half)]
        if kind == 1:
            half = D // 2
            return b_ref.at[source, at(start, n), pl.ds(part * half, half)]
        half = D // 2
        return wo_ref.at[
            at(source * C + core * (C // 2) + start, n), pl.ds(part * half, half)
        ]

    def quarter(kind, part, source):
        n = rows_of(kind)
        return piece(kind, part, source, n * (2 * first[part] + second[part]), n)

    def w_copy(kind, part, way, k, source):
        ref = quarter(kind, part, source)
        return remote(
            ref, ref, fz_s.at[kind, part, way, k], fz_r.at[kind, part, way, k], ahead[way]
        )

    def w_send(kind, k):
        if k == 0:
            for copy in {0: owned[:NZ], 1: owned[NZ : NZ + 1], 2: owned[NZ + 1 :]}[kind]:
                copy.wait()
        for part in range(2):
            for way in range(2):
                copy = w_copy(kind, part, way, k, sent(way, k))
                relays.append((sends(way, k), copy))

                @pl.when(sends(way, k))
                def _():
                    copy.start()

    def share_one(kind, part, way, k):
        ref = quarter(kind, part, got(way, k))
        return remote(
            ref,
            ref,
            fp_s.at[kind, part, way, k],
            fp_r.at[kind, part, way, k],
            (near[flip_second[part]], z),
        )

    def share_two(kind, part, way, k):
        n = 2 * rows_of(kind)
        ref = piece(kind, part, got(way, k), n * first[part], n)
        return remote(
            ref,
            ref,
            fq_s.at[kind, part, way, k],
            fq_r.at[kind, part, way, k],
            (near[flip_first[part]], z),
        )

    def w_come(kind, k):
        for part in range(2):
            for way in range(2):
                copy = w_copy(kind, part, way, k, got(way, k))
                share = share_one(kind, part, way, k)
                relays.append((comes(way, k), share))

                @pl.when(comes(way, k))
                def _():
                    copy.wait_recv()
                    share.start()

        if k + 1 < NZ - 1:
            w_send(kind, k + 1)

    def w_double(kind, k):
        for part in range(2):
            for way in range(2):
                source = got(way, k)
                n = rows_of(kind)
                start = n * (2 * first[part] + (1 - second[part]))
                ref = piece(kind, part, source, start, n)
                copy = remote(
                    ref,
                    ref,
                    fp_s.at[kind, part, way, k],
                    fp_r.at[kind, part, way, k],
                    (near[flip_second[part]], z),
                )
                share = share_two(kind, part, way, k)
                relays.append((comes(way, k), share))

                @pl.when(comes(way, k))
                def _():
                    copy.wait_recv()
                    share.start()

    def w_done(kind, k):
        for part in range(2):
            for way in range(2):
                n = 2 * rows_of(kind)
                ref = piece(kind, part, got(way, k), n * (1 - first[part]), n)
                copy = remote(
                    ref,
                    ref,
                    fq_s.at[kind, part, way, k],
                    fq_r.at[kind, part, way, k],
                    (near[flip_first[part]], z),
                )

                @pl.when(comes(way, k))
                def _():
                    copy.wait_recv()

    rows_k = k_s.shape[0]
    total = NZ * R

    def project(block):
        rows = at(block * R, R)
        bias = par_ref[...].astype(F32)
        q_s[rows, :] = (dot(h1[rows, :], wq[:, 0:C]) + bias[8:9, :]).astype(BF16)
        k_s[rows, :] = dot(h1[rows, :], wq[:, C : 2 * C]).astype(BF16)
        v_s[rows, :] = (dot(h1[rows, :], wq[:, 2 * C : 3 * C]) + bias[9:10, :]).astype(BF16)

    def project_own():
        if rows_k > total:
            k_s[total:rows_k, :] = jnp.zeros((rows_k - total, C), BF16)
            v_s[total:rows_k, :] = jnp.zeros((rows_k - total, C), BF16)
        project(z)

    def project_come(k):
        for way in range(2):

            @pl.when(comes(way, k))
            def _():
                project(got(way, k))

    outs = []
    p_copies = []

    def emit(src, dst, sem):
        copy = pltpu.make_async_copy(src, dst, out_sem.at[sem])
        copy.start()
        outs.append(copy)

    def emit_qkv():
        emit(h1, h1_out, 0)
        emit(q_s, q_out, 1)
        emit(k_s, k_out, 2)
        emit(v_s, v_out, 3)
        emit(wq, wq_out, 4)
        emit(par_f, par_out, 5)

    scale = math.log2(math.e) / math.sqrt(C // 4)
    text_len = len_ref[0]
    spans = widths(R, NZ)

    def o_copy(b):
        return remote(
            o_send.at[pl.ds(b * R, R)], o4.at[z], o_s.at[b], o_r.at[z], (w, jnp.int32(b))
        )

    def attention(b):
        width = spans[b]
        row = lax.broadcasted_iota(jnp.int32, (R, width), 0) + b * R
        col = lax.broadcasted_iota(jnp.int32, (R, width), 1)
        allowed = (col <= row) & ((col >= TEXT) | (col < text_len))
        mid_s[:, :width] = jnp.where(allowed, 0.0, -1e30)
        p_s = (big_one, big_two)[len(p_copies) % 2]
        if len(p_copies) > 1:
            p_copies[-2].wait()
        o_acc[...] = jnp.zeros_like(o_acc)

        @pl.loop(0, 4)
        def _(h):
            pick = lanes(R, C, h)
            q_h = q_s[b * R : (b + 1) * R, :] * pick.astype(BF16)
            s = dot_nt(q_h, k_s[:width, :]) + mid_s[:, :width]
            e = jnp.exp2((s - jnp.max(s, -1, keepdims=True)) * scale)
            p = (e * (1.0 / jnp.sum(e, -1, keepdims=True))).astype(BF16)
            p_s[at(h * R, R), :width] = p
            o_acc[...] += dot(p, v_s[:width, :]) * pick

        copy = pltpu.make_async_copy(
            p_s.at[:, pl.ds(0, width)], p_out.at[b, :, pl.ds(0, width)], out_sem.at[6 + b]
        )
        copy.start()
        p_copies.append(copy)
        o_send[b * R : (b + 1) * R, :] = o_acc[...].astype(BF16)
        send = o_copy(b)

        @pl.when(z != b)
        def _():
            send.start()

        @pl.when(z == b)
        def _():
            o4[z] = o_send[b * R : (b + 1) * R, :]

    def o_come():
        for d in range(NZ):
            copy = remote(
                o_send.at[pl.ds(d * R, R)], o4.at[d], o_s.at[d], o_r.at[d], (w, jnp.int32(d))
            )

            @pl.when(z != d)
            def _():
                copy.wait_send()
                copy.wait_recv()

    def sibling(j, half):
        part = wo_ref.at[at(zfrom[j] * C + half * (C // 2), C // 2)]
        return remote(part, part, sib_s.at[j], sib_r.at[j], (near[1], z))

    def wo_swap():
        for j in hops:
            go(sibling(j, core))

    def wo_done():
        for j in hops:
            sibling(j, 1 - core).wait_recv()

    gate, slope = big_one.at[pl.ds(0, 2 * R)], big_one.at[pl.ds(2 * R, 2 * R)]
    du = big_two.at[pl.ds(0, 2 * R)]
    mine, theirs = slice(0, R), slice(R, 2 * R)
    kept = {}
    shift = 4

    def swap(src, dst, i):
        return remote(src, dst, swap_s.at[i], swap_r.at[i], (near[1], z))

    swap_h = swap(h3.at[pl.ds(0, R)], h3.at[pl.ds(R, R)], 0)
    swap_m = swap(part.at[0], far_m, 1)
    swap_d = swap(dm.at[pl.ds(0, R)], dm.at[pl.ds(R, R)], 2)
    swap_u = swap(part.at[1], far_h, 3)

    def param(row):
        return par_f[row : row + 1, :]

    def project_out():
        branch = dot(o4[0], wo_ref[0:C, :])
        for s in range(1, NZ):
            branch += dot(o4[s], wo_ref[s * C : (s + 1) * C, :])
        n2, kept["r2"] = norm(branch + param(shift + 6))
        mid = x_ref[...].astype(F32) + n2 * param(1) + param(shift + 1)
        n2_s[...] = n2
        mid_s[:, :D] = mid
        n3, kept["r3"] = norm(mid)
        n3_s[...] = n3
        h3[mine, :] = (n3 * param(2) + param(shift + 2)).astype(BF16)
        go(swap_h)
        for copy in p_copies[-2:]:
            copy.wait()

    def hidden(rows):
        for s in range(NZ):
            cols = slice(s * FH, (s + 1) * FH)
            line = param(shift + 8 + s)
            bias = jnp.where(core == 0, line[:, :FH], line[:, FH:])
            u = dot(h3[rows, :], a_ref[:, cols]) + bias
            k = math.sqrt(2.0 / math.pi)
            sq = u * u
            t = jnp.tanh(u * (k + k * 0.044715 * sq))
            half = 0.5 + 0.5 * t
            gate[rows, cols] = (u * half).astype(BF16)
            slope[rows, cols] = (
                half + (0.5 * u) * (1.0 - t * t) * (k + 3.0 * k * 0.044715 * sq)
            ).astype(BF16)

    def hidden_mine():
        hidden(mine)

    def hidden_theirs():
        swap_h.wait_recv()
        hidden(theirs)

    def contract(rows):
        total = dot(gate[rows, 0:FH], b_ref[0])
        for s in range(1, NZ):
            total += dot(gate[rows, s * FH : (s + 1) * FH], b_ref[s])
        return total

    def contract_theirs():
        part[0] = contract(theirs).astype(BF16)
        go(swap_m)

    def contract_mine():
        kept["m"] = contract(mine)

    def last_norm():
        swap_m.wait_recv()
        n4, r4 = norm(kept["m"] + far_m[...].astype(F32) + param(shift + 7))
        act_ref[...] = (mid_s[:, :D] + n4 * param(3) + param(shift + 3)).astype(BF16)
        e = cot_ref[...].astype(F32)
        small_ref[...] = jnp.zeros_like(small_ref)
        small_ref[3:4, :] = rowsum(e * n4)
        small_ref[shift + 3 : shift + 4, :] = rowsum(e)
        dm_low = norm_back(e, n4, r4, param(3)).astype(BF16)
        dm[mine, :] = dm_low
        small_ref[shift + 7 : shift + 8, :] = rowsum(dm_low.astype(F32))
        go(swap_d)

    def unhidden(rows):
        for s in range(NZ):
            cols = slice(s * FH, (s + 1) * FH)
            du[rows, cols] = (
                dot_nt(dm[rows, :], b_ref[s]) * slope[rows, cols].astype(F32)
            ).astype(BF16)

    def unhidden_mine():
        unhidden(mine)

    def unhidden_theirs():
        swap_d.wait_recv()
        unhidden(theirs)

    def back_theirs():
        part[1] = dot_nt(du[theirs, :], a_ref[...]).astype(BF16)
        go(swap_u)

    def grad_fc2():
        for s in range(NZ):
            cols = slice(s * FH, (s + 1) * FH)
            g_s[0, s] = dot_tn(gate[:, cols], dm[...]).astype(BF16)
        emit(g_s.at[0], g_out.at[0], 6 + NZ)

    def grad_fc1():
        for s in range(NZ):
            cols = slice(s * FH, (s + 1) * FH)
            tile = dot_tn(h3[...], du[:, cols]).astype(BF16)
            low, left = (s // 2) * C, (s % 2) * FH
            for d in range(NZ):
                g_s[1, d, low : low + C, left : left + FH] = tile[d * C : (d + 1) * C, :]
            total = rowsum(du[:, cols].astype(F32))
            row = shift + 8 + s
            small_ref[row : row + 1, 0:FH] = jnp.where(core == 0, total, 0.0)
            small_ref[row : row + 1, FH:] = jnp.where(core == 0, 0.0, total)
        emit(g_s.at[1], g_out.at[1], 7 + NZ)

    def back_mine():
        kept["dh3"] = dot_nt(du[mine, :], a_ref[...])

    def norms_back():
        swap_u.wait_recv()
        dh3 = kept["dh3"] + far_h[...].astype(F32)
        n3 = n3_s[...]
        small_ref[2:3, :] = rowsum(dh3 * n3)
        small_ref[shift + 2 : shift + 3, :] = rowsum(dh3)
        dmid = cot_ref[...].astype(F32) + norm_back(dh3, n3, kept["r3"], param(2))
        dmid_ref[...] = dmid
        n2 = n2_s[...]
        small_ref[1:2, :] = rowsum(dmid * n2)
        small_ref[shift + 1 : shift + 2, :] = rowsum(dmid)
        da = norm_back(dmid, n2, kept["r2"], param(1)).astype(BF16)
        small_ref[shift + 6 : shift + 7, :] = rowsum(da.astype(F32))
        kept["da"] = da

    def back_out():
        for s in range(NZ):
            do_ref[s] = dot_nt(kept["da"], wo_ref[s * C : (s + 1) * C, :]).astype(BF16)

    def grad_out():
        for s in range(NZ):
            go_s[s] = dot_tn(o4[s], kept["da"]).astype(BF16)
        emit(go_s, go_out, 8 + NZ)

    for act, *where in (
        (start,),
        (w_send, 2, 0),
        (w_send, 0, 0),
        (first_norm,),
        (w_come, 2, 0),
        (w_come, 0, 0),
        (w_double, 2, 0),
        (w_come, 2, 1),
        (wq_send,),
        (w_come, 0, 1),
        (h1_send, 0),
        (w_double, 0, 0),
        (w_come, 0, 2),
        (w_come, 2, 2),
        (w_send, 1, 0),
        (w_double, 2, 1),
        (wq_pass,),
        (w_double, 2, 2),
        (h1_come, 0),
        (w_double, 0, 1),
        (h1_come, 1),
        (wq_wait,),
        (w_done, 2, 1),
        (w_double, 0, 2),
        (w_come, 1, 0),
        (project_own,),
        (w_done, 0, 1),
        (project_come, 1),
        (w_double, 1, 0),
        (project_come, 0),
        (h1_come, 2),
        (project_come, 2),
        (w_done, 2, 0),
        (attention, 1),
        (w_done, 2, 2),
        (wo_swap,),
        (w_come, 1, 1),
        (w_done, 1, 0),
        (attention, 3),
        (emit_qkv,),
        (w_double, 1, 1),
        (attention, 0),
        (wo_done,),
        (attention, 2),
        (w_come, 1, 2),
        (w_done, 0, 2),
        (w_double, 1, 2),
        (o_come,),
        (w_done, 0, 0),
        (project_out,),
        (hidden_mine,),
        (hidden_theirs,),
        (w_done, 1, 2),
        (w_done, 1, 1),
        (contract_theirs,),
        (contract_mine,),
        (last_norm,),
        (unhidden_mine,),
        (back_mine,),
        (unhidden_theirs,),
        (back_theirs,),
        (grad_fc2,),
        (norms_back,),
        (back_out,),
        (grad_fc1,),
        (grad_out,),
    ):
        act(*where)
    for ok, copy in relays:

        @pl.when(ok)
        def _():
            copy.wait_send()

    for copy in pending:
        copy.wait_send()
    for copy in outs:
        copy.wait()


def forward(NZ, inputs, cotangent, par, text_len, w_qkv, w_out, w_fc1, w_fc2):
    R, D = inputs.shape
    C = D // NZ
    FH = w_fc1.shape[1] // (2 * NZ)
    F = NZ * FH
    T = NZ * R
    wide = widths(R, NZ)[-1]
    shape = jax.ShapeDtypeStruct
    buf = pltpu.VMEM
    return pl.pallas_call(
        functools.partial(forward_kernel, NZ),
        out_shape=[
            shape((T, D), BF16),
            shape((T, C), BF16),
            shape((wide, C), BF16),
            shape((wide, C), BF16),
            shape((D, 3 * C), BF16),
            shape((16, D), F32),
            shape((NZ, 4 * R, wide), BF16),
            shape((R, D), BF16),
            shape((R, D), F32),
            shape((NZ, R, C), BF16),
            shape((2, NZ, FH, D), BF16),
            shape((NZ, C, D), BF16),
            shape((16, D), F32),
        ],
        in_specs=[VMEM, VMEM, SMEM, VMEM, ANY, ANY, ANY, ANY],
        out_specs=[ANY] * 7 + [VMEM, VMEM, VMEM, ANY, ANY, VMEM],
        scratch_shapes=[
            buf((NZ, 16, C), BF16),
            buf((16, D), F32),
            buf((NZ, C, 3 * C), BF16),
            buf((D, 3 * C), BF16),
            buf((D, F), BF16),
            buf((NZ, FH, D), BF16),
            buf((D, D), BF16),
            buf((T, D), BF16),
            buf((T, C), BF16),
            buf((wide, C), BF16),
            buf((wide, C), BF16),
            buf((R, wide), F32),
            buf((4 * R, F), BF16),
            buf((4 * R, F), BF16),
            buf((R, C), F32),
            buf((T, C), BF16),
            buf((NZ, R, C), BF16),
            buf((2 * R, D), BF16),
            buf((2 * R, D), BF16),
            buf((2, R, D), BF16),
            buf((R, D), BF16),
            buf((R, D), BF16),
            buf((R, D), F32),
            buf((R, D), F32),
            buf((2, NZ, FH, D), BF16),
            buf((NZ, C, D), BF16),
            DMA((4 * NZ + 4,)),
            DMA((NZ,)),
            DMA((NZ,)),
            DMA((NZ,)),
            DMA((NZ,)),
            DMA((NZ, GROUP)),
            DMA((NZ, GROUP)),
            DMA((2, NZ)),
            DMA((2, NZ)),
            DMA((3, 2, 2, NZ)),
            DMA((3, 2, 2, NZ)),
            DMA((3, 2, 2, NZ)),
            DMA((3, 2, 2, NZ)),
            DMA((3, 2, 2, NZ)),
            DMA((3, 2, 2, NZ)),
            DMA((NZ,)),
            DMA((NZ,)),
            DMA((NZ,)),
            DMA((NZ,)),
            DMA((10 + NZ,)),
            DMA((4,)),
            DMA((4,)),
        ],
        compiler_params=pltpu.CompilerParams(
            collective_id=0, has_side_effects=True, vmem_limit_bytes=60 * 2**20
        ),
    )(inputs, par, text_len, cotangent, w_qkv, w_out, w_fc1, w_fc2)


def reduce_kernel(
    NZ,
    x_ref,
    dmid_ref,
    par_ref,
    small_in,
    do4_ref,
    wq_ref,
    q_ref,
    k_ref,
    v_ref,
    h1_hbm,
    p_hbm,
    g_hbm,
    go_hbm,
    dx_ref,
    g_out,
    go_out,
    gq_out,
    small_out,
    h1,
    p_s,
    g,
    go_s,
    go_far,
    go_w,
    gq_s,
    gq_far,
    gq_w,
    r1,
    r1_o,
    r1_q,
    r2,
    r2_o,
    r2_q,
    rz,
    rz_o,
    f_g,
    f_o,
    f_q,
    do_all,
    do_st,
    q_st,
    ds_s,
    dq_f,
    dk_f,
    dv_f,
    dqkv,
    dh,
    rel,
    s_f,
    s_b,
    s_z,
    s_p,
    s_g,
    load_sem,
    p_sem,
    do_s,
    do_r,
    pair_s,
    pair_r,
    s1_s,
    s1_r,
    s2_s,
    s2_r,
    c1_s,
    c1_r,
    c2_s,
    c2_r,
    z_s,
    z_r,
    g_s,
    g_r,
    sib_s,
    sib_r,
    ru_s,
    ru_r,
    sz_s,
    sz_r,
    sp_s,
    sp_r,
    out_sem,
):
    R, D = x_ref.shape
    C = D // NZ
    T = NZ * R
    FH = g.shape[2]
    w, z, core, x, y = place()
    near = {j: flips(w, core, x, y, j) for j in range(1, GROUP)}
    zto = [lax.rem(z + j, NZ) for j in range(NZ)]
    zfrom = [lax.rem(z + NZ - j, NZ) for j in range(NZ)]
    hops = range(1, NZ)
    pending = []

    def go(copy):
        copy.start()
        pending.append(copy)

    pair = z + 1 - 2 * lax.rem(z, 2)
    across = lax.rem(z + 2, NZ)
    goals = (pair, lax.rem(pair + 2, NZ), across, z)
    chunks = [(kind, j) for j in range(NZ) for kind in range(2)]
    loads = [
        pltpu.make_async_copy(
            g_hbm.at[kind, goals[j]], g.at[kind, goals[j]], load_sem.at[i]
        )
        for i, (kind, j) in enumerate(chunks)
    ]
    loads.append(pltpu.make_async_copy(go_hbm, go_s, load_sem.at[len(chunks)]))
    loads.append(pltpu.make_async_copy(h1_hbm, h1, load_sem.at[len(chunks) + 1]))
    for copy in loads:
        copy.start()
    spans = widths(R, NZ)

    def load_p(b):
        span = pl.ds(0, spans[b])
        return pltpu.make_async_copy(
            p_hbm.at[b, :, span], p_s.at[b % 2, :, span], p_sem.at[b % 2]
        )

    load_p(NZ - 1).start()
    load_p(NZ - 2).start()

    meet([(w, zto[j]) for j in hops] + [(near[j], z) for j in range(1, GROUP)])

    first = (x, y)
    second = (y, x)
    flip_first = (2, 4)
    flip_second = (4, 2)
    half = (FH // 4, FH // 4, C // 4, C // 4)
    side_one = {2: r1_o, 3: r1_q}
    side_two = {2: r2_o, 3: r2_q}
    side_work = {2: go_w, 3: gq_w}
    final = {0: f_g.at[0], 1: f_g.at[1], 2: f_o, 3: f_q}
    out = {0: g_out.at[0], 1: g_out.at[1], 2: go_out, 3: gq_out}
    outs = []

    def index(kind, part, start, n):
        if kind < 2:
            return at(part * (FH // 2) + start, n), slice(None)
        width = side_work[kind].shape[2] // 2
        return at(start, n), pl.ds(part * width, width)

    def kept(kind, part):
        return half[kind] * first[part] + (half[kind] // 2) * second[part]

    def chunk_one(c, part):
        kind, j = chunks[c]
        n = half[kind]
        return remote(
            g.at[(kind, goals[j]) + index(kind, part, n * (1 - first[part]), n)],
            r1.at[c, part],
            c1_s.at[c, part],
            c1_r.at[c, part],
            (near[flip_first[part]], z),
        )

    def chunk_two(c, part):
        kind, j = chunks[c]
        n = half[kind] // 2
        start = 2 * n * first[part] + n * (1 - second[part])
        return remote(
            g.at[(kind, goals[j]) + index(kind, part, start, n)],
            r2.at[c, part],
            c2_s.at[c, part],
            c2_r.at[c, part],
            (near[flip_second[part]], z),
        )

    def launch(c):
        loads[c].wait()
        for part in range(2):
            go(chunk_one(c, part))

    def reduce_one(c):
        kind, j = chunks[c]
        n = half[kind]
        for part in range(2):
            chunk_one(c, part).wait_recv()
            idx = (kind, goals[j]) + index(kind, part, n * first[part], n)
            g[idx] += r1[c, part]
            go(chunk_two(c, part))

    def reduce_two(c):
        kind, j = chunks[c]
        n = half[kind] // 2
        for part in range(2):
            chunk_two(c, part).wait_recv()
            idx = (kind, goals[j]) + index(kind, part, kept(kind, part), n)
            g[idx] += r2[c, part]
            if j < 2:
                go(pairwise(kind, part, j))
            elif j == 2:
                cross(kind, part)

    def step_one(kind, part):
        n = half[kind]
        return remote(
            side_work[kind].at[(slice(None),) + index(kind, part, n * (1 - first[part]), n)],
            side_one[kind].at[part],
            s1_s.at[kind - 2, part],
            s1_r.at[kind - 2, part],
            (near[flip_first[part]], z),
        )

    def step_two(kind, part):
        n = half[kind] // 2
        start = 2 * n * first[part] + n * (1 - second[part])
        return remote(
            side_work[kind].at[(slice(None),) + index(kind, part, start, n)],
            side_two[kind].at[part],
            s2_s.at[kind - 2, part],
            s2_r.at[kind - 2, part],
            (near[flip_second[part]], z),
        )

    def add_one(kind):
        n = half[kind]
        for part in range(2):
            step_one(kind, part).wait_recv()
            idx = (slice(None),) + index(kind, part, n * first[part], n)
            side_work[kind][idx] += side_one[kind][part]
            go(step_two(kind, part))

    def add_two(kind):
        n = half[kind] // 2
        for part in range(2):
            step_two(kind, part).wait_recv()
            idx = (slice(None),) + index(kind, part, kept(kind, part), n)
            side_work[kind][idx] += side_two[kind][part]
            if kind == 2:
                for j in range(2):
                    go(pairwise(kind, part, j))
            else:
                for j in hops:
                    go(along(part, j))

    def held(kind, part, j):
        idx = (goals[j],) + index(kind, part, kept(kind, part), half[kind] // 2)
        return (g, (kind,) + idx) if kind < 2 else (go_w, idx)

    def pairwise(kind, part, j):
        ref, idx = held(kind, part, j)
        dst = rz.at[kind, part, j] if kind < 2 else rz_o.at[part, j]
        return remote(
            ref.at[idx], dst, z_s.at[kind, part, j], z_r.at[kind, part, j], (w, pair)
        )

    def crosswise(kind, part):
        ref, idx = held(kind, part, 2)
        dst = rz.at[kind, part, 2] if kind < 2 else rz_o.at[part, 2]
        return remote(
            ref.at[idx], dst, z_s.at[kind, part, 2], z_r.at[kind, part, 2], (w, across)
        )

    def cross(kind, part):
        pairwise(kind, part, 1).wait_recv()
        ref, idx = held(kind, part, 2)
        ref[idx] += rz[kind, part, 1] if kind < 2 else rz_o[part, 1]
        go(crosswise(kind, part))

    def cross_out():
        for part in range(2):
            cross(2, part)

    def along(part, j):
        idx = index(3, part, kept(3, part), half[3] // 2)
        return remote(
            gq_w.at[(zto[j],) + idx],
            f_q.at[(z,) + idx],
            z_s.at[3, part, j],
            z_r.at[3, part, j],
            (w, zto[j]),
        )

    def add_line(kind):
        for part in range(2):
            idx = index(kind, part, kept(kind, part), half[kind] // 2)
            if kind < 3:
                pairwise(kind, part, 0).wait_recv()
                crosswise(kind, part).wait_recv()
                ref, own = held(kind, part, 3)
                far = rz.at[kind] if kind < 2 else rz_o
                total = (
                    ref[own].astype(F32)
                    + far[part, 0].astype(F32)
                    + far[part, 2].astype(F32)
                ).astype(BF16)
                if kind < 2:
                    f_g[(kind,) + idx] = total
                else:
                    f_o[idx] = total
            else:
                for j in hops:
                    along(part, j).wait_recv()
                f_q[(z,) + idx] = gq_w[(z,) + idx]
            go(share_one(kind, part))

    def region(kind, part, start, n):
        idx = index(kind, part, start, n)
        if kind == 3:
            idx = (slice(None),) + idx
        return final[kind].at[idx]

    def share_one(kind, part):
        ref = region(kind, part, kept(kind, part), half[kind] // 2)
        return remote(
            ref,
            ref,
            g_s.at[kind, part, 0],
            g_r.at[kind, part, 0],
            (near[flip_second[part]], z),
        )

    def share_two(kind, part):
        ref = region(kind, part, half[kind] * first[part], half[kind])
        return remote(
            ref,
            ref,
            g_s.at[kind, part, 1],
            g_r.at[kind, part, 1],
            (near[flip_first[part]], z),
        )

    def relayed(kind):
        for part in range(2):
            n = half[kind] // 2
            start = half[kind] * first[part] + n * (1 - second[part])
            ref = region(kind, part, start, n)
            remote(
                ref,
                ref,
                g_s.at[kind, part, 0],
                g_r.at[kind, part, 0],
                (near[flip_second[part]], z),
            ).wait_recv()
            go(share_two(kind, part))

    def shared(kind):
        for part in range(2):
            ref = region(kind, part, half[kind] * (1 - first[part]), half[kind])
            remote(
                ref,
                ref,
                g_s.at[kind, part, 1],
                g_r.at[kind, part, 1],
                (near[flip_first[part]], z),
            ).wait_recv()
        go(
            remote(
                final[kind], out[kind].at[core], sib_s.at[kind], sib_r.at[kind], (near[1], z)
            )
        )
        copy = pltpu.make_async_copy(final[kind], out[kind].at[core], out_sem.at[kind])
        copy.start()
        outs.append(copy)

    CH = C // 2
    pair_o = remote(
        go_s.at[:, at((1 - core) * CH, CH)], go_far, pair_s.at[0], pair_r.at[0], (near[1], z)
    )
    pair_q = remote(
        gq_s.at[:, at((1 - core) * CH, CH)], gq_far, pair_s.at[1], pair_r.at[1], (near[1], z)
    )

    def do_block(j, rows):
        return remote(
            do4_ref.at[zto[j]], do_all.at[rows], do_s.at[j], do_r.at[j], (w, zto[j])
        )

    def do_send():
        for j in hops:
            go(do_block(j, at(z * R, R)))
        do_all[at(z * R, R), :] = do4_ref[z]

    def do_wait(b):
        j = lax.rem(z + NZ - b, NZ)
        block = remote(
            do4_ref.at[b], do_all.at[pl.ds(b * R, R)], do_s.at[j], do_r.at[j], (w, zto[0])
        )

        @pl.when(z != b)
        def _():
            block.wait_recv()

    def pair_out():
        loads[len(chunks)].wait()
        go(pair_o)

    def pair_out_done():
        pair_o.wait_recv()
        go_w[...] = go_s[:, at(core * CH, CH), :] + go_far[...]
        for part in range(2):
            go(step_one(2, part))

    def heads(b):
        width, slot = spans[b], b % 2
        block = slice(b * R, (b + 1) * R)
        load_p(b).wait()
        dq_f[...] = jnp.zeros_like(dq_f)

        @pl.loop(0, 4)
        def _(h):
            pick = lanes(R, C, h)
            rows = at(h * R, R)
            do_h = do_all[block, :] * pick.astype(BF16)
            do_st[rows, :] = do_h
            q_st[rows, :] = q_ref[block, :] * pick.astype(BF16)
            p = p_s[slot, rows, :width].astype(F32)
            t = p * dot_nt(do_h, v_ref[:width, :])
            ds = (t - p * jnp.sum(t, -1, keepdims=True)).astype(BF16)
            ds_s[rows, :width] = ds
            dq_f[...] += dot(ds, k_ref[:width, :]) * pick

        dqkv[block, 0:C] = (dq_f[...] * 0.125).astype(BF16)

    def keys(b):
        width, slot = spans[b], b % 2

        @pl.loop(0, width // 128)
        def _(n):
            cols = at(n * 128, 128, 128)
            dv = dot_tn(p_s[slot, :, cols], do_st[...])
            dk = dot_tn(ds_s[:, cols], q_st[...])
            if b == NZ - 1:
                dv_f[cols, :] = dv
                dk_f[cols, :] = dk
            else:
                dv_f[cols, :] += dv
                dk_f[cols, :] += dk

        if b >= 2:
            load_p(b - 2).start()
        block = slice(b * R, (b + 1) * R)
        dqkv[block, C : 2 * C] = (dk_f[block, :] * 0.125).astype(BF16)
        dqkv[block, 2 * C :] = dv_f[block, :].astype(BF16)

    def partial(d):
        dh[d] = dot_nt(dqkv[d * R : (d + 1) * R, :], wq_ref[...]).astype(BF16)

    def hand(j):
        dst = rel.at[j]
        return remote(dh.at[goals[j]], dst, ru_s.at[j], ru_r.at[j], (w, across if j == 2 else pair))

    def hand_over(d):
        for j in range(2):

            @pl.when(goals[j] == d)
            def _():
                hand(j).start()

    def hand_across(lower):
        @pl.when((z < NZ // 2) if lower else (z >= NZ // 2))
        def _():
            hand(1).wait_recv()
            dh[across] += rel[1]
            hand(2).start()

    def grad_qkv():
        loads[len(chunks) + 1].wait()
        for d in range(NZ):
            gq_s[d] = dot_tn(h1[:, d * C : (d + 1) * C], dqkv[...]).astype(BF16)
        go(pair_q)
        for d in range(NZ):
            s_f[d] = small_in[:, d * C : (d + 1) * C]
        s_f[z, 8:9, :] = rowsum(dqkv[:, 0:C].astype(F32))
        s_f[z, 9:10, :] = rowsum(dqkv[:, 2 * C :].astype(F32))

    def pair_qkv_done():
        pair_q.wait_recv()
        gq_w[...] = gq_s[:, at(core * CH, CH), :] + gq_far[...]
        for part in range(2):
            go(step_one(3, part))

    def line_copy(j):
        return remote(s_b.at[zto[j]], s_z.at[j], sz_s.at[j], sz_r.at[j], (w, zto[j]))

    def plane_copy(j):
        return remote(s_p, s_g.at[j], sp_s.at[j], sp_r.at[j], (near[j], z))

    def input_grad():
        hand(0).wait_recv()
        hand(2).wait_recv()
        dh1 = dh[z].astype(F32) + rel[0].astype(F32) + rel[2].astype(F32)
        n1, inverse = norm(x_ref[...].astype(F32))
        dx_ref[...] = (dmid_ref[...] + norm_back(dh1, n1, inverse, par_ref[0:1, :])).astype(BF16)
        gain = rowsum(dh1 * n1)
        shift = rowsum(dh1)
        for d in range(NZ):
            s_f[d, 0:1, :] = gain[:, d * C : (d + 1) * C]
            s_f[d, 4:5, :] = shift[:, d * C : (d + 1) * C]
        s_b[...] = s_f[...].astype(BF16)
        for j in hops:
            go(line_copy(j))

    def small_line():
        total = s_f[z]
        for j in hops:
            line_copy(j).wait_recv()
            total += s_z[j].astype(F32)
        small_out[...] = total
        s_p[...] = total.astype(BF16)
        for j in range(1, GROUP):
            go(plane_copy(j))

    def small_plane():
        total = small_out[...]
        for j in range(1, GROUP):
            plane_copy(j).wait_recv()
            total += s_g[j].astype(F32)
        small_out[...] = total

    for act, *where in (
        (launch, 0),
        (do_send,),
        (launch, 1),
        (reduce_one, 0),
        (launch, 2),
        (launch, 3),
        (do_wait, 3),
        (heads, 3),
        (launch, 4),
        (do_wait, 1),
        (pair_out,),
        (reduce_two, 0),
        (do_wait, 2),
        (keys, 3),
        (partial, 3),
        (heads, 2),
        (hand_over, 3),
        (reduce_one, 2),
        (keys, 2),
        (do_wait, 0),
        (partial, 2),
        (hand_over, 2),
        (reduce_one, 3),
        (reduce_one, 4),
        (heads, 1),
        (pair_out_done,),
        (reduce_two, 2),
        (keys, 1),
        (launch, 5),
        (partial, 1),
        (heads, 0),
        (keys, 0),
        (reduce_two, 3),
        (grad_qkv,),
        (reduce_two, 4),
        (partial, 0),
        (pair_qkv_done,),
        (add_one, 2),
        (hand_over, 0),
        (hand_over, 1),
        (add_one, 3),
        (reduce_one, 5),
        (launch, 6),
        (add_two, 3),
        (reduce_one, 1),
        (reduce_two, 5),
        (launch, 7),
        (reduce_one, 6),
        (reduce_two, 1),
        (hand_across, True),
        (hand_across, False),
        (reduce_one, 7),
        (add_line, 3),
        (reduce_two, 6),
        (reduce_two, 7),
        (add_line, 0),
        (add_two, 2),
        (relayed, 3),
        (add_line, 1),
        (relayed, 0),
        (relayed, 1),
        (shared, 0),
        (cross_out,),
        (input_grad,),
        (add_line, 2),
        (shared, 1),
        (shared, 3),
        (relayed, 2),
        (small_line,),
        (shared, 2),
        (small_plane,),
    ):
        act(*where)
    for kind in range(4):
        remote(
            final[kind], out[kind].at[1 - core], sib_s.at[kind], sib_r.at[kind], (near[1], z)
        ).wait_recv()
    for j in range(3):
        hand(j).wait_send()
    for copy in pending:
        copy.wait_send()
    for copy in outs:
        copy.wait()


def reduce(NZ, inputs, dmid, par, small, do4, wq, q, k, v, h1, p, g, go):
    R, D = inputs.shape
    C = D // NZ
    T = NZ * R
    FH = g.shape[2]
    wide = p.shape[2]
    shape = jax.ShapeDtypeStruct
    buf = pltpu.VMEM
    return pl.pallas_call(
        functools.partial(reduce_kernel, NZ),
        out_shape=[
            shape((R, D), BF16),
            shape((2, 2, FH, D), BF16),
            shape((2, C // 2, D), BF16),
            shape((2, NZ, C // 2, 3 * C), BF16),
            shape((16, C), F32),
        ],
        in_specs=[VMEM] * 9 + [ANY] * 4,
        out_specs=[VMEM, ANY, ANY, ANY, VMEM],
        scratch_shapes=[
            buf((T, D), BF16),
            buf((2, 4 * R, wide), BF16),
            buf((2, NZ, FH, D), BF16),
            buf((NZ, C, D), BF16),
            buf((NZ, C // 2, D), BF16),
            buf((NZ, C // 2, D), BF16),
            buf((NZ, C, 3 * C), BF16),
            buf((NZ, C // 2, 3 * C), BF16),
            buf((NZ, C // 2, 3 * C), BF16),
            buf((2 * NZ, 2, FH // 4, D), BF16),
            buf((2, NZ, C // 4, D // 2), BF16),
            buf((2, NZ, C // 4, 3 * C // 2), BF16),
            buf((2 * NZ, 2, FH // 8, D), BF16),
            buf((2, NZ, C // 8, D // 2), BF16),
            buf((2, NZ, C // 8, 3 * C // 2), BF16),
            buf((2, 2, NZ - 1, FH // 8, D), BF16),
            buf((2, NZ - 1, C // 8, D // 2), BF16),
            buf((2, FH, D), BF16),
            buf((C // 2, D), BF16),
            buf((NZ, C // 2, 3 * C), BF16),
            buf((T, C), BF16),
            buf((4 * R, C), BF16),
            buf((4 * R, C), BF16),
            buf((4 * R, wide), BF16),
            buf((R, C), F32),
            buf((wide, C), F32),
            buf((wide, C), F32),
            buf((T, 3 * C), BF16),
            buf((NZ, R, D), BF16),
            buf((3, R, D), BF16),
            buf((NZ, 16, C), F32),
            buf((NZ, 16, C), BF16),
            buf((NZ, 16, C), BF16),
            buf((16, C), BF16),
            buf((GROUP, 16, C), BF16),
            DMA((2 * NZ + 2,)),
            DMA((2,)),
            DMA((NZ,)),
            DMA((NZ,)),
            DMA((2,)),
            DMA((2,)),
            DMA((2, 2)),
            DMA((2, 2)),
            DMA((2, 2)),
            DMA((2, 2)),
            DMA((2 * NZ, 2)),
            DMA((2 * NZ, 2)),
            DMA((2 * NZ, 2)),
            DMA((2 * NZ, 2)),
            DMA((4, 2, NZ)),
            DMA((4, 2, NZ)),
            DMA((4, 2, 2)),
            DMA((4, 2, 2)),
            DMA((4,)),
            DMA((4,)),
            DMA((3,)),
            DMA((3,)),
            DMA((NZ,)),
            DMA((NZ,)),
            DMA((GROUP,)),
            DMA((GROUP,)),
            DMA((4,)),
        ],
        compiler_params=pltpu.CompilerParams(
            collective_id=2, has_side_effects=True, vmem_limit_bytes=60 * 2**20
        ),
    )(inputs, dmid, par, small, do4, wq, q, k, v, h1, p, g, go)


def widen_kernel(fc2, fc1, out, qkv, act, dx, small, d_fc2, d_fc1, d_out, d_qkv, d_act, d_dx, d_gain, d_shift):
    step = pl.program_id(0)
    C = d_qkv.shape[0]
    NZ = pl.num_programs(0) // 2
    d_fc2[...] = fc2[0, 0].astype(F32)
    d_fc1[...] = fc1[0, 0].astype(F32)
    d_out[...] = out[0].astype(F32)
    d_act[...] = act[...]
    d_dx[...] = dx[...]
    d_gain[...] = small[0:4, :]
    d_shift[...] = small[4:16, :]
    for t in range(3):
        cols = at(t * (d_qkv.shape[1] // 3) + lax.rem(step, NZ) * C, C, 128)
        d_qkv[at(lax.div(step, NZ) * (C // 2), C // 2), cols] = qkv[
            0, 0, :, t * C : (t + 1) * C
        ].astype(F32)


def widen(g, go, gq, act, dx, small):
    FH, D = g.shape[2:]
    NZ, CH = gq.shape[1:3]
    C = 2 * CH
    R = act.shape[0]
    steps = 2 * NZ
    part = D // steps
    shape = jax.ShapeDtypeStruct
    return pl.pallas_call(
        widen_kernel,
        grid=(steps,),
        out_shape=[
            shape((2 * FH, D), F32),
            shape((C, 2 * NZ * FH), F32),
            shape((C, D), F32),
            shape((C, 3 * D), F32),
            shape((R, D), BF16),
            shape((R, D), BF16),
            shape((4, C), F32),
            shape((12, C), F32),
        ],
        in_specs=[
            pl.BlockSpec((1, 1, 2 * FH // steps, D), lambda i: (0, i // NZ, i % NZ, 0)),
            pl.BlockSpec((1, 1, C, FH), lambda i: (1, i % 2, i // 2 // 2, i // 2 % 2)),
            pl.BlockSpec((1, C // steps, D), lambda i: (i // NZ, i % NZ, 0)),
            pl.BlockSpec((1, 1, CH, 3 * C), lambda i: (i // NZ, i % NZ, 0, 0)),
            pl.BlockSpec((R, part), lambda i: (0, i)),
            pl.BlockSpec((R, part), lambda i: (0, i)),
            pl.BlockSpec((16, C), lambda i: (0, 0)),
        ],
        out_specs=[
            pl.BlockSpec((2 * FH // steps, D), lambda i: (i, 0)),
            pl.BlockSpec((C, FH), lambda i: (0, i)),
            pl.BlockSpec((C // steps, D), lambda i: (i, 0)),
            pl.BlockSpec((C, 3 * D), lambda i: (0, 0)),
            pl.BlockSpec((R, part), lambda i: (0, i)),
            pl.BlockSpec((R, part), lambda i: (0, i)),
            pl.BlockSpec((4, C), lambda i: (0, 0)),
            pl.BlockSpec((12, C), lambda i: (0, 0)),
        ],
        compiler_params=pltpu.CompilerParams(vmem_limit_bytes=62 * 2**20),
    )(g, g, go, gq, act, dx, small)


def shards(NZ, W, inputs, w_qkv, w_out, w_fc1, w_fc2, norm_gain, shifts, text_len, cotangent):
    R, D = inputs.shape[1:]
    C = D // NZ
    FF = w_fc1.shape[1]
    FH = FF // (2 * NZ)
    par = jnp.concatenate([norm_gain, shifts], 0)
    h1, q, k, v, wq, par_f, p, act, dmid, do4, g, go, small = forward(
        NZ, inputs[0], cotangent[0], par, text_len, w_qkv, w_out, w_fc1, w_fc2
    )
    dx, g, go, gq, small = reduce(
        NZ, inputs[0], dmid, par_f, small, do4, wq, q, k, v, h1, p, g, go
    )
    fc2, fc1, out, qkv, act, dx, gain, shift = widen(g, go, gq, act, dx, small)
    grads = (qkv, out, fc1, fc2, gain, shift)
    if W > GROUP:
        groups = [list(range(i, W, GROUP)) for i in range(GROUP)]
        grads = lax.psum(grads, "wide", axis_index_groups=groups)
    return (act[None], dx[None]) + tuple(grads)


def solution(mesh):
    return jax.shard_map(
        functools.partial(shards, mesh.shape["narrow"], mesh.shape["wide"]),
        mesh=mesh,
        in_specs=(
            P("wide", "narrow", None),
            P("narrow", None),
            P("narrow", None),
            P("narrow", None),
            P("narrow", None),
            P(None, "narrow"),
            P(None, "narrow"),
            P("wide"),
            P("wide", "narrow", None),
        ),
        out_specs=(
            P("wide", "narrow", None),
            P("wide", "narrow", None),
            P("narrow", None),
            P("narrow", None),
            P("narrow", None),
            P("narrow", None),
            P(None, "narrow"),
            P(None, "narrow"),
        ),
        check_vma=False,
    )
```

```python
import functools
import math

import jax
import jax.numpy as jnp
from jax import lax
from jax.experimental import pallas as pl
from jax.experimental.pallas import tpu as pltpu
from jax.sharding import PartitionSpec as P

HEADS = 16
TEXT = 64
EPS = 1e-5
GROUP = 8
QUERIES = 256
MESH = pl.DeviceIdType.MESH
F32 = jnp.float32
BF16 = jnp.bfloat16
ANY = pl.BlockSpec(memory_space=pl.ANY)
VMEM = pl.BlockSpec(memory_space=pltpu.VMEM)
SMEM = pl.BlockSpec(memory_space=pltpu.SMEM)
DMA = pltpu.SemaphoreType.DMA


def at(start, size, step=16):
    return pl.ds(pl.multiple_of(start, step), size)


def place():
    w = lax.axis_index("wide")
    z = lax.axis_index("narrow")
    return w, z, lax.rem(w, 2), lax.rem(lax.div(w, 2), 2), lax.rem(lax.div(w, 4), 2)


def flips(w, core, x, y, j):
    return (
        w
        + (j & 1) * (1 - 2 * core)
        + ((j >> 1) & 1) * (2 - 4 * x)
        + ((j >> 2) & 1) * (4 - 8 * y)
    )


def remote(src, dst, send_sem, recv_sem, device):
    return pltpu.make_async_remote_copy(
        src_ref=src,
        dst_ref=dst,
        send_sem=send_sem,
        recv_sem=recv_sem,
        device_id=device,
        device_id_type=MESH,
    )


def meet(devices):
    barrier = pltpu.get_barrier_semaphore()
    for device in devices:
        pl.semaphore_signal(barrier, inc=1, device_id=device, device_id_type=MESH)
    pl.semaphore_wait(barrier, len(devices))


def dot(left, right):
    return lax.dot_general(left, right, (((1,), (0,)), ((), ())), preferred_element_type=F32)


def dot_nt(left, right):
    return lax.dot_general(left, right, (((1,), (1,)), ((), ())), preferred_element_type=F32)


def dot_tn(left, right):
    return lax.dot_general(left, right, (((0,), (0,)), ((), ())), preferred_element_type=F32)


def norm(values):
    centred = values - jnp.mean(values, -1, keepdims=True)
    inverse = lax.rsqrt(jnp.mean(centred * centred, -1, keepdims=True) + EPS)
    return centred * inverse, inverse


def norm_back(incoming, normed, inverse, gain):
    scaled = incoming * gain
    return inverse * (
        scaled
        - jnp.mean(scaled, -1, keepdims=True)
        - normed * jnp.mean(scaled * normed, -1, keepdims=True)
    )


def rowsum(values):
    return jnp.sum(values, 0, keepdims=True)


def lanes(rows, width, head):
    lane = lax.broadcasted_iota(jnp.int32, (rows, width), 1)
    size = width // 4
    return ((lane >= head * size) & (lane < head * size + size)).astype(F32)


def query_blocks(total):
    blocks = []
    for first in range(0, total, QUERIES):
        size = min(QUERIES, -(-(total - first) // 128) * 128)
        blocks.append((first, size, min(first + QUERIES, total)))
    return blocks


def forward_kernel(
    NZ,
    x_ref,
    gain_ref,
    shift_ref,
    len_ref,
    cot_ref,
    wqkv_ref,
    wout_ref,
    wfc1_ref,
    wfc2_ref,
    h1_out,
    q_out,
    k_out,
    v_out,
    wq_out,
    par_out,
    p_out,
    l_out,
    act_ref,
    dmid_ref,
    do_ref,
    g_out,
    go_out,
    small_ref,
    par_ref,
    par_all,
    par_f,
    stage,
    wq,
    a_ref,
    b_ref,
    wo_ref,
    h1,
    q_s,
    k_s,
    v_s,
    v_t,
    s_s,
    o_t,
    l_s,
    mid_s,
    big,
    o_send,
    o2,
    h3,
    dm,
    part,
    far_m,
    far_h,
    n3_s,
    g_s,
    go_s,
    loc_sem,
    par_s,
    par_r,
    wz_s,
    wz_r,
    wp_s,
    wp_r,
    h_s,
    h_r,
    fz_s,
    fz_r,
    fp_s,
    fp_r,
    fq_s,
    fq_r,
    sib_s,
    sib_r,
    o_s,
    o_r,
    out_sem,
    p_sem,
    swap_s,
    swap_r,
):
    R, D = x_ref.shape
    C = D // NZ
    FH = wfc1_ref.shape[1] // (2 * NZ)
    w, z, core, x, y = place()
    chip = x + 2 * y
    H = D // 2
    lower, upper = NZ // 2 - 1, NZ // 2
    own = (z == lower) | (z == upper)
    side = lax.div(z, NZ // 2)
    near = {j: flips(w, core, x, y, j) for j in range(1, GROUP)}
    zto = [lax.rem(z + j, NZ) for j in range(NZ)]
    zfrom = [lax.rem(z + NZ - j, NZ) for j in range(NZ)]
    hops = range(1, NZ)
    pending = []

    def go(copy):
        copy.start()
        pending.append(copy)

    first = (x, y)
    second = (y, x)
    flip_first = (2, 4)
    flip_second = (4, 2)
    local = 1 + 3 * NZ
    RW = C // GROUP
    staged = [
        pltpu.make_async_copy(
            wqkv_ref.at[:, pl.ds(t * D + d * H, H)],
            stage.at[d, :, pl.ds(t * H, H)],
            loc_sem.at[1 + 3 * d + t],
        )
        for d in range(2)
        for t in range(3)
    ]
    owned = [
        pltpu.make_async_copy(
            wfc1_ref.at[:, at((2 * j) * FH + core * FH, FH, 128)],
            a_ref.at[at(z * C, C), pl.ds(j * FH, FH)],
            loc_sem.at[local + j],
        )
        for j in range(NZ)
    ]
    owned.append(
        pltpu.make_async_copy(
            wfc2_ref.at[at(core * FH, FH)], b_ref.at[z], loc_sem.at[local + NZ]
        )
    )
    owned.append(
        pltpu.make_async_copy(wout_ref, wo_ref.at[at(z * C, C)], loc_sem.at[local + NZ + 1])
    )
    own_par = pltpu.make_async_copy(par_ref, par_all.at[z], loc_sem.at[0])
    own_wq = [
        pltpu.make_async_copy(stage.at[i], wq.at[at(z * C, C)], loc_sem.at[local + NZ + 2])
        for i in range(2)
    ]
    relays = []

    def other_chip(t):
        return (x + (t & 1) * (1 - 2 * x)) + 2 * (y + (t >> 1) * (1 - 2 * y))

    def when(ok, *copies):
        for copy in copies:
            relays.append((ok, copy))

        @pl.when(ok)
        def _():
            for copy in copies:
                copy.start()

    def par_copy(j, source):
        return remote(par_ref, par_all.at[source], par_s.at[j], par_r.at[j], (w, zto[j]))

    def start():
        par_ref[...] = jnp.concatenate(
            [gain_ref[...].astype(F32), shift_ref[...].astype(F32)], 0
        ).astype(BF16)
        for copy in (own_par, *staged, *owned):
            copy.start()
        meet([(w, zto[j]) for j in hops] + [(near[j], z) for j in range(1, GROUP)])
        for j in hops:
            go(par_copy(j, z))

    def eighth(chip_of):
        return core * (C // 2) + chip_of * RW

    def wq_line(i, source):
        return remote(
            stage.at[i, at(eighth(chip), RW)],
            wq.at[at(source * C + eighth(chip), RW)],
            wz_s.at[i],
            wz_r.at[source],
            (w, jnp.int32(lower + i)),
        )

    def wq_plane(source, t, owner):
        part = wq.at[at(source * C + eighth(owner), RW)]
        return remote(part, part, wp_s.at[source, t], wp_r.at[source, t], (near[2 * t], z))

    def wq_sibling(source, half_of):
        part = wq.at[at(source * C + half_of * (C // 2), C // 2)]
        return remote(part, part, wp_s.at[source, 0], wp_r.at[source, 0], (near[1], z))

    def wq_send():
        for copy in staged:
            copy.wait()
        for i in range(2):
            when(z != lower + i, wq_line(i, z))

            @pl.when(z == lower + i)
            def _():
                own_wq[i].start()

    def wq_pass():
        for source in range(NZ):
            ok = own & (z != source)
            arrival = wq_line(0, source)

            @pl.when(ok)
            def _():
                arrival.wait_recv()

            when(ok, *[wq_plane(source, t, chip) for t in range(1, 4)])

    def wq_swap():
        for source in range(NZ):
            ok = own & (z != source)
            arrivals = [wq_plane(source, t, other_chip(t)) for t in range(1, 4)]

            @pl.when(ok)
            def _():
                for copy in arrivals:
                    copy.wait_recv()

            when(ok, wq_sibling(source, core))

    def wq_wait():
        for i in range(2):

            @pl.when(z == lower + i)
            def _():
                own_wq[i].wait()

        for source in range(NZ):
            arrival = wq_sibling(source, 1 - core)

            @pl.when(own & (z != source))
            def _():
                arrival.wait_recv()

    def first_norm():
        normed, _ = norm(x_ref[...].astype(F32))
        own_par.wait()
        for j in hops:
            par_copy(j, zfrom[j]).wait_recv()
        for d in range(NZ):
            par_f[:, d * C : (d + 1) * C] = par_all[d].astype(F32)
        h1[at(z * R, R), :] = (normed * par_f[0:1, :] + par_f[4:5, :]).astype(BF16)

    def sends(way, k):
        if way == 0:
            return (z - k >= 0) & (z < NZ - 1)
        return (z + k <= NZ - 1) & (z > 0)

    def comes(way, k):
        return z - 1 - k >= 0 if way == 0 else z + 1 + k <= NZ - 1

    def sent(way, k):
        return jnp.maximum(z - k, 0) if way == 0 else jnp.minimum(z + k, NZ - 1)

    def got(way, k):
        return jnp.maximum(z - 1 - k, 0) if way == 0 else jnp.minimum(z + 1 + k, NZ - 1)

    ahead = ((w, jnp.minimum(z + 1, NZ - 1)), (w, jnp.maximum(z - 1, 0)))
    def h1_copy(way, k, block):
        ref = h1.at[at(block * R, R)]
        return remote(ref, ref, h_s.at[way, k], h_r.at[way, k], ahead[way])

    def h1_send(k):
        for way in range(2):
            toward = z <= lower if way == 0 else z >= upper
            when(sends(way, k) & toward, h1_copy(way, k, sent(way, k)))

    def h1_comes(way, k):
        return own & comes(way, k) & (z - 1 <= lower if way == 0 else z + 1 >= upper)

    def h1_come(k):
        for way in range(2):
            copy = h1_copy(way, k, got(way, k))

            @pl.when(h1_comes(way, k))
            def _():
                copy.wait_recv()

        if k + 1 < NZ // 2:
            h1_send(k + 1)

    def rows_of(kind):
        return (C // 4, FH // 4, C // 8)[kind]

    def piece(kind, part, source, start, n):
        if kind == 0:
            half = a_ref.shape[1] // 2
            return a_ref.at[at(source * C + start, n), pl.ds(part * half, half)]
        if kind == 1:
            half = D // 2
            return b_ref.at[source, at(start, n), pl.ds(part * half, half)]
        half = D // 2
        return wo_ref.at[
            at(source * C + core * (C // 2) + start, n), pl.ds(part * half, half)
        ]

    def quarter(kind, part, source):
        n = rows_of(kind)
        return piece(kind, part, source, n * (2 * first[part] + second[part]), n)

    def w_copy(kind, part, way, k, source):
        ref = quarter(kind, part, source)
        return remote(
            ref, ref, fz_s.at[kind, part, way, k], fz_r.at[kind, part, way, k], ahead[way]
        )

    def w_send(kind, k):
        if k == 0:
            for copy in {0: owned[:NZ], 1: owned[NZ : NZ + 1], 2: owned[NZ + 1 :]}[kind]:
                copy.wait()
        for part in range(2):
            for way in range(2):
                when(sends(way, k), w_copy(kind, part, way, k, sent(way, k)))

    def share_one(kind, part, way, k):
        ref = quarter(kind, part, got(way, k))
        return remote(
            ref,
            ref,
            fp_s.at[kind, part, way, k],
            fp_r.at[kind, part, way, k],
            (near[flip_second[part]], z),
        )

    def share_two(kind, part, way, k):
        n = 2 * rows_of(kind)
        ref = piece(kind, part, got(way, k), n * first[part], n)
        return remote(
            ref,
            ref,
            fq_s.at[kind, part, way, k],
            fq_r.at[kind, part, way, k],
            (near[flip_first[part]], z),
        )

    def w_come(kind, k):
        for part in range(2):
            for way in range(2):
                copy = w_copy(kind, part, way, k, got(way, k))
                share = share_one(kind, part, way, k)
                relays.append((comes(way, k), share))

                @pl.when(comes(way, k))
                def _():
                    copy.wait_recv()
                    share.start()

        if k + 1 < NZ - 1:
            w_send(kind, k + 1)

    def w_double(kind, k):
        for part in range(2):
            for way in range(2):
                source = got(way, k)
                n = rows_of(kind)
                start = n * (2 * first[part] + (1 - second[part]))
                ref = piece(kind, part, source, start, n)
                copy = remote(
                    ref,
                    ref,
                    fp_s.at[kind, part, way, k],
                    fp_r.at[kind, part, way, k],
                    (near[flip_second[part]], z),
                )
                share = share_two(kind, part, way, k)
                relays.append((comes(way, k), share))

                @pl.when(comes(way, k))
                def _():
                    copy.wait_recv()
                    share.start()

    def w_done(kind, k):
        for part in range(2):
            for way in range(2):
                n = 2 * rows_of(kind)
                ref = piece(kind, part, got(way, k), n * (1 - first[part]), n)
                copy = remote(
                    ref,
                    ref,
                    fq_s.at[kind, part, way, k],
                    fq_r.at[kind, part, way, k],
                    (near[flip_first[part]], z),
                )

                @pl.when(comes(way, k))
                def _():
                    copy.wait_recv()

    total = NZ * R

    def project(block):
        rows = at(block * R, R)
        gap = D - H
        bias = [
            jnp.where(z == lower, par_f[4 + t : 5 + t, 0:H], par_f[4 + t : 5 + t, gap:D])
            for t in (4, 5)
        ]
        q_s[rows, :] = (dot(h1[rows, :], wq[:, 0:H]) + bias[0]).astype(BF16)
        k_s[rows, :] = dot(h1[rows, :], wq[:, H : 2 * H]).astype(BF16)
        v_s[rows, :] = (dot(h1[rows, :], wq[:, 2 * H : 3 * H]) + bias[1]).astype(BF16)

    def project_own():
        pad = q_s.shape[0] - total

        @pl.when(own)
        def _():
            q_s[total:, :] = jnp.zeros((pad, H), BF16)
            project(z)

    def project_come(k):
        for way in range(2):

            @pl.when(h1_comes(way, k))
            def _():
                project(got(way, k))

    outs = []

    def emit(src, dst, sem):
        copy = pltpu.make_async_copy(src, dst, out_sem.at[sem])
        copy.start()
        outs.append(copy)

    guarded = []

    def emit_own(src, dst, sem):
        copy = pltpu.make_async_copy(src, dst, out_sem.at[sem])
        guarded.append(copy)

        @pl.when(own)
        def _():
            copy.start()

    def emit_qkv():
        emit_own(h1, h1_out, 0)
        emit_own(q_s, q_out, 1)
        emit_own(k_s, k_out, 2)
        emit_own(v_s, v_out, 3)
        emit_own(wq, wq_out, 4)
        emit(par_f, par_out, 5)

    scale = math.log2(math.e) / math.sqrt(C // 4)
    text_len = len_ref[0]
    spans = query_blocks(total)
    done = []

    def p_copy(g, i):
        first_query, size, keys = spans[i]
        return pltpu.make_async_copy(
            big.at[g, pl.ds(0, keys), pl.ds(0, 4 * size)],
            p_out.at[g, pl.ds(0, keys), pl.ds(4 * first_query, 4 * size)],
            p_sem.at[g],
        )

    def scores(i):
        first_query, size, keys = spans[i]
        queries = slice(first_query, first_query + size)
        span = keys - first_query
        row = lax.broadcasted_iota(jnp.int32, (span, size), 0)
        col = lax.broadcasted_iota(jnp.int32, (span, size), 1)
        later = jnp.where(row <= col, 0.0, -1e30)
        head_row = lax.broadcasted_iota(jnp.int32, (TEXT, size), 0)
        unread = jnp.where(head_row < text_len, 0.0, -1e30)

        @pl.loop(0, 2)
        def _(g):
            if done:
                p_copy(g, done[-1]).wait()
            cols = at(g * C, C, 128)
            if not done:
                v_t[g, :, :total] = jnp.transpose(v_s[:, cols].astype(F32)).astype(BF16)
            for h in range(4):
                q_h = q_s[queries, cols] * lanes(size, C, h).astype(BF16)
                s_s[:keys, :size] = dot_nt(k_s[:keys, cols], q_h)
                s_s[0:TEXT, :size] += unread
                s_s[first_query:keys, :size] += later
                s = s_s[:keys, :size]
                e = jnp.exp2((s - jnp.max(s, 0, keepdims=True)) * scale)
                share = 1.0 / jnp.sum(e, 0, keepdims=True)
                e = e.astype(BF16)
                big[g, :keys, h * size : (h + 1) * size] = e
                l_s[g, h, :, queries] = jnp.broadcast_to(share, (8, size))
                rows = slice(h * (C // 4), (h + 1) * (C // 4))
                o_t[rows, :size] = dot(v_t[g, rows, :keys], e) * share
            o_send[queries, cols] = jnp.transpose(o_t[:, :size]).astype(BF16)
            p_copy(g, i).start()

        done.append(i)

    def o_copy(b):
        return remote(
            o_send.at[pl.ds(b * R, R)], o2.at[side], o_s.at[b], o_r.at[side], (w, jnp.int32(b))
        )

    def attention(b):
        @pl.when(own)
        def _():
            last = len(spans) if b == NZ - 1 else b + 1
            for i in reversed(range(b, last)):
                scores(i)
            if b == 0:
                for g in range(2):
                    p_copy(g, 0).wait()

        when(own & (z != b), o_copy(b))

        @pl.when(z == b)
        def _():
            o2_own(b)

    def o2_own(b):
        if lower <= b <= upper:
            o2[b - lower] = o_send[b * R : (b + 1) * R, :]

    def o_come():
        for i in range(2):
            copy = remote(
                o_send.at[pl.ds(0, R)], o2.at[i], o_s.at[0], o_r.at[i], (w, jnp.int32(0))
            )

            @pl.when(z != lower + i)
            def _():
                copy.wait_recv()

    def emit_l():
        emit_own(l_s, l_out, 9 + NZ)

    def sibling(j, half):
        part = wo_ref.at[at(zfrom[j] * C + half * (C // 2), C // 2)]
        return remote(part, part, sib_s.at[j], sib_r.at[j], (near[1], z))

    def wo_swap():
        for j in hops:
            go(sibling(j, core))

    def wo_done():
        for j in hops:
            sibling(j, 1 - core).wait_recv()

    gate, slope = big.at[0, pl.ds(0, 2 * R)], big.at[0, pl.ds(2 * R, 2 * R)]
    du = big.at[1, pl.ds(0, 2 * R)]
    mine, theirs = slice(0, R), slice(R, 2 * R)
    kept = {}
    shift = 4

    def swap(src, dst, i):
        return remote(src, dst, swap_s.at[i], swap_r.at[i], (near[1], z))

    swap_h = swap(h3.at[pl.ds(0, R)], h3.at[pl.ds(R, R)], 0)
    swap_m = swap(part.at[0], far_m, 1)
    swap_d = swap(dm.at[pl.ds(0, R)], dm.at[pl.ds(R, R)], 2)
    swap_u = swap(part.at[1], far_h, 3)

    def param(row):
        return par_f[row : row + 1, :]

    def project_out():
        branch = dot(o2[0], wo_ref[0:H, :]) + dot(o2[1], wo_ref[H:D, :])
        n2, kept["r2"] = norm(branch + param(shift + 6))
        mid = x_ref[...].astype(F32) + n2 * param(1) + param(shift + 1)
        for s in range(NZ):
            s_s[s * R : (s + 1) * R, :] = n2[:, s * C : (s + 1) * C]
        mid_s[...] = mid
        n3, kept["r3"] = norm(mid)
        n3_s[...] = n3
        h3[mine, :] = (n3 * param(2) + param(shift + 2)).astype(BF16)
        go(swap_h)

    def hidden(rows):
        for s in range(NZ):
            cols = slice(s * FH, (s + 1) * FH)
            line = param(shift + 8 + s)
            bias = jnp.where(core == 0, line[:, :FH], line[:, FH:])
            u = dot(h3[rows, :], a_ref[:, cols]) + bias
            k = math.sqrt(2.0 / math.pi)
            sq = u * u
            t = jnp.tanh(u * (k + k * 0.044715 * sq))
            half = 0.5 + 0.5 * t
            gate[rows, cols] = (u * half).astype(BF16)
            slope[rows, cols] = (
                half + (0.5 * u) * (1.0 - t * t) * (k + 3.0 * k * 0.044715 * sq)
            ).astype(BF16)

    def hidden_mine():
        hidden(mine)

    def hidden_theirs():
        swap_h.wait_recv()
        hidden(theirs)

    def contract(rows):
        total = dot(gate[rows, 0:FH], b_ref[0])
        for s in range(1, NZ):
            total += dot(gate[rows, s * FH : (s + 1) * FH], b_ref[s])
        return total

    def contract_theirs():
        part[0] = contract(theirs).astype(BF16)
        go(swap_m)

    def contract_mine():
        kept["m"] = contract(mine)

    def last_norm():
        swap_m.wait_recv()
        n4, r4 = norm(kept["m"] + far_m[...].astype(F32) + param(shift + 7))
        act_ref[...] = (mid_s[...] + n4 * param(3) + param(shift + 3)).astype(BF16)
        e = cot_ref[...].astype(F32)
        small_ref[...] = jnp.zeros_like(small_ref)
        small_ref[3:4, :] = rowsum(e * n4)
        small_ref[shift + 3 : shift + 4, :] = rowsum(e)
        dm_low = norm_back(e, n4, r4, param(3)).astype(BF16)
        dm[mine, :] = dm_low
        small_ref[shift + 7 : shift + 8, :] = rowsum(dm_low.astype(F32))
        go(swap_d)

    def unhidden(rows):
        for s in range(NZ):
            cols = slice(s * FH, (s + 1) * FH)
            du[rows, cols] = (
                dot_nt(dm[rows, :], b_ref[s]) * slope[rows, cols].astype(F32)
            ).astype(BF16)

    def unhidden_mine():
        unhidden(mine)

    def unhidden_theirs():
        swap_d.wait_recv()
        unhidden(theirs)

    def back_theirs():
        part[1] = dot_nt(du[theirs, :], a_ref[...]).astype(BF16)
        go(swap_u)

    def grad_fc2():
        for s in range(NZ):
            cols = slice(s * FH, (s + 1) * FH)
            g_s[0, s] = dot_tn(gate[:, cols], dm[...]).astype(BF16)
        emit(g_s.at[0], g_out.at[0], 6 + NZ)

    def grad_fc1():
        for s in range(NZ):
            cols = slice(s * FH, (s + 1) * FH)
            tile = dot_tn(h3[...], du[:, cols]).astype(BF16)
            low, left = (s // 2) * C, (s % 2) * FH
            for d in range(NZ):
                g_s[1, d, low : low + C, left : left + FH] = tile[d * C : (d + 1) * C, :]
            total = rowsum(du[:, cols].astype(F32))
            row = shift + 8 + s
            small_ref[row : row + 1, 0:FH] = jnp.where(core == 0, total, 0.0)
            small_ref[row : row + 1, FH:] = jnp.where(core == 0, 0.0, total)
        emit(g_s.at[1], g_out.at[1], 7 + NZ)

    def back_mine():
        kept["dh3"] = dot_nt(du[mine, :], a_ref[...])

    def norms_back():
        swap_u.wait_recv()
        dh3 = kept["dh3"] + far_h[...].astype(F32)
        n3 = n3_s[...]
        small_ref[2:3, :] = rowsum(dh3 * n3)
        small_ref[shift + 2 : shift + 3, :] = rowsum(dh3)
        dmid = cot_ref[...].astype(F32) + norm_back(dh3, n3, kept["r3"], param(2))
        dmid_ref[...] = dmid
        n2 = jnp.concatenate([s_s[s * R : (s + 1) * R, :] for s in range(NZ)], 1)
        small_ref[1:2, :] = rowsum(dmid * n2)
        small_ref[shift + 1 : shift + 2, :] = rowsum(dmid)
        da = norm_back(dmid, n2, kept["r2"], param(1)).astype(BF16)
        small_ref[shift + 6 : shift + 7, :] = rowsum(da.astype(F32))
        kept["da"] = da

    def back_out():
        for i in range(2):
            do_ref[i] = dot_nt(kept["da"], wo_ref[i * H : (i + 1) * H, :]).astype(BF16)

    def grad_out():
        for i in range(2):
            go_s[2 * i : 2 * i + 2] = (
                dot_tn(o2[i], kept["da"]).astype(BF16).reshape(2, C, D)
            )
        emit(go_s, go_out, 8 + NZ)

    for act, *where in (
        (start,),
        (w_send, 2, 0),
        (wq_send,),
        (w_come, 2, 0),
        (first_norm,),
        (w_double, 2, 0),
        (h1_send, 0),
        (w_come, 2, 1),
        (w_send, 0, 0),
        (wq_pass,),
        (wq_swap,),
        (w_send, 1, 0),
        (h1_come, 0),
        (wq_wait,),
        (w_double, 2, 1),
        (w_come, 0, 0),
        (project_own,),
        (w_come, 1, 0),
        (project_come, 0),
        (w_double, 1, 0),
        (h1_come, 1),
        (project_come, 1),
        (w_double, 0, 0),
        (w_come, 0, 1),
        (attention, 3),
        (w_come, 1, 1),
        (attention, 2),
        (attention, 1),
        (w_come, 2, 2),
        (attention, 0),
        (w_double, 2, 2),
        (w_done, 2, 1),
        (w_double, 0, 1),
        (w_done, 2, 0),
        (w_done, 2, 2),
        (w_come, 0, 2),
        (w_double, 1, 1),
        (w_double, 0, 2),
        (w_come, 1, 2),
        (w_done, 1, 0),
        (w_done, 0, 0),
        (w_done, 0, 2),
        (emit_l,),
        (wo_swap,),
        (w_double, 1, 2),
        (o_come,),
        (w_done, 0, 1),
        (wo_done,),
        (project_out,),
        (emit_qkv,),
        (w_done, 1, 1),
        (hidden_mine,),
        (hidden_theirs,),
        (w_done, 1, 2),
        (contract_theirs,),
        (contract_mine,),
        (last_norm,),
        (unhidden_mine,),
        (back_mine,),
        (unhidden_theirs,),
        (back_theirs,),
        (grad_fc1,),
        (norms_back,),
        (grad_fc2,),
        (back_out,),
        (grad_out,),
    ):
        act(*where)
    for ok, copy in relays:

        @pl.when(ok)
        def _():
            copy.wait_send()

    for copy in pending:
        copy.wait_send()
    for copy in outs:
        copy.wait()

    @pl.when(own)
    def _():
        for copy in guarded:
            copy.wait()


def forward(NZ, inputs, cotangent, gain, shift, text_len, w_qkv, w_out, w_fc1, w_fc2):
    R, D = inputs.shape
    C = D // NZ
    FH = w_fc1.shape[1] // (2 * NZ)
    F = NZ * FH
    T = NZ * R
    TP = -(-T // 128) * 128
    H = D // 2
    shape = jax.ShapeDtypeStruct
    buf = pltpu.VMEM
    return pl.pallas_call(
        functools.partial(forward_kernel, NZ),
        out_shape=[
            shape((T, D), BF16),
            shape((TP, H), BF16),
            shape((T, H), BF16),
            shape((T, H), BF16),
            shape((D, 3 * H), BF16),
            shape((16, D), F32),
            shape((2, T, 4 * TP), BF16),
            shape((2, 4, 8, TP), F32),
            shape((R, D), BF16),
            shape((R, D), F32),
            shape((2, R, H), BF16),
            shape((2, NZ, FH, D), BF16),
            shape((NZ, C, D), BF16),
            shape((16, D), F32),
        ],
        in_specs=[VMEM, VMEM, VMEM, SMEM, VMEM, ANY, ANY, ANY, ANY],
        out_specs=[ANY] * 8 + [VMEM, VMEM, VMEM, ANY, ANY, VMEM],
        scratch_shapes=[
            buf((16, C), BF16),
            buf((NZ, 16, C), BF16),
            buf((16, D), F32),
            buf((2, C, 3 * H), BF16),
            buf((D, 3 * H), BF16),
            buf((D, F), BF16),
            buf((NZ, FH, D), BF16),
            buf((D, D), BF16),
            buf((T, D), BF16),
            buf((TP, H), BF16),
            buf((T, H), BF16),
            buf((T, H), BF16),
            buf((2, C, TP), BF16),
            buf((T, QUERIES), F32),
            buf((C, QUERIES), F32),
            buf((2, 4, 8, TP), F32),
            buf((R, D), F32),
            buf((2, 4 * R, F), BF16),
            buf((TP, H), BF16),
            buf((2, R, H), BF16),
            buf((2 * R, D), BF16),
            buf((2 * R, D), BF16),
            buf((2, R, D), BF16),
            buf((R, D), BF16),
            buf((R, D), BF16),
            buf((R, D), F32),
            buf((2, NZ, FH, D), BF16),
            buf((NZ, C, D), BF16),
            DMA((4 * NZ + 4,)),
            DMA((NZ,)),
            DMA((NZ,)),
            DMA((NZ,)),
            DMA((NZ,)),
            DMA((NZ, 4)),
            DMA((NZ, 4)),
            DMA((2, NZ)),
            DMA((2, NZ)),
            DMA((3, 2, 2, NZ)),
            DMA((3, 2, 2, NZ)),
            DMA((3, 2, 2, NZ)),
            DMA((3, 2, 2, NZ)),
            DMA((3, 2, 2, NZ)),
            DMA((3, 2, 2, NZ)),
            DMA((NZ,)),
            DMA((NZ,)),
            DMA((NZ,)),
            DMA((NZ,)),
            DMA((10 + NZ,)),
            DMA((2,)),
            DMA((4,)),
            DMA((4,)),
        ],
        compiler_params=pltpu.CompilerParams(
            collective_id=0, has_side_effects=True, vmem_limit_bytes=62 * 2**20
        ),
    )(inputs, gain, shift, text_len, cotangent, w_qkv, w_out, w_fc1, w_fc2)


def reduce_kernel(
    NZ,
    x_ref,
    dmid_ref,
    par_ref,
    small_in,
    do_ref,
    wq_hbm,
    q_hbm,
    k_hbm,
    v_hbm,
    l_hbm,
    h1_hbm,
    p_hbm,
    g_hbm,
    go_hbm,
    dx_ref,
    g_out,
    go_out,
    gq_out,
    small_out,
    wq_ref,
    q_ref,
    k_ref,
    v_ref,
    l_ref,
    p_s,
    g,
    go_far,
    go_w,
    gq_far,
    gq_w,
    r1,
    r1_o,
    r1_q,
    r2,
    r2_o,
    r2_q,
    rz,
    rz_o,
    rz_z,
    r1_z,
    r2_z,
    w_z,
    f_z,
    f_g,
    f_o,
    f_q,
    do_all,
    do_st,
    q_st,
    ds_s,
    dq_t,
    k_t,
    dk_f,
    dv_f,
    dqkv,
    dh,
    rel,
    s_f,
    s_b,
    s_z,
    s_p,
    s_g,
    load_sem,
    p_sem,
    do_s,
    do_r,
    pair_s,
    pair_r,
    s1_s,
    s1_r,
    s2_s,
    s2_r,
    c1_s,
    c1_r,
    c2_s,
    c2_r,
    z_s,
    z_r,
    zl_s,
    zl_r,
    g_s,
    g_r,
    sib_s,
    sib_r,
    ru_s,
    ru_r,
    sz_s,
    sz_r,
    sp_s,
    sp_r,
    out_sem,
):
    R, D = x_ref.shape
    C = D // NZ
    T = NZ * R
    FH = g.shape[2]
    H = D // 2
    w, z, core, x, y = place()
    lower, upper = NZ // 2 - 1, NZ // 2
    own = (z == lower) | (z == upper)
    side = lax.div(z, NZ // 2)
    partner = NZ - 1 - z
    outer = (NZ - 1) * side
    near = {j: flips(w, core, x, y, j) for j in range(1, GROUP)}
    zto = [lax.rem(z + j, NZ) for j in range(NZ)]
    zfrom = [lax.rem(z + NZ - j, NZ) for j in range(NZ)]
    hops = range(1, NZ)
    pending = []

    def go(copy):
        copy.start()
        pending.append(copy)

    guarded = []

    def when(ok, *copies):
        for copy in copies:
            guarded.append((ok, copy))

        @pl.when(ok)
        def _():
            for copy in copies:
                copy.start()

    pair = z + 1 - 2 * lax.rem(z, 2)
    across = lax.rem(z + 2, NZ)
    goals = (pair, lax.rem(pair + 2, NZ), across, z)
    chunks = [(kind, j) for j in range(NZ) for kind in range(2)]
    loads = [
        pltpu.make_async_copy(
            g_hbm.at[kind, goals[j]], g.at[kind, goals[j]], load_sem.at[i]
        )
        for i, (kind, j) in enumerate(chunks)
    ]
    CH = C // 2
    loads.append(
        pltpu.make_async_copy(
            go_hbm.at[:, at(core * CH, CH)], go_w, load_sem.at[len(chunks)]
        )
    )
    for copy in loads:
        copy.start()
    spans = query_blocks(T)
    visits = [(n, i) for n in range(2) for i in reversed(range(len(spans)))]

    def load_p(n):
        group, i = visits[n]
        first_query, size, keys = spans[i]
        return pltpu.make_async_copy(
            p_hbm.at[group, pl.ds(0, keys), pl.ds(4 * first_query, 4 * size)],
            p_s.at[n % 2, pl.ds(0, keys), pl.ds(0, 4 * size)],
            p_sem.at[n % 2],
        )

    load_h1 = pltpu.make_async_copy(h1_hbm, ds_s, load_sem.at[len(chunks) + 1])

    inner_loads = [
        pltpu.make_async_copy(src, dst, load_sem.at[len(chunks) + 2 + i])
        for i, (src, dst) in enumerate(
            ((v_hbm, v_ref), (q_hbm, q_ref), (k_hbm, k_ref), (l_hbm, l_ref), (wq_hbm, wq_ref))
        )
    ]

    @pl.when(own)
    def _():
        for copy in inner_loads[:4]:
            copy.start()
        load_p(0).start()
        load_p(1).start()
        inner_loads[4].start()

    meet([(w, zto[j]) for j in hops] + [(near[j], z) for j in range(1, GROUP)])

    first = (x, y)
    second = (y, x)
    flip_first = (2, 4)
    flip_second = (4, 2)
    FP = FH - FH // 4
    half = (FP // 4, FP // 4, C // 4, C // 4, FH // 8)
    side_one = {2: r1_o, 3: r1_q, 4: r1_z}
    side_two = {2: r2_o, 3: r2_q, 4: r2_z}
    side_work = {2: go_w, 3: gq_w, 4: w_z}
    final = {0: f_g.at[0], 1: f_g.at[1], 2: f_o, 3: f_q, 4: f_z}

    def out(kind, which):
        if kind < 2:
            return g_out.at[kind, which, pl.ds(0, FP)]
        if kind == 4:
            return g_out.at[:, which, pl.ds(FP, FH - FP)]
        return (go_out, gq_out)[kind - 2].at[which]

    outs = []

    def index(kind, part, start, n):
        if kind < 2:
            return at(part * (FP // 2) + start, n), slice(None)
        width = side_work[kind].shape[2] // 2
        return at(start, n), pl.ds(part * width, width)

    def kept(kind, part):
        return half[kind] * first[part] + (half[kind] // 2) * second[part]

    seen = set()

    def loaded(c):
        if c not in seen:
            seen.add(c)
            loads[c].wait()

    def chunk_one(c, part):
        kind, j = chunks[c]
        n = half[kind]
        return remote(
            g.at[(kind, goals[j]) + index(kind, part, n * (1 - first[part]), n)],
            r1.at[c, part],
            c1_s.at[c, part],
            c1_r.at[c, part],
            (near[flip_first[part]], z),
        )

    def chunk_two(c, part):
        kind, j = chunks[c]
        n = half[kind] // 2
        start = 2 * n * first[part] + n * (1 - second[part])
        return remote(
            g.at[(kind, goals[j]) + index(kind, part, start, n)],
            r2.at[c, part],
            c2_s.at[c, part],
            c2_r.at[c, part],
            (near[flip_second[part]], z),
        )

    def launch(c):
        loaded(c)
        for part in range(2):
            go(chunk_one(c, part))

    def reduce_one(c):
        kind, j = chunks[c]
        n = half[kind]
        for part in range(2):
            chunk_one(c, part).wait_recv()
            idx = (kind, goals[j]) + index(kind, part, n * first[part], n)
            g[idx] += r1[c, part]
            go(chunk_two(c, part))

    def reduce_two(c):
        kind, j = chunks[c]
        n = half[kind] // 2
        for part in range(2):
            chunk_two(c, part).wait_recv()
            idx = (kind, goals[j]) + index(kind, part, kept(kind, part), n)
            g[idx] += r2[c, part]
            if j < 2:
                go(pairwise(kind, part, j))
            elif j == 2:
                cross(kind, part)

    def step_one(kind, part):
        n = half[kind]
        return remote(
            side_work[kind].at[(slice(None),) + index(kind, part, n * (1 - first[part]), n)],
            side_one[kind].at[part],
            s1_s.at[kind - 2, part],
            s1_r.at[kind - 2, part],
            (near[flip_first[part]], z),
        )

    def step_two(kind, part):
        n = half[kind] // 2
        start = 2 * n * first[part] + n * (1 - second[part])
        return remote(
            side_work[kind].at[(slice(None),) + index(kind, part, start, n)],
            side_two[kind].at[part],
            s2_s.at[kind - 2, part],
            s2_r.at[kind - 2, part],
            (near[flip_second[part]], z),
        )

    def add_one(kind):
        n = half[kind]
        for part in range(2):
            arrival, onward = step_one(kind, part), step_two(kind, part)
            idx = (slice(None),) + index(kind, part, n * first[part], n)

            def add():
                arrival.wait_recv()
                side_work[kind][idx] += side_one[kind][part]

            if kind != 3:
                add()
                go(onward)
            else:
                pl.when(own)(add)
                when(own, onward)

    def add_two(kind):
        n = half[kind] // 2
        for part in range(2):
            arrival = step_two(kind, part)
            idx = (slice(None),) + index(kind, part, kept(kind, part), n)

            def add():
                arrival.wait_recv()
                side_work[kind][idx] += side_two[kind][part]

            if kind != 3:
                add()
                for j in range(2 if kind == 2 else 0):
                    go(pairwise(kind, part, j))
            else:
                pl.when(own)(add)
                when(own, *[along(part, j, side) for j in hops])

    def held(kind, part, j):
        idx = (goals[j],) + index(kind, part, kept(kind, part), half[kind] // 2)
        return (g, (kind,) + idx) if kind < 2 else (go_w, idx)

    def pairwise(kind, part, j):
        ref, idx = held(kind, part, j)
        dst = rz.at[kind, part, j] if kind < 2 else rz_o.at[part, j]
        return remote(
            ref.at[idx], dst, z_s.at[kind, part, j], z_r.at[kind, part, j], (w, pair)
        )

    def crosswise(kind, part):
        ref, idx = held(kind, part, 2)
        dst = rz.at[kind, part, 2] if kind < 2 else rz_o.at[part, 2]
        return remote(
            ref.at[idx], dst, z_s.at[kind, part, 2], z_r.at[kind, part, 2], (w, across)
        )

    def cross(kind, part):
        pairwise(kind, part, 1).wait_recv()
        ref, idx = held(kind, part, 2)
        ref[idx] += rz[kind, part, 1] if kind < 2 else rz_o[part, 1]
        go(crosswise(kind, part))

    def block(j):
        return g.at[:, goals[j], pl.ds(FP, FH - FP)]

    def line_copy_z(j):
        return remote(
            block(j), rz_z.at[j], zl_s.at[j], zl_r.at[j], (w, across if j == 2 else pair)
        )

    def rows_start():
        for j in range(2):
            for kind in range(2):
                loaded(2 * j + kind)
            go(line_copy_z(j))

    def rows_cross():
        line_copy_z(1).wait_recv()
        for kind in range(2):
            loaded(2 * 2 + kind)
        block(2)[...] += rz_z[1]
        go(line_copy_z(2))

    def rows_plane():
        line_copy_z(0).wait_recv()
        line_copy_z(2).wait_recv()
        for kind in range(2):
            loaded(2 * 3 + kind)
        w_z[...] = (
            block(3)[...].astype(F32) + rz_z[0].astype(F32) + rz_z[2].astype(F32)
        ).astype(BF16)
        for part in range(2):
            go(step_one(4, part))

    def cross_out():
        for part in range(2):
            cross(2, part)

    def along(part, j, source):
        idx = index(3, part, kept(3, part), half[3] // 2)
        return remote(
            gq_w.at[(zto[j],) + idx],
            f_q.at[(source,) + idx],
            z_s.at[3, part, j],
            z_r.at[3, part, source],
            (w, zto[j]),
        )

    def add_line(kind):
        for part in range(2):
            idx = index(kind, part, kept(kind, part), half[kind] // 2)
            if kind < 3:
                pairwise(kind, part, 0).wait_recv()
                crosswise(kind, part).wait_recv()
                ref, own = held(kind, part, 3)
                far = rz.at[kind] if kind < 2 else rz_o
                total = (
                    ref[own].astype(F32)
                    + far[part, 0].astype(F32)
                    + far[part, 2].astype(F32)
                ).astype(BF16)
                if kind < 2:
                    f_g[(kind,) + idx] = total
                else:
                    f_o[idx] = total
            elif kind == 4:
                f_z[(slice(None),) + idx] = w_z[(slice(None),) + idx]
            else:
                for i in range(2):
                    arrival = along(part, 1, i)

                    @pl.when(z != lower + i)
                    def _():
                        arrival.wait_recv()

                    @pl.when(z == lower + i)
                    def _():
                        f_q[(i,) + idx] = gq_w[(lower + i,) + idx]
            go(share_one(kind, part))

    def region(kind, part, start, n):
        idx = index(kind, part, start, n)
        if kind > 2:
            idx = (slice(None),) + idx
        return final[kind].at[idx]

    def share_one(kind, part):
        ref = region(kind, part, kept(kind, part), half[kind] // 2)
        return remote(
            ref,
            ref,
            g_s.at[kind, part, 0],
            g_r.at[kind, part, 0],
            (near[flip_second[part]], z),
        )

    def share_two(kind, part):
        ref = region(kind, part, half[kind] * first[part], half[kind])
        return remote(
            ref,
            ref,
            g_s.at[kind, part, 1],
            g_r.at[kind, part, 1],
            (near[flip_first[part]], z),
        )

    def relayed(kind):
        for part in range(2):
            n = half[kind] // 2
            start = half[kind] * first[part] + n * (1 - second[part])
            ref = region(kind, part, start, n)
            remote(
                ref,
                ref,
                g_s.at[kind, part, 0],
                g_r.at[kind, part, 0],
                (near[flip_second[part]], z),
            ).wait_recv()
            go(share_two(kind, part))

    def shared(kind):
        for part in range(2):
            ref = region(kind, part, half[kind] * (1 - first[part]), half[kind])
            remote(
                ref,
                ref,
                g_s.at[kind, part, 1],
                g_r.at[kind, part, 1],
                (near[flip_first[part]], z),
            ).wait_recv()
        go(
            remote(
                final[kind], out(kind, core), sib_s.at[kind], sib_r.at[kind], (near[1], z)
            )
        )
        copy = pltpu.make_async_copy(final[kind], out(kind, core), out_sem.at[kind])
        copy.start()
        outs.append(copy)

    pair_o = remote(
        go_hbm.at[:, at((1 - core) * CH, CH)], go_far, pair_s.at[NZ], pair_r.at[NZ], (near[1], z)
    )

    def gq_part(d, half_of):
        return p_s.at[d // 2, at((d % 2) * C + half_of * CH, CH)]

    pair_q = [
        remote(gq_part(d, 1 - core), gq_far.at[d], pair_s.at[d], pair_r.at[d], (near[1], z))
        for d in range(NZ)
    ]

    def do_copy(i, block, rows):
        return remote(
            do_ref.at[i], do_all.at[rows], do_s.at[i], do_r.at[block], (w, jnp.int32(lower + i))
        )

    def do_send():
        for i in range(2):
            when(z != lower + i, do_copy(i, z, at(z * R, R)))

            @pl.when(z == lower + i)
            def _():
                do_all[(lower + i) * R : (lower + i + 1) * R, :] = do_ref[i]
                do_all[T:, :] = jnp.zeros((do_all.shape[0] - T, H), BF16)

    def do_wait(b):
        arrival = do_copy(0, b, pl.ds(b * R, R))

        @pl.when(own & (z != b))
        def _():
            arrival.wait_recv()

    def pair_out():
        loads[len(chunks)].wait()
        go(pair_o)

    def pair_out_done():
        pair_o.wait_recv()
        go_w[...] += go_far[...]
        for part in range(2):
            go(step_one(2, part))

    def visit(n):
        group, i = visits[n]
        first_query, size, keys = spans[i]
        queries = slice(first_query, first_query + size)
        cols = slice(group * C, (group + 1) * C)
        slot = n % 2
        load_p(n).wait()
        if n == 0:
            for copy in inner_loads:
                copy.wait()
        if i == len(spans) - 1:
            k_t[:, :T] = jnp.transpose(k_ref[:, cols].astype(F32)).astype(BF16)
        for h in range(4):
            pick = lanes(size, C, h).astype(BF16)
            here = slice(h * size, (h + 1) * size)
            do_h = do_all[queries, cols] * pick
            q_st[here, :] = q_ref[queries, cols] * pick
            share = l_ref[group, h, :, queries]
            p = p_s[slot, :keys, here].astype(F32) * share[0:1, :]
            t = p * dot_nt(v_ref[:keys, cols], do_h)
            ds = (t - p * jnp.sum(t, 0, keepdims=True)).astype(BF16)
            ds_s[:keys, here] = ds
            rows = slice(h * (C // 4), (h + 1) * (C // 4))
            dq_t[rows, :size] = dot(k_t[rows, :keys], ds)
            do_st[here, :] = (do_h.astype(F32) * jnp.transpose(share)[:, 0:1]).astype(BF16)
        dv = dot(p_s[slot, :keys, : 4 * size], do_st[: 4 * size, :])
        dk = dot(ds_s[:keys, : 4 * size], q_st[: 4 * size, :])
        if i == len(spans) - 1:
            dv_f[...] = dv
            dk_f[...] = dk
        else:
            dv_f[:keys, :] += dv
            dk_f[:keys, :] += dk
        if n + 2 < len(visits):
            load_p(n + 2).start()
        ready = slice(first_query, keys)
        kept_rows = min(size, T - first_query)
        dq = jnp.transpose(dq_t[:, :size])[:kept_rows, :] * 0.125
        dqkv[first_query : first_query + kept_rows, cols] = dq.astype(BF16)
        dqkv[ready, H + group * C : H + (group + 1) * C] = (dk_f[ready, :] * 0.125).astype(BF16)
        dqkv[ready, 2 * H + group * C : 2 * H + (group + 1) * C] = dv_f[ready, :].astype(BF16)

    def visit_block(group, b):
        @pl.when(own)
        def _():
            for n, (of, i) in enumerate(visits):
                if of == group and (i == b or (b == NZ - 1 and i > b)):
                    visit(n)

    def heads(b):
        visit_block(0, b)

    def keys(b):
        visit_block(1, b)

    def partial(d):
        @pl.when(own)
        def _():
            dh[d] = dot_nt(dqkv[d * R : (d + 1) * R, :], wq_ref[...]).astype(BF16)

    def hand(d, slot):
        return remote(
            dh.at[d], rel.at[slot], ru_s.at[slot], ru_r.at[slot], (w, jnp.int32(partner))
        )

    def hand_over(d):
        holder = upper if d <= lower else lower
        slot = 0 if lower <= d <= upper else 1
        when(z == holder, hand(d, slot))

    outward = remote(dh.at[outer], rel.at[0], ru_s.at[2], ru_r.at[2], (w, outer))

    def hand_out():
        arrival = hand(0, 1)

        @pl.when(own)
        def _():
            arrival.wait_recv()
            dh[outer] += rel[1]

        when(own, outward)

    def fetch_h1():
        @pl.when(own)
        def _():
            load_h1.start()

    def grad_qkv():
        for d in range(NZ):
            s_f[d] = small_in[:, d * C : (d + 1) * C]

        @pl.when(own)
        def _():
            load_h1.wait()
            for d in range(NZ):
                p_s[d // 2, (d % 2) * C : (d % 2 + 1) * C, :] = dot_tn(
                    ds_s[:, d * C : (d + 1) * C], dqkv[...]
                ).astype(BF16)
            for row, start in ((8, 0), (9, 2 * H)):
                total = rowsum(dqkv[:, start : start + H].astype(F32))
                for half_of in range(2):
                    s_f[2 * side + half_of, row : row + 1, :] = total[
                        :, half_of * C : (half_of + 1) * C
                    ]

        when(own, *pair_q)

    def pair_qkv_done():
        @pl.when(own)
        def _():
            for d in range(NZ):
                pair_q[d].wait_recv()
                gq_w[d] = gq_part(d, core)[...] + gq_far[d]

        when(own, *[step_one(3, part) for part in range(2)])

    def line_copy(j):
        return remote(s_b.at[zto[j]], s_z.at[j], sz_s.at[j], sz_r.at[j], (w, zto[j]))

    def plane_copy(j):
        return remote(s_p, s_g.at[j], sp_s.at[j], sp_r.at[j], (near[j], z))

    def input_grad():
        inner = hand(0, 0)

        @pl.when(own)
        def _():
            inner.wait_recv()
            rel[0] += dh[z]

        @pl.when(jnp.logical_not(own))
        def _():
            outward.wait_recv()

        dh1 = rel[0].astype(F32)
        n1, inverse = norm(x_ref[...].astype(F32))
        dx_ref[...] = (dmid_ref[...] + norm_back(dh1, n1, inverse, par_ref[0:1, :])).astype(BF16)
        gain = rowsum(dh1 * n1)
        shift = rowsum(dh1)
        for d in range(NZ):
            s_f[d, 0:1, :] = gain[:, d * C : (d + 1) * C]
            s_f[d, 4:5, :] = shift[:, d * C : (d + 1) * C]
        s_b[...] = s_f[...].astype(BF16)
        for j in hops:
            go(line_copy(j))

    def small_line():
        total = s_f[z]
        for j in hops:
            line_copy(j).wait_recv()
            total += s_z[j].astype(F32)
        small_out[...] = total
        s_p[...] = total.astype(BF16)
        for j in range(1, GROUP):
            go(plane_copy(j))

    def small_plane():
        total = small_out[...]
        for j in range(1, GROUP):
            plane_copy(j).wait_recv()
            total += s_g[j].astype(F32)
        small_out[...] = total

    for act, *where in (
        (do_send,),
        (launch, 0),
        (pair_out,),
        (launch, 1),
        (launch, 2),
        (launch, 3),
        (launch, 4),
        (reduce_one, 0),
        (do_wait, 2),
        (rows_start,),
        (launch, 5),
        (do_wait, 3),
        (heads, 3),
        (do_wait, 1),
        (heads, 2),
        (reduce_one, 3),
        (reduce_one, 4),
        (do_wait, 0),
        (reduce_one, 2),
        (launch, 6),
        (heads, 1),
        (heads, 0),
        (pair_out_done,),
        (keys, 3),
        (rows_cross,),
        (reduce_two, 3),
        (reduce_one, 5),
        (reduce_one, 1),
        (keys, 2),
        (add_one, 2),
        (launch, 7),
        (keys, 1),
        (keys, 0),
        (fetch_h1,),
        (reduce_two, 5),
        (partial, 0),
        (reduce_one, 6),
        (grad_qkv,),
        (reduce_two, 2),
        (reduce_two, 1),
        (reduce_one, 7),
        (reduce_two, 4),
        (partial, 1),
        (pair_qkv_done,),
        (reduce_two, 6),
        (reduce_two, 7),
        (partial, 3),
        (reduce_two, 0),
        (hand_over, 0),
        (hand_over, 3),
        (rows_plane,),
        (add_line, 1),
        (add_one, 3),
        (partial, 2),
        (add_two, 2),
        (add_two, 3),
        (add_line, 0),
        (hand_over, 2),
        (add_one, 4),
        (hand_over, 1),
        (hand_out,),
        (relayed, 1),
        (relayed, 0),
        (add_line, 3),
        (add_two, 4),
        (add_line, 4),
        (relayed, 3),
        (shared, 0),
        (relayed, 4),
        (cross_out,),
        (input_grad,),
        (add_line, 2),
        (shared, 3),
        (relayed, 2),
        (shared, 1),
        (small_line,),
        (shared, 4),
        (shared, 2),
        (small_plane,),
    ):
        act(*where)
    for kind in range(5):
        remote(
            final[kind], out(kind, 1 - core), sib_s.at[kind], sib_r.at[kind], (near[1], z)
        ).wait_recv()
    for ok, copy in guarded:
        pl.when(ok)(copy.wait_send)
    for copy in pending:
        copy.wait_send()
    for copy in outs:
        copy.wait()


def reduce(NZ, inputs, dmid, par, small, do, wq, q, k, v, share, h1, p, g, go):
    R, D = inputs.shape
    C = D // NZ
    H = D // 2
    T = NZ * R
    TP = q.shape[0]
    FH = g.shape[2]
    FP = FH - FH // 4
    shape = jax.ShapeDtypeStruct
    buf = pltpu.VMEM
    return pl.pallas_call(
        functools.partial(reduce_kernel, NZ),
        out_shape=[
            shape((R, D), BF16),
            shape((2, 2, FH, D), BF16),
            shape((2, C // 2, D), BF16),
            shape((2, 2, C // 2, 3 * H), BF16),
            shape((16, C), F32),
        ],
        in_specs=[VMEM] * 5 + [ANY] * 9,
        out_specs=[VMEM, ANY, ANY, ANY, VMEM],
        scratch_shapes=[
            buf(wq.shape, BF16),
            buf(q.shape, BF16),
            buf(k.shape, BF16),
            buf(v.shape, BF16),
            buf(share.shape, F32),
            buf((2, T, 3 * H), BF16),
            buf((2, NZ, FH, D), BF16),
            buf((NZ, C // 2, D), BF16),
            buf((NZ, C // 2, D), BF16),
            buf((NZ, C // 2, 3 * H), BF16),
            buf((NZ, C // 2, 3 * H), BF16),
            buf((2 * NZ, 2, FP // 4, D), BF16),
            buf((2, NZ, C // 4, D // 2), BF16),
            buf((2, NZ, C // 4, 3 * H // 2), BF16),
            buf((2 * NZ, 2, FP // 8, D), BF16),
            buf((2, NZ, C // 8, D // 2), BF16),
            buf((2, NZ, C // 8, 3 * H // 2), BF16),
            buf((2, 2, NZ - 1, FP // 8, D), BF16),
            buf((2, NZ - 1, C // 8, D // 2), BF16),
            buf((3, 2, FH - FP, D), BF16),
            buf((2, 2, FH // 8, D // 2), BF16),
            buf((2, 2, FH // 16, D // 2), BF16),
            buf((2, FH - FP, D), BF16),
            buf((2, FH - FP, D), BF16),
            buf((2, FP, D), BF16),
            buf((C // 2, D), BF16),
            buf((2, C // 2, 3 * H), BF16),
            buf((TP, H), BF16),
            buf((4 * QUERIES, C), BF16),
            buf((4 * QUERIES, C), BF16),
            buf((T, 4 * QUERIES), BF16),
            buf((C, QUERIES), F32),
            buf((C, TP), BF16),
            buf((T, C), F32),
            buf((T, C), F32),
            buf((T, 3 * H), BF16),
            buf((NZ, R, D), BF16),
            buf((2, R, D), BF16),
            buf((NZ, 16, C), F32),
            buf((NZ, 16, C), BF16),
            buf((NZ, 16, C), BF16),
            buf((16, C), BF16),
            buf((GROUP, 16, C), BF16),
            DMA((2 * NZ + 7,)),
            DMA((2,)),
            DMA((2,)),
            DMA((NZ,)),
            DMA((NZ + 1,)),
            DMA((NZ + 1,)),
            DMA((3, 2)),
            DMA((3, 2)),
            DMA((3, 2)),
            DMA((3, 2)),
            DMA((2 * NZ, 2)),
            DMA((2 * NZ, 2)),
            DMA((2 * NZ, 2)),
            DMA((2 * NZ, 2)),
            DMA((4, 2, NZ)),
            DMA((4, 2, NZ)),
            DMA((3,)),
            DMA((3,)),
            DMA((5, 2, 2)),
            DMA((5, 2, 2)),
            DMA((5,)),
            DMA((5,)),
            DMA((3,)),
            DMA((3,)),
            DMA((NZ,)),
            DMA((NZ,)),
            DMA((GROUP,)),
            DMA((GROUP,)),
            DMA((5,)),
        ],
        compiler_params=pltpu.CompilerParams(
            collective_id=2, has_side_effects=True, vmem_limit_bytes=63 * 2**20
        ),
    )(inputs, dmid, par, small, do, wq, q, k, v, share, h1, p, g, go)


def widen_kernel(fc2, fc1, out, qkv, act, dx, small, d_fc2, d_fc1, d_out, d_qkv, d_act, d_dx, d_gain, d_shift):
    step = pl.program_id(0)
    d_fc2[...] = fc2[0, 0].astype(F32)
    d_fc1[...] = fc1[0, 0].astype(F32)
    d_out[...] = out[0].astype(F32)
    d_act[...] = act[...]
    d_dx[...] = dx[...]
    d_gain[...] = small[0:4, :]
    d_shift[...] = small[4:16, :]
    width = qkv.shape[3] // 3
    for t in range(3):
        cols = at(t * (d_qkv.shape[1] // 3) + lax.rem(step, 2) * width, width, 128)
        d_qkv[:, cols] = qkv[0, 0, :, t * width : (t + 1) * width].astype(F32)


def widen(g, go, gq, act, dx, small):
    FH, D = g.shape[2:]
    CH = gq.shape[2]
    C = 2 * CH
    NZ = D // C
    R = act.shape[0]
    steps = 2 * NZ
    part = D // steps
    shape = jax.ShapeDtypeStruct
    return pl.pallas_call(
        widen_kernel,
        grid=(steps,),
        out_shape=[
            shape((2 * FH, D), F32),
            shape((C, 2 * NZ * FH), F32),
            shape((C, D), F32),
            shape((C, 3 * D), F32),
            shape((R, D), BF16),
            shape((R, D), BF16),
            shape((4, C), F32),
            shape((12, C), F32),
        ],
        in_specs=[
            pl.BlockSpec((1, 1, 2 * FH // steps, D), lambda i: (0, i // NZ, i % NZ, 0)),
            pl.BlockSpec((1, 1, C, FH), lambda i: (1, i % 2, i // 2 // 2, i // 2 % 2)),
            pl.BlockSpec((1, C // steps, D), lambda i: (i // NZ, i % NZ, 0)),
            pl.BlockSpec(
                (1, 1, CH // 2, gq.shape[3]), lambda i: (i // 4, i % 2, i // 2 % 2, 0)
            ),
            pl.BlockSpec((R, part), lambda i: (0, i)),
            pl.BlockSpec((R, part), lambda i: (0, i)),
            pl.BlockSpec((16, C), lambda i: (0, 0)),
        ],
        out_specs=[
            pl.BlockSpec((2 * FH // steps, D), lambda i: (i, 0)),
            pl.BlockSpec((C, FH), lambda i: (0, i)),
            pl.BlockSpec((C // steps, D), lambda i: (i, 0)),
            pl.BlockSpec((CH // 2, 3 * D), lambda i: (i // 2, 0)),
            pl.BlockSpec((R, part), lambda i: (0, i)),
            pl.BlockSpec((R, part), lambda i: (0, i)),
            pl.BlockSpec((4, C), lambda i: (0, 0)),
            pl.BlockSpec((12, C), lambda i: (0, 0)),
        ],
        compiler_params=pltpu.CompilerParams(vmem_limit_bytes=62 * 2**20),
    )(g, g, go, gq, act, dx, small)


def shards(NZ, W, inputs, w_qkv, w_out, w_fc1, w_fc2, norm_gain, shifts, text_len, cotangent):
    R, D = inputs.shape[1:]
    C = D // NZ
    FF = w_fc1.shape[1]
    FH = FF // (2 * NZ)
    h1, q, k, v, wq, par_f, p, share, act, dmid, do, g, go, small = forward(
        NZ, inputs[0], cotangent[0], norm_gain, shifts, text_len, w_qkv, w_out, w_fc1, w_fc2
    )
    dx, g, go, gq, small = reduce(
        NZ, inputs[0], dmid, par_f, small, do, wq, q, k, v, share, h1, p, g, go
    )
    fc2, fc1, out, qkv, act, dx, gain, shift = widen(g, go, gq, act, dx, small)
    grads = (qkv, out, fc1, fc2, gain, shift)
    if W > GROUP:
        groups = [list(range(i, W, GROUP)) for i in range(GROUP)]
        grads = lax.psum(grads, "wide", axis_index_groups=groups)
    return (act[None], dx[None]) + tuple(grads)


def solution(mesh):
    return jax.shard_map(
        functools.partial(shards, mesh.shape["narrow"], mesh.shape["wide"]),
        mesh=mesh,
        in_specs=(
            P("wide", "narrow", None),
            P("narrow", None),
            P("narrow", None),
            P("narrow", None),
            P("narrow", None),
            P(None, "narrow"),
            P(None, "narrow"),
            P("wide"),
            P("wide", "narrow", None),
        ),
        out_specs=(
            P("wide", "narrow", None),
            P("wide", "narrow", None),
            P("narrow", None),
            P("narrow", None),
            P("narrow", None),
            P("narrow", None),
            P(None, "narrow"),
            P(None, "narrow"),
        ),
        check_vma=False,
    )
```

```python
import functools
import math

import jax
import jax.numpy as jnp
from jax import lax
from jax.experimental import pallas as pl
from jax.experimental.pallas import tpu as pltpu
from jax.sharding import PartitionSpec as P

HEADS = 16
TEXT = 64
EPS = 1e-5
GROUP = 8
QUERIES = 256
EARLY = 1
EARLY_LINE = 2
MESH = pl.DeviceIdType.MESH
F32 = jnp.float32
BF16 = jnp.bfloat16
ANY = pl.BlockSpec(memory_space=pl.ANY)
VMEM = pl.BlockSpec(memory_space=pltpu.VMEM)
SMEM = pl.BlockSpec(memory_space=pltpu.SMEM)
DMA = pltpu.SemaphoreType.DMA


def at(start, size, step=16):
    return pl.ds(pl.multiple_of(start, step), size)


def place():
    w = lax.axis_index("wide")
    z = lax.axis_index("narrow")
    return w, z, lax.rem(w, 2), lax.rem(lax.div(w, 2), 2), lax.rem(lax.div(w, 4), 2)


def flips(w, core, x, y, j):
    return (
        w
        + (j & 1) * (1 - 2 * core)
        + ((j >> 1) & 1) * (2 - 4 * x)
        + ((j >> 2) & 1) * (4 - 8 * y)
    )


def remote(src, dst, send_sem, recv_sem, device):
    return pltpu.make_async_remote_copy(
        src_ref=src,
        dst_ref=dst,
        send_sem=send_sem,
        recv_sem=recv_sem,
        device_id=device,
        device_id_type=MESH,
    )


def meet(devices):
    barrier = pltpu.get_barrier_semaphore()
    for device in devices:
        pl.semaphore_signal(barrier, inc=1, device_id=device, device_id_type=MESH)
    pl.semaphore_wait(barrier, len(devices))


def dot(left, right):
    return lax.dot_general(left, right, (((1,), (0,)), ((), ())), preferred_element_type=F32)


def dot_nt(left, right):
    return lax.dot_general(left, right, (((1,), (1,)), ((), ())), preferred_element_type=F32)


def dot_tn(left, right):
    return lax.dot_general(left, right, (((0,), (0,)), ((), ())), preferred_element_type=F32)


def norm(values):
    centred = values - jnp.mean(values, -1, keepdims=True)
    inverse = lax.rsqrt(jnp.mean(centred * centred, -1, keepdims=True) + EPS)
    return centred * inverse, inverse


def norm_back(incoming, normed, inverse, gain):
    scaled = incoming * gain
    return inverse * (
        scaled
        - jnp.mean(scaled, -1, keepdims=True)
        - normed * jnp.mean(scaled * normed, -1, keepdims=True)
    )


def rowsum(values):
    return jnp.sum(values, 0, keepdims=True)


def lanes(rows, width, head):
    lane = lax.broadcasted_iota(jnp.int32, (rows, width), 1)
    size = width // 4
    return ((lane >= head * size) & (lane < head * size + size)).astype(F32)


def query_blocks(total):
    blocks = []
    for first in range(0, total, QUERIES):
        size = min(QUERIES, -(-(total - first) // 128) * 128)
        blocks.append((first, size, min(first + QUERIES, total)))
    return blocks


def forward_kernel(
    NZ,
    x_ref,
    gain_ref,
    shift_ref,
    len_ref,
    cot_ref,
    wqkv_ref,
    wout_ref,
    wfc1_ref,
    wfc2_ref,
    h1_out,
    q_out,
    k_out,
    v_out,
    wq_out,
    par_out,
    p_out,
    l_out,
    act_ref,
    dmid_ref,
    do_ref,
    g_out,
    go_out,
    early_out,
    early_line_out,
    small_ref,
    par_ref,
    par_all,
    par_f,
    stage,
    wq,
    a_ref,
    b_ref,
    wo_ref,
    h1,
    q_s,
    k_s,
    v_s,
    v_t,
    s_s,
    o_t,
    l_s,
    mid_s,
    big,
    o_send,
    o2,
    h3,
    dm,
    part,
    far_m,
    far_h,
    g_s,
    go_s,
    loc_sem,
    par_s,
    par_r,
    wz_s,
    wz_r,
    wp_s,
    wp_r,
    h_s,
    h_r,
    fz_s,
    fz_r,
    fp_s,
    fp_r,
    fq_s,
    fq_r,
    sib_s,
    sib_r,
    o_s,
    o_r,
    out_sem,
    p_sem,
    swap_s,
    swap_r,
    early_s,
    early_r,
    early_line_s,
    early_line_r,
):
    R, D = x_ref.shape
    C = D // NZ
    FH = wfc1_ref.shape[1] // (2 * NZ)
    w, z, core, x, y = place()
    chip = x + 2 * y
    H = D // 2
    lower, upper = NZ // 2 - 1, NZ // 2
    own = (z == lower) | (z == upper)
    side = lax.div(z, NZ // 2)
    near = {j: flips(w, core, x, y, j) for j in range(1, GROUP)}
    zto = [lax.rem(z + j, NZ) for j in range(NZ)]
    zfrom = [lax.rem(z + NZ - j, NZ) for j in range(NZ)]
    hops = range(1, NZ)
    pending = []

    def go(copy):
        copy.start()
        pending.append(copy)

    first = (x, y)
    second = (y, x)
    flip_first = (2, 4)
    flip_second = (4, 2)
    local = 1 + 3 * NZ
    RW = C // GROUP
    staged = [
        pltpu.make_async_copy(
            wqkv_ref.at[:, pl.ds(t * D + d * H, H)],
            stage.at[d, :, pl.ds(t * H, H)],
            loc_sem.at[1 + 3 * d + t],
        )
        for d in range(2)
        for t in range(3)
    ]
    owned = [
        pltpu.make_async_copy(
            wfc1_ref.at[:, at((2 * j) * FH + core * FH, FH, 128)],
            a_ref.at[at(z * C, C), pl.ds(j * FH, FH)],
            loc_sem.at[local + j],
        )
        for j in range(NZ)
    ]
    owned.append(
        pltpu.make_async_copy(
            wfc2_ref.at[at(core * FH, FH)], b_ref.at[z], loc_sem.at[local + NZ]
        )
    )
    owned.append(
        pltpu.make_async_copy(wout_ref, wo_ref.at[at(z * C, C)], loc_sem.at[local + NZ + 1])
    )
    own_par = pltpu.make_async_copy(par_ref, par_all.at[z], loc_sem.at[0])
    own_wq = [
        pltpu.make_async_copy(stage.at[i], wq.at[at(z * C, C)], loc_sem.at[local + NZ + 2])
        for i in range(2)
    ]
    relays = []

    def other_chip(t):
        return (x + (t & 1) * (1 - 2 * x)) + 2 * (y + (t >> 1) * (1 - 2 * y))

    def when(ok, *copies):
        for copy in copies:
            relays.append((ok, copy))

        @pl.when(ok)
        def _():
            for copy in copies:
                copy.start()

    def par_copy(j, source):
        return remote(par_ref, par_all.at[source], par_s.at[j], par_r.at[j], (w, zto[j]))

    def start():
        par_ref[...] = jnp.concatenate(
            [gain_ref[...].astype(F32), shift_ref[...].astype(F32)], 0
        ).astype(BF16)
        for copy in (own_par, *staged, *owned):
            copy.start()
        meet([(w, zto[j]) for j in hops] + [(near[j], z) for j in range(1, GROUP)])
        for j in hops:
            go(par_copy(j, z))

    def eighth(chip_of):
        return core * (C // 2) + chip_of * RW

    def wq_line(i, source):
        return remote(
            stage.at[i, at(eighth(chip), RW)],
            wq.at[at(source * C + eighth(chip), RW)],
            wz_s.at[i],
            wz_r.at[source],
            (w, jnp.int32(lower + i)),
        )

    def wq_plane(source, t, owner):
        part = wq.at[at(source * C + eighth(owner), RW)]
        return remote(part, part, wp_s.at[source, t], wp_r.at[source, t], (near[2 * t], z))

    def wq_sibling(source, half_of):
        part = wq.at[at(source * C + half_of * (C // 2), C // 2)]
        return remote(part, part, wp_s.at[source, 0], wp_r.at[source, 0], (near[1], z))

    def wq_send():
        for copy in staged:
            copy.wait()
        for i in range(2):
            when(z != lower + i, wq_line(i, z))

            @pl.when(z == lower + i)
            def _():
                own_wq[i].start()

    def wq_pass():
        for source in range(NZ):
            ok = own & (z != source)
            arrival = wq_line(0, source)

            @pl.when(ok)
            def _():
                arrival.wait_recv()

            when(ok, *[wq_plane(source, t, chip) for t in range(1, 4)])

    def wq_swap():
        for source in range(NZ):
            ok = own & (z != source)
            arrivals = [wq_plane(source, t, other_chip(t)) for t in range(1, 4)]

            @pl.when(ok)
            def _():
                for copy in arrivals:
                    copy.wait_recv()

            when(ok, wq_sibling(source, core))

    def wq_wait():
        for i in range(2):

            @pl.when(z == lower + i)
            def _():
                own_wq[i].wait()

        for source in range(NZ):
            arrival = wq_sibling(source, 1 - core)

            @pl.when(own & (z != source))
            def _():
                arrival.wait_recv()

    def first_norm():
        normed, _ = norm(x_ref[...].astype(F32))
        own_par.wait()
        for j in hops:
            par_copy(j, zfrom[j]).wait_recv()
        for d in range(NZ):
            par_f[:, d * C : (d + 1) * C] = par_all[d].astype(F32)
        h1[at(z * R, R), :] = (normed * par_f[0:1, :] + par_f[4:5, :]).astype(BF16)

    def sends(way, k):
        if way == 0:
            return (z - k >= 0) & (z < NZ - 1)
        return (z + k <= NZ - 1) & (z > 0)

    def comes(way, k):
        return z - 1 - k >= 0 if way == 0 else z + 1 + k <= NZ - 1

    def sent(way, k):
        return jnp.maximum(z - k, 0) if way == 0 else jnp.minimum(z + k, NZ - 1)

    def got(way, k):
        return jnp.maximum(z - 1 - k, 0) if way == 0 else jnp.minimum(z + 1 + k, NZ - 1)

    ahead = ((w, jnp.minimum(z + 1, NZ - 1)), (w, jnp.maximum(z - 1, 0)))
    def h1_copy(way, k, block):
        ref = h1.at[at(block * R, R)]
        return remote(ref, ref, h_s.at[way, k], h_r.at[way, k], ahead[way])

    def h1_send(k):
        for way in range(2):
            toward = z <= lower if way == 0 else z >= upper
            when(sends(way, k) & toward, h1_copy(way, k, sent(way, k)))

    def h1_comes(way, k):
        return own & comes(way, k) & (z - 1 <= lower if way == 0 else z + 1 >= upper)

    def h1_come(k):
        for way in range(2):
            copy = h1_copy(way, k, got(way, k))

            @pl.when(h1_comes(way, k))
            def _():
                copy.wait_recv()

        if k + 1 < NZ // 2:
            h1_send(k + 1)

    def rows_of(kind):
        return (C // 4, FH // 4, C // 8)[kind]

    def piece(kind, part, source, start, n):
        if kind == 0:
            half = a_ref.shape[1] // 2
            return a_ref.at[at(source * C + start, n), pl.ds(part * half, half)]
        if kind == 1:
            half = D // 2
            return b_ref.at[source, at(start, n), pl.ds(part * half, half)]
        half = D // 2
        return wo_ref.at[
            at(source * C + core * (C // 2) + start, n), pl.ds(part * half, half)
        ]

    def quarter(kind, part, source):
        n = rows_of(kind)
        return piece(kind, part, source, n * (2 * first[part] + second[part]), n)

    def w_copy(kind, part, way, k, source):
        ref = quarter(kind, part, source)
        return remote(
            ref, ref, fz_s.at[kind, part, way, k], fz_r.at[kind, part, way, k], ahead[way]
        )

    def w_send(kind, k):
        if k == 0:
            for copy in {0: owned[:NZ], 1: owned[NZ : NZ + 1], 2: owned[NZ + 1 :]}[kind]:
                copy.wait()
        for part in range(2):
            for way in range(2):
                when(sends(way, k), w_copy(kind, part, way, k, sent(way, k)))

    def share_one(kind, part, way, k):
        ref = quarter(kind, part, got(way, k))
        return remote(
            ref,
            ref,
            fp_s.at[kind, part, way, k],
            fp_r.at[kind, part, way, k],
            (near[flip_second[part]], z),
        )

    def share_two(kind, part, way, k):
        n = 2 * rows_of(kind)
        ref = piece(kind, part, got(way, k), n * first[part], n)
        return remote(
            ref,
            ref,
            fq_s.at[kind, part, way, k],
            fq_r.at[kind, part, way, k],
            (near[flip_first[part]], z),
        )

    def w_come(kind, k):
        for part in range(2):
            for way in range(2):
                copy = w_copy(kind, part, way, k, got(way, k))
                share = share_one(kind, part, way, k)
                relays.append((comes(way, k), share))

                @pl.when(comes(way, k))
                def _():
                    copy.wait_recv()
                    share.start()

        if k + 1 < NZ - 1:
            w_send(kind, k + 1)

    def w_double(kind, k):
        for part in range(2):
            for way in range(2):
                source = got(way, k)
                n = rows_of(kind)
                start = n * (2 * first[part] + (1 - second[part]))
                ref = piece(kind, part, source, start, n)
                copy = remote(
                    ref,
                    ref,
                    fp_s.at[kind, part, way, k],
                    fp_r.at[kind, part, way, k],
                    (near[flip_second[part]], z),
                )
                share = share_two(kind, part, way, k)
                relays.append((comes(way, k), share))

                @pl.when(comes(way, k))
                def _():
                    copy.wait_recv()
                    share.start()

    def w_done(kind, k):
        for part in range(2):
            for way in range(2):
                n = 2 * rows_of(kind)
                ref = piece(kind, part, got(way, k), n * (1 - first[part]), n)
                copy = remote(
                    ref,
                    ref,
                    fq_s.at[kind, part, way, k],
                    fq_r.at[kind, part, way, k],
                    (near[flip_first[part]], z),
                )

                @pl.when(comes(way, k))
                def _():
                    copy.wait_recv()

    total = NZ * R

    def project(block):
        rows = at(block * R, R)
        gap = D - H
        bias = [
            jnp.where(z == lower, par_f[4 + t : 5 + t, 0:H], par_f[4 + t : 5 + t, gap:D])
            for t in (4, 5)
        ]
        q_s[rows, :] = (dot(h1[rows, :], wq[:, 0:H]) + bias[0]).astype(BF16)
        k_s[rows, :] = dot(h1[rows, :], wq[:, H : 2 * H]).astype(BF16)
        v_s[rows, :] = (dot(h1[rows, :], wq[:, 2 * H : 3 * H]) + bias[1]).astype(BF16)

    def project_own():
        pad = q_s.shape[0] - total

        @pl.when(own)
        def _():
            q_s[total:, :] = jnp.zeros((pad, H), BF16)
            project(z)

    def project_come(k):
        for way in range(2):

            @pl.when(h1_comes(way, k))
            def _():
                project(got(way, k))

    outs = []

    def emit(src, dst, sem):
        copy = pltpu.make_async_copy(src, dst, out_sem.at[sem])
        copy.start()
        outs.append(copy)

    guarded = []

    def emit_own(src, dst, sem):
        copy = pltpu.make_async_copy(src, dst, out_sem.at[sem])
        guarded.append(copy)

        @pl.when(own)
        def _():
            copy.start()

    def emit_qkv():
        emit_own(h1, h1_out, 0)
        emit_own(q_s, q_out, 1)
        emit_own(k_s, k_out, 2)
        emit_own(v_s, v_out, 3)
        emit_own(wq, wq_out, 4)
        emit(par_f, par_out, 5)

    scale = math.log2(math.e) / math.sqrt(C // 4)
    text_len = len_ref[0]
    spans = query_blocks(total)
    done = []

    def p_copy(g, i):
        first_query, size, keys = spans[i]
        return pltpu.make_async_copy(
            big.at[g, pl.ds(0, keys), pl.ds(0, 4 * size)],
            p_out.at[g, pl.ds(0, keys), pl.ds(4 * first_query, 4 * size)],
            p_sem.at[g],
        )

    def scores(i):
        first_query, size, keys = spans[i]
        queries = slice(first_query, first_query + size)
        span = keys - first_query
        row = lax.broadcasted_iota(jnp.int32, (span, size), 0)
        col = lax.broadcasted_iota(jnp.int32, (span, size), 1)
        later = jnp.where(row <= col, 0.0, -1e30)
        head_row = lax.broadcasted_iota(jnp.int32, (TEXT, size), 0)
        unread = jnp.where(head_row < text_len, 0.0, -1e30)

        @pl.loop(0, 2)
        def _(g):
            if done:
                p_copy(g, done[-1]).wait()
            cols = at(g * C, C, 128)
            if not done:
                v_t[g, :, :total] = jnp.transpose(v_s[:, cols].astype(F32)).astype(BF16)
            for pair_of in range(0, 4, 2):
                q_two = jnp.concatenate(
                    [
                        q_s[queries, cols] * lanes(size, C, h).astype(BF16)
                        for h in (pair_of, pair_of + 1)
                    ],
                    0,
                )
                both = dot_nt(k_s[:keys, cols], q_two)
                for t in range(2):
                    h = pair_of + t
                    s_s[t, :keys, :size] = both[:, t * size : (t + 1) * size]
                    s_s[t, 0:TEXT, :size] += unread
                    s_s[t, first_query:keys, :size] += later
                    s = s_s[t, :keys, :size]
                    e = jnp.exp2((s - jnp.max(s, 0, keepdims=True)) * scale)
                    share = 1.0 / jnp.sum(e, 0, keepdims=True)
                    e = e.astype(BF16)
                    big[g, :keys, h * size : (h + 1) * size] = e
                    l_s[g, h, :, queries] = jnp.broadcast_to(share, (8, size))
                    rows = slice(h * (C // 4), (h + 1) * (C // 4))
                    o_t[rows, :size] = dot(v_t[g, rows, :keys], e) * share
            o_send[queries, cols] = jnp.transpose(o_t[:, :size]).astype(BF16)
            p_copy(g, i).start()

        done.append(i)

    def o_copy(b):
        return remote(
            o_send.at[pl.ds(b * R, R)], o2.at[side], o_s.at[b], o_r.at[side], (w, jnp.int32(b))
        )

    def attention(b):
        @pl.when(own)
        def _():
            last = len(spans) if b == NZ - 1 else b + 1
            for i in reversed(range(b, last)):
                scores(i)
            if b == 0:
                for g in range(2):
                    p_copy(g, 0).wait()

        when(own & (z != b), o_copy(b))

        @pl.when(z == b)
        def _():
            o2_own(b)

    def o2_own(b):
        if lower <= b <= upper:
            o2[b - lower] = o_send[b * R : (b + 1) * R, :]

    def o_come():
        for i in range(2):
            copy = remote(
                o_send.at[pl.ds(0, R)], o2.at[i], o_s.at[0], o_r.at[i], (w, jnp.int32(0))
            )

            @pl.when(z != lower + i)
            def _():
                copy.wait_recv()

    def emit_l():
        emit_own(l_s, l_out, 9 + NZ)

    def sibling(j, half):
        part = wo_ref.at[at(zfrom[j] * C + half * (C // 2), C // 2)]
        return remote(part, part, sib_s.at[j], sib_r.at[j], (near[1], z))

    def wo_swap():
        for j in hops:
            go(sibling(j, core))

    def wo_done():
        for j in hops:
            sibling(j, 1 - core).wait_recv()

    gate, slope = big.at[0, pl.ds(0, 2 * R)], big.at[0, pl.ds(2 * R, 2 * R)]
    du = big.at[1, pl.ds(0, 2 * R)]
    mine, theirs = slice(0, R), slice(R, 2 * R)
    kept = {}
    shift = 4

    def swap(src, dst, i):
        return remote(src, dst, swap_s.at[i], swap_r.at[i], (near[1], z))

    swap_h = swap(h3.at[pl.ds(0, R)], h3.at[pl.ds(R, R)], 0)
    swap_m = swap(part.at[0], far_m, 1)
    swap_d = swap(dm.at[pl.ds(0, R)], dm.at[pl.ds(R, R)], 2)
    swap_u = swap(part.at[1], far_h, 3)

    def param(row):
        return par_f[row : row + 1, :]

    def project_out():
        branch = dot(o2[0], wo_ref[0:H, :]) + dot(o2[1], wo_ref[H:D, :])
        n2, kept["r2"] = norm(branch + param(shift + 6))
        mid = x_ref[...].astype(F32) + n2 * param(1) + param(shift + 1)
        for s in range(NZ):
            s_s[0, s * R : (s + 1) * R, :] = n2[:, s * C : (s + 1) * C]
        mid_s[...] = mid
        n3, kept["r3"] = norm(mid)
        for s in range(NZ):
            s_s[1, s * R : (s + 1) * R, :] = n3[:, s * C : (s + 1) * C]
        h3[mine, :] = (n3 * param(2) + param(shift + 2)).astype(BF16)
        go(swap_h)

    def hidden(rows):
        for s in range(NZ):
            cols = slice(s * FH, (s + 1) * FH)
            line = param(shift + 8 + s)
            bias = jnp.where(core == 0, line[:, :FH], line[:, FH:])
            u = dot(h3[rows, :], a_ref[:, cols]) + bias
            k = math.sqrt(2.0 / math.pi)
            sq = u * u
            t = jnp.tanh(u * (k + k * 0.044715 * sq))
            half = 0.5 + 0.5 * t
            gate[rows, cols] = (u * half).astype(BF16)
            slope[rows, cols] = (
                half + (0.5 * u) * (1.0 - t * t) * (k + 3.0 * k * 0.044715 * sq)
            ).astype(BF16)

    def hidden_mine():
        hidden(mine)

    def hidden_theirs():
        swap_h.wait_recv()
        hidden(theirs)

    def contract(rows):
        total = dot(gate[rows, 0:FH], b_ref[0])
        for s in range(1, NZ):
            total += dot(gate[rows, s * FH : (s + 1) * FH], b_ref[s])
        return total

    def contract_theirs():
        part[0] = contract(theirs).astype(BF16)
        go(swap_m)

    def contract_mine():
        kept["m"] = contract(mine)

    def last_norm():
        swap_m.wait_recv()
        n4, r4 = norm(kept["m"] + far_m[...].astype(F32) + param(shift + 7))
        act_ref[...] = (mid_s[...] + n4 * param(3) + param(shift + 3)).astype(BF16)
        e = cot_ref[...].astype(F32)
        small_ref[...] = jnp.zeros_like(small_ref)
        small_ref[3:4, :] = rowsum(e * n4)
        small_ref[shift + 3 : shift + 4, :] = rowsum(e)
        dm_low = norm_back(e, n4, r4, param(3)).astype(BF16)
        dm[mine, :] = dm_low
        small_ref[shift + 7 : shift + 8, :] = rowsum(dm_low.astype(F32))
        go(swap_d)

    def unhidden(rows):
        for s in range(NZ):
            cols = slice(s * FH, (s + 1) * FH)
            du[rows, cols] = (
                dot_nt(dm[rows, :], b_ref[s]) * slope[rows, cols].astype(F32)
            ).astype(BF16)

    def unhidden_mine():
        unhidden(mine)

    def arrived():
        if not kept.get("dm"):
            swap_d.wait_recv()
            kept["dm"] = True

    def unhidden_theirs():
        arrived()
        unhidden(theirs)

    def back_theirs():
        part[1] = dot_nt(du[theirs, :], a_ref[...]).astype(BF16)
        go(swap_u)

    def grad_fc2():
        arrived()
        for s in range(NZ):
            cols = slice(s * FH, (s + 1) * FH)
            g_s[0, s] = dot_tn(gate[:, cols], dm[...]).astype(BF16)
        emit(g_s.at[0], g_out.at[0], 6 + NZ)

    FP = FH - FH // 4
    pair = z + 1 - 2 * lax.rem(z, 2)
    goals = (pair, lax.rem(pair + 2, NZ), lax.rem(z + 2, NZ), z)

    def early(j, part):
        n = FP // 4
        return remote(
            g_s.at[0, goals[j], at(part * (FP // 2) + n * (1 - first[part]), n)],
            early_out.at[j, part],
            early_s.at[j, part],
            early_r.at[j, part],
            (near[flip_first[part]], z),
        )

    def early_line(j):
        return remote(
            g_s.at[0, goals[j], pl.ds(FP, FH - FP)],
            early_line_out.at[j],
            early_line_s.at[j],
            early_line_r.at[j],
            (w, pair),
        )

    def early_start():
        for j in range(EARLY):
            for part in range(2):
                go(early(j, part))
        for j in range(EARLY_LINE):
            go(early_line(j))

    def early_done():
        for j in range(EARLY):
            for part in range(2):
                early(j, part).wait_recv()
        for j in range(EARLY_LINE):
            early_line(j).wait_recv()

    def grad_fc1():
        for s in range(NZ):
            cols = slice(s * FH, (s + 1) * FH)
            tile = dot_tn(h3[...], du[:, cols]).astype(BF16)
            low, left = (s // 2) * C, (s % 2) * FH
            for d in range(NZ):
                g_s[1, d, low : low + C, left : left + FH] = tile[d * C : (d + 1) * C, :]
            total = rowsum(du[:, cols].astype(F32))
            row = shift + 8 + s
            small_ref[row : row + 1, 0:FH] = jnp.where(core == 0, total, 0.0)
            small_ref[row : row + 1, FH:] = jnp.where(core == 0, 0.0, total)
        emit(g_s.at[1], g_out.at[1], 7 + NZ)

    def back_mine():
        kept["dh3"] = dot_nt(du[mine, :], a_ref[...])

    def norms_back():
        swap_u.wait_recv()
        dh3 = kept["dh3"] + far_h[...].astype(F32)
        n3 = jnp.concatenate([s_s[1, s * R : (s + 1) * R, :] for s in range(NZ)], 1)
        small_ref[2:3, :] = rowsum(dh3 * n3)
        small_ref[shift + 2 : shift + 3, :] = rowsum(dh3)
        dmid = cot_ref[...].astype(F32) + norm_back(dh3, n3, kept["r3"], param(2))
        for s in range(NZ):
            dmid_ref[s * R : (s + 1) * R, :] = dmid[:, s * C : (s + 1) * C]
        n2 = jnp.concatenate([s_s[0, s * R : (s + 1) * R, :] for s in range(NZ)], 1)
        small_ref[1:2, :] = rowsum(dmid * n2)
        small_ref[shift + 1 : shift + 2, :] = rowsum(dmid)
        da = norm_back(dmid, n2, kept["r2"], param(1)).astype(BF16)
        small_ref[shift + 6 : shift + 7, :] = rowsum(da.astype(F32))
        kept["da"] = da

    def back_out():
        for i in range(2):
            do_ref[i] = dot_nt(kept["da"], wo_ref[i * H : (i + 1) * H, :]).astype(BF16)

    def grad_out():
        for i in range(2):
            go_s[2 * i : 2 * i + 2] = (
                dot_tn(o2[i], kept["da"]).astype(BF16).reshape(2, C, D)
            )
        emit(go_s, go_out, 8 + NZ)

    for act, *where in (
        (start,),
        (w_send, 2, 0),
        (wq_send,),
        (w_come, 2, 0),
        (first_norm,),
        (w_double, 2, 0),
        (h1_send, 0),
        (w_come, 2, 1),
        (w_send, 0, 0),
        (wq_pass,),
        (wq_swap,),
        (w_send, 1, 0),
        (h1_come, 0),
        (wq_wait,),
        (w_double, 2, 1),
        (w_come, 0, 0),
        (project_own,),
        (w_come, 1, 0),
        (project_come, 0),
        (w_double, 1, 0),
        (h1_come, 1),
        (project_come, 1),
        (w_double, 0, 0),
        (w_come, 0, 1),
        (attention, 3),
        (w_come, 1, 1),
        (attention, 2),
        (attention, 1),
        (w_come, 2, 2),
        (attention, 0),
        (w_double, 2, 2),
        (w_done, 2, 1),
        (w_double, 0, 1),
        (w_done, 2, 0),
        (w_done, 2, 2),
        (w_come, 0, 2),
        (w_double, 1, 1),
        (w_double, 0, 2),
        (w_come, 1, 2),
        (w_done, 1, 0),
        (w_done, 0, 0),
        (w_done, 0, 2),
        (emit_l,),
        (wo_swap,),
        (w_double, 1, 2),
        (o_come,),
        (w_done, 0, 1),
        (wo_done,),
        (project_out,),
        (emit_qkv,),
        (w_done, 1, 1),
        (hidden_mine,),
        (hidden_theirs,),
        (w_done, 1, 2),
        (contract_theirs,),
        (contract_mine,),
        (last_norm,),
        (unhidden_mine,),
        (grad_fc2,),
        (early_start,),
        (unhidden_theirs,),
        (back_mine,),
        (back_theirs,),
        (grad_fc1,),
        (norms_back,),
        (grad_out,),
        (back_out,),
        (early_done,),
    ):
        act(*where)
    for ok, copy in relays:

        @pl.when(ok)
        def _():
            copy.wait_send()

    for copy in pending:
        copy.wait_send()
    for copy in outs:
        copy.wait()

    @pl.when(own)
    def _():
        for copy in guarded:
            copy.wait()


def forward(NZ, inputs, cotangent, gain, shift, text_len, w_qkv, w_out, w_fc1, w_fc2):
    R, D = inputs.shape
    C = D // NZ
    FH = w_fc1.shape[1] // (2 * NZ)
    F = NZ * FH
    T = NZ * R
    TP = -(-T // 128) * 128
    H = D // 2
    shape = jax.ShapeDtypeStruct
    buf = pltpu.VMEM
    return pl.pallas_call(
        functools.partial(forward_kernel, NZ),
        out_shape=[
            shape((T, D), BF16),
            shape((TP, H), BF16),
            shape((T, H), BF16),
            shape((T, H), BF16),
            shape((D, 3 * H), BF16),
            shape((16, D), F32),
            shape((2, T, 4 * TP), BF16),
            shape((2, 4, 8, TP), F32),
            shape((R, D), BF16),
            shape((T, C), F32),
            shape((2, R, H), BF16),
            shape((2, NZ, FH, D), BF16),
            shape((NZ, C, D), BF16),
            shape((EARLY, 2, (FH - FH // 4) // 4, D), BF16),
            shape((EARLY_LINE, FH // 4, D), BF16),
            shape((16, D), F32),
        ],
        in_specs=[VMEM, VMEM, VMEM, SMEM, VMEM, ANY, ANY, ANY, ANY],
        out_specs=[ANY] * 8 + [VMEM, VMEM, VMEM, ANY, ANY, ANY, ANY, VMEM],
        scratch_shapes=[
            buf((16, C), BF16),
            buf((NZ, 16, C), BF16),
            buf((16, D), F32),
            buf((2, C, 3 * H), BF16),
            buf((D, 3 * H), BF16),
            buf((D, F), BF16),
            buf((NZ, FH, D), BF16),
            buf((D, D), BF16),
            buf((T, D), BF16),
            buf((TP, H), BF16),
            buf((T, H), BF16),
            buf((T, H), BF16),
            buf((2, C, TP), BF16),
            buf((2, T, QUERIES), F32),
            buf((C, QUERIES), F32),
            buf((2, 4, 8, TP), F32),
            buf((R, D), F32),
            buf((2, 4 * R, F), BF16),
            buf((TP, H), BF16),
            buf((2, R, H), BF16),
            buf((2 * R, D), BF16),
            buf((2 * R, D), BF16),
            buf((2, R, D), BF16),
            buf((R, D), BF16),
            buf((R, D), BF16),
            buf((2, NZ, FH, D), BF16),
            buf((NZ, C, D), BF16),
            DMA((4 * NZ + 4,)),
            DMA((NZ,)),
            DMA((NZ,)),
            DMA((NZ,)),
            DMA((NZ,)),
            DMA((NZ, 4)),
            DMA((NZ, 4)),
            DMA((2, NZ)),
            DMA((2, NZ)),
            DMA((3, 2, 2, NZ)),
            DMA((3, 2, 2, NZ)),
            DMA((3, 2, 2, NZ)),
            DMA((3, 2, 2, NZ)),
            DMA((3, 2, 2, NZ)),
            DMA((3, 2, 2, NZ)),
            DMA((NZ,)),
            DMA((NZ,)),
            DMA((NZ,)),
            DMA((NZ,)),
            DMA((10 + NZ,)),
            DMA((2,)),
            DMA((4,)),
            DMA((4,)),
            DMA((EARLY, 2)),
            DMA((EARLY, 2)),
            DMA((EARLY_LINE,)),
            DMA((EARLY_LINE,)),
        ],
        compiler_params=pltpu.CompilerParams(
            collective_id=0, has_side_effects=True, vmem_limit_bytes=62 * 2**20
        ),
    )(inputs, gain, shift, text_len, cotangent, w_qkv, w_out, w_fc1, w_fc2)


def reduce_kernel(
    NZ,
    x_ref,
    dmid_hbm,
    par_ref,
    small_in,
    do_ref,
    wq_hbm,
    q_hbm,
    k_hbm,
    v_hbm,
    l_hbm,
    h1_hbm,
    p_hbm,
    g_hbm,
    go_hbm,
    early_hbm,
    early_line_hbm,
    dx_ref,
    g_out,
    go_out,
    gq_out,
    small_out,
    wq_ref,
    q_ref,
    k_ref,
    v_ref,
    l_ref,
    p_s,
    g,
    go_far,
    go_w,
    gq_far,
    gq_w,
    r1,
    r1_o,
    r1_q,
    r2,
    r2_o,
    r2_q,
    rz,
    rz_o,
    rz_z,
    r1_z,
    r2_z,
    w_z,
    f_z,
    f_g,
    f_o,
    f_q,
    do_all,
    do_st,
    q_st,
    ds_s,
    dq_t,
    k_t,
    dk_f,
    dv_f,
    dqkv,
    dh,
    rel,
    s_f,
    s_b,
    s_z,
    s_p,
    s_g,
    load_sem,
    early_sem,
    p_sem,
    do_s,
    do_r,
    pair_s,
    pair_r,
    s1_s,
    s1_r,
    s2_s,
    s2_r,
    c1_s,
    c1_r,
    c2_s,
    c2_r,
    z_s,
    z_r,
    zl_s,
    zl_r,
    g_s,
    g_r,
    sib_s,
    sib_r,
    ru_s,
    ru_r,
    sz_s,
    sz_r,
    sp_s,
    sp_r,
    out_sem,
):
    R, D = x_ref.shape
    C = D // NZ
    T = NZ * R
    FH = g.shape[2]
    H = D // 2
    w, z, core, x, y = place()
    lower, upper = NZ // 2 - 1, NZ // 2
    own = (z == lower) | (z == upper)
    side = lax.div(z, NZ // 2)
    partner = NZ - 1 - z
    outer = (NZ - 1) * side
    near = {j: flips(w, core, x, y, j) for j in range(1, GROUP)}
    zto = [lax.rem(z + j, NZ) for j in range(NZ)]
    zfrom = [lax.rem(z + NZ - j, NZ) for j in range(NZ)]
    hops = range(1, NZ)
    pending = []

    def go(copy):
        copy.start()
        pending.append(copy)

    guarded = []

    def when(ok, *copies):
        for copy in copies:
            guarded.append((ok, copy))

        @pl.when(ok)
        def _():
            for copy in copies:
                copy.start()

    pair = z + 1 - 2 * lax.rem(z, 2)
    across = lax.rem(z + 2, NZ)
    goals = (pair, lax.rem(pair + 2, NZ), across, z)
    chunks = [(kind, j) for j in range(NZ) for kind in range(2)]
    loads = [
        pltpu.make_async_copy(
            g_hbm.at[kind, goals[j]], g.at[kind, goals[j]], load_sem.at[i]
        )
        for i, (kind, j) in enumerate(chunks)
    ]
    CH = C // 2
    loads.append(
        pltpu.make_async_copy(
            go_hbm.at[:, at(core * CH, CH)], go_w, load_sem.at[len(chunks)]
        )
    )
    for copy in loads:
        copy.start()
    spans = query_blocks(T)
    visits = [(n, i) for n in range(2) for i in reversed(range(len(spans)))]

    def load_p(n):
        group, i = visits[n]
        first_query, size, keys = spans[i]
        return pltpu.make_async_copy(
            p_hbm.at[group, pl.ds(0, keys), pl.ds(4 * first_query, 4 * size)],
            p_s.at[n % 2, pl.ds(0, keys), pl.ds(0, 4 * size)],
            p_sem.at[n % 2],
        )

    load_h1 = pltpu.make_async_copy(h1_hbm, ds_s, load_sem.at[len(chunks) + 1])

    inner_loads = [
        pltpu.make_async_copy(src, dst, load_sem.at[len(chunks) + 2 + i])
        for i, (src, dst) in enumerate(
            ((v_hbm, v_ref), (q_hbm, q_ref), (k_hbm, k_ref), (l_hbm, l_ref), (wq_hbm, wq_ref))
        )
    ]

    @pl.when(own)
    def _():
        for copy in inner_loads[:4]:
            copy.start()
        load_p(0).start()
        load_p(1).start()
        inner_loads[4].start()

    meet([(w, zto[j]) for j in hops] + [(near[j], z) for j in range(1, GROUP)])

    first = (x, y)
    second = (y, x)
    flip_first = (2, 4)
    flip_second = (4, 2)
    FP = FH - FH // 4
    half = (FP // 4, FP // 4, C // 4, C // 4, FH // 8)
    side_one = {2: r1_o, 3: r1_q, 4: r1_z}
    side_two = {2: r2_o, 3: r2_q, 4: r2_z}
    side_work = {2: go_w, 3: gq_w, 4: w_z}
    final = {0: f_g.at[0], 1: f_g.at[1], 2: f_o, 3: f_q, 4: f_z}

    def out(kind, which):
        if kind < 2:
            return g_out.at[kind, which, pl.ds(0, FP)]
        if kind == 4:
            return g_out.at[:, which, pl.ds(FP, FH - FP)]
        return (go_out, gq_out)[kind - 2].at[which]

    outs = []

    def index(kind, part, start, n):
        if kind < 2:
            return at(part * (FP // 2) + start, n), slice(None)
        width = side_work[kind].shape[2] // 2
        return at(start, n), pl.ds(part * width, width)

    def kept(kind, part):
        return half[kind] * first[part] + (half[kind] // 2) * second[part]

    seen = set()

    def loaded(c):
        if c not in seen:
            seen.add(c)
            loads[c].wait()

    def chunk_one(c, part):
        kind, j = chunks[c]
        n = half[kind]
        return remote(
            g.at[(kind, goals[j]) + index(kind, part, n * (1 - first[part]), n)],
            r1.at[c, part],
            c1_s.at[c, part],
            c1_r.at[c, part],
            (near[flip_first[part]], z),
        )

    def chunk_two(c, part):
        kind, j = chunks[c]
        n = half[kind] // 2
        start = 2 * n * first[part] + n * (1 - second[part])
        return remote(
            g.at[(kind, goals[j]) + index(kind, part, start, n)],
            r2.at[c, part],
            c2_s.at[c, part],
            c2_r.at[c, part],
            (near[flip_second[part]], z),
        )

    fetched = {
        2 * j: pltpu.make_async_copy(early_hbm.at[j], r1.at[2 * j], early_sem.at[j])
        for j in range(EARLY)
    }
    fetched_line = [
        pltpu.make_async_copy(early_line_hbm.at[j], rz_z.at[j, 0], early_sem.at[EARLY + j])
        for j in range(EARLY_LINE)
    ]
    for copy in (*fetched.values(), *fetched_line):
        copy.start()

    def launch(c):
        loaded(c)
        if c not in fetched:
            for part in range(2):
                go(chunk_one(c, part))

    def reduce_one(c):
        kind, j = chunks[c]
        n = half[kind]
        if c in fetched:
            fetched[c].wait()
        for part in range(2):
            if c not in fetched:
                chunk_one(c, part).wait_recv()
            idx = (kind, goals[j]) + index(kind, part, n * first[part], n)
            g[idx] += r1[c, part]
            go(chunk_two(c, part))

    def reduce_two(c):
        kind, j = chunks[c]
        n = half[kind] // 2
        for part in range(2):
            chunk_two(c, part).wait_recv()
            idx = (kind, goals[j]) + index(kind, part, kept(kind, part), n)
            g[idx] += r2[c, part]
            if j < 2:
                go(pairwise(kind, part, j))
            elif j == 2:
                cross(kind, part)

    def step_one(kind, part):
        n = half[kind]
        return remote(
            side_work[kind].at[(slice(None),) + index(kind, part, n * (1 - first[part]), n)],
            side_one[kind].at[part],
            s1_s.at[kind - 2, part],
            s1_r.at[kind - 2, part],
            (near[flip_first[part]], z),
        )

    def step_two(kind, part):
        n = half[kind] // 2
        start = 2 * n * first[part] + n * (1 - second[part])
        return remote(
            side_work[kind].at[(slice(None),) + index(kind, part, start, n)],
            side_two[kind].at[part],
            s2_s.at[kind - 2, part],
            s2_r.at[kind - 2, part],
            (near[flip_second[part]], z),
        )

    def add_one(kind):
        n = half[kind]
        for part in range(2):
            arrival, onward = step_one(kind, part), step_two(kind, part)
            idx = (slice(None),) + index(kind, part, n * first[part], n)

            def add():
                arrival.wait_recv()
                side_work[kind][idx] += side_one[kind][part]

            if kind != 3:
                add()
                go(onward)
            else:
                pl.when(own)(add)
                when(own, onward)

    def add_two(kind):
        n = half[kind] // 2
        for part in range(2):
            arrival = step_two(kind, part)
            idx = (slice(None),) + index(kind, part, kept(kind, part), n)

            def add():
                arrival.wait_recv()
                side_work[kind][idx] += side_two[kind][part]

            if kind != 3:
                add()
                for j in range(2 if kind == 2 else 0):
                    go(pairwise(kind, part, j))
            else:
                pl.when(own)(add)
                when(own, *[along(part, j, side) for j in hops])

    def held(kind, part, j):
        idx = (goals[j],) + index(kind, part, kept(kind, part), half[kind] // 2)
        return (g, (kind,) + idx) if kind < 2 else (go_w, idx)

    def pairwise(kind, part, j):
        ref, idx = held(kind, part, j)
        dst = rz.at[kind, part, j] if kind < 2 else rz_o.at[part, j]
        return remote(
            ref.at[idx], dst, z_s.at[kind, part, j], z_r.at[kind, part, j], (w, pair)
        )

    def crosswise(kind, part):
        ref, idx = held(kind, part, 2)
        dst = rz.at[kind, part, 2] if kind < 2 else rz_o.at[part, 2]
        return remote(
            ref.at[idx], dst, z_s.at[kind, part, 2], z_r.at[kind, part, 2], (w, across)
        )

    def cross(kind, part):
        pairwise(kind, part, 1).wait_recv()
        ref, idx = held(kind, part, 2)
        ref[idx] += rz[kind, part, 1] if kind < 2 else rz_o[part, 1]
        go(crosswise(kind, part))

    def block(j):
        return g.at[:, goals[j], pl.ds(FP, FH - FP)]

    def line_copy_z(j):
        if j == 2:
            return remote(block(2), rz_z.at[2], zl_s.at[2], zl_r.at[2], (w, across))
        if j < EARLY_LINE:
            src, dst = g.at[1, goals[j], pl.ds(FP, FH - FP)], rz_z.at[j, 1]
        else:
            src, dst = block(j), rz_z.at[j]
        return remote(src, dst, zl_s.at[j], zl_r.at[j], (w, pair))

    def rows_start():
        for j in range(2):
            for kind in range(2):
                loaded(2 * j + kind)
            go(line_copy_z(j))

    def line_arrived(j):
        line_copy_z(j).wait_recv()
        if j < EARLY_LINE:
            fetched_line[j].wait()

    def rows_cross():
        line_arrived(1)
        for kind in range(2):
            loaded(2 * 2 + kind)
        block(2)[...] += rz_z[1]
        go(line_copy_z(2))

    def rows_plane():
        line_arrived(0)
        line_copy_z(2).wait_recv()
        for kind in range(2):
            loaded(2 * 3 + kind)
        w_z[...] = (
            block(3)[...].astype(F32) + rz_z[0].astype(F32) + rz_z[2].astype(F32)
        ).astype(BF16)
        for part in range(2):
            go(step_one(4, part))

    def cross_out():
        for part in range(2):
            cross(2, part)

    def along(part, j, source):
        idx = index(3, part, kept(3, part), half[3] // 2)
        return remote(
            gq_w.at[(zto[j],) + idx],
            f_q.at[(source,) + idx],
            z_s.at[3, part, j],
            z_r.at[3, part, source],
            (w, zto[j]),
        )

    def add_line(kind):
        for part in range(2):
            idx = index(kind, part, kept(kind, part), half[kind] // 2)
            if kind < 3:
                pairwise(kind, part, 0).wait_recv()
                crosswise(kind, part).wait_recv()
                ref, own = held(kind, part, 3)
                far = rz.at[kind] if kind < 2 else rz_o
                total = (
                    ref[own].astype(F32)
                    + far[part, 0].astype(F32)
                    + far[part, 2].astype(F32)
                ).astype(BF16)
                if kind < 2:
                    f_g[(kind,) + idx] = total
                else:
                    f_o[idx] = total
            elif kind == 4:
                f_z[(slice(None),) + idx] = w_z[(slice(None),) + idx]
            else:
                for i in range(2):
                    arrival = along(part, 1, i)

                    @pl.when(z != lower + i)
                    def _():
                        arrival.wait_recv()

                    @pl.when(z == lower + i)
                    def _():
                        f_q[(i,) + idx] = gq_w[(lower + i,) + idx]
            go(share_one(kind, part))

    def region(kind, part, start, n):
        idx = index(kind, part, start, n)
        if kind > 2:
            idx = (slice(None),) + idx
        return final[kind].at[idx]

    def share_one(kind, part):
        ref = region(kind, part, kept(kind, part), half[kind] // 2)
        return remote(
            ref,
            ref,
            g_s.at[kind, part, 0],
            g_r.at[kind, part, 0],
            (near[flip_second[part]], z),
        )

    def share_two(kind, part):
        ref = region(kind, part, half[kind] * first[part], half[kind])
        return remote(
            ref,
            ref,
            g_s.at[kind, part, 1],
            g_r.at[kind, part, 1],
            (near[flip_first[part]], z),
        )

    def relayed(kind):
        for part in range(2):
            n = half[kind] // 2
            start = half[kind] * first[part] + n * (1 - second[part])
            ref = region(kind, part, start, n)
            remote(
                ref,
                ref,
                g_s.at[kind, part, 0],
                g_r.at[kind, part, 0],
                (near[flip_second[part]], z),
            ).wait_recv()
            go(share_two(kind, part))

    def shared(kind):
        for part in range(2):
            ref = region(kind, part, half[kind] * (1 - first[part]), half[kind])
            remote(
                ref,
                ref,
                g_s.at[kind, part, 1],
                g_r.at[kind, part, 1],
                (near[flip_first[part]], z),
            ).wait_recv()
        go(
            remote(
                final[kind], out(kind, core), sib_s.at[kind], sib_r.at[kind], (near[1], z)
            )
        )
        copy = pltpu.make_async_copy(final[kind], out(kind, core), out_sem.at[kind])
        copy.start()
        outs.append(copy)

    pair_o = remote(
        go_hbm.at[:, at((1 - core) * CH, CH)], go_far, pair_s.at[NZ], pair_r.at[NZ], (near[1], z)
    )

    def gq_part(d, half_of):
        return p_s.at[d // 2, at((d % 2) * C + half_of * CH, CH)]

    pair_q = [
        remote(gq_part(d, 1 - core), gq_far.at[d], pair_s.at[d], pair_r.at[d], (near[1], z))
        for d in range(NZ)
    ]

    def do_copy(i, block, rows):
        return remote(
            do_ref.at[i], do_all.at[rows], do_s.at[i], do_r.at[block], (w, jnp.int32(lower + i))
        )

    def do_send():
        for i in range(2):
            when(z != lower + i, do_copy(i, z, at(z * R, R)))

            @pl.when(z == lower + i)
            def _():
                do_all[(lower + i) * R : (lower + i + 1) * R, :] = do_ref[i]
                do_all[T:, :] = jnp.zeros((do_all.shape[0] - T, H), BF16)

    def do_wait(b):
        arrival = do_copy(0, b, pl.ds(b * R, R))

        @pl.when(own & (z != b))
        def _():
            arrival.wait_recv()

    def pair_out():
        loads[len(chunks)].wait()
        go(pair_o)

    def pair_out_done():
        pair_o.wait_recv()
        go_w[...] += go_far[...]
        for part in range(2):
            go(step_one(2, part))

    def visit(n):
        group, i = visits[n]
        first_query, size, keys = spans[i]
        queries = slice(first_query, first_query + size)
        cols = slice(group * C, (group + 1) * C)
        slot = n % 2
        load_p(n).wait()
        if n == 0:
            for copy in inner_loads:
                copy.wait()
        if i == len(spans) - 1:
            k_t[:, :T] = jnp.transpose(k_ref[:, cols].astype(F32)).astype(BF16)
        for pair_of in range(0, 4, 2):
            two = []
            for h in (pair_of, pair_of + 1):
                pick = lanes(size, C, h).astype(BF16)
                here = slice(h * size, (h + 1) * size)
                do_h = do_all[queries, cols] * pick
                q_st[here, :] = q_ref[queries, cols] * pick
                share = l_ref[group, h, :, queries]
                do_st[here, :] = (do_h.astype(F32) * jnp.transpose(share)[:, 0:1]).astype(BF16)
                two.append(do_h)
            both = dot_nt(v_ref[:keys, cols], jnp.concatenate(two, 0))
            for t in range(2):
                h = pair_of + t
                here = slice(h * size, (h + 1) * size)
                p = p_s[slot, :keys, here].astype(F32) * l_ref[group, h, 0:1, queries]
                product = p * both[:, t * size : (t + 1) * size]
                ds = (product - p * jnp.sum(product, 0, keepdims=True)).astype(BF16)
                ds_s[:keys, here] = ds
                rows = slice(h * (C // 4), (h + 1) * (C // 4))
                dq_t[rows, :size] = dot(k_t[rows, :keys], ds)
        dv = dot(p_s[slot, :keys, : 4 * size], do_st[: 4 * size, :])
        dk = dot(ds_s[:keys, : 4 * size], q_st[: 4 * size, :])
        if i == len(spans) - 1:
            dv_f[...] = dv
            dk_f[...] = dk
        else:
            dv_f[:keys, :] += dv
            dk_f[:keys, :] += dk
        if n + 2 < len(visits):
            load_p(n + 2).start()
        ready = slice(first_query, keys)
        kept_rows = min(size, T - first_query)
        dq = jnp.transpose(dq_t[:, :size])[:kept_rows, :] * 0.125
        dqkv[first_query : first_query + kept_rows, cols] = dq.astype(BF16)
        dqkv[ready, H + group * C : H + (group + 1) * C] = (dk_f[ready, :] * 0.125).astype(BF16)
        dqkv[ready, 2 * H + group * C : 2 * H + (group + 1) * C] = dv_f[ready, :].astype(BF16)

    def visit_block(group, b):
        @pl.when(own)
        def _():
            for n, (of, i) in enumerate(visits):
                if of == group and (i == b or (b == NZ - 1 and i > b)):
                    visit(n)

    def heads(b):
        visit_block(0, b)

    def keys(b):
        visit_block(1, b)

    def partial(d):
        @pl.when(own)
        def _():
            dh[d] = dot_nt(dqkv[d * R : (d + 1) * R, :], wq_ref[...]).astype(BF16)

    def hand(d, slot):
        return remote(
            dh.at[d], rel.at[slot], ru_s.at[slot], ru_r.at[slot], (w, jnp.int32(partner))
        )

    def hand_over(d):
        holder = upper if d <= lower else lower
        slot = 0 if lower <= d <= upper else 1
        when(z == holder, hand(d, slot))

    outward = remote(dh.at[outer], rel.at[0], ru_s.at[2], ru_r.at[2], (w, outer))

    def hand_out():
        arrival = hand(0, 1)

        @pl.when(own)
        def _():
            arrival.wait_recv()
            dh[outer] += rel[1]

        when(own, outward)

    load_dmid = pltpu.make_async_copy(dmid_hbm, dk_f, load_sem.at[len(chunks) + 7])

    def fetch_h1():
        load_dmid.start()

        @pl.when(own)
        def _():
            load_h1.start()

    def grad_qkv():
        for d in range(NZ):
            s_f[d] = small_in[:, d * C : (d + 1) * C]

        @pl.when(own)
        def _():
            load_h1.wait()
            for d in range(NZ):
                p_s[d // 2, (d % 2) * C : (d % 2 + 1) * C, :] = dot_tn(
                    ds_s[:, d * C : (d + 1) * C], dqkv[...]
                ).astype(BF16)
            for row, start in ((8, 0), (9, 2 * H)):
                total = rowsum(dqkv[:, start : start + H].astype(F32))
                for half_of in range(2):
                    s_f[2 * side + half_of, row : row + 1, :] = total[
                        :, half_of * C : (half_of + 1) * C
                    ]

        when(own, *pair_q)

    def pair_qkv_done():
        @pl.when(own)
        def _():
            for d in range(NZ):
                pair_q[d].wait_recv()
                gq_w[d] = gq_part(d, core)[...] + gq_far[d]

        when(own, *[step_one(3, part) for part in range(2)])

    def line_copy(j):
        return remote(s_b.at[zto[j]], s_z.at[j], sz_s.at[j], sz_r.at[j], (w, zto[j]))

    def plane_copy(j):
        return remote(s_p, s_g.at[j], sp_s.at[j], sp_r.at[j], (near[j], z))

    def input_grad():
        inner = hand(0, 0)

        @pl.when(own)
        def _():
            inner.wait_recv()
            rel[0] += dh[z]

        @pl.when(jnp.logical_not(own))
        def _():
            outward.wait_recv()

        dh1 = rel[0].astype(F32)
        n1, inverse = norm(x_ref[...].astype(F32))
        load_dmid.wait()
        dmid = jnp.concatenate([dk_f[s * R : (s + 1) * R, :] for s in range(NZ)], 1)
        dx_ref[...] = (dmid + norm_back(dh1, n1, inverse, par_ref[0:1, :])).astype(BF16)
        gain = rowsum(dh1 * n1)
        shift = rowsum(dh1)
        for d in range(NZ):
            s_f[d, 0:1, :] = gain[:, d * C : (d + 1) * C]
            s_f[d, 4:5, :] = shift[:, d * C : (d + 1) * C]
        s_b[...] = s_f[...].astype(BF16)
        for j in hops:
            go(line_copy(j))

    def small_line():
        total = s_f[z]
        for j in hops:
            line_copy(j).wait_recv()
            total += s_z[j].astype(F32)
        small_out[...] = total
        s_p[...] = total.astype(BF16)
        for j in range(1, GROUP):
            go(plane_copy(j))

    def small_plane():
        total = small_out[...]
        for j in range(1, GROUP):
            plane_copy(j).wait_recv()
            total += s_g[j].astype(F32)
        small_out[...] = total

    for act, *where in (
        (do_send,),
        (launch, 0),
        (launch, 1),
        (launch, 2),
        (rows_start,),
        (launch, 3),
        (do_wait, 1),
        (do_wait, 2),
        (pair_out,),
        (reduce_one, 1),
        (pair_out_done,),
        (launch, 4),
        (reduce_one, 2),
        (launch, 5),
        (do_wait, 3),
        (heads, 3),
        (heads, 2),
        (do_wait, 0),
        (heads, 1),
        (rows_cross,),
        (heads, 0),
        (add_one, 2),
        (launch, 6),
        (keys, 3),
        (reduce_one, 4),
        (keys, 2),
        (reduce_two, 2),
        (keys, 1),
        (keys, 0),
        (reduce_one, 6),
        (add_two, 2),
        (fetch_h1,),
        (partial, 0),
        (reduce_one, 0),
        (reduce_two, 4),
        (reduce_two, 6),
        (cross_out,),
        (partial, 3),
        (launch, 7),
        (reduce_one, 5),
        (reduce_two, 1),
        (rows_plane,),
        (reduce_one, 3),
        (grad_qkv,),
        (hand_over, 3),
        (reduce_two, 0),
        (hand_over, 0),
        (reduce_one, 7),
        (partial, 2),
        (pair_qkv_done,),
        (add_line, 2),
        (add_one, 4),
        (partial, 1),
        (reduce_two, 3),
        (add_one, 3),
        (reduce_two, 5),
        (add_line, 0),
        (relayed, 2),
        (add_two, 3),
        (hand_over, 2),
        (reduce_two, 7),
        (relayed, 0),
        (add_two, 4),
        (hand_out,),
        (hand_over, 1),
        (add_line, 1),
        (add_line, 4),
        (shared, 2),
        (relayed, 1),
        (add_line, 3),
        (shared, 0),
        (relayed, 4),
        (shared, 1),
        (relayed, 3),
        (input_grad,),
        (shared, 4),
        (small_line,),
        (shared, 3),
        (small_plane,),
    ):
        act(*where)
    for kind in range(5):
        remote(
            final[kind], out(kind, 1 - core), sib_s.at[kind], sib_r.at[kind], (near[1], z)
        ).wait_recv()
    for ok, copy in guarded:
        pl.when(ok)(copy.wait_send)
    for copy in pending:
        copy.wait_send()
    for copy in outs:
        copy.wait()


def reduce(NZ, inputs, dmid, par, small, do, wq, q, k, v, share, h1, p, g, go, early, early_line):
    R, D = inputs.shape
    C = D // NZ
    H = D // 2
    T = NZ * R
    TP = q.shape[0]
    FH = g.shape[2]
    FP = FH - FH // 4
    shape = jax.ShapeDtypeStruct
    buf = pltpu.VMEM
    return pl.pallas_call(
        functools.partial(reduce_kernel, NZ),
        out_shape=[
            shape((R, D), BF16),
            shape((2, 2, FH, D), BF16),
            shape((2, C // 2, D), BF16),
            shape((2, 2, C // 2, 3 * H), BF16),
            shape((16, C), F32),
        ],
        in_specs=[VMEM, ANY, VMEM, VMEM, VMEM] + [ANY] * 11,
        out_specs=[VMEM, ANY, ANY, ANY, VMEM],
        scratch_shapes=[
            buf(wq.shape, BF16),
            buf(q.shape, BF16),
            buf(k.shape, BF16),
            buf(v.shape, BF16),
            buf(share.shape, F32),
            buf((2, T, 3 * H), BF16),
            buf((2, NZ, FH, D), BF16),
            buf((NZ, C // 2, D), BF16),
            buf((NZ, C // 2, D), BF16),
            buf((NZ, C // 2, 3 * H), BF16),
            buf((NZ, C // 2, 3 * H), BF16),
            buf((2 * NZ, 2, FP // 4, D), BF16),
            buf((2, NZ, C // 4, D // 2), BF16),
            buf((2, NZ, C // 4, 3 * H // 2), BF16),
            buf((2 * NZ, 2, FP // 8, D), BF16),
            buf((2, NZ, C // 8, D // 2), BF16),
            buf((2, NZ, C // 8, 3 * H // 2), BF16),
            buf((2, 2, NZ - 1, FP // 8, D), BF16),
            buf((2, NZ - 1, C // 8, D // 2), BF16),
            buf((3, 2, FH - FP, D), BF16),
            buf((2, 2, FH // 8, D // 2), BF16),
            buf((2, 2, FH // 16, D // 2), BF16),
            buf((2, FH - FP, D), BF16),
            buf((2, FH - FP, D), BF16),
            buf((2, FP, D), BF16),
            buf((C // 2, D), BF16),
            buf((2, C // 2, 3 * H), BF16),
            buf((TP, H), BF16),
            buf((4 * QUERIES, C), BF16),
            buf((4 * QUERIES, C), BF16),
            buf((T, 4 * QUERIES), BF16),
            buf((C, QUERIES), F32),
            buf((C, TP), BF16),
            buf((T, C), F32),
            buf((T, C), F32),
            buf((T, 3 * H), BF16),
            buf((NZ, R, D), BF16),
            buf((2, R, D), BF16),
            buf((NZ, 16, C), F32),
            buf((NZ, 16, C), BF16),
            buf((NZ, 16, C), BF16),
            buf((16, C), BF16),
            buf((GROUP, 16, C), BF16),
            DMA((2 * NZ + 8,)),
            DMA((EARLY + EARLY_LINE,)),
            DMA((2,)),
            DMA((2,)),
            DMA((NZ,)),
            DMA((NZ + 1,)),
            DMA((NZ + 1,)),
            DMA((3, 2)),
            DMA((3, 2)),
            DMA((3, 2)),
            DMA((3, 2)),
            DMA((2 * NZ, 2)),
            DMA((2 * NZ, 2)),
            DMA((2 * NZ, 2)),
            DMA((2 * NZ, 2)),
            DMA((4, 2, NZ)),
            DMA((4, 2, NZ)),
            DMA((3,)),
            DMA((3,)),
            DMA((5, 2, 2)),
            DMA((5, 2, 2)),
            DMA((5,)),
            DMA((5,)),
            DMA((3,)),
            DMA((3,)),
            DMA((NZ,)),
            DMA((NZ,)),
            DMA((GROUP,)),
            DMA((GROUP,)),
            DMA((5,)),
        ],
        compiler_params=pltpu.CompilerParams(
            collective_id=2, has_side_effects=True, vmem_limit_bytes=63 * 2**20
        ),
    )(inputs, dmid, par, small, do, wq, q, k, v, share, h1, p, g, go, early, early_line)


def widen_kernel(fc2, fc1, out, qkv, act, dx, small, d_fc2, d_fc1, d_out, d_qkv, d_act, d_dx, d_gain, d_shift):
    step = pl.program_id(0)
    d_fc2[...] = fc2[0, 0].astype(F32)
    d_fc1[...] = fc1[0, 0].astype(F32)
    d_out[...] = out[0].astype(F32)
    d_act[...] = act[...]
    d_dx[...] = dx[...]
    d_gain[...] = small[0:4, :]
    d_shift[...] = small[4:16, :]
    width = qkv.shape[3] // 3
    for t in range(3):
        cols = at(t * (d_qkv.shape[1] // 3) + lax.rem(step, 2) * width, width, 128)
        d_qkv[:, cols] = qkv[0, 0, :, t * width : (t + 1) * width].astype(F32)


def widen(g, go, gq, act, dx, small):
    FH, D = g.shape[2:]
    CH = gq.shape[2]
    C = 2 * CH
    NZ = D // C
    R = act.shape[0]
    steps = 2 * NZ
    part = D // steps
    shape = jax.ShapeDtypeStruct
    return pl.pallas_call(
        widen_kernel,
        grid=(steps,),
        out_shape=[
            shape((2 * FH, D), F32),
            shape((C, 2 * NZ * FH), F32),
            shape((C, D), F32),
            shape((C, 3 * D), F32),
            shape((R, D), BF16),
            shape((R, D), BF16),
            shape((4, C), F32),
            shape((12, C), F32),
        ],
        in_specs=[
            pl.BlockSpec((1, 1, 2 * FH // steps, D), lambda i: (0, i // NZ, i % NZ, 0)),
            pl.BlockSpec((1, 1, C, FH), lambda i: (1, i % 2, i // 2 // 2, i // 2 % 2)),
            pl.BlockSpec((1, C // steps, D), lambda i: (i // NZ, i % NZ, 0)),
            pl.BlockSpec(
                (1, 1, CH // 2, gq.shape[3]), lambda i: (i // 4, i % 2, i // 2 % 2, 0)
            ),
            pl.BlockSpec((R, part), lambda i: (0, i)),
            pl.BlockSpec((R, part), lambda i: (0, i)),
            pl.BlockSpec((16, C), lambda i: (0, 0)),
        ],
        out_specs=[
            pl.BlockSpec((2 * FH // steps, D), lambda i: (i, 0)),
            pl.BlockSpec((C, FH), lambda i: (0, i)),
            pl.BlockSpec((C // steps, D), lambda i: (i, 0)),
            pl.BlockSpec((CH // 2, 3 * D), lambda i: (i // 2, 0)),
            pl.BlockSpec((R, part), lambda i: (0, i)),
            pl.BlockSpec((R, part), lambda i: (0, i)),
            pl.BlockSpec((4, C), lambda i: (0, 0)),
            pl.BlockSpec((12, C), lambda i: (0, 0)),
        ],
        compiler_params=pltpu.CompilerParams(vmem_limit_bytes=62 * 2**20),
    )(g, g, go, gq, act, dx, small)


def shards(NZ, W, inputs, w_qkv, w_out, w_fc1, w_fc2, norm_gain, shifts, text_len, cotangent):
    R, D = inputs.shape[1:]
    C = D // NZ
    FF = w_fc1.shape[1]
    FH = FF // (2 * NZ)
    h1, q, k, v, wq, par_f, p, share, act, dmid, do, g, go, early, early_line, small = forward(
        NZ, inputs[0], cotangent[0], norm_gain, shifts, text_len, w_qkv, w_out, w_fc1, w_fc2
    )
    dx, g, go, gq, small = reduce(
        NZ, inputs[0], dmid, par_f, small, do, wq, q, k, v, share, h1, p, g, go, early, early_line
    )
    fc2, fc1, out, qkv, act, dx, gain, shift = widen(g, go, gq, act, dx, small)
    grads = (qkv, out, fc1, fc2, gain, shift)
    if W > GROUP:
        groups = [list(range(i, W, GROUP)) for i in range(GROUP)]
        grads = lax.psum(grads, "wide", axis_index_groups=groups)
    return (act[None], dx[None]) + tuple(grads)


def solution(mesh):
    return jax.shard_map(
        functools.partial(shards, mesh.shape["narrow"], mesh.shape["wide"]),
        mesh=mesh,
        in_specs=(
            P("wide", "narrow", None),
            P("narrow", None),
            P("narrow", None),
            P("narrow", None),
            P("narrow", None),
            P(None, "narrow"),
            P(None, "narrow"),
            P("wide"),
            P("wide", "narrow", None),
        ),
        out_specs=(
            P("wide", "narrow", None),
            P("wide", "narrow", None),
            P("narrow", None),
            P("narrow", None),
            P("narrow", None),
            P("narrow", None),
            P(None, "narrow"),
            P(None, "narrow"),
        ),
        check_vma=False,
    )
```

```python
import functools
import math

import jax
import jax.numpy as jnp
from jax import lax
from jax.experimental import pallas as pl
from jax.experimental.pallas import tpu as pltpu
from jax.sharding import PartitionSpec as P

HEADS = 16
TEXT = 64
EPS = 1e-5
GROUP = 8
QUERIES = 256
EARLY = 1
EARLY_LINE = 2
MESH = pl.DeviceIdType.MESH
F32 = jnp.float32
BF16 = jnp.bfloat16
ANY = pl.BlockSpec(memory_space=pl.ANY)
VMEM = pl.BlockSpec(memory_space=pltpu.VMEM)
SMEM = pl.BlockSpec(memory_space=pltpu.SMEM)
DMA = pltpu.SemaphoreType.DMA


def at(start, size, step=16):
    return pl.ds(pl.multiple_of(start, step), size)


def place():
    w = lax.axis_index("wide")
    z = lax.axis_index("narrow")
    return w, z, lax.rem(w, 2), lax.rem(lax.div(w, 2), 2), lax.rem(lax.div(w, 4), 2)


def flips(w, core, x, y, j):
    return (
        w
        + (j & 1) * (1 - 2 * core)
        + ((j >> 1) & 1) * (2 - 4 * x)
        + ((j >> 2) & 1) * (4 - 8 * y)
    )


def remote(src, dst, send_sem, recv_sem, device):
    return pltpu.make_async_remote_copy(
        src_ref=src,
        dst_ref=dst,
        send_sem=send_sem,
        recv_sem=recv_sem,
        device_id=device,
        device_id_type=MESH,
    )


def meet(devices):
    barrier = pltpu.get_barrier_semaphore()
    for device in devices:
        pl.semaphore_signal(barrier, inc=1, device_id=device, device_id_type=MESH)
    pl.semaphore_wait(barrier, len(devices))


def dot(left, right):
    return lax.dot_general(left, right, (((1,), (0,)), ((), ())), preferred_element_type=F32)


def dot_nt(left, right):
    return lax.dot_general(left, right, (((1,), (1,)), ((), ())), preferred_element_type=F32)


def dot_tn(left, right):
    return lax.dot_general(left, right, (((0,), (0,)), ((), ())), preferred_element_type=F32)


def norm(values):
    centred = values - jnp.mean(values, -1, keepdims=True)
    inverse = lax.rsqrt(jnp.mean(centred * centred, -1, keepdims=True) + EPS)
    return centred * inverse, inverse


def norm_back(incoming, normed, inverse, gain):
    scaled = incoming * gain
    return inverse * (
        scaled
        - jnp.mean(scaled, -1, keepdims=True)
        - normed * jnp.mean(scaled * normed, -1, keepdims=True)
    )


def rowsum(values):
    return jnp.sum(values, 0, keepdims=True)


def lanes(rows, width, head):
    lane = lax.broadcasted_iota(jnp.int32, (rows, width), 1)
    size = width // 4
    return ((lane >= head * size) & (lane < head * size + size)).astype(F32)


def query_blocks(total):
    blocks = []
    for first in range(0, total, QUERIES):
        size = min(QUERIES, -(-(total - first) // 128) * 128)
        blocks.append((first, size, min(first + QUERIES, total)))
    return blocks


def forward_kernel(
    NZ,
    x_ref,
    gain_ref,
    shift_ref,
    len_ref,
    cot_ref,
    wqkv_ref,
    wout_ref,
    wfc1_ref,
    wfc2_ref,
    h1_out,
    q_out,
    k_out,
    v_out,
    wq_out,
    par_out,
    p_out,
    l_out,
    act_ref,
    dmid_ref,
    do_ref,
    g_out,
    go_out,
    early_out,
    early_line_out,
    small_ref,
    par_ref,
    par_all,
    par_f,
    stage,
    wq,
    a_ref,
    b_ref,
    wo_ref,
    h1,
    q_s,
    k_s,
    v_s,
    v_t,
    s_s,
    o_t,
    l_s,
    mid_s,
    big,
    o_send,
    o2,
    h3,
    dm,
    part,
    far_m,
    far_h,
    g_s,
    go_s,
    loc_sem,
    par_s,
    par_r,
    wz_s,
    wz_r,
    wp_s,
    wp_r,
    h_s,
    h_r,
    fz_s,
    fz_r,
    fp_s,
    fp_r,
    fq_s,
    fq_r,
    sib_s,
    sib_r,
    o_s,
    o_r,
    out_sem,
    p_sem,
    swap_s,
    swap_r,
    early_s,
    early_r,
    early_line_s,
    early_line_r,
):
    R, D = x_ref.shape
    C = D // NZ
    FH = wfc1_ref.shape[1] // (2 * NZ)
    w, z, core, x, y = place()
    chip = x + 2 * y
    H = D // 2
    lower, upper = NZ // 2 - 1, NZ // 2
    own = (z == lower) | (z == upper)
    side = lax.div(z, NZ // 2)
    near = {j: flips(w, core, x, y, j) for j in range(1, GROUP)}
    zto = [lax.rem(z + j, NZ) for j in range(NZ)]
    zfrom = [lax.rem(z + NZ - j, NZ) for j in range(NZ)]
    hops = range(1, NZ)
    pending = []

    def go(copy):
        copy.start()
        pending.append(copy)

    first = (x, y)
    second = (y, x)
    flip_first = (2, 4)
    flip_second = (4, 2)
    local = 1 + 3 * NZ
    RW = C // GROUP
    staged = [
        pltpu.make_async_copy(
            wqkv_ref.at[:, pl.ds(t * D + d * H, H)],
            stage.at[d, :, pl.ds(t * H, H)],
            loc_sem.at[1 + 3 * d + t],
        )
        for d in range(2)
        for t in range(3)
    ]
    owned = [
        pltpu.make_async_copy(
            wfc1_ref.at[:, at((2 * j) * FH + core * FH, FH, 128)],
            a_ref.at[at(z * C, C), pl.ds(j * FH, FH)],
            loc_sem.at[local + j],
        )
        for j in range(NZ)
    ]
    owned.append(
        pltpu.make_async_copy(
            wfc2_ref.at[at(core * FH, FH)], b_ref.at[z], loc_sem.at[local + NZ]
        )
    )
    owned.append(
        pltpu.make_async_copy(wout_ref, wo_ref.at[at(z * C, C)], loc_sem.at[local + NZ + 1])
    )
    own_par = pltpu.make_async_copy(par_ref, par_all.at[z], loc_sem.at[0])
    own_wq = [
        pltpu.make_async_copy(stage.at[i], wq.at[at(z * C, C)], loc_sem.at[local + NZ + 2])
        for i in range(2)
    ]
    relays = []

    def other_chip(t):
        return (x + (t & 1) * (1 - 2 * x)) + 2 * (y + (t >> 1) * (1 - 2 * y))

    def when(ok, *copies):
        for copy in copies:
            relays.append((ok, copy))

        @pl.when(ok)
        def _():
            for copy in copies:
                copy.start()

    def par_copy(j, source):
        return remote(par_ref, par_all.at[source], par_s.at[j], par_r.at[j], (w, zto[j]))

    def start():
        par_ref[...] = jnp.concatenate(
            [gain_ref[...].astype(F32), shift_ref[...].astype(F32)], 0
        ).astype(BF16)
        for copy in (own_par, *staged, *owned):
            copy.start()
        meet([(w, zto[j]) for j in hops] + [(near[j], z) for j in range(1, GROUP)])
        for j in hops:
            go(par_copy(j, z))

    def eighth(chip_of):
        return core * (C // 2) + chip_of * RW

    def wq_line(i, source):
        return remote(
            stage.at[i, at(eighth(chip), RW)],
            wq.at[at(source * C + eighth(chip), RW)],
            wz_s.at[i],
            wz_r.at[source],
            (w, jnp.int32(lower + i)),
        )

    def wq_plane(source, t, owner):
        part = wq.at[at(source * C + eighth(owner), RW)]
        return remote(part, part, wp_s.at[source, t], wp_r.at[source, t], (near[2 * t], z))

    def wq_sibling(source, half_of):
        part = wq.at[at(source * C + half_of * (C // 2), C // 2)]
        return remote(part, part, wp_s.at[source, 0], wp_r.at[source, 0], (near[1], z))

    def wq_send():
        for copy in staged:
            copy.wait()
        for i in range(2):
            when(z != lower + i, wq_line(i, z))

            @pl.when(z == lower + i)
            def _():
                own_wq[i].start()

    def wq_pass():
        for source in range(NZ):
            ok = own & (z != source)
            arrival = wq_line(0, source)

            @pl.when(ok)
            def _():
                arrival.wait_recv()

            when(ok, *[wq_plane(source, t, chip) for t in range(1, 4)])

    def wq_swap():
        for source in range(NZ):
            ok = own & (z != source)
            arrivals = [wq_plane(source, t, other_chip(t)) for t in range(1, 4)]

            @pl.when(ok)
            def _():
                for copy in arrivals:
                    copy.wait_recv()

            when(ok, wq_sibling(source, core))

    def wq_wait():
        for i in range(2):

            @pl.when(z == lower + i)
            def _():
                own_wq[i].wait()

        for source in range(NZ):
            arrival = wq_sibling(source, 1 - core)

            @pl.when(own & (z != source))
            def _():
                arrival.wait_recv()

    def first_norm():
        normed, _ = norm(x_ref[...].astype(F32))
        own_par.wait()
        for j in hops:
            par_copy(j, zfrom[j]).wait_recv()
        for d in range(NZ):
            par_f[:, d * C : (d + 1) * C] = par_all[d].astype(F32)
        h1[at(z * R, R), :] = (normed * par_f[0:1, :] + par_f[4:5, :]).astype(BF16)

    def sends(way, k):
        if way == 0:
            return (z - k >= 0) & (z < NZ - 1)
        return (z + k <= NZ - 1) & (z > 0)

    def comes(way, k):
        return z - 1 - k >= 0 if way == 0 else z + 1 + k <= NZ - 1

    def sent(way, k):
        return jnp.maximum(z - k, 0) if way == 0 else jnp.minimum(z + k, NZ - 1)

    def got(way, k):
        return jnp.maximum(z - 1 - k, 0) if way == 0 else jnp.minimum(z + 1 + k, NZ - 1)

    ahead = ((w, jnp.minimum(z + 1, NZ - 1)), (w, jnp.maximum(z - 1, 0)))
    def h1_copy(way, k, block):
        ref = h1.at[at(block * R, R)]
        return remote(ref, ref, h_s.at[way, k], h_r.at[way, k], ahead[way])

    def h1_send(k):
        for way in range(2):
            toward = z <= lower if way == 0 else z >= upper
            when(sends(way, k) & toward, h1_copy(way, k, sent(way, k)))

    def h1_comes(way, k):
        return own & comes(way, k) & (z - 1 <= lower if way == 0 else z + 1 >= upper)

    def h1_come(k):
        for way in range(2):
            copy = h1_copy(way, k, got(way, k))

            @pl.when(h1_comes(way, k))
            def _():
                copy.wait_recv()

        if k + 1 < NZ // 2:
            h1_send(k + 1)

    def rows_of(kind):
        return (C // 4, FH // 4, C // 8)[kind]

    def piece(kind, part, source, start, n):
        if kind == 0:
            half = a_ref.shape[1] // 2
            return a_ref.at[at(source * C + start, n), pl.ds(part * half, half)]
        if kind == 1:
            half = D // 2
            return b_ref.at[source, at(start, n), pl.ds(part * half, half)]
        half = D // 2
        return wo_ref.at[
            at(source * C + core * (C // 2) + start, n), pl.ds(part * half, half)
        ]

    def quarter(kind, part, source):
        n = rows_of(kind)
        return piece(kind, part, source, n * (2 * first[part] + second[part]), n)

    def w_copy(kind, part, way, k, source):
        ref = quarter(kind, part, source)
        return remote(
            ref, ref, fz_s.at[kind, part, way, k], fz_r.at[kind, part, way, k], ahead[way]
        )

    def w_send(kind, k):
        if k == 0:
            for copy in {0: owned[:NZ], 1: owned[NZ : NZ + 1], 2: owned[NZ + 1 :]}[kind]:
                copy.wait()
        for part in range(2):
            for way in range(2):
                when(sends(way, k), w_copy(kind, part, way, k, sent(way, k)))

    def share_one(kind, part, way, k):
        ref = quarter(kind, part, got(way, k))
        return remote(
            ref,
            ref,
            fp_s.at[kind, part, way, k],
            fp_r.at[kind, part, way, k],
            (near[flip_second[part]], z),
        )

    def share_two(kind, part, way, k):
        n = 2 * rows_of(kind)
        ref = piece(kind, part, got(way, k), n * first[part], n)
        return remote(
            ref,
            ref,
            fq_s.at[kind, part, way, k],
            fq_r.at[kind, part, way, k],
            (near[flip_first[part]], z),
        )

    def w_come(kind, k):
        for part in range(2):
            for way in range(2):
                copy = w_copy(kind, part, way, k, got(way, k))
                share = share_one(kind, part, way, k)
                relays.append((comes(way, k), share))

                @pl.when(comes(way, k))
                def _():
                    copy.wait_recv()
                    share.start()

        if k + 1 < NZ - 1:
            w_send(kind, k + 1)

    def w_double(kind, k):
        for part in range(2):
            for way in range(2):
                source = got(way, k)
                n = rows_of(kind)
                start = n * (2 * first[part] + (1 - second[part]))
                ref = piece(kind, part, source, start, n)
                copy = remote(
                    ref,
                    ref,
                    fp_s.at[kind, part, way, k],
                    fp_r.at[kind, part, way, k],
                    (near[flip_second[part]], z),
                )
                share = share_two(kind, part, way, k)
                relays.append((comes(way, k), share))

                @pl.when(comes(way, k))
                def _():
                    copy.wait_recv()
                    share.start()

    def w_done(kind, k):
        for part in range(2):
            for way in range(2):
                n = 2 * rows_of(kind)
                ref = piece(kind, part, got(way, k), n * (1 - first[part]), n)
                copy = remote(
                    ref,
                    ref,
                    fq_s.at[kind, part, way, k],
                    fq_r.at[kind, part, way, k],
                    (near[flip_first[part]], z),
                )

                @pl.when(comes(way, k))
                def _():
                    copy.wait_recv()

    total = NZ * R

    def project(block):
        rows = at(block * R, R)
        gap = D - H
        bias = [
            jnp.where(z == lower, par_f[4 + t : 5 + t, 0:H], par_f[4 + t : 5 + t, gap:D])
            for t in (4, 5)
        ]
        q_s[rows, :] = (dot(h1[rows, :], wq[:, 0:H]) + bias[0]).astype(BF16)
        k_s[rows, :] = dot(h1[rows, :], wq[:, H : 2 * H]).astype(BF16)
        v_s[rows, :] = (dot(h1[rows, :], wq[:, 2 * H : 3 * H]) + bias[1]).astype(BF16)

    def project_own():
        pad = q_s.shape[0] - total

        @pl.when(own)
        def _():
            q_s[total:, :] = jnp.zeros((pad, H), BF16)
            project(z)

    def project_come(k):
        for way in range(2):

            @pl.when(h1_comes(way, k))
            def _():
                project(got(way, k))

    outs = []

    def emit(src, dst, sem):
        copy = pltpu.make_async_copy(src, dst, out_sem.at[sem])
        copy.start()
        outs.append(copy)

    guarded = []

    def emit_own(src, dst, sem):
        copy = pltpu.make_async_copy(src, dst, out_sem.at[sem])
        guarded.append(copy)

        @pl.when(own)
        def _():
            copy.start()

    def emit_qkv():
        emit_own(h1, h1_out, 0)
        emit_own(q_s, q_out, 1)
        emit_own(k_s, k_out, 2)
        emit_own(v_s, v_out, 3)
        emit_own(wq, wq_out, 4)
        emit(par_f, par_out, 5)

    scale = math.log2(math.e) / math.sqrt(C // 4)
    text_len = len_ref[0]
    spans = query_blocks(total)
    done = []

    def p_copy(g, i):
        first_query, size, keys = spans[i]
        return pltpu.make_async_copy(
            big.at[g, pl.ds(0, keys), pl.ds(0, 4 * size)],
            p_out.at[g, pl.ds(0, keys), pl.ds(4 * first_query, 4 * size)],
            p_sem.at[g],
        )

    def scores(i):
        first_query, size, keys = spans[i]
        queries = slice(first_query, first_query + size)
        span = keys - first_query
        row = lax.broadcasted_iota(jnp.int32, (span, size), 0)
        col = lax.broadcasted_iota(jnp.int32, (span, size), 1)
        later = jnp.where(row <= col, 0.0, -1e30)
        head_row = lax.broadcasted_iota(jnp.int32, (TEXT, size), 0)
        unread = jnp.where(head_row < text_len, 0.0, -1e30)

        @pl.loop(0, 2)
        def _(g):
            if done:
                p_copy(g, done[-1]).wait()
            cols = at(g * C, C, 128)
            if not done:
                v_t[g, :, :total] = jnp.transpose(v_s[:, cols].astype(F32)).astype(BF16)
            for pair_of in range(0, 4, 2):
                q_two = jnp.concatenate(
                    [
                        q_s[queries, cols] * lanes(size, C, h).astype(BF16)
                        for h in (pair_of, pair_of + 1)
                    ],
                    0,
                )
                both = dot_nt(k_s[:keys, cols], q_two)
                for t in range(2):
                    h = pair_of + t
                    s_s[t, :keys, :size] = both[:, t * size : (t + 1) * size]
                    s_s[t, 0:TEXT, :size] += unread
                    s_s[t, first_query:keys, :size] += later
                    s = s_s[t, :keys, :size]
                    e = jnp.exp2((s - jnp.max(s, 0, keepdims=True)) * scale)
                    share = 1.0 / jnp.sum(e, 0, keepdims=True)
                    e = e.astype(BF16)
                    big[g, :keys, h * size : (h + 1) * size] = e
                    l_s[g, h, :, queries] = jnp.broadcast_to(share, (8, size))
                    rows = slice(h * (C // 4), (h + 1) * (C // 4))
                    o_t[rows, :size] = dot(v_t[g, rows, :keys], e) * share
            o_send[queries, cols] = jnp.transpose(o_t[:, :size]).astype(BF16)
            p_copy(g, i).start()

        done.append(i)

    def o_copy(b):
        return remote(
            o_send.at[pl.ds(b * R, R)], o2.at[side], o_s.at[b], o_r.at[side], (w, jnp.int32(b))
        )

    def attention(b):
        @pl.when(own)
        def _():
            last = len(spans) if b == NZ - 1 else b + 1
            for i in reversed(range(b, last)):
                scores(i)
            if b == 0:
                for g in range(2):
                    p_copy(g, 0).wait()

        when(own & (z != b), o_copy(b))

        @pl.when(z == b)
        def _():
            o2_own(b)

    def o2_own(b):
        if lower <= b <= upper:
            o2[b - lower] = o_send[b * R : (b + 1) * R, :]

    def o_come():
        for i in range(2):
            copy = remote(
                o_send.at[pl.ds(0, R)], o2.at[i], o_s.at[0], o_r.at[i], (w, jnp.int32(0))
            )

            @pl.when(z != lower + i)
            def _():
                copy.wait_recv()

    def emit_l():
        emit_own(l_s, l_out, 9 + NZ)

    def sibling(j, half):
        part = wo_ref.at[at(zfrom[j] * C + half * (C // 2), C // 2)]
        return remote(part, part, sib_s.at[j], sib_r.at[j], (near[1], z))

    def wo_swap():
        for j in hops:
            go(sibling(j, core))

    def wo_done():
        for j in hops:
            sibling(j, 1 - core).wait_recv()

    gate, slope = big.at[0, pl.ds(0, 2 * R)], big.at[0, pl.ds(2 * R, 2 * R)]
    du = big.at[1, pl.ds(0, 2 * R)]
    mine, theirs = slice(0, R), slice(R, 2 * R)
    kept = {}
    shift = 4

    def swap(src, dst, i):
        return remote(src, dst, swap_s.at[i], swap_r.at[i], (near[1], z))

    swap_h = swap(h3.at[pl.ds(0, R)], h3.at[pl.ds(R, R)], 0)
    swap_m = swap(part.at[0], far_m, 1)
    swap_d = swap(dm.at[pl.ds(0, R)], dm.at[pl.ds(R, R)], 2)
    swap_u = swap(part.at[1], far_h, 3)

    def param(row):
        return par_f[row : row + 1, :]

    def project_out():
        branch = dot(o2[0], wo_ref[0:H, :]) + dot(o2[1], wo_ref[H:D, :])
        n2, kept["r2"] = norm(branch + param(shift + 6))
        mid = x_ref[...].astype(F32) + n2 * param(1) + param(shift + 1)
        for s in range(NZ):
            s_s[0, s * R : (s + 1) * R, :] = n2[:, s * C : (s + 1) * C]
        mid_s[...] = mid
        n3, kept["r3"] = norm(mid)
        for s in range(NZ):
            s_s[1, s * R : (s + 1) * R, :] = n3[:, s * C : (s + 1) * C]
        h3[mine, :] = (n3 * param(2) + param(shift + 2)).astype(BF16)
        go(swap_h)

    def hidden(rows):
        for s in range(NZ):
            cols = slice(s * FH, (s + 1) * FH)
            line = param(shift + 8 + s)
            bias = jnp.where(core == 0, line[:, :FH], line[:, FH:])
            u = dot(h3[rows, :], a_ref[:, cols]) + bias
            k = math.sqrt(2.0 / math.pi)
            sq = u * u
            t = jnp.tanh(u * (k + k * 0.044715 * sq))
            half = 0.5 + 0.5 * t
            gate[rows, cols] = (u * half).astype(BF16)
            slope[rows, cols] = (
                half + (0.5 * u) * (1.0 - t * t) * (k + 3.0 * k * 0.044715 * sq)
            ).astype(BF16)

    def hidden_mine():
        hidden(mine)

    def hidden_theirs():
        swap_h.wait_recv()
        hidden(theirs)

    def contract(rows):
        total = dot(gate[rows, 0:FH], b_ref[0])
        for s in range(1, NZ):
            total += dot(gate[rows, s * FH : (s + 1) * FH], b_ref[s])
        return total

    def contract_theirs():
        part[0] = contract(theirs).astype(BF16)
        go(swap_m)

    def contract_mine():
        kept["m"] = contract(mine)

    def last_norm():
        swap_m.wait_recv()
        n4, r4 = norm(kept["m"] + far_m[...].astype(F32) + param(shift + 7))
        act_ref[...] = (mid_s[...] + n4 * param(3) + param(shift + 3)).astype(BF16)
        e = cot_ref[...].astype(F32)
        small_ref[...] = jnp.zeros_like(small_ref)
        small_ref[3:4, :] = rowsum(e * n4)
        small_ref[shift + 3 : shift + 4, :] = rowsum(e)
        dm_low = norm_back(e, n4, r4, param(3)).astype(BF16)
        dm[mine, :] = dm_low
        small_ref[shift + 7 : shift + 8, :] = rowsum(dm_low.astype(F32))
        go(swap_d)

    def unhidden(rows):
        for s in range(NZ):
            cols = slice(s * FH, (s + 1) * FH)
            du[rows, cols] = (
                dot_nt(dm[rows, :], b_ref[s]) * slope[rows, cols].astype(F32)
            ).astype(BF16)

    def unhidden_mine():
        unhidden(mine)

    def arrived():
        if not kept.get("dm"):
            swap_d.wait_recv()
            kept["dm"] = True

    def unhidden_theirs():
        arrived()
        unhidden(theirs)

    def back_theirs():
        part[1] = dot_nt(du[theirs, :], a_ref[...]).astype(BF16)
        go(swap_u)

    def grad_fc2():
        arrived()
        for s in range(NZ):
            cols = slice(s * FH, (s + 1) * FH)
            g_s[0, s] = dot_tn(gate[:, cols], dm[...]).astype(BF16)
        emit(g_s.at[0], g_out.at[0], 6 + NZ)

    FP = FH - FH // 4
    pair = z + 1 - 2 * lax.rem(z, 2)
    goals = (pair, lax.rem(pair + 2, NZ), lax.rem(z + 2, NZ), z)

    def early(j, part):
        n = FP // 4
        return remote(
            g_s.at[0, goals[j], at(part * (FP // 2) + n * (1 - first[part]), n)],
            early_out.at[j, part],
            early_s.at[j, part],
            early_r.at[j, part],
            (near[flip_first[part]], z),
        )

    def early_line(j):
        return remote(
            g_s.at[0, goals[j], pl.ds(FP, FH - FP)],
            early_line_out.at[j],
            early_line_s.at[j],
            early_line_r.at[j],
            (w, pair),
        )

    def early_start():
        for j in range(EARLY):
            for part in range(2):
                go(early(j, part))
        for j in range(EARLY_LINE):
            go(early_line(j))

    def early_done():
        for j in range(EARLY):
            for part in range(2):
                early(j, part).wait_recv()
        for j in range(EARLY_LINE):
            early_line(j).wait_recv()

    def grad_fc1():
        for s in range(NZ):
            cols = slice(s * FH, (s + 1) * FH)
            tile = dot_tn(h3[...], du[:, cols]).astype(BF16)
            low, left = (s // 2) * C, (s % 2) * FH
            for d in range(NZ):
                g_s[1, d, low : low + C, left : left + FH] = tile[d * C : (d + 1) * C, :]
            total = rowsum(du[:, cols].astype(F32))
            row = shift + 8 + s
            small_ref[row : row + 1, 0:FH] = jnp.where(core == 0, total, 0.0)
            small_ref[row : row + 1, FH:] = jnp.where(core == 0, 0.0, total)
        emit(g_s.at[1], g_out.at[1], 7 + NZ)

    def back_mine():
        kept["dh3"] = dot_nt(du[mine, :], a_ref[...])

    def norms_back():
        swap_u.wait_recv()
        dh3 = kept["dh3"] + far_h[...].astype(F32)
        n3 = jnp.concatenate([s_s[1, s * R : (s + 1) * R, :] for s in range(NZ)], 1)
        small_ref[2:3, :] = rowsum(dh3 * n3)
        small_ref[shift + 2 : shift + 3, :] = rowsum(dh3)
        dmid = cot_ref[...].astype(F32) + norm_back(dh3, n3, kept["r3"], param(2))
        for s in range(NZ):
            dmid_ref[s * R : (s + 1) * R, :] = dmid[:, s * C : (s + 1) * C]
        n2 = jnp.concatenate([s_s[0, s * R : (s + 1) * R, :] for s in range(NZ)], 1)
        small_ref[1:2, :] = rowsum(dmid * n2)
        small_ref[shift + 1 : shift + 2, :] = rowsum(dmid)
        da = norm_back(dmid, n2, kept["r2"], param(1)).astype(BF16)
        small_ref[shift + 6 : shift + 7, :] = rowsum(da.astype(F32))
        kept["da"] = da

    def back_out():
        for i in range(2):
            do_ref[i] = dot_nt(kept["da"], wo_ref[i * H : (i + 1) * H, :]).astype(BF16)

    def grad_out():
        for i in range(2):
            go_s[2 * i : 2 * i + 2] = (
                dot_tn(o2[i], kept["da"]).astype(BF16).reshape(2, C, D)
            )
        emit(go_s, go_out, 8 + NZ)

    for act, *where in (
        (start,),
        (w_send, 2, 0),
        (wq_send,),
        (w_come, 2, 0),
        (first_norm,),
        (h1_send, 0),
        (w_double, 2, 0),
        (w_come, 2, 1),
        (w_send, 0, 0),
        (wq_pass,),
        (w_send, 1, 0),
        (wq_swap,),
        (h1_come, 0),
        (wq_wait,),
        (w_double, 2, 1),
        (w_come, 0, 0),
        (project_own,),
        (w_come, 1, 0),
        (project_come, 0),
        (w_double, 1, 0),
        (h1_come, 1),
        (project_come, 1),
        (w_double, 0, 0),
        (w_come, 0, 1),
        (attention, 3),
        (w_come, 1, 1),
        (attention, 2),
        (w_done, 2, 1),
        (attention, 1),
        (w_come, 2, 2),
        (attention, 0),
        (w_double, 2, 2),
        (w_double, 0, 1),
        (w_done, 2, 0),
        (w_done, 2, 2),
        (w_come, 0, 2),
        (w_double, 1, 1),
        (w_double, 0, 2),
        (w_come, 1, 2),
        (w_done, 1, 0),
        (w_done, 0, 0),
        (w_done, 0, 2),
        (emit_l,),
        (wo_swap,),
        (w_double, 1, 2),
        (o_come,),
        (w_done, 0, 1),
        (wo_done,),
        (project_out,),
        (emit_qkv,),
        (w_done, 1, 1),
        (hidden_mine,),
        (hidden_theirs,),
        (w_done, 1, 2),
        (contract_theirs,),
        (contract_mine,),
        (last_norm,),
        (unhidden_mine,),
        (grad_fc2,),
        (early_start,),
        (unhidden_theirs,),
        (back_mine,),
        (back_theirs,),
        (grad_fc1,),
        (norms_back,),
        (grad_out,),
        (back_out,),
        (early_done,),
    ):
        act(*where)
    for ok, copy in relays:

        @pl.when(ok)
        def _():
            copy.wait_send()

    for copy in pending:
        copy.wait_send()
    for copy in outs:
        copy.wait()

    @pl.when(own)
    def _():
        for copy in guarded:
            copy.wait()


def forward(NZ, inputs, cotangent, gain, shift, text_len, w_qkv, w_out, w_fc1, w_fc2):
    R, D = inputs.shape
    C = D // NZ
    FH = w_fc1.shape[1] // (2 * NZ)
    F = NZ * FH
    T = NZ * R
    TP = -(-T // 128) * 128
    H = D // 2
    shape = jax.ShapeDtypeStruct
    buf = pltpu.VMEM
    return pl.pallas_call(
        functools.partial(forward_kernel, NZ),
        out_shape=[
            shape((T, D), BF16),
            shape((TP, H), BF16),
            shape((T, H), BF16),
            shape((T, H), BF16),
            shape((D, 3 * H), BF16),
            shape((16, D), F32),
            shape((2, T, 4 * TP), BF16),
            shape((2, 4, 8, TP), F32),
            shape((R, D), BF16),
            shape((T, C), F32),
            shape((2, R, H), BF16),
            shape((2, NZ, FH, D), BF16),
            shape((NZ, C, D), BF16),
            shape((EARLY, 2, (FH - FH // 4) // 4, D), BF16),
            shape((EARLY_LINE, FH // 4, D), BF16),
            shape((16, D), F32),
        ],
        in_specs=[VMEM, VMEM, VMEM, SMEM, VMEM, ANY, ANY, ANY, ANY],
        out_specs=[ANY] * 8 + [VMEM, VMEM, VMEM, ANY, ANY, ANY, ANY, VMEM],
        scratch_shapes=[
            buf((16, C), BF16),
            buf((NZ, 16, C), BF16),
            buf((16, D), F32),
            buf((2, C, 3 * H), BF16),
            buf((D, 3 * H), BF16),
            buf((D, F), BF16),
            buf((NZ, FH, D), BF16),
            buf((D, D), BF16),
            buf((T, D), BF16),
            buf((TP, H), BF16),
            buf((T, H), BF16),
            buf((T, H), BF16),
            buf((2, C, TP), BF16),
            buf((2, T, QUERIES), F32),
            buf((C, QUERIES), F32),
            buf((2, 4, 8, TP), F32),
            buf((R, D), F32),
            buf((2, 4 * R, F), BF16),
            buf((TP, H), BF16),
            buf((2, R, H), BF16),
            buf((2 * R, D), BF16),
            buf((2 * R, D), BF16),
            buf((2, R, D), BF16),
            buf((R, D), BF16),
            buf((R, D), BF16),
            buf((2, NZ, FH, D), BF16),
            buf((NZ, C, D), BF16),
            DMA((4 * NZ + 4,)),
            DMA((NZ,)),
            DMA((NZ,)),
            DMA((NZ,)),
            DMA((NZ,)),
            DMA((NZ, 4)),
            DMA((NZ, 4)),
            DMA((2, NZ)),
            DMA((2, NZ)),
            DMA((3, 2, 2, NZ)),
            DMA((3, 2, 2, NZ)),
            DMA((3, 2, 2, NZ)),
            DMA((3, 2, 2, NZ)),
            DMA((3, 2, 2, NZ)),
            DMA((3, 2, 2, NZ)),
            DMA((NZ,)),
            DMA((NZ,)),
            DMA((NZ,)),
            DMA((NZ,)),
            DMA((10 + NZ,)),
            DMA((2,)),
            DMA((4,)),
            DMA((4,)),
            DMA((EARLY, 2)),
            DMA((EARLY, 2)),
            DMA((EARLY_LINE,)),
            DMA((EARLY_LINE,)),
        ],
        compiler_params=pltpu.CompilerParams(
            collective_id=0, has_side_effects=True, vmem_limit_bytes=62 * 2**20
        ),
    )(inputs, gain, shift, text_len, cotangent, w_qkv, w_out, w_fc1, w_fc2)


def reduce_kernel(
    NZ,
    x_ref,
    dmid_hbm,
    par_ref,
    small_in,
    do_ref,
    wq_hbm,
    q_hbm,
    k_hbm,
    v_hbm,
    l_hbm,
    h1_hbm,
    p_hbm,
    g_hbm,
    go_hbm,
    early_hbm,
    early_line_hbm,
    dx_ref,
    g_out,
    go_out,
    gq_out,
    small_out,
    wq_ref,
    q_ref,
    k_ref,
    v_ref,
    l_ref,
    p_s,
    g,
    go_far,
    go_w,
    gq_far,
    gq_w,
    r1,
    r1_o,
    r1_q,
    r2,
    r2_o,
    r2_q,
    rz,
    rz_o,
    rz_z,
    r1_z,
    r2_z,
    w_z,
    f_z,
    f_g,
    f_o,
    f_q,
    do_all,
    do_st,
    q_st,
    ds_s,
    dq_t,
    k_t,
    dk_f,
    dv_f,
    dqkv,
    dh,
    rel,
    s_f,
    s_b,
    s_z,
    s_p,
    s_g,
    load_sem,
    early_sem,
    p_sem,
    do_s,
    do_r,
    pair_s,
    pair_r,
    s1_s,
    s1_r,
    s2_s,
    s2_r,
    c1_s,
    c1_r,
    c2_s,
    c2_r,
    z_s,
    z_r,
    zl_s,
    zl_r,
    g_s,
    g_r,
    sib_s,
    sib_r,
    ru_s,
    ru_r,
    sz_s,
    sz_r,
    sp_s,
    sp_r,
    out_sem,
):
    R, D = x_ref.shape
    C = D // NZ
    T = NZ * R
    FH = g.shape[2]
    H = D // 2
    w, z, core, x, y = place()
    lower, upper = NZ // 2 - 1, NZ // 2
    own = (z == lower) | (z == upper)
    side = lax.div(z, NZ // 2)
    partner = NZ - 1 - z
    outer = (NZ - 1) * side
    near = {j: flips(w, core, x, y, j) for j in range(1, GROUP)}
    zto = [lax.rem(z + j, NZ) for j in range(NZ)]
    zfrom = [lax.rem(z + NZ - j, NZ) for j in range(NZ)]
    hops = range(1, NZ)
    pending = []

    def go(copy):
        copy.start()
        pending.append(copy)

    guarded = []

    def when(ok, *copies):
        for copy in copies:
            guarded.append((ok, copy))

        @pl.when(ok)
        def _():
            for copy in copies:
                copy.start()

    pair = z + 1 - 2 * lax.rem(z, 2)
    across = lax.rem(z + 2, NZ)
    goals = (pair, lax.rem(pair + 2, NZ), across, z)
    chunks = [(kind, j) for j in range(NZ) for kind in range(2)]
    loads = [
        pltpu.make_async_copy(
            g_hbm.at[kind, goals[j]], g.at[kind, goals[j]], load_sem.at[i]
        )
        for i, (kind, j) in enumerate(chunks)
    ]
    CH = C // 2
    loads.append(
        pltpu.make_async_copy(
            go_hbm.at[:, at(core * CH, CH)], go_w, load_sem.at[len(chunks)]
        )
    )
    for copy in loads:
        copy.start()
    spans = query_blocks(T)
    visits = [(n, i) for n in range(2) for i in reversed(range(len(spans)))]

    def load_p(n):
        group, i = visits[n]
        first_query, size, keys = spans[i]
        return pltpu.make_async_copy(
            p_hbm.at[group, pl.ds(0, keys), pl.ds(4 * first_query, 4 * size)],
            p_s.at[n % 2, pl.ds(0, keys), pl.ds(0, 4 * size)],
            p_sem.at[n % 2],
        )

    load_h1 = pltpu.make_async_copy(h1_hbm, ds_s, load_sem.at[len(chunks) + 1])

    inner_loads = [
        pltpu.make_async_copy(src, dst, load_sem.at[len(chunks) + 2 + i])
        for i, (src, dst) in enumerate(
            ((v_hbm, v_ref), (q_hbm, q_ref), (k_hbm, k_ref), (l_hbm, l_ref), (wq_hbm, wq_ref))
        )
    ]

    @pl.when(own)
    def _():
        for copy in inner_loads[:4]:
            copy.start()
        load_p(0).start()
        load_p(1).start()
        inner_loads[4].start()

    meet([(w, zto[j]) for j in hops] + [(near[j], z) for j in range(1, GROUP)])

    first = (x, y)
    second = (y, x)
    flip_first = (2, 4)
    flip_second = (4, 2)
    FP = FH - FH // 4
    half = (FP // 4, FP // 4, C // 4, C // 4, FH // 8)
    side_one = {2: r1_o, 3: r1_q, 4: r1_z}
    side_two = {2: r2_o, 3: r2_q, 4: r2_z}
    side_work = {2: go_w, 3: gq_w, 4: w_z}
    final = {0: f_g.at[0], 1: f_g.at[1], 2: f_o, 3: f_q, 4: f_z}

    def out(kind, which):
        if kind < 2:
            return g_out.at[kind, which, pl.ds(0, FP)]
        if kind == 4:
            return g_out.at[:, which, pl.ds(FP, FH - FP)]
        return (go_out, gq_out)[kind - 2].at[which]

    outs = []

    def index(kind, part, start, n):
        if kind < 2:
            return at(part * (FP // 2) + start, n), slice(None)
        width = side_work[kind].shape[2] // 2
        return at(start, n), pl.ds(part * width, width)

    def kept(kind, part):
        return half[kind] * first[part] + (half[kind] // 2) * second[part]

    seen = set()

    def loaded(c):
        if c not in seen:
            seen.add(c)
            loads[c].wait()

    def chunk_one(c, part):
        kind, j = chunks[c]
        n = half[kind]
        return remote(
            g.at[(kind, goals[j]) + index(kind, part, n * (1 - first[part]), n)],
            r1.at[c, part],
            c1_s.at[c, part],
            c1_r.at[c, part],
            (near[flip_first[part]], z),
        )

    def chunk_two(c, part):
        kind, j = chunks[c]
        n = half[kind] // 2
        start = 2 * n * first[part] + n * (1 - second[part])
        return remote(
            g.at[(kind, goals[j]) + index(kind, part, start, n)],
            r2.at[c, part],
            c2_s.at[c, part],
            c2_r.at[c, part],
            (near[flip_second[part]], z),
        )

    fetched = {
        2 * j: pltpu.make_async_copy(early_hbm.at[j], r1.at[2 * j], early_sem.at[j])
        for j in range(EARLY)
    }
    fetched_line = [
        pltpu.make_async_copy(early_line_hbm.at[j], rz_z.at[j, 0], early_sem.at[EARLY + j])
        for j in range(EARLY_LINE)
    ]
    for copy in (*fetched.values(), *fetched_line):
        copy.start()

    def launch(c):
        loaded(c)
        if c not in fetched:
            for part in range(2):
                go(chunk_one(c, part))

    def reduce_one(c):
        kind, j = chunks[c]
        n = half[kind]
        if c in fetched:
            fetched[c].wait()
        for part in range(2):
            if c not in fetched:
                chunk_one(c, part).wait_recv()
            idx = (kind, goals[j]) + index(kind, part, n * first[part], n)
            g[idx] += r1[c, part]
            go(chunk_two(c, part))

    def reduce_two(c):
        kind, j = chunks[c]
        n = half[kind] // 2
        for part in range(2):
            chunk_two(c, part).wait_recv()
            idx = (kind, goals[j]) + index(kind, part, kept(kind, part), n)
            g[idx] += r2[c, part]
            if j < 2:
                go(pairwise(kind, part, j))
            elif j == 2:
                cross(kind, part)

    def step_one(kind, part):
        n = half[kind]
        return remote(
            side_work[kind].at[(slice(None),) + index(kind, part, n * (1 - first[part]), n)],
            side_one[kind].at[part],
            s1_s.at[kind - 2, part],
            s1_r.at[kind - 2, part],
            (near[flip_first[part]], z),
        )

    def step_two(kind, part):
        n = half[kind] // 2
        start = 2 * n * first[part] + n * (1 - second[part])
        return remote(
            side_work[kind].at[(slice(None),) + index(kind, part, start, n)],
            side_two[kind].at[part],
            s2_s.at[kind - 2, part],
            s2_r.at[kind - 2, part],
            (near[flip_second[part]], z),
        )

    def add_one(kind):
        n = half[kind]
        for part in range(2):
            arrival, onward = step_one(kind, part), step_two(kind, part)
            idx = (slice(None),) + index(kind, part, n * first[part], n)

            def add():
                arrival.wait_recv()
                side_work[kind][idx] += side_one[kind][part]

            if kind != 3:
                add()
                go(onward)
            else:
                pl.when(own)(add)
                when(own, onward)

    def add_two(kind):
        n = half[kind] // 2
        for part in range(2):
            arrival = step_two(kind, part)
            idx = (slice(None),) + index(kind, part, kept(kind, part), n)

            def add():
                arrival.wait_recv()
                side_work[kind][idx] += side_two[kind][part]

            if kind != 3:
                add()
                for j in range(2 if kind == 2 else 0):
                    go(pairwise(kind, part, j))
            else:
                pl.when(own)(add)
                when(own, *[along(part, j, side) for j in hops])

    def held(kind, part, j):
        idx = (goals[j],) + index(kind, part, kept(kind, part), half[kind] // 2)
        return (g, (kind,) + idx) if kind < 2 else (go_w, idx)

    def pairwise(kind, part, j):
        ref, idx = held(kind, part, j)
        dst = rz.at[kind, part, j] if kind < 2 else rz_o.at[part, j]
        return remote(
            ref.at[idx], dst, z_s.at[kind, part, j], z_r.at[kind, part, j], (w, pair)
        )

    def crosswise(kind, part):
        ref, idx = held(kind, part, 2)
        dst = rz.at[kind, part, 2] if kind < 2 else rz_o.at[part, 2]
        return remote(
            ref.at[idx], dst, z_s.at[kind, part, 2], z_r.at[kind, part, 2], (w, across)
        )

    def cross(kind, part):
        pairwise(kind, part, 1).wait_recv()
        ref, idx = held(kind, part, 2)
        ref[idx] += rz[kind, part, 1] if kind < 2 else rz_o[part, 1]
        go(crosswise(kind, part))

    def block(j):
        return g.at[:, goals[j], pl.ds(FP, FH - FP)]

    def line_copy_z(j):
        if j == 2:
            return remote(block(2), rz_z.at[2], zl_s.at[2], zl_r.at[2], (w, across))
        if j < EARLY_LINE:
            src, dst = g.at[1, goals[j], pl.ds(FP, FH - FP)], rz_z.at[j, 1]
        else:
            src, dst = block(j), rz_z.at[j]
        return remote(src, dst, zl_s.at[j], zl_r.at[j], (w, pair))

    def rows_start():
        for j in range(2):
            for kind in range(2):
                loaded(2 * j + kind)
            go(line_copy_z(j))

    def line_arrived(j):
        line_copy_z(j).wait_recv()
        if j < EARLY_LINE:
            fetched_line[j].wait()

    def rows_cross():
        line_arrived(1)
        for kind in range(2):
            loaded(2 * 2 + kind)
        block(2)[...] += rz_z[1]
        go(line_copy_z(2))

    def rows_plane():
        line_arrived(0)
        line_copy_z(2).wait_recv()
        for kind in range(2):
            loaded(2 * 3 + kind)
        w_z[...] = (
            block(3)[...].astype(F32) + rz_z[0].astype(F32) + rz_z[2].astype(F32)
        ).astype(BF16)
        for part in range(2):
            go(step_one(4, part))

    def cross_out():
        for part in range(2):
            cross(2, part)

    def along(part, j, source):
        idx = index(3, part, kept(3, part), half[3] // 2)
        return remote(
            gq_w.at[(zto[j],) + idx],
            f_q.at[(source,) + idx],
            z_s.at[3, part, j],
            z_r.at[3, part, source],
            (w, zto[j]),
        )

    def add_line(kind):
        for part in range(2):
            idx = index(kind, part, kept(kind, part), half[kind] // 2)
            if kind < 3:
                pairwise(kind, part, 0).wait_recv()
                crosswise(kind, part).wait_recv()
                ref, own = held(kind, part, 3)
                far = rz.at[kind] if kind < 2 else rz_o
                total = (
                    ref[own].astype(F32)
                    + far[part, 0].astype(F32)
                    + far[part, 2].astype(F32)
                ).astype(BF16)
                if kind < 2:
                    f_g[(kind,) + idx] = total
                else:
                    f_o[idx] = total
            elif kind == 4:
                f_z[(slice(None),) + idx] = w_z[(slice(None),) + idx]
            else:
                for i in range(2):
                    arrival = along(part, 1, i)

                    @pl.when(z != lower + i)
                    def _():
                        arrival.wait_recv()

                    @pl.when(z == lower + i)
                    def _():
                        f_q[(i,) + idx] = gq_w[(lower + i,) + idx]
            go(share_one(kind, part))

    def region(kind, part, start, n):
        idx = index(kind, part, start, n)
        if kind > 2:
            idx = (slice(None),) + idx
        return final[kind].at[idx]

    def share_one(kind, part):
        ref = region(kind, part, kept(kind, part), half[kind] // 2)
        return remote(
            ref,
            ref,
            g_s.at[kind, part, 0],
            g_r.at[kind, part, 0],
            (near[flip_second[part]], z),
        )

    def share_two(kind, part):
        ref = region(kind, part, half[kind] * first[part], half[kind])
        return remote(
            ref,
            ref,
            g_s.at[kind, part, 1],
            g_r.at[kind, part, 1],
            (near[flip_first[part]], z),
        )

    def relayed(kind):
        for part in range(2):
            n = half[kind] // 2
            start = half[kind] * first[part] + n * (1 - second[part])
            ref = region(kind, part, start, n)
            remote(
                ref,
                ref,
                g_s.at[kind, part, 0],
                g_r.at[kind, part, 0],
                (near[flip_second[part]], z),
            ).wait_recv()
            go(share_two(kind, part))

    def shared(kind):
        for part in range(2):
            ref = region(kind, part, half[kind] * (1 - first[part]), half[kind])
            remote(
                ref,
                ref,
                g_s.at[kind, part, 1],
                g_r.at[kind, part, 1],
                (near[flip_first[part]], z),
            ).wait_recv()
        go(
            remote(
                final[kind], out(kind, core), sib_s.at[kind], sib_r.at[kind], (near[1], z)
            )
        )
        copy = pltpu.make_async_copy(final[kind], out(kind, core), out_sem.at[kind])
        copy.start()
        outs.append(copy)

    pair_o = remote(
        go_hbm.at[:, at((1 - core) * CH, CH)], go_far, pair_s.at[NZ], pair_r.at[NZ], (near[1], z)
    )

    def gq_part(d, half_of):
        return p_s.at[d // 2, at((d % 2) * C + half_of * CH, CH)]

    pair_q = [
        remote(gq_part(d, 1 - core), gq_far.at[d], pair_s.at[d], pair_r.at[d], (near[1], z))
        for d in range(NZ)
    ]

    def do_copy(i, block, rows):
        return remote(
            do_ref.at[i], do_all.at[rows], do_s.at[i], do_r.at[block], (w, jnp.int32(lower + i))
        )

    def do_send():
        for i in range(2):
            when(z != lower + i, do_copy(i, z, at(z * R, R)))

            @pl.when(z == lower + i)
            def _():
                do_all[(lower + i) * R : (lower + i + 1) * R, :] = do_ref[i]
                do_all[T:, :] = jnp.zeros((do_all.shape[0] - T, H), BF16)

    def do_wait(b):
        arrival = do_copy(0, b, pl.ds(b * R, R))

        @pl.when(own & (z != b))
        def _():
            arrival.wait_recv()

    def pair_out():
        loads[len(chunks)].wait()
        go(pair_o)

    def pair_out_done():
        pair_o.wait_recv()
        go_w[...] += go_far[...]
        for part in range(2):
            go(step_one(2, part))

    def visit(n):
        group, i = visits[n]
        first_query, size, keys = spans[i]
        queries = slice(first_query, first_query + size)
        cols = slice(group * C, (group + 1) * C)
        slot = n % 2
        load_p(n).wait()
        if n == 0:
            for copy in inner_loads:
                copy.wait()
        if i == len(spans) - 1:
            k_t[:, :T] = jnp.transpose(k_ref[:, cols].astype(F32)).astype(BF16)
        for pair_of in range(0, 4, 2):
            two = []
            for h in (pair_of, pair_of + 1):
                pick = lanes(size, C, h).astype(BF16)
                here = slice(h * size, (h + 1) * size)
                do_h = do_all[queries, cols] * pick
                q_st[here, :] = q_ref[queries, cols] * pick
                share = l_ref[group, h, :, queries]
                do_st[here, :] = (do_h.astype(F32) * jnp.transpose(share)[:, 0:1]).astype(BF16)
                two.append(do_h)
            both = dot_nt(v_ref[:keys, cols], jnp.concatenate(two, 0))
            for t in range(2):
                h = pair_of + t
                here = slice(h * size, (h + 1) * size)
                p = p_s[slot, :keys, here].astype(F32) * l_ref[group, h, 0:1, queries]
                product = p * both[:, t * size : (t + 1) * size]
                ds = (product - p * jnp.sum(product, 0, keepdims=True)).astype(BF16)
                ds_s[:keys, here] = ds
                rows = slice(h * (C // 4), (h + 1) * (C // 4))
                dq_t[rows, :size] = dot(k_t[rows, :keys], ds)
        dv = dot(p_s[slot, :keys, : 4 * size], do_st[: 4 * size, :])
        dk = dot(ds_s[:keys, : 4 * size], q_st[: 4 * size, :])
        if i == len(spans) - 1:
            dv_f[...] = dv
            dk_f[...] = dk
        else:
            dv_f[:keys, :] += dv
            dk_f[:keys, :] += dk
        if n + 2 < len(visits):
            load_p(n + 2).start()
        ready = slice(first_query, keys)
        kept_rows = min(size, T - first_query)
        dq = jnp.transpose(dq_t[:, :size])[:kept_rows, :] * 0.125
        dqkv[first_query : first_query + kept_rows, cols] = dq.astype(BF16)
        dqkv[ready, H + group * C : H + (group + 1) * C] = (dk_f[ready, :] * 0.125).astype(BF16)
        dqkv[ready, 2 * H + group * C : 2 * H + (group + 1) * C] = dv_f[ready, :].astype(BF16)

    def visit_block(group, b):
        @pl.when(own)
        def _():
            for n, (of, i) in enumerate(visits):
                if of == group and (i == b or (b == NZ - 1 and i > b)):
                    visit(n)

    def heads(b):
        visit_block(0, b)

    def keys(b):
        visit_block(1, b)

    def partial(d):
        @pl.when(own)
        def _():
            dh[d] = dot_nt(dqkv[d * R : (d + 1) * R, :], wq_ref[...]).astype(BF16)

    def hand(d, slot):
        return remote(
            dh.at[d], rel.at[slot], ru_s.at[slot], ru_r.at[slot], (w, jnp.int32(partner))
        )

    def hand_over(d):
        holder = upper if d <= lower else lower
        slot = 0 if lower <= d <= upper else 1
        when(z == holder, hand(d, slot))

    outward = remote(dh.at[outer], rel.at[0], ru_s.at[2], ru_r.at[2], (w, outer))

    def hand_out():
        arrival = hand(0, 1)

        @pl.when(own)
        def _():
            arrival.wait_recv()
            dh[outer] += rel[1]

        when(own, outward)

    load_dmid = pltpu.make_async_copy(dmid_hbm, dk_f, load_sem.at[len(chunks) + 7])

    def fetch_h1():
        load_dmid.start()

        @pl.when(own)
        def _():
            load_h1.start()

    def grad_qkv():
        for d in range(NZ):
            s_f[d] = small_in[:, d * C : (d + 1) * C]

        @pl.when(own)
        def _():
            load_h1.wait()
            for d in range(NZ):
                p_s[d // 2, (d % 2) * C : (d % 2 + 1) * C, :] = dot_tn(
                    ds_s[:, d * C : (d + 1) * C], dqkv[...]
                ).astype(BF16)
            for row, start in ((8, 0), (9, 2 * H)):
                total = rowsum(dqkv[:, start : start + H].astype(F32))
                for half_of in range(2):
                    s_f[2 * side + half_of, row : row + 1, :] = total[
                        :, half_of * C : (half_of + 1) * C
                    ]

        when(own, *pair_q)

    def pair_qkv_done():
        @pl.when(own)
        def _():
            for d in range(NZ):
                pair_q[d].wait_recv()
                gq_w[d] = gq_part(d, core)[...] + gq_far[d]

        when(own, *[step_one(3, part) for part in range(2)])

    def line_copy(j):
        return remote(s_b.at[zto[j]], s_z.at[j], sz_s.at[j], sz_r.at[j], (w, zto[j]))

    def plane_copy(j):
        return remote(s_p, s_g.at[j], sp_s.at[j], sp_r.at[j], (near[j], z))

    def input_grad():
        inner = hand(0, 0)

        @pl.when(own)
        def _():
            inner.wait_recv()
            rel[0] += dh[z]

        @pl.when(jnp.logical_not(own))
        def _():
            outward.wait_recv()

        dh1 = rel[0].astype(F32)
        n1, inverse = norm(x_ref[...].astype(F32))
        load_dmid.wait()
        dmid = jnp.concatenate([dk_f[s * R : (s + 1) * R, :] for s in range(NZ)], 1)
        dx_ref[...] = (dmid + norm_back(dh1, n1, inverse, par_ref[0:1, :])).astype(BF16)
        gain = rowsum(dh1 * n1)
        shift = rowsum(dh1)
        for d in range(NZ):
            s_f[d, 0:1, :] = gain[:, d * C : (d + 1) * C]
            s_f[d, 4:5, :] = shift[:, d * C : (d + 1) * C]
        s_b[...] = s_f[...].astype(BF16)
        for j in hops:
            go(line_copy(j))

    def small_line():
        total = s_f[z]
        for j in hops:
            line_copy(j).wait_recv()
            total += s_z[j].astype(F32)
        small_out[...] = total
        s_p[...] = total.astype(BF16)
        for j in range(1, GROUP):
            go(plane_copy(j))

    def small_plane():
        total = small_out[...]
        for j in range(1, GROUP):
            plane_copy(j).wait_recv()
            total += s_g[j].astype(F32)
        small_out[...] = total

    for act, *where in (
        (do_send,),
        (launch, 0),
        (launch, 1),
        (launch, 2),
        (rows_start,),
        (launch, 3),
        (pair_out,),
        (pair_out_done,),
        (do_wait, 2),
        (reduce_one, 2),
        (do_wait, 1),
        (do_wait, 3),
        (launch, 4),
        (launch, 5),
        (heads, 3),
        (heads, 2),
        (do_wait, 0),
        (heads, 1),
        (add_one, 2),
        (reduce_one, 3),
        (heads, 0),
        (rows_cross,),
        (launch, 6),
        (keys, 3),
        (reduce_one, 5),
        (reduce_one, 0),
        (keys, 2),
        (add_two, 2),
        (keys, 1),
        (reduce_one, 4),
        (reduce_two, 3),
        (keys, 0),
        (reduce_two, 2),
        (reduce_one, 6),
        (launch, 7),
        (cross_out,),
        (partial, 0),
        (fetch_h1,),
        (reduce_two, 5),
        (rows_plane,),
        (hand_over, 0),
        (partial, 3),
        (reduce_one, 1),
        (hand_over, 3),
        (grad_qkv,),
        (add_one, 4),
        (reduce_two, 1),
        (reduce_one, 7),
        (pair_qkv_done,),
        (reduce_two, 4),
        (add_two, 4),
        (partial, 2),
        (reduce_two, 7),
        (add_line, 4),
        (reduce_two, 0),
        (reduce_two, 6),
        (add_line, 2),
        (add_one, 3),
        (partial, 1),
        (add_line, 1),
        (add_two, 3),
        (hand_out,),
        (relayed, 2),
        (relayed, 4),
        (hand_over, 2),
        (add_line, 0),
        (shared, 2),
        (relayed, 1),
        (hand_over, 1),
        (add_line, 3),
        (shared, 1),
        (shared, 4),
        (relayed, 0),
        (relayed, 3),
        (input_grad,),
        (shared, 0),
        (small_line,),
        (shared, 3),
        (small_plane,),
    ):
        act(*where)
    for kind in range(5):
        remote(
            final[kind], out(kind, 1 - core), sib_s.at[kind], sib_r.at[kind], (near[1], z)
        ).wait_recv()
    for ok, copy in guarded:
        pl.when(ok)(copy.wait_send)
    for copy in pending:
        copy.wait_send()
    for copy in outs:
        copy.wait()


def reduce(NZ, inputs, dmid, par, small, do, wq, q, k, v, share, h1, p, g, go, early, early_line):
    R, D = inputs.shape
    C = D // NZ
    H = D // 2
    T = NZ * R
    TP = q.shape[0]
    FH = g.shape[2]
    FP = FH - FH // 4
    shape = jax.ShapeDtypeStruct
    buf = pltpu.VMEM
    return pl.pallas_call(
        functools.partial(reduce_kernel, NZ),
        out_shape=[
            shape((R, D), BF16),
            shape((2, 2, FH, D), BF16),
            shape((2, C // 2, D), BF16),
            shape((2, 2, C // 2, 3 * H), BF16),
            shape((16, C), F32),
        ],
        in_specs=[VMEM, ANY, VMEM, VMEM, VMEM] + [ANY] * 11,
        out_specs=[VMEM, ANY, ANY, ANY, VMEM],
        scratch_shapes=[
            buf(wq.shape, BF16),
            buf(q.shape, BF16),
            buf(k.shape, BF16),
            buf(v.shape, BF16),
            buf(share.shape, F32),
            buf((2, T, 3 * H), BF16),
            buf((2, NZ, FH, D), BF16),
            buf((NZ, C // 2, D), BF16),
            buf((NZ, C // 2, D), BF16),
            buf((NZ, C // 2, 3 * H), BF16),
            buf((NZ, C // 2, 3 * H), BF16),
            buf((2 * NZ, 2, FP // 4, D), BF16),
            buf((2, NZ, C // 4, D // 2), BF16),
            buf((2, NZ, C // 4, 3 * H // 2), BF16),
            buf((2 * NZ, 2, FP // 8, D), BF16),
            buf((2, NZ, C // 8, D // 2), BF16),
            buf((2, NZ, C // 8, 3 * H // 2), BF16),
            buf((2, 2, NZ - 1, FP // 8, D), BF16),
            buf((2, NZ - 1, C // 8, D // 2), BF16),
            buf((3, 2, FH - FP, D), BF16),
            buf((2, 2, FH // 8, D // 2), BF16),
            buf((2, 2, FH // 16, D // 2), BF16),
            buf((2, FH - FP, D), BF16),
            buf((2, FH - FP, D), BF16),
            buf((2, FP, D), BF16),
            buf((C // 2, D), BF16),
            buf((2, C // 2, 3 * H), BF16),
            buf((TP, H), BF16),
            buf((4 * QUERIES, C), BF16),
            buf((4 * QUERIES, C), BF16),
            buf((T, 4 * QUERIES), BF16),
            buf((C, QUERIES), F32),
            buf((C, TP), BF16),
            buf((T, C), F32),
            buf((T, C), F32),
            buf((T, 3 * H), BF16),
            buf((NZ, R, D), BF16),
            buf((2, R, D), BF16),
            buf((NZ, 16, C), F32),
            buf((NZ, 16, C), BF16),
            buf((NZ, 16, C), BF16),
            buf((16, C), BF16),
            buf((GROUP, 16, C), BF16),
            DMA((2 * NZ + 8,)),
            DMA((EARLY + EARLY_LINE,)),
            DMA((2,)),
            DMA((2,)),
            DMA((NZ,)),
            DMA((NZ + 1,)),
            DMA((NZ + 1,)),
            DMA((3, 2)),
            DMA((3, 2)),
            DMA((3, 2)),
            DMA((3, 2)),
            DMA((2 * NZ, 2)),
            DMA((2 * NZ, 2)),
            DMA((2 * NZ, 2)),
            DMA((2 * NZ, 2)),
            DMA((4, 2, NZ)),
            DMA((4, 2, NZ)),
            DMA((3,)),
            DMA((3,)),
            DMA((5, 2, 2)),
            DMA((5, 2, 2)),
            DMA((5,)),
            DMA((5,)),
            DMA((3,)),
            DMA((3,)),
            DMA((NZ,)),
            DMA((NZ,)),
            DMA((GROUP,)),
            DMA((GROUP,)),
            DMA((5,)),
        ],
        compiler_params=pltpu.CompilerParams(
            collective_id=2, has_side_effects=True, vmem_limit_bytes=63 * 2**20
        ),
    )(inputs, dmid, par, small, do, wq, q, k, v, share, h1, p, g, go, early, early_line)


def widen_kernel(fc2, fc1, out, qkv, act, dx, small, d_fc2, d_fc1, d_out, d_qkv, d_act, d_dx, d_gain, d_shift):
    step = pl.program_id(0)
    d_fc2[...] = fc2[0, 0].astype(F32)
    d_fc1[...] = fc1[0, 0].astype(F32)
    d_out[...] = out[0].astype(F32)
    d_act[...] = act[...]
    d_dx[...] = dx[...]
    d_gain[...] = small[0:4, :]
    d_shift[...] = small[4:16, :]
    width = qkv.shape[3] // 3
    for t in range(3):
        cols = at(t * (d_qkv.shape[1] // 3) + lax.rem(step, 2) * width, width, 128)
        d_qkv[:, cols] = qkv[0, 0, :, t * width : (t + 1) * width].astype(F32)


def widen(g, go, gq, act, dx, small):
    FH, D = g.shape[2:]
    CH = gq.shape[2]
    C = 2 * CH
    NZ = D // C
    R = act.shape[0]
    steps = 2 * NZ
    part = D // steps
    shape = jax.ShapeDtypeStruct
    return pl.pallas_call(
        widen_kernel,
        grid=(steps,),
        out_shape=[
            shape((2 * FH, D), F32),
            shape((C, 2 * NZ * FH), F32),
            shape((C, D), F32),
            shape((C, 3 * D), F32),
            shape((R, D), BF16),
            shape((R, D), BF16),
            shape((4, C), F32),
            shape((12, C), F32),
        ],
        in_specs=[
            pl.BlockSpec((1, 1, 2 * FH // steps, D), lambda i: (0, i // NZ, i % NZ, 0)),
            pl.BlockSpec((1, 1, C, FH), lambda i: (1, i % 2, i // 2 // 2, i // 2 % 2)),
            pl.BlockSpec((1, C // steps, D), lambda i: (i // NZ, i % NZ, 0)),
            pl.BlockSpec(
                (1, 1, CH // 2, gq.shape[3]), lambda i: (i // 4, i % 2, i // 2 % 2, 0)
            ),
            pl.BlockSpec((R, part), lambda i: (0, i)),
            pl.BlockSpec((R, part), lambda i: (0, i)),
            pl.BlockSpec((16, C), lambda i: (0, 0)),
        ],
        out_specs=[
            pl.BlockSpec((2 * FH // steps, D), lambda i: (i, 0)),
            pl.BlockSpec((C, FH), lambda i: (0, i)),
            pl.BlockSpec((C // steps, D), lambda i: (i, 0)),
            pl.BlockSpec((CH // 2, 3 * D), lambda i: (i // 2, 0)),
            pl.BlockSpec((R, part), lambda i: (0, i)),
            pl.BlockSpec((R, part), lambda i: (0, i)),
            pl.BlockSpec((4, C), lambda i: (0, 0)),
            pl.BlockSpec((12, C), lambda i: (0, 0)),
        ],
        compiler_params=pltpu.CompilerParams(vmem_limit_bytes=62 * 2**20),
    )(g, g, go, gq, act, dx, small)


def shards(NZ, W, inputs, w_qkv, w_out, w_fc1, w_fc2, norm_gain, shifts, text_len, cotangent):
    R, D = inputs.shape[1:]
    C = D // NZ
    FF = w_fc1.shape[1]
    FH = FF // (2 * NZ)
    h1, q, k, v, wq, par_f, p, share, act, dmid, do, g, go, early, early_line, small = forward(
        NZ, inputs[0], cotangent[0], norm_gain, shifts, text_len, w_qkv, w_out, w_fc1, w_fc2
    )
    dx, g, go, gq, small = reduce(
        NZ, inputs[0], dmid, par_f, small, do, wq, q, k, v, share, h1, p, g, go, early, early_line
    )
    fc2, fc1, out, qkv, act, dx, gain, shift = widen(g, go, gq, act, dx, small)
    grads = (qkv, out, fc1, fc2, gain, shift)
    if W > GROUP:
        groups = [list(range(i, W, GROUP)) for i in range(GROUP)]
        grads = lax.psum(grads, "wide", axis_index_groups=groups)
    return (act[None], dx[None]) + tuple(grads)


def solution(mesh):
    return jax.shard_map(
        functools.partial(shards, mesh.shape["narrow"], mesh.shape["wide"]),
        mesh=mesh,
        in_specs=(
            P("wide", "narrow", None),
            P("narrow", None),
            P("narrow", None),
            P("narrow", None),
            P("narrow", None),
            P(None, "narrow"),
            P(None, "narrow"),
            P("wide"),
            P("wide", "narrow", None),
        ),
        out_specs=(
            P("wide", "narrow", None),
            P("wide", "narrow", None),
            P("narrow", None),
            P("narrow", None),
            P("narrow", None),
            P("narrow", None),
            P(None, "narrow"),
            P(None, "narrow"),
        ),
        check_vma=False,
    )
```

```python
import functools
import math

import jax
import jax.numpy as jnp
from jax import lax
from jax.experimental import pallas as pl
from jax.experimental.pallas import tpu as pltpu
from jax.sharding import PartitionSpec as P

HEADS = 16
TEXT = 64
EPS = 1e-5
GROUP = 8
QUERIES = 256
EARLY = 1
EARLY_LINE = 2
MESH = pl.DeviceIdType.MESH
F32 = jnp.float32
BF16 = jnp.bfloat16
ANY = pl.BlockSpec(memory_space=pl.ANY)
VMEM = pl.BlockSpec(memory_space=pltpu.VMEM)
SMEM = pl.BlockSpec(memory_space=pltpu.SMEM)
DMA = pltpu.SemaphoreType.DMA


def at(start, size, step=16):
    return pl.ds(pl.multiple_of(start, step), size)


def place():
    w = lax.axis_index("wide")
    z = lax.axis_index("narrow")
    return w, z, lax.rem(w, 2), lax.rem(lax.div(w, 2), 2), lax.rem(lax.div(w, 4), 2)


def flips(w, core, x, y, j):
    return (
        w
        + (j & 1) * (1 - 2 * core)
        + ((j >> 1) & 1) * (2 - 4 * x)
        + ((j >> 2) & 1) * (4 - 8 * y)
    )


def remote(src, dst, send_sem, recv_sem, device):
    return pltpu.make_async_remote_copy(
        src_ref=src,
        dst_ref=dst,
        send_sem=send_sem,
        recv_sem=recv_sem,
        device_id=device,
        device_id_type=MESH,
    )


def meet(devices):
    barrier = pltpu.get_barrier_semaphore()
    for device in devices:
        pl.semaphore_signal(barrier, inc=1, device_id=device, device_id_type=MESH)
    pl.semaphore_wait(barrier, len(devices))


def dot(left, right):
    return lax.dot_general(left, right, (((1,), (0,)), ((), ())), preferred_element_type=F32)


def dot_nt(left, right):
    return lax.dot_general(left, right, (((1,), (1,)), ((), ())), preferred_element_type=F32)


def dot_tn(left, right):
    return lax.dot_general(left, right, (((0,), (0,)), ((), ())), preferred_element_type=F32)


def norm(values):
    centred = values - jnp.mean(values, -1, keepdims=True)
    inverse = lax.rsqrt(jnp.mean(centred * centred, -1, keepdims=True) + EPS)
    return centred * inverse, inverse


def norm_back(incoming, normed, inverse, gain):
    scaled = incoming * gain
    return inverse * (
        scaled
        - jnp.mean(scaled, -1, keepdims=True)
        - normed * jnp.mean(scaled * normed, -1, keepdims=True)
    )


def rowsum(values):
    return jnp.sum(values, 0, keepdims=True)


def lanes(rows, width, head):
    lane = lax.broadcasted_iota(jnp.int32, (rows, width), 1)
    size = width // 4
    return ((lane >= head * size) & (lane < head * size + size)).astype(F32)


def query_blocks(total):
    blocks = []
    for first in range(0, total, QUERIES):
        size = min(QUERIES, -(-(total - first) // 128) * 128)
        blocks.append((first, size, min(first + QUERIES, total)))
    return blocks


def forward_kernel(
    NZ,
    x_ref,
    gain_ref,
    shift_ref,
    len_ref,
    cot_ref,
    wqkv_ref,
    wout_ref,
    wfc1_ref,
    wfc2_ref,
    h1_out,
    q_out,
    k_out,
    v_out,
    wq_out,
    par_out,
    p_out,
    l_out,
    act_ref,
    dmid_ref,
    do_ref,
    g_out,
    go_out,
    early_out,
    early_line_out,
    small_ref,
    par_ref,
    par_all,
    par_f,
    stage,
    wq,
    a_ref,
    b_ref,
    wo_ref,
    h1,
    q_s,
    k_s,
    v_s,
    v_t,
    s_s,
    o_t,
    l_s,
    mid_s,
    big,
    o_send,
    o2,
    h3,
    dm,
    part,
    far_m,
    far_h,
    g_s,
    go_s,
    loc_sem,
    par_s,
    par_r,
    wz_s,
    wz_r,
    wp_s,
    wp_r,
    h_s,
    h_r,
    fz_s,
    fz_r,
    fp_s,
    fp_r,
    fq_s,
    fq_r,
    sib_s,
    sib_r,
    o_s,
    o_r,
    out_sem,
    p_sem,
    swap_s,
    swap_r,
    early_s,
    early_r,
    early_line_s,
    early_line_r,
):
    R, D = x_ref.shape
    C = D // NZ
    FH = wfc1_ref.shape[1] // (2 * NZ)
    w, z, core, x, y = place()
    chip = x + 2 * y
    H = D // 2
    lower, upper = NZ // 2 - 1, NZ // 2
    own = (z == lower) | (z == upper)
    side = lax.div(z, NZ // 2)
    near = {j: flips(w, core, x, y, j) for j in range(1, GROUP)}
    zto = [lax.rem(z + j, NZ) for j in range(NZ)]
    zfrom = [lax.rem(z + NZ - j, NZ) for j in range(NZ)]
    hops = range(1, NZ)
    pending = []

    def go(copy):
        copy.start()
        pending.append(copy)

    first = (x, y)
    second = (y, x)
    flip_first = (2, 4)
    flip_second = (4, 2)
    local = 1 + 3 * NZ
    RW = C // GROUP
    staged = [
        pltpu.make_async_copy(
            wqkv_ref.at[:, pl.ds(t * D + d * H, H)],
            stage.at[d, :, pl.ds(t * H, H)],
            loc_sem.at[1 + 3 * d + t],
        )
        for d in range(2)
        for t in range(3)
    ]
    owned = [
        pltpu.make_async_copy(
            wfc1_ref.at[:, at((2 * j) * FH + core * FH, FH, 128)],
            a_ref.at[at(z * C, C), pl.ds(j * FH, FH)],
            loc_sem.at[local + j],
        )
        for j in range(NZ)
    ]
    owned.append(
        pltpu.make_async_copy(
            wfc2_ref.at[at(core * FH, FH)], b_ref.at[z], loc_sem.at[local + NZ]
        )
    )
    owned.append(
        pltpu.make_async_copy(wout_ref, wo_ref.at[at(z * C, C)], loc_sem.at[local + NZ + 1])
    )
    own_par = pltpu.make_async_copy(par_ref, par_all.at[z], loc_sem.at[0])
    own_wq = [
        pltpu.make_async_copy(stage.at[i], wq.at[at(z * C, C)], loc_sem.at[local + NZ + 2])
        for i in range(2)
    ]
    relays = []

    def other_chip(t):
        return (x + (t & 1) * (1 - 2 * x)) + 2 * (y + (t >> 1) * (1 - 2 * y))

    def when(ok, *copies):
        for copy in copies:
            relays.append((ok, copy))

        @pl.when(ok)
        def _():
            for copy in copies:
                copy.start()

    def par_copy(j, source):
        return remote(par_ref, par_all.at[source], par_s.at[j], par_r.at[j], (w, zto[j]))

    def start():
        par_ref[...] = jnp.concatenate(
            [gain_ref[...].astype(F32), shift_ref[...].astype(F32)], 0
        ).astype(BF16)
        for copy in (own_par, *staged, *owned):
            copy.start()
        meet([(w, zto[j]) for j in hops] + [(near[j], z) for j in range(1, GROUP)])
        for j in hops:
            go(par_copy(j, z))

    def eighth(chip_of):
        return core * (C // 2) + chip_of * RW

    def wq_line(i, source):
        return remote(
            stage.at[i, at(eighth(chip), RW)],
            wq.at[at(source * C + eighth(chip), RW)],
            wz_s.at[i],
            wz_r.at[source],
            (w, jnp.int32(lower + i)),
        )

    def wq_plane(source, t, owner):
        part = wq.at[at(source * C + eighth(owner), RW)]
        return remote(part, part, wp_s.at[source, t], wp_r.at[source, t], (near[2 * t], z))

    def wq_sibling(source, half_of):
        part = wq.at[at(source * C + half_of * (C // 2), C // 2)]
        return remote(part, part, wp_s.at[source, 0], wp_r.at[source, 0], (near[1], z))

    def wq_send():
        for copy in staged:
            copy.wait()
        for i in range(2):
            when(z != lower + i, wq_line(i, z))

            @pl.when(z == lower + i)
            def _():
                own_wq[i].start()

    def wq_pass():
        for source in range(NZ):
            ok = own & (z != source)
            arrival = wq_line(0, source)

            @pl.when(ok)
            def _():
                arrival.wait_recv()

            when(ok, *[wq_plane(source, t, chip) for t in range(1, 4)])

    def wq_swap():
        for source in range(NZ):
            ok = own & (z != source)
            arrivals = [wq_plane(source, t, other_chip(t)) for t in range(1, 4)]

            @pl.when(ok)
            def _():
                for copy in arrivals:
                    copy.wait_recv()

            when(ok, wq_sibling(source, core))

    def wq_wait():
        for i in range(2):

            @pl.when(z == lower + i)
            def _():
                own_wq[i].wait()

        for source in range(NZ):
            arrival = wq_sibling(source, 1 - core)

            @pl.when(own & (z != source))
            def _():
                arrival.wait_recv()

    def first_norm():
        normed, _ = norm(x_ref[...].astype(F32))
        own_par.wait()
        for j in hops:
            par_copy(j, zfrom[j]).wait_recv()
        for d in range(NZ):
            par_f[:, d * C : (d + 1) * C] = par_all[d].astype(F32)
        h1[at(z * R, R), :] = (normed * par_f[0:1, :] + par_f[4:5, :]).astype(BF16)

    def sends(way, k):
        if way == 0:
            return (z - k >= 0) & (z < NZ - 1)
        return (z + k <= NZ - 1) & (z > 0)

    def comes(way, k):
        return z - 1 - k >= 0 if way == 0 else z + 1 + k <= NZ - 1

    def sent(way, k):
        return jnp.maximum(z - k, 0) if way == 0 else jnp.minimum(z + k, NZ - 1)

    def got(way, k):
        return jnp.maximum(z - 1 - k, 0) if way == 0 else jnp.minimum(z + 1 + k, NZ - 1)

    ahead = ((w, jnp.minimum(z + 1, NZ - 1)), (w, jnp.maximum(z - 1, 0)))
    def h1_copy(way, k, block):
        ref = h1.at[at(block * R, R)]
        return remote(ref, ref, h_s.at[way, k], h_r.at[way, k], ahead[way])

    def h1_send(k):
        for way in range(2):
            toward = z <= lower if way == 0 else z >= upper
            when(sends(way, k) & toward, h1_copy(way, k, sent(way, k)))

    def h1_comes(way, k):
        return own & comes(way, k) & (z - 1 <= lower if way == 0 else z + 1 >= upper)

    def h1_come(k):
        for way in range(2):
            copy = h1_copy(way, k, got(way, k))

            @pl.when(h1_comes(way, k))
            def _():
                copy.wait_recv()

        if k + 1 < NZ // 2:
            h1_send(k + 1)

    def rows_of(kind):
        return (C // 4, FH // 4, C // 8)[kind]

    def piece(kind, part, source, start, n):
        if kind == 0:
            half = a_ref.shape[1] // 2
            return a_ref.at[at(source * C + start, n), pl.ds(part * half, half)]
        if kind == 1:
            half = D // 2
            return b_ref.at[source, at(start, n), pl.ds(part * half, half)]
        half = D // 2
        return wo_ref.at[
            at(source * C + core * (C // 2) + start, n), pl.ds(part * half, half)
        ]

    def quarter(kind, part, source):
        n = rows_of(kind)
        return piece(kind, part, source, n * (2 * first[part] + second[part]), n)

    def w_copy(kind, part, way, k, source):
        ref = quarter(kind, part, source)
        return remote(
            ref, ref, fz_s.at[kind, part, way, k], fz_r.at[kind, part, way, k], ahead[way]
        )

    def w_send(kind, k):
        if k == 0:
            for copy in {0: owned[:NZ], 1: owned[NZ : NZ + 1], 2: owned[NZ + 1 :]}[kind]:
                copy.wait()
        for part in range(2):
            for way in range(2):
                when(sends(way, k), w_copy(kind, part, way, k, sent(way, k)))

    def share_one(kind, part, way, k):
        ref = quarter(kind, part, got(way, k))
        return remote(
            ref,
            ref,
            fp_s.at[kind, part, way, k],
            fp_r.at[kind, part, way, k],
            (near[flip_second[part]], z),
        )

    def share_two(kind, part, way, k):
        n = 2 * rows_of(kind)
        ref = piece(kind, part, got(way, k), n * first[part], n)
        return remote(
            ref,
            ref,
            fq_s.at[kind, part, way, k],
            fq_r.at[kind, part, way, k],
            (near[flip_first[part]], z),
        )

    def w_come(kind, k):
        for part in range(2):
            for way in range(2):
                copy = w_copy(kind, part, way, k, got(way, k))
                share = share_one(kind, part, way, k)
                relays.append((comes(way, k), share))

                @pl.when(comes(way, k))
                def _():
                    copy.wait_recv()
                    share.start()

        if k + 1 < NZ - 1:
            w_send(kind, k + 1)

    def w_double(kind, k):
        for part in range(2):
            for way in range(2):
                source = got(way, k)
                n = rows_of(kind)
                start = n * (2 * first[part] + (1 - second[part]))
                ref = piece(kind, part, source, start, n)
                copy = remote(
                    ref,
                    ref,
                    fp_s.at[kind, part, way, k],
                    fp_r.at[kind, part, way, k],
                    (near[flip_second[part]], z),
                )
                share = share_two(kind, part, way, k)
                relays.append((comes(way, k), share))

                @pl.when(comes(way, k))
                def _():
                    copy.wait_recv()
                    share.start()

    def w_done(kind, k):
        for part in range(2):
            for way in range(2):
                n = 2 * rows_of(kind)
                ref = piece(kind, part, got(way, k), n * (1 - first[part]), n)
                copy = remote(
                    ref,
                    ref,
                    fq_s.at[kind, part, way, k],
                    fq_r.at[kind, part, way, k],
                    (near[flip_first[part]], z),
                )

                @pl.when(comes(way, k))
                def _():
                    copy.wait_recv()

    total = NZ * R

    def project(block):
        rows = at(block * R, R)
        gap = D - H
        bias = [
            jnp.where(z == lower, par_f[4 + t : 5 + t, 0:H], par_f[4 + t : 5 + t, gap:D])
            for t in (4, 5)
        ]
        q_s[rows, :] = (dot(h1[rows, :], wq[:, 0:H]) + bias[0]).astype(BF16)
        k_s[rows, :] = dot(h1[rows, :], wq[:, H : 2 * H]).astype(BF16)
        v_s[rows, :] = (dot(h1[rows, :], wq[:, 2 * H : 3 * H]) + bias[1]).astype(BF16)

    def project_own():
        pad = q_s.shape[0] - total

        @pl.when(own)
        def _():
            q_s[total:, :] = jnp.zeros((pad, H), BF16)
            project(z)

    def project_come(k):
        for way in range(2):

            @pl.when(h1_comes(way, k))
            def _():
                project(got(way, k))

    outs = []

    def emit(src, dst, sem):
        copy = pltpu.make_async_copy(src, dst, out_sem.at[sem])
        copy.start()
        outs.append(copy)

    guarded = []

    def emit_own(src, dst, sem):
        copy = pltpu.make_async_copy(src, dst, out_sem.at[sem])
        guarded.append(copy)

        @pl.when(own)
        def _():
            copy.start()

    def emit_qkv():
        emit_own(h1, h1_out, 0)
        emit_own(q_s, q_out, 1)
        emit_own(k_s, k_out, 2)
        emit_own(v_s, v_out, 3)
        emit_own(wq, wq_out, 4)
        emit(par_f, par_out, 5)

    scale = math.log2(math.e) / math.sqrt(C // 4)
    text_len = len_ref[0]
    spans = query_blocks(total)
    done = []

    def p_copy(g, i):
        first_query, size, keys = spans[i]
        return pltpu.make_async_copy(
            big.at[g, pl.ds(0, keys), pl.ds(0, 4 * size)],
            p_out.at[g, pl.ds(0, keys), pl.ds(4 * first_query, 4 * size)],
            p_sem.at[g],
        )

    def scores(i):
        first_query, size, keys = spans[i]
        queries = slice(first_query, first_query + size)
        span = keys - first_query
        row = lax.broadcasted_iota(jnp.int32, (span, size), 0)
        col = lax.broadcasted_iota(jnp.int32, (span, size), 1)
        later = jnp.where(row <= col, 0.0, -1e30)
        head_row = lax.broadcasted_iota(jnp.int32, (TEXT, size), 0)
        unread = jnp.where(head_row < text_len, 0.0, -1e30)

        @pl.loop(0, 2)
        def _(g):
            if done:
                p_copy(g, done[-1]).wait()
            cols = at(g * C, C, 128)
            if not done:
                v_t[g, :, :total] = jnp.transpose(v_s[:, cols].astype(F32)).astype(BF16)
            for pair_of in range(0, 4, 2):
                q_two = jnp.concatenate(
                    [
                        q_s[queries, cols] * lanes(size, C, h).astype(BF16)
                        for h in (pair_of, pair_of + 1)
                    ],
                    0,
                )
                both = dot_nt(k_s[:keys, cols], q_two)
                for t in range(2):
                    h = pair_of + t
                    s_s[t, :keys, :size] = both[:, t * size : (t + 1) * size]
                    s_s[t, 0:TEXT, :size] += unread
                    s_s[t, first_query:keys, :size] += later
                    s = s_s[t, :keys, :size]
                    e = jnp.exp2((s - jnp.max(s, 0, keepdims=True)) * scale)
                    share = 1.0 / jnp.sum(e, 0, keepdims=True)
                    e = e.astype(BF16)
                    big[g, :keys, h * size : (h + 1) * size] = e
                    l_s[g, h, :, queries] = jnp.broadcast_to(share, (8, size))
                    rows = slice(h * (C // 4), (h + 1) * (C // 4))
                    o_t[rows, :size] = dot(v_t[g, rows, :keys], e) * share
            o_send[queries, cols] = jnp.transpose(o_t[:, :size]).astype(BF16)
            p_copy(g, i).start()

        done.append(i)

    def o_copy(b):
        return remote(
            o_send.at[pl.ds(b * R, R)], o2.at[side], o_s.at[b], o_r.at[side], (w, jnp.int32(b))
        )

    def attention(b):
        @pl.when(own)
        def _():
            last = len(spans) if b == NZ - 1 else b + 1
            for i in reversed(range(b, last)):
                scores(i)
            if b == 0:
                for g in range(2):
                    p_copy(g, 0).wait()

        when(own & (z != b), o_copy(b))

        @pl.when(z == b)
        def _():
            o2_own(b)

    def o2_own(b):
        if lower <= b <= upper:
            o2[b - lower] = o_send[b * R : (b + 1) * R, :]

    def o_come():
        for i in range(2):
            copy = remote(
                o_send.at[pl.ds(0, R)], o2.at[i], o_s.at[0], o_r.at[i], (w, jnp.int32(0))
            )

            @pl.when(z != lower + i)
            def _():
                copy.wait_recv()

    def emit_l():
        emit_own(l_s, l_out, 9 + NZ)

    def sibling(j, half):
        part = wo_ref.at[at(zfrom[j] * C + half * (C // 2), C // 2)]
        return remote(part, part, sib_s.at[j], sib_r.at[j], (near[1], z))

    def wo_swap():
        for j in hops:
            go(sibling(j, core))

    def wo_done():
        for j in hops:
            sibling(j, 1 - core).wait_recv()

    gate, slope = big.at[0, pl.ds(0, 2 * R)], big.at[0, pl.ds(2 * R, 2 * R)]
    du = big.at[1, pl.ds(0, 2 * R)]
    mine, theirs = slice(0, R), slice(R, 2 * R)
    kept = {}
    shift = 4

    def swap(src, dst, i):
        return remote(src, dst, swap_s.at[i], swap_r.at[i], (near[1], z))

    swap_h = swap(h3.at[pl.ds(0, R)], h3.at[pl.ds(R, R)], 0)
    swap_m = swap(part.at[0], far_m, 1)
    swap_d = swap(dm.at[pl.ds(0, R)], dm.at[pl.ds(R, R)], 2)
    swap_u = swap(part.at[1], far_h, 3)

    def param(row):
        return par_f[row : row + 1, :]

    def project_out():
        branch = dot(o2[0], wo_ref[0:H, :]) + dot(o2[1], wo_ref[H:D, :])
        n2, kept["r2"] = norm(branch + param(shift + 6))
        mid = x_ref[...].astype(F32) + n2 * param(1) + param(shift + 1)
        for s in range(NZ):
            s_s[0, s * R : (s + 1) * R, :] = n2[:, s * C : (s + 1) * C]
        mid_s[...] = mid
        n3, kept["r3"] = norm(mid)
        for s in range(NZ):
            s_s[1, s * R : (s + 1) * R, :] = n3[:, s * C : (s + 1) * C]
        h3[mine, :] = (n3 * param(2) + param(shift + 2)).astype(BF16)
        go(swap_h)

    def hidden(rows):
        for s in range(NZ):
            cols = slice(s * FH, (s + 1) * FH)
            line = param(shift + 8 + s)
            bias = jnp.where(core == 0, line[:, :FH], line[:, FH:])
            u = dot(h3[rows, :], a_ref[:, cols]) + bias
            k = math.sqrt(2.0 / math.pi)
            sq = u * u
            t = jnp.tanh(u * (k + k * 0.044715 * sq))
            half = 0.5 + 0.5 * t
            gate[rows, cols] = (u * half).astype(BF16)
            slope[rows, cols] = (
                half + (0.5 * u) * (1.0 - t * t) * (k + 3.0 * k * 0.044715 * sq)
            ).astype(BF16)

    def hidden_mine():
        hidden(mine)

    def hidden_theirs():
        swap_h.wait_recv()
        hidden(theirs)

    def contract(rows):
        total = dot(gate[rows, 0:FH], b_ref[0])
        for s in range(1, NZ):
            total += dot(gate[rows, s * FH : (s + 1) * FH], b_ref[s])
        return total

    def contract_theirs():
        part[0] = contract(theirs).astype(BF16)
        go(swap_m)

    def contract_mine():
        kept["m"] = contract(mine)

    def last_norm():
        swap_m.wait_recv()
        n4, r4 = norm(kept["m"] + far_m[...].astype(F32) + param(shift + 7))
        act_ref[...] = (mid_s[...] + n4 * param(3) + param(shift + 3)).astype(BF16)
        e = cot_ref[...].astype(F32)
        small_ref[...] = jnp.zeros_like(small_ref)
        small_ref[3:4, :] = rowsum(e * n4)
        small_ref[shift + 3 : shift + 4, :] = rowsum(e)
        dm_low = norm_back(e, n4, r4, param(3)).astype(BF16)
        dm[mine, :] = dm_low
        small_ref[shift + 7 : shift + 8, :] = rowsum(dm_low.astype(F32))
        go(swap_d)

    def unhidden(rows):
        for s in range(NZ):
            cols = slice(s * FH, (s + 1) * FH)
            du[rows, cols] = (
                dot_nt(dm[rows, :], b_ref[s]) * slope[rows, cols].astype(F32)
            ).astype(BF16)

    def unhidden_mine():
        unhidden(mine)

    def arrived():
        if not kept.get("dm"):
            swap_d.wait_recv()
            kept["dm"] = True

    def unhidden_theirs():
        arrived()
        unhidden(theirs)

    def back_theirs():
        part[1] = dot_nt(du[theirs, :], a_ref[...]).astype(BF16)
        go(swap_u)

    def grad_fc2():
        arrived()
        for s in range(NZ):
            cols = slice(s * FH, (s + 1) * FH)
            g_s[0, s] = dot_tn(gate[:, cols], dm[...]).astype(BF16)
        emit(g_s.at[0], g_out.at[0], 6 + NZ)

    FP = FH - FH // 4
    pair = z + 1 - 2 * lax.rem(z, 2)
    goals = (pair, lax.rem(pair + 2, NZ), lax.rem(z + 2, NZ), z)

    def early(j, part):
        n = FP // 4
        return remote(
            g_s.at[0, goals[j], at(part * (FP // 2) + n * (1 - first[part]), n)],
            early_out.at[j, part],
            early_s.at[j, part],
            early_r.at[j, part],
            (near[flip_first[part]], z),
        )

    def early_line(j):
        return remote(
            g_s.at[0, goals[j], pl.ds(FP, FH - FP)],
            early_line_out.at[j],
            early_line_s.at[j],
            early_line_r.at[j],
            (w, pair),
        )

    def early_start():
        for j in range(EARLY):
            for part in range(2):
                go(early(j, part))
        for j in range(EARLY_LINE):
            go(early_line(j))

    def early_done():
        for j in range(EARLY):
            for part in range(2):
                early(j, part).wait_recv()
        for j in range(EARLY_LINE):
            early_line(j).wait_recv()

    def grad_fc1():
        for s in range(NZ):
            cols = slice(s * FH, (s + 1) * FH)
            tile = dot_tn(h3[...], du[:, cols]).astype(BF16)
            low, left = (s // 2) * C, (s % 2) * FH
            for d in range(NZ):
                g_s[1, d, low : low + C, left : left + FH] = tile[d * C : (d + 1) * C, :]
            total = rowsum(du[:, cols].astype(F32))
            row = shift + 8 + s
            small_ref[row : row + 1, 0:FH] = jnp.where(core == 0, total, 0.0)
            small_ref[row : row + 1, FH:] = jnp.where(core == 0, 0.0, total)
        emit(g_s.at[1], g_out.at[1], 7 + NZ)

    def back_mine():
        kept["dh3"] = dot_nt(du[mine, :], a_ref[...])

    def norms_back():
        swap_u.wait_recv()
        dh3 = kept["dh3"] + far_h[...].astype(F32)
        n3 = jnp.concatenate([s_s[1, s * R : (s + 1) * R, :] for s in range(NZ)], 1)
        small_ref[2:3, :] = rowsum(dh3 * n3)
        small_ref[shift + 2 : shift + 3, :] = rowsum(dh3)
        dmid = cot_ref[...].astype(F32) + norm_back(dh3, n3, kept["r3"], param(2))
        for s in range(NZ):
            dmid_ref[s * R : (s + 1) * R, :] = dmid[:, s * C : (s + 1) * C]
        n2 = jnp.concatenate([s_s[0, s * R : (s + 1) * R, :] for s in range(NZ)], 1)
        small_ref[1:2, :] = rowsum(dmid * n2)
        small_ref[shift + 1 : shift + 2, :] = rowsum(dmid)
        da = norm_back(dmid, n2, kept["r2"], param(1)).astype(BF16)
        small_ref[shift + 6 : shift + 7, :] = rowsum(da.astype(F32))
        kept["da"] = da

    def back_out():
        for i in range(2):
            do_ref[i] = dot_nt(kept["da"], wo_ref[i * H : (i + 1) * H, :]).astype(BF16)

    def grad_out():
        for i in range(2):
            go_s[2 * i : 2 * i + 2] = (
                dot_tn(o2[i], kept["da"]).astype(BF16).reshape(2, C, D)
            )
        emit(go_s, go_out, 8 + NZ)

    for act, *where in (
        (start,),
        (w_send, 2, 0),
        (wq_send,),
        (w_come, 2, 0),
        (first_norm,),
        (h1_send, 0),
        (w_double, 2, 0),
        (w_come, 2, 1),
        (w_send, 0, 0),
        (wq_pass,),
        (w_send, 1, 0),
        (wq_swap,),
        (h1_come, 0),
        (wq_wait,),
        (w_double, 2, 1),
        (w_come, 0, 0),
        (project_own,),
        (w_come, 1, 0),
        (project_come, 0),
        (w_double, 1, 0),
        (h1_come, 1),
        (project_come, 1),
        (w_double, 0, 0),
        (w_come, 0, 1),
        (attention, 3),
        (w_come, 1, 1),
        (attention, 2),
        (w_done, 2, 1),
        (attention, 1),
        (w_come, 2, 2),
        (attention, 0),
        (w_double, 2, 2),
        (w_double, 0, 1),
        (w_done, 2, 0),
        (w_done, 2, 2),
        (w_come, 0, 2),
        (w_double, 1, 1),
        (w_double, 0, 2),
        (w_come, 1, 2),
        (w_done, 1, 0),
        (w_done, 0, 0),
        (w_done, 0, 2),
        (emit_l,),
        (wo_swap,),
        (w_double, 1, 2),
        (o_come,),
        (w_done, 0, 1),
        (wo_done,),
        (project_out,),
        (emit_qkv,),
        (w_done, 1, 1),
        (hidden_mine,),
        (hidden_theirs,),
        (w_done, 1, 2),
        (contract_theirs,),
        (contract_mine,),
        (last_norm,),
        (unhidden_mine,),
        (grad_fc2,),
        (early_start,),
        (unhidden_theirs,),
        (back_mine,),
        (back_theirs,),
        (grad_fc1,),
        (norms_back,),
        (grad_out,),
        (back_out,),
        (early_done,),
    ):
        act(*where)
    for ok, copy in relays:

        @pl.when(ok)
        def _():
            copy.wait_send()

    for copy in pending:
        copy.wait_send()
    for copy in outs:
        copy.wait()

    @pl.when(own)
    def _():
        for copy in guarded:
            copy.wait()


def forward(NZ, inputs, cotangent, gain, shift, text_len, w_qkv, w_out, w_fc1, w_fc2):
    R, D = inputs.shape
    C = D // NZ
    FH = w_fc1.shape[1] // (2 * NZ)
    F = NZ * FH
    T = NZ * R
    TP = -(-T // 128) * 128
    H = D // 2
    shape = jax.ShapeDtypeStruct
    buf = pltpu.VMEM
    return pl.pallas_call(
        functools.partial(forward_kernel, NZ),
        out_shape=[
            shape((T, D), BF16),
            shape((TP, H), BF16),
            shape((T, H), BF16),
            shape((T, H), BF16),
            shape((D, 3 * H), BF16),
            shape((16, D), F32),
            shape((2, T, 4 * TP), BF16),
            shape((2, 4, 8, TP), F32),
            shape((R, D), BF16),
            shape((T, C), F32),
            shape((2, R, H), BF16),
            shape((2, NZ, FH, D), BF16),
            shape((NZ, C, D), BF16),
            shape((EARLY, 2, (FH - FH // 4) // 4, D), BF16),
            shape((EARLY_LINE, FH // 4, D), BF16),
            shape((16, D), F32),
        ],
        in_specs=[VMEM, VMEM, VMEM, SMEM, VMEM, ANY, ANY, ANY, ANY],
        out_specs=[ANY] * 8 + [VMEM, VMEM, VMEM, ANY, ANY, ANY, ANY, VMEM],
        scratch_shapes=[
            buf((16, C), BF16),
            buf((NZ, 16, C), BF16),
            buf((16, D), F32),
            buf((2, C, 3 * H), BF16),
            buf((D, 3 * H), BF16),
            buf((D, F), BF16),
            buf((NZ, FH, D), BF16),
            buf((D, D), BF16),
            buf((T, D), BF16),
            buf((TP, H), BF16),
            buf((T, H), BF16),
            buf((T, H), BF16),
            buf((2, C, TP), BF16),
            buf((2, T, QUERIES), F32),
            buf((C, QUERIES), F32),
            buf((2, 4, 8, TP), F32),
            buf((R, D), F32),
            buf((2, 4 * R, F), BF16),
            buf((TP, H), BF16),
            buf((2, R, H), BF16),
            buf((2 * R, D), BF16),
            buf((2 * R, D), BF16),
            buf((2, R, D), BF16),
            buf((R, D), BF16),
            buf((R, D), BF16),
            buf((2, NZ, FH, D), BF16),
            buf((NZ, C, D), BF16),
            DMA((4 * NZ + 4,)),
            DMA((NZ,)),
            DMA((NZ,)),
            DMA((NZ,)),
            DMA((NZ,)),
            DMA((NZ, 4)),
            DMA((NZ, 4)),
            DMA((2, NZ)),
            DMA((2, NZ)),
            DMA((3, 2, 2, NZ)),
            DMA((3, 2, 2, NZ)),
            DMA((3, 2, 2, NZ)),
            DMA((3, 2, 2, NZ)),
            DMA((3, 2, 2, NZ)),
            DMA((3, 2, 2, NZ)),
            DMA((NZ,)),
            DMA((NZ,)),
            DMA((NZ,)),
            DMA((NZ,)),
            DMA((10 + NZ,)),
            DMA((2,)),
            DMA((4,)),
            DMA((4,)),
            DMA((EARLY, 2)),
            DMA((EARLY, 2)),
            DMA((EARLY_LINE,)),
            DMA((EARLY_LINE,)),
        ],
        compiler_params=pltpu.CompilerParams(
            collective_id=0, has_side_effects=True, vmem_limit_bytes=62 * 2**20
        ),
    )(inputs, gain, shift, text_len, cotangent, w_qkv, w_out, w_fc1, w_fc2)


def reduce_kernel(
    NZ,
    x_ref,
    dmid_hbm,
    par_ref,
    small_in,
    do_ref,
    wq_hbm,
    q_hbm,
    k_hbm,
    v_hbm,
    l_hbm,
    h1_hbm,
    p_hbm,
    g_hbm,
    go_hbm,
    early_hbm,
    early_line_hbm,
    dx_ref,
    g_out,
    go_out,
    gq_out,
    small_out,
    wq_ref,
    q_ref,
    k_ref,
    v_ref,
    l_ref,
    p_s,
    g,
    go_far,
    go_w,
    gq_far,
    gq_w,
    r1,
    r1_o,
    r1_q,
    r2,
    r2_o,
    r2_q,
    rz,
    rz_o,
    rz_z,
    r1_z,
    r2_z,
    w_z,
    f_z,
    f_g,
    f_o,
    f_q,
    do_all,
    do_st,
    q_st,
    ds_s,
    dq_t,
    k_t,
    dk_f,
    dv_f,
    dqkv,
    dh,
    rel,
    s_f,
    s_b,
    s_z,
    s_p,
    s_g,
    load_sem,
    early_sem,
    p_sem,
    do_s,
    do_r,
    pair_s,
    pair_r,
    s1_s,
    s1_r,
    s2_s,
    s2_r,
    c1_s,
    c1_r,
    c2_s,
    c2_r,
    z_s,
    z_r,
    zl_s,
    zl_r,
    g_s,
    g_r,
    sib_s,
    sib_r,
    ru_s,
    ru_r,
    sz_s,
    sz_r,
    sp_s,
    sp_r,
    out_sem,
):
    R, D = x_ref.shape
    C = D // NZ
    T = NZ * R
    FH = g.shape[2]
    H = D // 2
    w, z, core, x, y = place()
    lower, upper = NZ // 2 - 1, NZ // 2
    own = (z == lower) | (z == upper)
    side = lax.div(z, NZ // 2)
    partner = NZ - 1 - z
    outer = (NZ - 1) * side
    near = {j: flips(w, core, x, y, j) for j in range(1, GROUP)}
    zto = [lax.rem(z + j, NZ) for j in range(NZ)]
    zfrom = [lax.rem(z + NZ - j, NZ) for j in range(NZ)]
    hops = range(1, NZ)
    pending = []

    def go(copy):
        copy.start()
        pending.append(copy)

    guarded = []

    def when(ok, *copies):
        for copy in copies:
            guarded.append((ok, copy))

        @pl.when(ok)
        def _():
            for copy in copies:
                copy.start()

    pair = z + 1 - 2 * lax.rem(z, 2)
    across = lax.rem(z + 2, NZ)
    goals = (pair, lax.rem(pair + 2, NZ), across, z)
    chunks = [(kind, j) for j in range(NZ) for kind in range(2)]
    loads = [
        pltpu.make_async_copy(
            g_hbm.at[kind, goals[j]], g.at[kind, goals[j]], load_sem.at[i]
        )
        for i, (kind, j) in enumerate(chunks)
    ]
    CH = C // 2
    loads.append(
        pltpu.make_async_copy(
            go_hbm.at[:, at(core * CH, CH)], go_w, load_sem.at[len(chunks)]
        )
    )
    for copy in loads:
        copy.start()
    spans = query_blocks(T)
    visits = [(n, i) for n in range(2) for i in reversed(range(len(spans)))]

    def load_p(n):
        group, i = visits[n]
        first_query, size, keys = spans[i]
        return pltpu.make_async_copy(
            p_hbm.at[group, pl.ds(0, keys), pl.ds(4 * first_query, 4 * size)],
            p_s.at[n % 2, pl.ds(0, keys), pl.ds(0, 4 * size)],
            p_sem.at[n % 2],
        )

    load_h1 = pltpu.make_async_copy(h1_hbm, ds_s, load_sem.at[len(chunks) + 1])

    inner_loads = [
        pltpu.make_async_copy(src, dst, load_sem.at[len(chunks) + 2 + i])
        for i, (src, dst) in enumerate(
            ((v_hbm, v_ref), (q_hbm, q_ref), (k_hbm, k_ref), (l_hbm, l_ref), (wq_hbm, wq_ref))
        )
    ]

    @pl.when(own)
    def _():
        for copy in inner_loads[:4]:
            copy.start()
        load_p(0).start()
        load_p(1).start()
        inner_loads[4].start()

    meet([(w, zto[j]) for j in hops] + [(near[j], z) for j in range(1, GROUP)])

    first = (x, y)
    second = (y, x)
    flip_first = (2, 4)
    flip_second = (4, 2)
    FP = FH - FH // 4
    half = (FP // 4, FP // 4, C // 4, C // 4, FH // 8)
    side_one = {2: r1_o, 3: r1_q, 4: r1_z}
    side_two = {2: r2_o, 3: r2_q, 4: r2_z}
    side_work = {2: go_w, 3: gq_w, 4: w_z}
    final = {0: f_g.at[0], 1: f_g.at[1], 2: f_o, 3: f_q, 4: f_z}

    def out(kind, which):
        if kind < 2:
            return g_out.at[kind, which, pl.ds(0, FP)]
        if kind == 4:
            return g_out.at[:, which, pl.ds(FP, FH - FP)]
        return (go_out, gq_out)[kind - 2].at[which]

    outs = []

    def index(kind, part, start, n):
        if kind < 2:
            return at(part * (FP // 2) + start, n), slice(None)
        width = side_work[kind].shape[2] // 2
        return at(start, n), pl.ds(part * width, width)

    def kept(kind, part):
        return half[kind] * first[part] + (half[kind] // 2) * second[part]

    seen = set()

    def loaded(c):
        if c not in seen:
            seen.add(c)
            loads[c].wait()

    def chunk_one(c, part):
        kind, j = chunks[c]
        n = half[kind]
        return remote(
            g.at[(kind, goals[j]) + index(kind, part, n * (1 - first[part]), n)],
            r1.at[c, part],
            c1_s.at[c, part],
            c1_r.at[c, part],
            (near[flip_first[part]], z),
        )

    def chunk_two(c, part):
        kind, j = chunks[c]
        n = half[kind] // 2
        start = 2 * n * first[part] + n * (1 - second[part])
        return remote(
            g.at[(kind, goals[j]) + index(kind, part, start, n)],
            r2.at[c, part],
            c2_s.at[c, part],
            c2_r.at[c, part],
            (near[flip_second[part]], z),
        )

    fetched = {
        2 * j: pltpu.make_async_copy(early_hbm.at[j], r1.at[2 * j], early_sem.at[j])
        for j in range(EARLY)
    }
    fetched_line = [
        pltpu.make_async_copy(early_line_hbm.at[j], rz_z.at[j, 0], early_sem.at[EARLY + j])
        for j in range(EARLY_LINE)
    ]
    for copy in (*fetched.values(), *fetched_line):
        copy.start()

    def launch(c):
        loaded(c)
        if c not in fetched:
            for part in range(2):
                go(chunk_one(c, part))

    def reduce_one(c):
        kind, j = chunks[c]
        n = half[kind]
        if c in fetched:
            fetched[c].wait()
        for part in range(2):
            if c not in fetched:
                chunk_one(c, part).wait_recv()
            idx = (kind, goals[j]) + index(kind, part, n * first[part], n)
            g[idx] += r1[c, part]
            go(chunk_two(c, part))

    def reduce_two(c):
        kind, j = chunks[c]
        n = half[kind] // 2
        for part in range(2):
            chunk_two(c, part).wait_recv()
            idx = (kind, goals[j]) + index(kind, part, kept(kind, part), n)
            g[idx] += r2[c, part]
            if j < 2:
                go(pairwise(kind, part, j))
            elif j == 2:
                cross(kind, part)

    def step_one(kind, part):
        n = half[kind]
        return remote(
            side_work[kind].at[(slice(None),) + index(kind, part, n * (1 - first[part]), n)],
            side_one[kind].at[part],
            s1_s.at[kind - 2, part],
            s1_r.at[kind - 2, part],
            (near[flip_first[part]], z),
        )

    def step_two(kind, part):
        n = half[kind] // 2
        start = 2 * n * first[part] + n * (1 - second[part])
        return remote(
            side_work[kind].at[(slice(None),) + index(kind, part, start, n)],
            side_two[kind].at[part],
            s2_s.at[kind - 2, part],
            s2_r.at[kind - 2, part],
            (near[flip_second[part]], z),
        )

    def add_one(kind):
        n = half[kind]
        for part in range(2):
            arrival, onward = step_one(kind, part), step_two(kind, part)
            idx = (slice(None),) + index(kind, part, n * first[part], n)

            def add():
                arrival.wait_recv()
                side_work[kind][idx] += side_one[kind][part]

            if kind != 3:
                add()
                go(onward)
            else:
                pl.when(own)(add)
                when(own, onward)

    def add_two(kind):
        n = half[kind] // 2
        for part in range(2):
            arrival = step_two(kind, part)
            idx = (slice(None),) + index(kind, part, kept(kind, part), n)

            def add():
                arrival.wait_recv()
                side_work[kind][idx] += side_two[kind][part]

            if kind != 3:
                add()
                for j in range(2 if kind == 2 else 0):
                    go(pairwise(kind, part, j))
            else:
                pl.when(own)(add)
                when(own, *[along(part, j, side) for j in hops])

    def held(kind, part, j):
        idx = (goals[j],) + index(kind, part, kept(kind, part), half[kind] // 2)
        return (g, (kind,) + idx) if kind < 2 else (go_w, idx)

    def pairwise(kind, part, j):
        ref, idx = held(kind, part, j)
        dst = rz.at[kind, part, j] if kind < 2 else rz_o.at[part, j]
        return remote(
            ref.at[idx], dst, z_s.at[kind, part, j], z_r.at[kind, part, j], (w, pair)
        )

    def crosswise(kind, part):
        ref, idx = held(kind, part, 2)
        dst = rz.at[kind, part, 2] if kind < 2 else rz_o.at[part, 2]
        return remote(
            ref.at[idx], dst, z_s.at[kind, part, 2], z_r.at[kind, part, 2], (w, across)
        )

    def cross(kind, part):
        pairwise(kind, part, 1).wait_recv()
        ref, idx = held(kind, part, 2)
        ref[idx] += rz[kind, part, 1] if kind < 2 else rz_o[part, 1]
        go(crosswise(kind, part))

    def block(j):
        return g.at[:, goals[j], pl.ds(FP, FH - FP)]

    def line_copy_z(j):
        if j == 2:
            return remote(block(2), rz_z.at[2], zl_s.at[2], zl_r.at[2], (w, across))
        if j < EARLY_LINE:
            src, dst = g.at[1, goals[j], pl.ds(FP, FH - FP)], rz_z.at[j, 1]
        else:
            src, dst = block(j), rz_z.at[j]
        return remote(src, dst, zl_s.at[j], zl_r.at[j], (w, pair))

    def rows_start():
        for j in range(2):
            for kind in range(2):
                loaded(2 * j + kind)
            go(line_copy_z(j))

    def line_arrived(j):
        line_copy_z(j).wait_recv()
        if j < EARLY_LINE:
            fetched_line[j].wait()

    def rows_cross():
        line_arrived(1)
        for kind in range(2):
            loaded(2 * 2 + kind)
        block(2)[...] += rz_z[1]
        go(line_copy_z(2))

    def rows_plane():
        line_arrived(0)
        line_copy_z(2).wait_recv()
        for kind in range(2):
            loaded(2 * 3 + kind)
        w_z[...] = (
            block(3)[...].astype(F32) + rz_z[0].astype(F32) + rz_z[2].astype(F32)
        ).astype(BF16)
        for part in range(2):
            go(step_one(4, part))

    def cross_out():
        for part in range(2):
            cross(2, part)

    def along(part, j, source):
        idx = index(3, part, kept(3, part), half[3] // 2)
        return remote(
            gq_w.at[(zto[j],) + idx],
            f_q.at[(source,) + idx],
            z_s.at[3, part, j],
            z_r.at[3, part, source],
            (w, zto[j]),
        )

    def add_line(kind):
        for part in range(2):
            idx = index(kind, part, kept(kind, part), half[kind] // 2)
            if kind < 3:
                pairwise(kind, part, 0).wait_recv()
                crosswise(kind, part).wait_recv()
                ref, own = held(kind, part, 3)
                far = rz.at[kind] if kind < 2 else rz_o
                total = (
                    ref[own].astype(F32)
                    + far[part, 0].astype(F32)
                    + far[part, 2].astype(F32)
                ).astype(BF16)
                if kind < 2:
                    f_g[(kind,) + idx] = total
                else:
                    f_o[idx] = total
            elif kind == 4:
                f_z[(slice(None),) + idx] = w_z[(slice(None),) + idx]
            else:
                for i in range(2):
                    arrival = along(part, 1, i)

                    @pl.when(z != lower + i)
                    def _():
                        arrival.wait_recv()

                    @pl.when(z == lower + i)
                    def _():
                        f_q[(i,) + idx] = gq_w[(lower + i,) + idx]
            go(share_one(kind, part))

    def region(kind, part, start, n):
        idx = index(kind, part, start, n)
        if kind > 2:
            idx = (slice(None),) + idx
        return final[kind].at[idx]

    def share_one(kind, part):
        ref = region(kind, part, kept(kind, part), half[kind] // 2)
        return remote(
            ref,
            ref,
            g_s.at[kind, part, 0],
            g_r.at[kind, part, 0],
            (near[flip_second[part]], z),
        )

    def share_two(kind, part):
        ref = region(kind, part, half[kind] * first[part], half[kind])
        return remote(
            ref,
            ref,
            g_s.at[kind, part, 1],
            g_r.at[kind, part, 1],
            (near[flip_first[part]], z),
        )

    def relayed(kind):
        for part in range(2):
            n = half[kind] // 2
            start = half[kind] * first[part] + n * (1 - second[part])
            ref = region(kind, part, start, n)
            remote(
                ref,
                ref,
                g_s.at[kind, part, 0],
                g_r.at[kind, part, 0],
                (near[flip_second[part]], z),
            ).wait_recv()
            go(share_two(kind, part))

    def shared(kind):
        for part in range(2):
            ref = region(kind, part, half[kind] * (1 - first[part]), half[kind])
            remote(
                ref,
                ref,
                g_s.at[kind, part, 1],
                g_r.at[kind, part, 1],
                (near[flip_first[part]], z),
            ).wait_recv()
        go(
            remote(
                final[kind], out(kind, core), sib_s.at[kind], sib_r.at[kind], (near[1], z)
            )
        )
        copy = pltpu.make_async_copy(final[kind], out(kind, core), out_sem.at[kind])
        copy.start()
        outs.append(copy)

    pair_o = remote(
        go_hbm.at[:, at((1 - core) * CH, CH)], go_far, pair_s.at[NZ], pair_r.at[NZ], (near[1], z)
    )

    def gq_part(d, half_of):
        return p_s.at[d // 2, at((d % 2) * C + half_of * CH, CH)]

    pair_q = [
        remote(gq_part(d, 1 - core), gq_far.at[d], pair_s.at[d], pair_r.at[d], (near[1], z))
        for d in range(NZ)
    ]

    def do_copy(i, block, rows):
        return remote(
            do_ref.at[i], do_all.at[rows], do_s.at[i], do_r.at[block], (w, jnp.int32(lower + i))
        )

    def do_send():
        for i in range(2):
            when(z != lower + i, do_copy(i, z, at(z * R, R)))

            @pl.when(z == lower + i)
            def _():
                do_all[(lower + i) * R : (lower + i + 1) * R, :] = do_ref[i]
                do_all[T:, :] = jnp.zeros((do_all.shape[0] - T, H), BF16)

    def do_wait(b):
        arrival = do_copy(0, b, pl.ds(b * R, R))

        @pl.when(own & (z != b))
        def _():
            arrival.wait_recv()

    def pair_out():
        loads[len(chunks)].wait()
        go(pair_o)

    def pair_out_done():
        pair_o.wait_recv()
        go_w[...] += go_far[...]
        for part in range(2):
            go(step_one(2, part))

    def visit(n):
        group, i = visits[n]
        first_query, size, keys = spans[i]
        queries = slice(first_query, first_query + size)
        cols = slice(group * C, (group + 1) * C)
        slot = n % 2
        load_p(n).wait()
        if n == 0:
            for copy in inner_loads:
                copy.wait()
        if i == len(spans) - 1:
            k_t[:, :T] = jnp.transpose(k_ref[:, cols].astype(F32)).astype(BF16)
        for pair_of in range(0, 4, 2):
            two = []
            for h in (pair_of, pair_of + 1):
                pick = lanes(size, C, h).astype(BF16)
                here = slice(h * size, (h + 1) * size)
                do_h = do_all[queries, cols] * pick
                q_st[here, :] = q_ref[queries, cols] * pick
                share = l_ref[group, h, :, queries]
                do_st[here, :] = (do_h.astype(F32) * jnp.transpose(share)[:, 0:1]).astype(BF16)
                two.append(do_h)
            both = dot_nt(v_ref[:keys, cols], jnp.concatenate(two, 0))
            for t in range(2):
                h = pair_of + t
                here = slice(h * size, (h + 1) * size)
                p = p_s[slot, :keys, here].astype(F32) * l_ref[group, h, 0:1, queries]
                product = p * both[:, t * size : (t + 1) * size]
                ds = (product - p * jnp.sum(product, 0, keepdims=True)).astype(BF16)
                ds_s[:keys, here] = ds
                rows = slice(h * (C // 4), (h + 1) * (C // 4))
                dq_t[rows, :size] = dot(k_t[rows, :keys], ds)
        dv = dot(p_s[slot, :keys, : 4 * size], do_st[: 4 * size, :])
        dk = dot(ds_s[:keys, : 4 * size], q_st[: 4 * size, :])
        if i == len(spans) - 1:
            dv_f[...] = dv
            dk_f[...] = dk
        else:
            dv_f[:keys, :] += dv
            dk_f[:keys, :] += dk
        if n + 2 < len(visits):
            load_p(n + 2).start()
        ready = slice(first_query, keys)
        kept_rows = min(size, T - first_query)
        dq = jnp.transpose(dq_t[:, :size])[:kept_rows, :] * 0.125
        dqkv[first_query : first_query + kept_rows, cols] = dq.astype(BF16)
        dqkv[ready, H + group * C : H + (group + 1) * C] = (dk_f[ready, :] * 0.125).astype(BF16)
        dqkv[ready, 2 * H + group * C : 2 * H + (group + 1) * C] = dv_f[ready, :].astype(BF16)

    def visit_block(group, b):
        @pl.when(own)
        def _():
            for n, (of, i) in enumerate(visits):
                if of == group and (i == b or (b == NZ - 1 and i > b)):
                    visit(n)

    def heads(b):
        visit_block(0, b)

    def keys(b):
        visit_block(1, b)

    def partial(d):
        @pl.when(own)
        def _():
            dh[d] = dot_nt(dqkv[d * R : (d + 1) * R, :], wq_ref[...]).astype(BF16)

    def hand(d, slot):
        return remote(
            dh.at[d], rel.at[slot], ru_s.at[slot], ru_r.at[slot], (w, jnp.int32(partner))
        )

    def hand_over(d):
        holder = upper if d <= lower else lower
        slot = 0 if lower <= d <= upper else 1
        when(z == holder, hand(d, slot))

    outward = remote(dh.at[outer], rel.at[0], ru_s.at[2], ru_r.at[2], (w, outer))

    def hand_out():
        arrival = hand(0, 1)

        @pl.when(own)
        def _():
            arrival.wait_recv()
            dh[outer] += rel[1]

        when(own, outward)

    load_dmid = pltpu.make_async_copy(dmid_hbm, dk_f, load_sem.at[len(chunks) + 7])

    def fetch_h1():
        load_dmid.start()

        @pl.when(own)
        def _():
            load_h1.start()

    def grad_qkv():
        for d in range(NZ):
            s_f[d] = small_in[:, d * C : (d + 1) * C]

        @pl.when(own)
        def _():
            load_h1.wait()
            for d in range(NZ):
                p_s[d // 2, (d % 2) * C : (d % 2 + 1) * C, :] = dot_tn(
                    ds_s[:, d * C : (d + 1) * C], dqkv[...]
                ).astype(BF16)
            for row, start in ((8, 0), (9, 2 * H)):
                total = rowsum(dqkv[:, start : start + H].astype(F32))
                for half_of in range(2):
                    s_f[2 * side + half_of, row : row + 1, :] = total[
                        :, half_of * C : (half_of + 1) * C
                    ]

        when(own, *pair_q)

    def pair_qkv_done():
        @pl.when(own)
        def _():
            for d in range(NZ):
                pair_q[d].wait_recv()
                gq_w[d] = gq_part(d, core)[...] + gq_far[d]

        when(own, *[step_one(3, part) for part in range(2)])

    def line_copy(j):
        return remote(s_b.at[zto[j]], s_z.at[j], sz_s.at[j], sz_r.at[j], (w, zto[j]))

    def plane_copy(j):
        return remote(s_p, s_g.at[j], sp_s.at[j], sp_r.at[j], (near[j], z))

    def input_grad():
        inner = hand(0, 0)

        @pl.when(own)
        def _():
            inner.wait_recv()
            rel[0] += dh[z]

        @pl.when(jnp.logical_not(own))
        def _():
            outward.wait_recv()

        dh1 = rel[0].astype(F32)
        n1, inverse = norm(x_ref[...].astype(F32))
        load_dmid.wait()
        dmid = jnp.concatenate([dk_f[s * R : (s + 1) * R, :] for s in range(NZ)], 1)
        dx_ref[...] = (dmid + norm_back(dh1, n1, inverse, par_ref[0:1, :])).astype(BF16)
        gain = rowsum(dh1 * n1)
        shift = rowsum(dh1)
        for d in range(NZ):
            s_f[d, 0:1, :] = gain[:, d * C : (d + 1) * C]
            s_f[d, 4:5, :] = shift[:, d * C : (d + 1) * C]
        s_b[...] = s_f[...].astype(BF16)
        for j in hops:
            go(line_copy(j))

    def small_line():
        total = s_f[z]
        for j in hops:
            line_copy(j).wait_recv()
            total += s_z[j].astype(F32)
        small_out[...] = total
        s_p[...] = total.astype(BF16)
        for j in range(1, GROUP):
            go(plane_copy(j))

    def small_plane():
        total = small_out[...]
        for j in range(1, GROUP):
            plane_copy(j).wait_recv()
            total += s_g[j].astype(F32)
        small_out[...] = total

    for act, *where in (
        (do_send,),
        (launch, 0),
        (pair_out,),
        (launch, 1),
        (pair_out_done,),
        (launch, 2),
        (reduce_one, 0),
        (launch, 3),
        (rows_start,),
        (add_one, 2),
        (launch, 4),
        (do_wait, 2),
        (do_wait, 1),
        (launch, 5),
        (do_wait, 3),
        (heads, 3),
        (heads, 2),
        (do_wait, 0),
        (heads, 1),
        (reduce_one, 1),
        (reduce_one, 2),
        (launch, 6),
        (rows_cross,),
        (add_two, 2),
        (heads, 0),
        (keys, 3),
        (reduce_one, 4),
        (keys, 2),
        (cross_out,),
        (reduce_one, 3),
        (reduce_two, 2),
        (keys, 1),
        (keys, 0),
        (partial, 3),
        (reduce_one, 6),
        (reduce_two, 1),
        (fetch_h1,),
        (launch, 7),
        (grad_qkv,),
        (reduce_one, 5),
        (reduce_two, 4),
        (reduce_one, 7),
        (hand_over, 3),
        (partial, 0),
        (hand_over, 0),
        (add_line, 2),
        (pair_qkv_done,),
        (rows_plane,),
        (reduce_two, 0),
        (reduce_two, 6),
        (reduce_two, 3),
        (partial, 2),
        (reduce_two, 7),
        (add_line, 0),
        (reduce_two, 5),
        (add_one, 3),
        (relayed, 2),
        (add_one, 4),
        (relayed, 0),
        (partial, 1),
        (add_two, 3),
        (hand_over, 1),
        (hand_over, 2),
        (hand_out,),
        (add_two, 4),
        (add_line, 4),
        (add_line, 1),
        (relayed, 4),
        (add_line, 3),
        (shared, 2),
        (shared, 4),
        (relayed, 1),
        (shared, 0),
        (relayed, 3),
        (input_grad,),
        (shared, 1),
        (small_line,),
        (shared, 3),
        (small_plane,),
    ):
        act(*where)
    for kind in range(5):
        remote(
            final[kind], out(kind, 1 - core), sib_s.at[kind], sib_r.at[kind], (near[1], z)
        ).wait_recv()
    for ok, copy in guarded:
        pl.when(ok)(copy.wait_send)
    for copy in pending:
        copy.wait_send()
    for copy in outs:
        copy.wait()


def reduce(NZ, inputs, dmid, par, small, do, wq, q, k, v, share, h1, p, g, go, early, early_line):
    R, D = inputs.shape
    C = D // NZ
    H = D // 2
    T = NZ * R
    TP = q.shape[0]
    FH = g.shape[2]
    FP = FH - FH // 4
    shape = jax.ShapeDtypeStruct
    buf = pltpu.VMEM
    return pl.pallas_call(
        functools.partial(reduce_kernel, NZ),
        out_shape=[
            shape((R, D), BF16),
            shape((2, 2, FH, D), BF16),
            shape((2, C // 2, D), BF16),
            shape((2, 2, C // 2, 3 * H), BF16),
            shape((16, C), F32),
        ],
        in_specs=[VMEM, ANY, VMEM, VMEM, VMEM] + [ANY] * 11,
        out_specs=[VMEM, ANY, ANY, ANY, VMEM],
        scratch_shapes=[
            buf(wq.shape, BF16),
            buf(q.shape, BF16),
            buf(k.shape, BF16),
            buf(v.shape, BF16),
            buf(share.shape, F32),
            buf((2, T, 3 * H), BF16),
            buf((2, NZ, FH, D), BF16),
            buf((NZ, C // 2, D), BF16),
            buf((NZ, C // 2, D), BF16),
            buf((NZ, C // 2, 3 * H), BF16),
            buf((NZ, C // 2, 3 * H), BF16),
            buf((2 * NZ, 2, FP // 4, D), BF16),
            buf((2, NZ, C // 4, D // 2), BF16),
            buf((2, NZ, C // 4, 3 * H // 2), BF16),
            buf((2 * NZ, 2, FP // 8, D), BF16),
            buf((2, NZ, C // 8, D // 2), BF16),
            buf((2, NZ, C // 8, 3 * H // 2), BF16),
            buf((2, 2, NZ - 1, FP // 8, D), BF16),
            buf((2, NZ - 1, C // 8, D // 2), BF16),
            buf((3, 2, FH - FP, D), BF16),
            buf((2, 2, FH // 8, D // 2), BF16),
            buf((2, 2, FH // 16, D // 2), BF16),
            buf((2, FH - FP, D), BF16),
            buf((2, FH - FP, D), BF16),
            buf((2, FP, D), BF16),
            buf((C // 2, D), BF16),
            buf((2, C // 2, 3 * H), BF16),
            buf((TP, H), BF16),
            buf((4 * QUERIES, C), BF16),
            buf((4 * QUERIES, C), BF16),
            buf((T, 4 * QUERIES), BF16),
            buf((C, QUERIES), F32),
            buf((C, TP), BF16),
            buf((T, C), F32),
            buf((T, C), F32),
            buf((T, 3 * H), BF16),
            buf((NZ, R, D), BF16),
            buf((2, R, D), BF16),
            buf((NZ, 16, C), F32),
            buf((NZ, 16, C), BF16),
            buf((NZ, 16, C), BF16),
            buf((16, C), BF16),
            buf((GROUP, 16, C), BF16),
            DMA((2 * NZ + 8,)),
            DMA((EARLY + EARLY_LINE,)),
            DMA((2,)),
            DMA((2,)),
            DMA((NZ,)),
            DMA((NZ + 1,)),
            DMA((NZ + 1,)),
            DMA((3, 2)),
            DMA((3, 2)),
            DMA((3, 2)),
            DMA((3, 2)),
            DMA((2 * NZ, 2)),
            DMA((2 * NZ, 2)),
            DMA((2 * NZ, 2)),
            DMA((2 * NZ, 2)),
            DMA((4, 2, NZ)),
            DMA((4, 2, NZ)),
            DMA((3,)),
            DMA((3,)),
            DMA((5, 2, 2)),
            DMA((5, 2, 2)),
            DMA((5,)),
            DMA((5,)),
            DMA((3,)),
            DMA((3,)),
            DMA((NZ,)),
            DMA((NZ,)),
            DMA((GROUP,)),
            DMA((GROUP,)),
            DMA((5,)),
        ],
        compiler_params=pltpu.CompilerParams(
            collective_id=2, has_side_effects=True, vmem_limit_bytes=63 * 2**20
        ),
    )(inputs, dmid, par, small, do, wq, q, k, v, share, h1, p, g, go, early, early_line)


def widen_kernel(fc2, fc1, out, qkv, act, dx, small, d_fc2, d_fc1, d_out, d_qkv, d_act, d_dx, d_gain, d_shift):
    step = pl.program_id(0)
    d_fc2[...] = fc2[0, 0].astype(F32)
    d_fc1[...] = fc1[0, 0].astype(F32)
    d_out[...] = out[0].astype(F32)
    d_act[...] = act[...]
    d_dx[...] = dx[...]
    d_gain[...] = small[0:4, :]
    d_shift[...] = small[4:16, :]
    width = qkv.shape[3] // 3
    for t in range(3):
        cols = at(t * (d_qkv.shape[1] // 3) + lax.rem(step, 2) * width, width, 128)
        d_qkv[:, cols] = qkv[0, 0, :, t * width : (t + 1) * width].astype(F32)


def widen(g, go, gq, act, dx, small):
    FH, D = g.shape[2:]
    CH = gq.shape[2]
    C = 2 * CH
    NZ = D // C
    R = act.shape[0]
    steps = 2 * NZ
    part = D // steps
    shape = jax.ShapeDtypeStruct
    return pl.pallas_call(
        widen_kernel,
        grid=(steps,),
        out_shape=[
            shape((2 * FH, D), F32),
            shape((C, 2 * NZ * FH), F32),
            shape((C, D), F32),
            shape((C, 3 * D), F32),
            shape((R, D), BF16),
            shape((R, D), BF16),
            shape((4, C), F32),
            shape((12, C), F32),
        ],
        in_specs=[
            pl.BlockSpec((1, 1, 2 * FH // steps, D), lambda i: (0, i // NZ, i % NZ, 0)),
            pl.BlockSpec((1, 1, C, FH), lambda i: (1, i % 2, i // 2 // 2, i // 2 % 2)),
            pl.BlockSpec((1, C // steps, D), lambda i: (i // NZ, i % NZ, 0)),
            pl.BlockSpec(
                (1, 1, CH // 2, gq.shape[3]), lambda i: (i // 4, i % 2, i // 2 % 2, 0)
            ),
            pl.BlockSpec((R, part), lambda i: (0, i)),
            pl.BlockSpec((R, part), lambda i: (0, i)),
            pl.BlockSpec((16, C), lambda i: (0, 0)),
        ],
        out_specs=[
            pl.BlockSpec((2 * FH // steps, D), lambda i: (i, 0)),
            pl.BlockSpec((C, FH), lambda i: (0, i)),
            pl.BlockSpec((C // steps, D), lambda i: (i, 0)),
            pl.BlockSpec((CH // 2, 3 * D), lambda i: (i // 2, 0)),
            pl.BlockSpec((R, part), lambda i: (0, i)),
            pl.BlockSpec((R, part), lambda i: (0, i)),
            pl.BlockSpec((4, C), lambda i: (0, 0)),
            pl.BlockSpec((12, C), lambda i: (0, 0)),
        ],
        compiler_params=pltpu.CompilerParams(vmem_limit_bytes=62 * 2**20),
    )(g, g, go, gq, act, dx, small)


def shards(NZ, W, inputs, w_qkv, w_out, w_fc1, w_fc2, norm_gain, shifts, text_len, cotangent):
    R, D = inputs.shape[1:]
    C = D // NZ
    FF = w_fc1.shape[1]
    FH = FF // (2 * NZ)
    h1, q, k, v, wq, par_f, p, share, act, dmid, do, g, go, early, early_line, small = forward(
        NZ, inputs[0], cotangent[0], norm_gain, shifts, text_len, w_qkv, w_out, w_fc1, w_fc2
    )
    dx, g, go, gq, small = reduce(
        NZ, inputs[0], dmid, par_f, small, do, wq, q, k, v, share, h1, p, g, go, early, early_line
    )
    fc2, fc1, out, qkv, act, dx, gain, shift = widen(g, go, gq, act, dx, small)
    grads = (qkv, out, fc1, fc2, gain, shift)
    if W > GROUP:
        groups = [list(range(i, W, GROUP)) for i in range(GROUP)]
        grads = lax.psum(grads, "wide", axis_index_groups=groups)
    return (act[None], dx[None]) + tuple(grads)


def solution(mesh):
    return jax.shard_map(
        functools.partial(shards, mesh.shape["narrow"], mesh.shape["wide"]),
        mesh=mesh,
        in_specs=(
            P("wide", "narrow", None),
            P("narrow", None),
            P("narrow", None),
            P("narrow", None),
            P("narrow", None),
            P(None, "narrow"),
            P(None, "narrow"),
            P("wide"),
            P("wide", "narrow", None),
        ),
        out_specs=(
            P("wide", "narrow", None),
            P("wide", "narrow", None),
            P("narrow", None),
            P("narrow", None),
            P("narrow", None),
            P("narrow", None),
            P(None, "narrow"),
            P(None, "narrow"),
        ),
        check_vma=False,
    )
```
